32 devices in a mesh: grp: 2 (over x), row: 8 (over z, y), node: 2 (over core).
Axes of the slice: x: 2, y: 2, z: 4, core: 2. Of those that a mesh axis runs over, the one named last changes fastest.
Arguments:
- pair_rep: bfloat16 [384, 192, 128], P(('grp', 'row', 'node')), parts along dimension 0, may hold values from -6 to 6
- length: int32 [2], P('grp'), parts along dimension 0, may hold values from 96 to 192
- ln_pair: float32 [128], replicated, may hold values from 0.1 to 1.9
- tri_in: bfloat16 [4, 128, 128], replicated, may hold values from -0.5 to 0.5
- tri_gate: bfloat16 [128, 128], replicated, may hold values from -0.5 to 0.5
- ln_hidden: float32 [128], replicated, may hold values from 0.1 to 1.9
- tri_out: bfloat16 [128, 128], replicated, may hold values from -0.5 to 0.5
- ln_att: float32 [128], replicated, may hold values from 0.1 to 1.9
- att_q: bfloat16 [128, 128], replicated, may hold values from -3 to 3
- att_k: bfloat16 [128, 128], replicated, may hold values from -3 to 3
- att_v: bfloat16 [128, 128], replicated, may hold values from -0.5 to 0.5
- att_bias: bfloat16 [128, 4], replicated, may hold values from -0.5 to 0.5
- att_gate: bfloat16 [128, 128], replicated, may hold values from -0.5 to 0.5
- att_out: bfloat16 [128, 128], replicated, may hold values from -0.5 to 0.5
Outputs:
- attended: bfloat16 [384, 192, 128], P('grp', ('row', 'node')), parts along dimension 0
The draws below stay inside these ranges and needn't reach their ends.
There are 2 independent parts, one for each index of `grp`. The reference program is written for one: setup_inputs(seed, part) draws one part's arguments, and reference() takes and returns one part's arrays. A program takes and returns all parts, laid end to end along the dimension named above; an argument that names none is the same for every part. Nothing has to cross between parts.
All inputs are finite; a program needn't handle non-finite values.
Results may differ from the reference program's by a relative error of at most 0.0081.
Values may be sent and summed in bfloat16 or wider, within the bound.
No kernel may reach another device: no remote copies, remote signals or barrier semaphores. Data moves between devices by JAX's collectives and lax.ppermute only.
A program may use at most 128 MiB of HBM per device.

```python
import jax
import jax.numpy as jnp
from jax import lax

C = 128
CH = 128
HEADS = 4
HEAD_DIM = 32
N = 192


def draw_att_q(key, part):
    key = jax.random.fold_in(key, 11)
    own_part = jax.random.normal(key, (C, HEADS * HEAD_DIM), jnp.float32)
    values = own_part * C ** (-0.5)
    return jnp.clip(values, -3.0, 3.0).astype(jnp.bfloat16)


def draw_att_k(key, part):
    key = jax.random.fold_in(key, 23)
    own_part = jax.random.normal(key, (C, HEADS * HEAD_DIM), jnp.float32)
    values = own_part * C ** (-0.5)
    return jnp.clip(values, -3.0, 3.0).astype(jnp.bfloat16)


def levels(rng, dims, shards, low, largest):
    gain, own = 1.0, jax.random.fold_in(rng, 6)
    for position, shards_of in shards:
        steps = jnp.exp(jax.random.uniform(jax.random.fold_in(own, position), (shards_of,), jnp.float32, low / len(shards), largest / len(shards)))
        gain = gain * jnp.repeat(steps, dims[position] // shards_of).reshape([-1 if axis == position else 1 for axis in range(len(dims))])
    return gain


def gaussian(key, dims, scale, most, pieces=(), kind=jnp.bfloat16):
    loudness = levels(key, dims, pieces, -0.22, 0.18) if pieces else 1.0
    array = jax.random.normal(key, dims, jnp.float32) * scale * loudness
    return jnp.minimum(jnp.maximum(array, -most), most).astype(kind)


def setup_inputs(seed: int = 0, part: int = 0) -> dict:
    key_list = jax.random.split(jax.random.key(seed), 15)
    own_keys = jax.random.split(jax.random.fold_in(key_list[14], part), 15)
    pair_rep = gaussian(own_keys[0], (N, N, C), 1.0, 6.0, ((0, 16),))
    length = jax.random.randint(own_keys[1], (1,), N // 2, N + 1).astype(jnp.int32)
    ln_pair = jnp.clip(1.0 + 0.18 * jax.random.normal(key_list[2], (C,), jnp.float32), 0.1, 1.9)
    tri_in = gaussian(key_list[3], (4, C, CH), C ** -0.5, 0.5)
    tri_gate = gaussian(key_list[4], (C, C), C ** -0.5, 0.5)
    ln_hidden = jnp.clip(1.0 + 0.18 * jax.random.normal(key_list[5], (CH,), jnp.float32), 0.1, 1.9)
    tri_out = gaussian(key_list[6], (CH, C), CH ** -0.5, 0.5)
    ln_att = jnp.clip(1.0 + 0.18 * jax.random.normal(key_list[7], (C,), jnp.float32), 0.1, 1.9)
    att_q = draw_att_q(jax.random.fold_in(key_list[14], 71), part)
    att_k = draw_att_k(jax.random.fold_in(key_list[14], 71), part)
    att_v = gaussian(key_list[10], (C, HEADS * HEAD_DIM), C ** -0.5, 0.5)
    att_bias = gaussian(key_list[11], (C, HEADS), C ** -0.5, 0.5)
    att_gate = gaussian(key_list[12], (C, HEADS * HEAD_DIM), C ** -0.5, 0.5)
    att_out = gaussian(key_list[13], (HEADS * HEAD_DIM, C), (HEADS * HEAD_DIM) ** -0.5, 0.5)
    return dict(pair_rep=pair_rep, length=length, ln_pair=ln_pair, tri_in=tri_in, tri_gate=tri_gate, ln_hidden=ln_hidden, tri_out=tri_out, ln_att=ln_att, att_q=att_q, att_k=att_k, att_v=att_v, att_bias=att_bias, att_gate=att_gate, att_out=att_out)


eps = 1e-05

def layer_norm(values, gain_vec, reduce_axis):
    average = lax.optimization_barrier(jnp.mean(values, axis=reduce_axis, keepdims=True))
    centred = values - average
    variance = lax.optimization_barrier(jnp.mean(centred * centred, axis=reduce_axis, keepdims=True))
    return centred * lax.rsqrt(variance + eps) * gain_vec

def reference(pair_rep, length, ln_pair, tri_in, tri_gate, ln_hidden, tri_out, ln_att, att_q, att_k, att_v, att_bias, att_gate, att_out):
    f32 = jnp.float32
    bf16 = jnp.bfloat16
    crop_len = pair_rep.shape[0]
    key_live = jnp.arange(crop_len, dtype=jnp.int32) < length[0]
    pair_mask = (key_live[:, None] & key_live[None, :]).astype(f32)
    normed = layer_norm(pair_rep.astype(f32), ln_pair, -1).astype(bf16)
    projected = jnp.einsum('ijc,pce->pije', normed.astype(f32), tri_in.astype(f32))
    left_edge = (jax.nn.sigmoid(projected[0]) * projected[1] * pair_mask[:, :, None]).astype(bf16)
    right_edge = (jax.nn.sigmoid(projected[2]) * projected[3] * pair_mask[:, :, None]).astype(bf16)
    gating = jax.nn.sigmoid(jnp.einsum('ijc,cd->ijd', normed.astype(f32), tri_gate.astype(f32)))
    outer_sum = jnp.einsum('ikc,jkc->ijc', left_edge.astype(f32), right_edge.astype(f32))
    hidden_norm = layer_norm(outer_sum, ln_hidden, -1).astype(bf16)
    update = jnp.einsum('ije,ed->ijd', hidden_norm.astype(f32), tri_out.astype(f32))
    first_out = (pair_rep.astype(f32) + gating * update).astype(bf16)
    col_norm = layer_norm(first_out.astype(f32), ln_att, -1).astype(bf16)
    joined_w = jnp.concatenate([att_q, att_k, att_v, att_gate], axis=1).astype(f32)
    joined_proj = jnp.einsum('ijc,ce->ije', col_norm.astype(f32), joined_w)
    proj_width = att_q.shape[1]
    head_count = att_bias.shape[1]
    head_dim = proj_width // head_count
    query_proj = joined_proj[..., :proj_width].astype(bf16)
    key_proj = joined_proj[..., proj_width:2 * proj_width].astype(bf16)
    value_proj = joined_proj[..., 2 * proj_width:3 * proj_width].astype(bf16)
    att_gating = jax.nn.sigmoid(joined_proj[..., 3 * proj_width:])
    bias_all = jnp.einsum('kic,ch->hki', col_norm.astype(f32), att_bias.astype(f32)).astype(bf16).astype(f32)
    score_scale = head_dim ** (-0.5)

    def one_column(column):
        query_col = lax.dynamic_index_in_dim(query_proj, column, 1, keepdims=False).reshape(crop_len, head_count, head_dim).astype(f32)
        key_col = lax.dynamic_index_in_dim(key_proj, column, 1, keepdims=False).reshape(crop_len, head_count, head_dim).astype(f32)
        value_col = lax.dynamic_index_in_dim(value_proj, column, 1, keepdims=False).reshape(crop_len, head_count, head_dim).astype(f32)
        scores = jnp.einsum('khd,ihd->hki', key_col, query_col) * score_scale + bias_all
        scores = jnp.where(key_live[None, :, None], scores, -1000000000.0)
        row_max = lax.optimization_barrier(jnp.max(scores, axis=1, keepdims=True))
        exp_scores = jnp.exp(scores - row_max)
        attn_probs = (exp_scores / lax.optimization_barrier(jnp.sum(exp_scores, axis=1, keepdims=True))).astype(bf16)
        return jnp.einsum('hki,khd->ihd', attn_probs.astype(f32), value_col).reshape(crop_len, proj_width)
    attended = jnp.swapaxes(lax.map(one_column, jnp.arange(crop_len, dtype=jnp.int32)), 0, 1)
    gated = (attended * att_gating).astype(bf16)
    return (first_out.astype(f32) + jnp.einsum('ije,ed->ijd', gated.astype(f32), att_out.astype(f32))).astype(bf16)
```

```python
import jax
import jax.numpy as jnp
from jax import lax
from jax.experimental import pallas as pl
from jax.experimental.pallas import tpu as pltpu
from jax.sharding import PartitionSpec as P

EPS = 1e-05
LANES = 128
LOG2E = 1.4426950408889634
F32 = jnp.float32
BF16 = jnp.bfloat16
AXES = ("row", "node")
VMEM_BYTES = 48 * 1024 * 1024


def norm_last(values, gain):
    average = jnp.mean(values, axis=-1, keepdims=True)
    centred = values - average
    variance = jnp.mean(centred * centred, axis=-1, keepdims=True)
    return centred * lax.rsqrt(variance + EPS) * gain


def sigmoid(values):
    return 0.5 * jnp.tanh(0.5 * values) + 0.5


def dot(a, b, a_dim, b_dim):
    return lax.dot_general(a, b, (((a_dim,), (b_dim,)), ((), ())), preferred_element_type=F32)


def call(kernel, out_shape, args, scratch=(), smem=(), name=None):
    specs = [
        pl.BlockSpec(memory_space=pltpu.SMEM if n in smem else pltpu.VMEM) for n in range(len(args))
    ]
    single = not isinstance(out_shape, (list, tuple))
    vmem = pl.BlockSpec(memory_space=pltpu.VMEM)
    return pl.pallas_call(
        kernel,
        out_shape=out_shape,
        in_specs=specs,
        out_specs=vmem if single else [vmem] * len(out_shape),
        scratch_shapes=list(scratch),
        compiler_params=pltpu.CompilerParams(vmem_limit_bytes=VMEM_BYTES),
        name=name,
    )(*args)


class Sizes:
    def __init__(self, rows, crop, devices, channels):
        self.rows, self.crop, self.devices = rows, crop, devices
        self.half = rows // 2
        self.whole = crop // LANES
        self.rest = crop % LANES
        self.tiles = rows * crop // LANES
        self.chans = channels // devices
        self.fold = max(1, 16 // self.chans)
        while self.tiles % self.fold:
            self.fold //= 2
        self.fold_tiles = self.tiles // self.fold
        self.channels = channels

    def place(self, source, local):
        h, q = divmod(local, self.half)
        return h * (self.crop // 2) + source * self.half + q


def residue_of(sz, place):
    h = (place >= sz.crop // 2).astype(jnp.int32)
    rem = place - h * (sz.crop // 2)
    source = rem // sz.half
    return source * sz.rows + h * sz.half + (rem - source * sz.half)


def edges_kernel(sz, len_ref, x_ref, ln_ref, w_ref, out_ref, norm_ref):
    length, first = len_ref[0], len_ref[1]
    cd, two = sz.chans, 2 * sz.chans
    ch = sz.channels
    r = lax.broadcasted_iota(jnp.int32, (2 * ch, 2 * ch), 0)
    e = lax.broadcasted_iota(jnp.int32, (2 * ch, 2 * ch), 1)
    target = ((r // cd) % 2) * ch + (r // two) * cd + r % cd
    pick = (target == e).astype(BF16)
    gate_w = dot(pick, jnp.concatenate([w_ref[0], w_ref[2]], axis=1), 1, 1).astype(BF16)
    value_w = dot(pick, jnp.concatenate([w_ref[1], w_ref[3]], axis=1), 1, 1).astype(BF16)
    gain = ln_ref[...]
    main = sz.whole * LANES
    for row in range(sz.rows):
        normed = norm_last(x_ref[row].astype(F32), gain).astype(BF16)
        norm_ref[pl.ds(row * main, main), :] = normed[:main]
        if sz.rest:
            h, q = divmod(row, sz.half)
            norm_ref[pl.ds(sz.rows * main + q * LANES + h * sz.rest, sz.rest), :] = normed[main:]
    lane = lax.broadcasted_iota(jnp.int32, (1, LANES), 1)

    def live(tile):
        if tile < sz.rows * sz.whole:
            row, m = divmod(tile, sz.whole)
            return ((first + row < length) & (m * LANES + lane < length)).astype(F32)
        q = tile - sz.rows * sz.whole
        second = lane >= sz.rest
        row = first + q + jnp.where(second, sz.half, 0)
        k = main + lane - jnp.where(second, sz.rest, 0)
        return ((row < length) & (k < length)).astype(F32)

    step = 2 if sz.tiles % 2 == 0 else 1
    for tile in range(0, sz.tiles, step):
        n = norm_ref[pl.ds(tile * LANES, step * LANES), :]
        mask = jnp.concatenate([live(tile + s) for s in range(step)], axis=1)
        edge = sigmoid(dot(gate_w, n, 1, 1)) * dot(value_w, n, 1, 1) * mask
        out_ref[:, :, tile * LANES : (tile + step) * LANES] = edge.reshape(
            sz.devices, two, step * LANES
        ).astype(BF16)


def outer_kernel(sz, e_ref, out_ref, main_ref, rest_ref, omain_ref, orest_ref):
    cd, two = sz.chans, 2 * sz.chans
    n, w, half = sz.crop, sz.whole, sz.half
    for s in range(sz.devices):
        for tile in range(sz.tiles):
            block = e_ref[s, :, tile * LANES : (tile + 1) * LANES].astype(F32)
            if tile < sz.rows * w:
                row, m = divmod(tile, w)
                main_ref[m, pl.ds(sz.place(s, row) * two, two), :] = block
            else:
                q = tile - sz.rows * w
                rest_ref[pl.ds((s * half + q) * two, two), :] = block

    def matrix(index):
        parts = [main_ref[m, pl.ds(index, n, stride=two), :].astype(BF16) for m in range(w)]
        if sz.rest:
            t = rest_ref[pl.ds(index, n // 2, stride=two), :].astype(BF16)
            parts.append(jnp.concatenate([t[:, : sz.rest], t[:, sz.rest :]], axis=0))
        return jnp.concatenate(parts, axis=1) if len(parts) > 1 else parts[0]

    for c in range(cd):
        outer = dot(matrix(cd + c), matrix(c), 1, 1)
        for m in range(w):
            omain_ref[m, pl.ds(c, n, stride=cd), :] = outer[:, m * LANES : (m + 1) * LANES]
        if sz.rest:
            orest_ref[pl.ds(c, n // 2, stride=cd), :] = jnp.concatenate(
                [outer[: n // 2, w * LANES :], outer[n // 2 :, w * LANES :]], axis=1
            )
    for s in range(sz.devices):
        for t in range(sz.fold_tiles):
            blocks = []
            for f in range(sz.fold):
                tile = f * sz.fold_tiles + t
                if tile < sz.rows * w:
                    row, m = divmod(tile, w)
                    blocks.append(omain_ref[m, pl.ds(sz.place(s, row) * cd, cd), :])
                else:
                    q = tile - sz.rows * w
                    blocks.append(orest_ref[pl.ds((s * half + q) * cd, cd), :])
            block = jnp.concatenate(blocks, axis=0) if len(blocks) > 1 else blocks[0]
            out_ref[s, :, t * LANES : (t + 1) * LANES] = block.astype(BF16)


def update_kernel(
    sz, o_ref, x_ref, lnp_ref, gate_ref, lnh_ref, tri_ref, lna_ref, biasw_ref,
    first_ref, col_ref, bias_ref, cols_ref,
):
    n, w, half, ch = sz.crop, sz.whole, sz.half, sz.channels
    for s in range(sz.devices):
        for row in range(sz.rows):
            cols_ref[pl.ds(sz.place(s, row) * 16, sz.rows), :] = x_ref[s * sz.rows + row].astype(F32)
    gain_h = jnp.transpose(jnp.broadcast_to(lnh_ref[...], (ch, ch)))
    tri = tri_ref[...]

    def update(tile):
        f, t = divmod(tile, sz.fold_tiles)
        block = o_ref[:, :, t * LANES : (t + 1) * LANES].astype(F32)
        block = block[:, f * sz.chans : (f + 1) * sz.chans, :].reshape(ch, LANES)
        average = jnp.mean(block, axis=0, keepdims=True)
        centred = block - average
        variance = jnp.mean(centred * centred, axis=0, keepdims=True)
        hidden = (centred * lax.rsqrt(variance + EPS) * gain_h).astype(BF16)
        return dot(hidden, tri, 0, 0)

    rest = [update(sz.rows * w + q) for q in range(half)] if sz.rest else None
    for j in range(sz.rows):
        parts = [update(j * w + m) for m in range(w)]
        if sz.rest:
            h, q = divmod(j, half)
            parts.append(rest[q][h * sz.rest : (h + 1) * sz.rest])
        change = jnp.concatenate(parts, axis=0) if len(parts) > 1 else parts[0]
        x = cols_ref[pl.ds(j, n, stride=16), :]
        normed = norm_last(x, lnp_ref[...]).astype(BF16)
        gating = sigmoid(dot(normed, gate_ref[...], 1, 0))
        first = (x + gating * change).astype(BF16)
        first_ref[j] = first
        col = norm_last(first.astype(F32), lna_ref[...]).astype(BF16)
        col_ref[j] = col
        heads = biasw_ref.shape[1]
        bias_ref[pl.ds(j * heads, heads), :] = dot(biasw_ref[...], col, 0, 1)


def project_kernel(sz, col_ref, q_ref, k_ref, v_ref, g_ref, qo_ref, ko_ref, vo_ref, go_ref):
    n, ch = sz.crop, sz.channels
    qk = jnp.concatenate([q_ref[...], k_ref[...]], axis=1)
    vg = jnp.transpose(jnp.concatenate([v_ref[...], g_ref[...]], axis=1).astype(F32)).astype(BF16)
    width = q_ref.shape[1]
    for j in range(sz.rows):
        col = col_ref[j]
        both = dot(col, qk, 1, 0)
        qo_ref[j] = both[:, :width].astype(BF16)
        ko_ref[j] = both[:, width:].astype(BF16)
        other = dot(vg, col, 1, 1)
        vo_ref[j] = other[:width].astype(BF16)
        go_ref[j] = sigmoid(other[width:])


def attend_kernel(
    sz, heads, len_ref, q_ref, k_ref, v_ref, g_ref, first_ref, bias_ref, aout_ref,
    out_ref, rows_ref, biasT_ref, sum_ref,
):
    n, w, ch = sz.crop, sz.whole, sz.channels
    length = len_ref[0]
    width = q_ref.shape[2]
    hd = width // heads
    per = sz.half * heads
    for s in range(sz.devices):
        block = bias_ref[s].astype(F32) * LOG2E
        for h in range(2):
            part = block[h * per : (h + 1) * per]
            at = pl.ds((h * sz.devices + s) * per, per)
            for m in range(w):
                rows_ref[m, at, :] = part[:, m * LANES : (m + 1) * LANES]
            if sz.rest:
                rows_ref[w, at, : sz.rest] = part[:, w * LANES :]
    key = residue_of(sz, lax.broadcasted_iota(jnp.int32, (n, LANES), 0))
    dead = jnp.where(key < length, 0.0, -1e9 * LOG2E).astype(F32)
    halves = []
    for head in range(heads):
        b = [
            jnp.transpose(rows_ref[m, pl.ds(head, n, stride=heads), :])
            for m in range(w + (sz.rest > 0))
        ]
        if sz.rest:
            b[w] = b[w][: sz.rest]
        b = jnp.concatenate(b, axis=0) if len(b) > 1 else b[0]
        for m in range(w):
            biasT_ref[:, (head * w + m) * LANES : (head * w + m + 1) * LANES] = (
                b[:, m * LANES : (m + 1) * LANES] + dead
            )
        if sz.rest:
            halves.append(b[:, w * LANES :])
    per_tile = LANES // sz.rest if sz.rest else 1
    base = heads * w
    if sz.rest:
        for t in range(heads // per_tile):
            biasT_ref[:, (base + t) * LANES : (base + t + 1) * LANES] = (
                jnp.concatenate(halves[t * per_tile : (t + 1) * per_tile], axis=1) + dead
            )
    lane = lax.broadcasted_iota(jnp.int32, (1, width), 1)
    head_masks = [((lane >= h * hd) & (lane < (h + 1) * hd)).astype(BF16) for h in range(heads)]
    scale = (hd ** (-0.5)) * LOG2E
    for j in range(sz.rows):
        q = q_ref[j]
        masked = [q * head_masks[h] for h in range(heads)]
        pieces = [masked[h][: w * LANES] for h in range(heads)]
        if sz.rest:
            pieces += [masked[h][w * LANES :] for h in range(heads)]
        stacked = jnp.concatenate(pieces, axis=0)
        scores = dot(k_ref[j], stacked, 1, 1) * scale + biasT_ref[...]
        top = jnp.max(scores, axis=0, keepdims=True)
        weights = jnp.exp2(scores - top)
        total = jnp.sum(weights, axis=0, keepdims=True)
        mixed = dot(v_ref[j], weights.astype(BF16), 1, 0)
        inverse = 1.0 / total
        mains, rests = [], []
        for h in range(heads):
            sl = slice(h * w * LANES, (h + 1) * w * LANES)
            mains.append(mixed[h * hd : (h + 1) * hd, sl] * inverse[:, sl])
            if sz.rest:
                t, part = divmod(h, per_tile)
                sl = slice((base + t) * LANES, (base + t + 1) * LANES)
                piece = mixed[h * hd : (h + 1) * hd, sl] * inverse[:, sl]
                rests.append(piece[:, part * sz.rest : (part + 1) * sz.rest])
        attended = jnp.concatenate(mains, axis=0)
        if sz.rest:
            attended = jnp.concatenate([attended, jnp.concatenate(rests, axis=0)], axis=1)
        gated = (attended * g_ref[j]).astype(BF16)
        total_out = first_ref[j].astype(F32) + dot(gated, aout_ref[...], 0, 0)
        sum_ref[pl.ds(j, n, stride=16), :] = total_out
    for s in range(sz.devices):
        for row in range(sz.rows):
            out_ref[s * sz.rows + row] = sum_ref[pl.ds(sz.place(s, row) * 16, sz.rows), :].astype(
                BF16
            )


def shards(
    devices,
    pair_rep, length, ln_pair, tri_in, tri_gate, ln_hidden, tri_out, ln_att,
    att_q, att_k, att_v, att_bias, att_gate, att_out,
):
    rows, crop, ch = pair_rep.shape
    heads = att_bias.shape[1]
    sz = Sizes(rows, crop, devices, ch)
    n, cd = crop, sz.chans
    first_row = lax.axis_index(AXES) * rows
    info = jnp.stack([length[0], first_row.astype(jnp.int32)])
    columns = lax.all_to_all(pair_rep, AXES, split_axis=1, concat_axis=0, tiled=True)

    def bound(kernel, *extra):
        def run(*refs):
            return kernel(sz, *extra, *refs)

        return run

    shape = jax.ShapeDtypeStruct
    edges = call(
        bound(edges_kernel),
        shape((devices, 2 * cd, rows * crop), BF16),
        (info, pair_rep, ln_pair[None], tri_in),
        scratch=[pltpu.VMEM((rows * crop, ch), BF16)],
        smem=(0,),
        name="edges",
    )
    edges = lax.all_to_all(edges, AXES, split_axis=0, concat_axis=0, tiled=True)
    rest_rows = max(n // 2, 8)
    outer = call(
        bound(outer_kernel),
        shape((devices, sz.fold * cd, rows * crop // sz.fold), BF16),
        (edges,),
        scratch=[
            pltpu.VMEM((sz.whole, n * 2 * cd, LANES), F32),
            pltpu.VMEM((rest_rows * 2 * cd, LANES), F32),
            pltpu.VMEM((sz.whole, n * cd, LANES), F32),
            pltpu.VMEM((rest_rows * cd, LANES), F32),
        ],
        name="outer",
    )
    outer = lax.all_to_all(outer, AXES, split_axis=0, concat_axis=0, tiled=True)
    first, col, bias = call(
        bound(update_kernel),
        [
            shape((rows, n, ch), BF16),
            shape((rows, n, ch), BF16),
            shape((rows * heads, n), F32),
        ],
        (outer, columns, ln_pair[None], tri_gate, ln_hidden[None], tri_out, ln_att[None], att_bias),
        scratch=[pltpu.VMEM((n * 16, ch), F32)],
        name="update",
    )
    bias_all = lax.all_gather(bias.astype(BF16), AXES, axis=0, tiled=False)
    query, key, value, gate = call(
        bound(project_kernel),
        [
            shape((rows, n, att_q.shape[1]), BF16),
            shape((rows, n, att_q.shape[1]), BF16),
            shape((rows, att_q.shape[1], n), BF16),
            shape((rows, att_q.shape[1], n), F32),
        ],
        (col, att_q, att_k, att_v, att_gate),
        name="project",
    )
    return call(
        bound(attend_kernel, heads),
        shape((n, rows, ch), BF16),
        (info, query, key, value, gate, first, bias_all, att_out),
        scratch=[
            pltpu.VMEM((-(-n // LANES), n * heads, LANES), F32),
            pltpu.VMEM((n, heads * n), F32),
            pltpu.VMEM((n * 16, ch), F32),
        ],
        smem=(0,),
        name="attend",
    )


def solution(mesh):
    devices = mesh.shape["row"] * mesh.shape["node"]

    def body(*args):
        return shards(devices, *args)

    return jax.shard_map(
        body,
        mesh=mesh,
        in_specs=(P(("grp", "row", "node"), None, None), P("grp")) + (P(),) * 12,
        out_specs=P("grp", AXES, None),
        check_vma=False,
    )
```

```python
import jax
import jax.numpy as jnp
from jax import lax
from jax.experimental import pallas as pl
from jax.experimental.pallas import tpu as pltpu
from jax.sharding import PartitionSpec as P

EPS = 1e-05
LANES = 128
LOG2E = 1.4426950408889634
F32 = jnp.float32
BF16 = jnp.bfloat16
AXES = ("row", "node")
VMEM_BYTES = 48 * 1024 * 1024


def norm_last(values, gain):
    average = jnp.mean(values, axis=-1, keepdims=True)
    centred = values - average
    variance = jnp.mean(centred * centred, axis=-1, keepdims=True)
    return centred * lax.rsqrt(variance + EPS) * gain


def sigmoid(values):
    return 0.5 * jnp.tanh(0.5 * values) + 0.5


def dot(a, b, a_dim, b_dim):
    return lax.dot_general(a, b, (((a_dim,), (b_dim,)), ((), ())), preferred_element_type=F32)


def call(kernel, out_shape, args, scratch=(), smem=(), name=None):
    specs = [
        pl.BlockSpec(memory_space=pltpu.SMEM if n in smem else pltpu.VMEM) for n in range(len(args))
    ]
    single = not isinstance(out_shape, (list, tuple))
    vmem = pl.BlockSpec(memory_space=pltpu.VMEM)
    return pl.pallas_call(
        kernel,
        out_shape=out_shape,
        in_specs=specs,
        out_specs=vmem if single else [vmem] * len(out_shape),
        scratch_shapes=list(scratch),
        compiler_params=pltpu.CompilerParams(vmem_limit_bytes=VMEM_BYTES),
        name=name,
    )(*args)


class Sizes:
    def __init__(self, rows, crop, devices, channels):
        self.rows, self.crop, self.devices = rows, crop, devices
        self.half = rows // 2
        self.whole = crop // LANES
        self.rest = crop % LANES
        self.tiles = rows * crop // LANES
        self.chans = channels // devices
        self.fold = max(1, 16 // self.chans)
        while self.tiles % self.fold:
            self.fold //= 2
        self.fold_tiles = self.tiles // self.fold
        self.channels = channels

        self.block = rows * rows
        self.block_tiles = -(-self.block // (2 * self.chans))


def edges_kernel(sz, len_ref, x_ref, ln_ref, w_ref, out_ref, norm_ref, pair_ref):
    length, first = len_ref[0], len_ref[1]
    cd, two = sz.chans, 2 * sz.chans
    ch = sz.channels
    r = lax.broadcasted_iota(jnp.int32, (2 * ch, 2 * ch), 0)
    e = lax.broadcasted_iota(jnp.int32, (2 * ch, 2 * ch), 1)
    target = ((r // cd) % 2) * ch + (r // two) * cd + r % cd
    pick = (target == e).astype(BF16)
    gate_w = dot(pick, jnp.concatenate([w_ref[0], w_ref[2]], axis=1), 1, 1).astype(BF16)
    value_w = dot(pick, jnp.concatenate([w_ref[1], w_ref[3]], axis=1), 1, 1).astype(BF16)
    gain = ln_ref[...]
    main = sz.whole * LANES
    for row in range(sz.rows):
        x = x_ref[row].astype(F32)
        for d in range(sz.devices):
            pair_ref[d, row * sz.rows : (row + 1) * sz.rows, :] = x[d * sz.rows : (d + 1) * sz.rows]
        normed = norm_last(x, gain).astype(BF16)
        norm_ref[pl.ds(row * main, main), :] = normed[:main]
        if sz.rest:
            h, q = divmod(row, sz.half)
            norm_ref[pl.ds(sz.rows * main + q * LANES + h * sz.rest, sz.rest), :] = normed[main:]
    for d in range(sz.devices):
        for t in range(sz.block_tiles):
            at = (sz.tiles + t) * LANES
            out_ref[d, :, at : at + LANES] = pair_ref[d, t * two : (t + 1) * two, :].astype(BF16)
    lane = lax.broadcasted_iota(jnp.int32, (1, LANES), 1)

    def live(tile):
        if tile < sz.rows * sz.whole:
            row, m = divmod(tile, sz.whole)
            return ((first + row < length) & (m * LANES + lane < length)).astype(F32)
        q = tile - sz.rows * sz.whole
        second = lane >= sz.rest
        row = first + q + jnp.where(second, sz.half, 0)
        k = main + lane - jnp.where(second, sz.rest, 0)
        return ((row < length) & (k < length)).astype(F32)

    step = 2 if sz.tiles % 2 == 0 else 1
    for tile in range(0, sz.tiles, step):
        n = norm_ref[pl.ds(tile * LANES, step * LANES), :]
        mask = jnp.concatenate([live(tile + s) for s in range(step)], axis=1)
        edge = sigmoid(dot(gate_w, n, 1, 1)) * dot(value_w, n, 1, 1) * mask
        out_ref[:, :, tile * LANES : (tile + step) * LANES] = edge.reshape(
            sz.devices, two, step * LANES
        ).astype(BF16)


def outer_kernel(sz, e_ref, out_ref, main_ref, rest_ref, omain_ref, orest_ref):
    cd, two = sz.chans, 2 * sz.chans
    n, w, half = sz.crop, sz.whole, sz.half
    for s in range(sz.devices):
        for tile in range(sz.tiles):
            block = e_ref[s, :, tile * LANES : (tile + 1) * LANES].astype(F32)
            if tile < sz.rows * w:
                row, m = divmod(tile, w)
                main_ref[m, pl.ds((s * sz.rows + row) * two, two), :] = block
            else:
                at = s * sz.rows + tile - sz.rows * w
                rest_ref[pl.ds(at * two, two), :] = block
                rest_ref[pl.ds((at + half) * two, two), :] = pltpu.roll(block, sz.rest, 1)

    def matrix(index):
        parts = [main_ref[m, pl.ds(index, n, stride=two), :].astype(BF16) for m in range(w)]
        if sz.rest:
            parts.append(rest_ref[pl.ds(index, n, stride=two), :].astype(BF16)[:, : sz.rest])
        return jnp.concatenate(parts, axis=1) if len(parts) > 1 else parts[0]

    for c in range(cd):
        outer = dot(matrix(cd + c), matrix(c), 1, 1)
        for m in range(w):
            omain_ref[m, pl.ds(c, n, stride=cd), :] = outer[:, m * LANES : (m + 1) * LANES]
        if sz.rest:
            part = outer[:, w * LANES :]
            orest_ref[pl.ds(c, n, stride=cd), :] = jnp.concatenate([part, part], axis=1)
    low = lax.broadcasted_iota(jnp.int32, (cd, LANES), 1) < sz.rest
    for s in range(sz.devices):
        for t in range(sz.fold_tiles):
            blocks = []
            for f in range(sz.fold):
                tile = f * sz.fold_tiles + t
                if tile < sz.rows * w:
                    row, m = divmod(tile, w)
                    blocks.append(omain_ref[m, pl.ds((s * sz.rows + row) * cd, cd), :])
                else:
                    at = s * sz.rows + tile - sz.rows * w
                    one = orest_ref[pl.ds(at * cd, cd), :]
                    blocks.append(jnp.where(low, one, orest_ref[pl.ds((at + half) * cd, cd), :]))
            block = jnp.concatenate(blocks, axis=0) if len(blocks) > 1 else blocks[0]
            out_ref[s, :, t * LANES : (t + 1) * LANES] = block.astype(BF16)


def update_kernel(
    sz, o_ref, x_ref, lnp_ref, gate_ref, lnh_ref, tri_ref, lna_ref, biasw_ref,
    first_ref, col_ref, bias_ref, cols_ref, brow_ref,
):
    n, w, half, ch = sz.crop, sz.whole, sz.half, sz.channels
    two = 2 * sz.chans
    for s in range(sz.devices):
        for t in range(sz.block_tiles):
            at = (sz.tiles + t) * LANES
            cols_ref[pl.ds(s * sz.block + t * two, two), :] = x_ref[s, :, at : at + LANES].astype(F32)
    gain_h = jnp.transpose(jnp.broadcast_to(lnh_ref[...], (ch, ch)))
    tri = tri_ref[...]

    def update(tile):
        f, t = divmod(tile, sz.fold_tiles)
        block = o_ref[:, :, t * LANES : (t + 1) * LANES].astype(F32)
        block = block[:, f * sz.chans : (f + 1) * sz.chans, :].reshape(ch, LANES)
        average = jnp.mean(block, axis=0, keepdims=True)
        centred = block - average
        variance = jnp.mean(centred * centred, axis=0, keepdims=True)
        hidden = (centred * lax.rsqrt(variance + EPS) * gain_h).astype(BF16)
        return dot(hidden, tri, 0, 0)

    rest = [update(sz.rows * w + q) for q in range(half)] if sz.rest else None
    for j in range(sz.rows):
        parts = [update(j * w + m) for m in range(w)]
        if sz.rest:
            h, q = divmod(j, half)
            parts.append(rest[q][h * sz.rest : (h + 1) * sz.rest])
        change = jnp.concatenate(parts, axis=0) if len(parts) > 1 else parts[0]
        x = cols_ref[pl.ds(j, n, stride=sz.rows), :]
        normed = norm_last(x, lnp_ref[...]).astype(BF16)
        gating = sigmoid(dot(normed, gate_ref[...], 1, 0))
        first = (x + gating * change).astype(BF16)
        first_ref[j] = first
        col = norm_last(first.astype(F32), lna_ref[...]).astype(BF16)
        col_ref[j] = col
        heads = biasw_ref.shape[1]
        brow_ref[pl.ds(j * heads, heads), :] = dot(biasw_ref[...], col, 0, 1)
    bias_ref[...] = brow_ref[...].astype(BF16)


def project_kernel(sz, col_ref, q_ref, k_ref, v_ref, g_ref, qo_ref, ko_ref, vo_ref, go_ref):
    n, ch = sz.crop, sz.channels
    qk = jnp.concatenate([q_ref[...], k_ref[...]], axis=1)
    vg = jnp.transpose(jnp.concatenate([v_ref[...], g_ref[...]], axis=1).astype(F32)).astype(BF16)
    width = q_ref.shape[1]
    for j in range(sz.rows):
        col = col_ref[j]
        both = dot(col, qk, 1, 0)
        qo_ref[j] = both[:, :width].astype(BF16)
        ko_ref[j] = both[:, width:].astype(BF16)
        other = dot(vg, col, 1, 1)
        vo_ref[j] = other[:width].astype(BF16)
        go_ref[j] = sigmoid(other[width:])


def attend_kernel(
    sz, heads, steps, len_ref, q_ref, k_ref, v_ref, g_ref, first_ref, aout_ref, *refs
):
    bias_refs, (out_ref, rows_ref, biasT_ref) = refs[:-3], refs[-3:]
    n, w, ch = sz.crop, sz.whole, sz.channels
    length, me = len_ref[0], len_ref[2]
    width = q_ref.shape[2]
    hd = width // heads
    per = sz.rows * heads
    for ref, offsets in zip(bias_refs, steps):
        for place, offset in enumerate(offsets):
            at = pl.ds(pl.multiple_of((me ^ offset) * per, 8), per)
            part = ref[place].astype(F32) * LOG2E
            for m in range(w):
                rows_ref[m, at, :] = part[:, m * LANES : (m + 1) * LANES]
            if sz.rest:
                rows_ref[w, at, : sz.rest] = part[:, w * LANES :]
    key = lax.broadcasted_iota(jnp.int32, (n, LANES), 0)
    dead = jnp.where(key < length, 0.0, -1e9 * LOG2E).astype(F32)
    halves = []
    for head in range(heads):
        b = [
            jnp.transpose(rows_ref[m, pl.ds(head, n, stride=heads), :])
            for m in range(w + (sz.rest > 0))
        ]
        if sz.rest:
            b[w] = b[w][: sz.rest]
        b = jnp.concatenate(b, axis=0) if len(b) > 1 else b[0]
        for m in range(w):
            biasT_ref[:, (head * w + m) * LANES : (head * w + m + 1) * LANES] = (
                b[:, m * LANES : (m + 1) * LANES] + dead
            )
        if sz.rest:
            halves.append(b[:, w * LANES :])
    per_tile = LANES // sz.rest if sz.rest else 1
    base = heads * w
    if sz.rest:
        for t in range(heads // per_tile):
            biasT_ref[:, (base + t) * LANES : (base + t + 1) * LANES] = (
                jnp.concatenate(halves[t * per_tile : (t + 1) * per_tile], axis=1) + dead
            )
    lane = lax.broadcasted_iota(jnp.int32, (1, width), 1)
    head_masks = [((lane >= h * hd) & (lane < (h + 1) * hd)).astype(BF16) for h in range(heads)]
    scale = (hd ** (-0.5)) * LOG2E
    for j in range(sz.rows):
        q = q_ref[j]
        masked = [q * head_masks[h] for h in range(heads)]
        pieces = [masked[h][: w * LANES] for h in range(heads)]
        if sz.rest:
            pieces += [masked[h][w * LANES :] for h in range(heads)]
        stacked = jnp.concatenate(pieces, axis=0)
        scores = dot(k_ref[j], stacked, 1, 1) * scale + biasT_ref[...]
        top = jnp.max(scores, axis=0, keepdims=True)
        weights = jnp.exp2(scores - top)
        total = jnp.sum(weights, axis=0, keepdims=True)
        mixed = dot(v_ref[j], weights.astype(BF16), 1, 0)
        inverse = 1.0 / total
        mains, rests = [], []
        for h in range(heads):
            sl = slice(h * w * LANES, (h + 1) * w * LANES)
            mains.append(mixed[h * hd : (h + 1) * hd, sl] * inverse[:, sl])
            if sz.rest:
                t, part = divmod(h, per_tile)
                sl = slice((base + t) * LANES, (base + t + 1) * LANES)
                piece = mixed[h * hd : (h + 1) * hd, sl] * inverse[:, sl]
                rests.append(piece[:, part * sz.rest : (part + 1) * sz.rest])
        attended = jnp.concatenate(mains, axis=0)
        if sz.rest:
            attended = jnp.concatenate([attended, jnp.concatenate(rests, axis=0)], axis=1)
        gated = (attended * g_ref[j]).astype(BF16)
        total_out = first_ref[j].astype(F32) + dot(gated, aout_ref[...], 0, 0)
        out_ref[j] = total_out.astype(BF16)


def spread(block, devices):
    pieces, offsets = [block[None]], [[0]]
    bit = devices // 2
    while bit:
        held = jnp.concatenate(pieces, axis=0) if len(pieces) > 1 else pieces[0]
        got = lax.ppermute(held, AXES, [(d, d ^ bit) for d in range(devices)])
        known = [o for part in offsets for o in part]
        pieces.append(got)
        offsets.append([o ^ bit for o in known])
        bit //= 2
    return pieces, offsets


def shards(
    devices,
    pair_rep, length, ln_pair, tri_in, tri_gate, ln_hidden, tri_out, ln_att,
    att_q, att_k, att_v, att_bias, att_gate, att_out,
):
    rows, crop, ch = pair_rep.shape
    heads = att_bias.shape[1]
    sz = Sizes(rows, crop, devices, ch)
    n, cd = crop, sz.chans
    me = lax.axis_index(AXES).astype(jnp.int32)
    info = jnp.stack([length[0], me * rows, me])

    def bound(kernel, *extra):
        def run(*refs):
            return kernel(sz, *extra, *refs)

        return run

    shape = jax.ShapeDtypeStruct
    edges = call(
        bound(edges_kernel),
        shape((devices, 2 * cd, (sz.tiles + sz.block_tiles) * LANES), BF16),
        (info, pair_rep, ln_pair[None], tri_in),
        scratch=[
            pltpu.VMEM((rows * crop, ch), BF16),
            pltpu.VMEM((devices, sz.block_tiles * 2 * cd, ch), F32),
        ],
        smem=(0,),
        name="edges",
    )
    edges = lax.all_to_all(edges, AXES, split_axis=0, concat_axis=0, tiled=True)
    rest_rows = n if sz.rest else 8
    outer = call(
        bound(outer_kernel),
        shape((devices, sz.fold * cd, rows * crop // sz.fold), BF16),
        (edges,),
        scratch=[
            pltpu.VMEM((sz.whole, n * 2 * cd, LANES), F32),
            pltpu.VMEM((rest_rows * 2 * cd, LANES), F32),
            pltpu.VMEM((sz.whole, n * cd, LANES), F32),
            pltpu.VMEM((rest_rows * cd, LANES), F32),
        ],
        name="outer",
    )
    outer = lax.all_to_all(outer, AXES, split_axis=0, concat_axis=0, tiled=True)
    first, col, bias = call(
        bound(update_kernel),
        [
            shape((rows, n, ch), BF16),
            shape((rows, n, ch), BF16),
            shape((rows * heads, n), BF16),
        ],
        (outer, edges, ln_pair[None], tri_gate, ln_hidden[None], tri_out, ln_att[None], att_bias),
        scratch=[
            pltpu.VMEM((devices * sz.block + 2 * cd, ch), F32),
            pltpu.VMEM((rows * heads, n), F32),
        ],
        name="update",
    )
    pieces, steps = spread(bias, devices)
    query, key, value, gate = call(
        bound(project_kernel),
        [
            shape((rows, n, att_q.shape[1]), BF16),
            shape((rows, n, att_q.shape[1]), BF16),
            shape((rows, att_q.shape[1], n), BF16),
            shape((rows, att_q.shape[1], n), F32),
        ],
        (col, att_q, att_k, att_v, att_gate),
        name="project",
    )
    out = call(
        bound(attend_kernel, heads, steps),
        shape((rows, n, ch), BF16),
        (info, query, key, value, gate, first, att_out, *pieces),
        scratch=[
            pltpu.VMEM((-(-n // LANES), n * heads, LANES), F32),
            pltpu.VMEM((n, heads * n), F32),
        ],
        smem=(0,),
        name="attend",
    )
    return jnp.swapaxes(out, 0, 1)


def solution(mesh):
    devices = mesh.shape["row"] * mesh.shape["node"]

    def body(*args):
        return shards(devices, *args)

    return jax.shard_map(
        body,
        mesh=mesh,
        in_specs=(P(("grp", "row", "node"), None, None), P("grp")) + (P(),) * 12,
        out_specs=P("grp", AXES, None),
        check_vma=False,
    )
```

```python
import jax
import jax.numpy as jnp
from jax import lax
from jax.experimental import pallas as pl
from jax.experimental.pallas import tpu as pltpu
from jax.sharding import PartitionSpec as P

EPS = 1e-05
LANES = 128
LOG2E = 1.4426950408889634
F32 = jnp.float32
BF16 = jnp.bfloat16
AXES = ("row", "node")
VMEM_BYTES = 48 * 1024 * 1024


def norm_last(values, gain):
    average = jnp.mean(values, axis=-1, keepdims=True)
    centred = values - average
    variance = jnp.mean(centred * centred, axis=-1, keepdims=True)
    return centred * lax.rsqrt(variance + EPS) * gain


def sigmoid(values):
    return 0.5 * jnp.tanh(0.5 * values) + 0.5


def dot(a, b, a_dim, b_dim):
    return lax.dot_general(a, b, (((a_dim,), (b_dim,)), ((), ())), preferred_element_type=F32)


def call(kernel, out_shape, args, scratch=(), smem=(), name=None):
    specs = [
        pl.BlockSpec(memory_space=pltpu.SMEM if n in smem else pltpu.VMEM) for n in range(len(args))
    ]
    single = not isinstance(out_shape, (list, tuple))
    vmem = pl.BlockSpec(memory_space=pltpu.VMEM)
    return pl.pallas_call(
        kernel,
        out_shape=out_shape,
        in_specs=specs,
        out_specs=vmem if single else [vmem] * len(out_shape),
        scratch_shapes=list(scratch),
        compiler_params=pltpu.CompilerParams(vmem_limit_bytes=VMEM_BYTES),
        name=name,
    )(*args)


class Sizes:
    def __init__(self, rows, crop, devices, channels):
        self.rows, self.crop, self.devices, self.channels = rows, crop, devices, channels
        self.half = rows // 2
        self.group = devices // 2
        self.columns = rows * self.group
        self.whole = crop // LANES
        self.rest = crop % LANES
        self.tiles = rows * crop // LANES
        self.chans = channels // self.group
        self.block = rows * rows
        self.block_tiles = -(-self.block // self.chans)


def edges_kernel(sz, len_ref, x_ref, ln_ref, w_ref, *refs):
    near, far, pair = refs[: sz.group], refs[sz.group : 2 * sz.group], refs[2 * sz.group : -2]
    norm_ref, pair_ref = refs[-2:]
    length, first, me = len_ref[0], len_ref[1], len_ref[2]
    cd, ch = sz.chans, sz.channels
    mine = me & (sz.group - 1)
    r = lax.broadcasted_iota(jnp.int32, (ch, ch), 0)
    e = lax.broadcasted_iota(jnp.int32, (ch, ch), 1)
    pick = (((r // cd) ^ mine) * cd + r % cd == e).astype(BF16)
    weights = [dot(pick, w_ref[p], 1, 1).astype(BF16) for p in range(4)]
    gate_w = jnp.concatenate([weights[0], weights[2]], axis=0)
    value_w = jnp.concatenate([weights[1], weights[3]], axis=0)
    gain = ln_ref[...]
    main = sz.whole * LANES
    for row in range(sz.rows):
        x = x_ref[row].astype(F32)
        for d in range(sz.devices):
            pair_ref[d, row * sz.rows : (row + 1) * sz.rows, :] = x[d * sz.rows : (d + 1) * sz.rows]
        normed = norm_last(x, gain).astype(BF16)
        norm_ref[pl.ds(row * main, main), :] = normed[:main]
        if sz.rest:
            h, q = divmod(row, sz.half)
            norm_ref[pl.ds(sz.rows * main + q * LANES + h * sz.rest, sz.rest), :] = normed[main:]
    for r in range(sz.group):
        for t in range(sz.block_tiles):
            at = (2 * sz.tiles + t) * LANES
            rows = slice(t * cd, (t + 1) * cd)
            near[r][:, at : at + LANES] = pair_ref[me ^ r, rows, :].astype(BF16)
            pair[r][:, t * LANES : (t + 1) * LANES] = pair_ref[me ^ (sz.group + r), rows, :].astype(
                BF16
            )
    lane = lax.broadcasted_iota(jnp.int32, (1, LANES), 1)

    def live(tile):
        if tile < sz.rows * sz.whole:
            row, m = divmod(tile, sz.whole)
            return ((first + row < length) & (m * LANES + lane < length)).astype(F32)
        q = tile - sz.rows * sz.whole
        second = lane >= sz.rest
        row = first + q + jnp.where(second, sz.half, 0)
        k = main + lane - jnp.where(second, sz.rest, 0)
        return ((row < length) & (k < length)).astype(F32)

    step = 2 if sz.tiles % 2 == 0 else 1
    for tile in range(0, sz.tiles, step):
        n = norm_ref[pl.ds(tile * LANES, step * LANES), :]
        mask = jnp.concatenate([live(tile + s) for s in range(step)], axis=1)
        edge = sigmoid(dot(gate_w, n, 1, 1)) * dot(value_w, n, 1, 1) * mask
        edge = edge.astype(BF16)
        to = slice(tile * LANES, (tile + step) * LANES)
        right_to = slice((sz.tiles + tile) * LANES, (sz.tiles + tile + step) * LANES)
        for r in range(sz.group):
            left = edge[r * cd : (r + 1) * cd]
            near[r][:, to] = left
            far[r][:, to] = left
            near[r][:, right_to] = edge[ch + r * cd : ch + (r + 1) * cd]


def outer_kernel(sz, len_ref, *refs):
    near, far = refs[: sz.group], refs[sz.group : 2 * sz.group]
    outs = refs[2 * sz.group : 3 * sz.group]
    lmain_ref, lrest_ref, rmain_ref, rrest_ref, omain_ref, orest_ref = refs[3 * sz.group :]
    me = len_ref[2]
    mine = me & (sz.group - 1)
    cd, n, w, half = sz.chans, sz.crop, sz.whole, sz.half

    def unpack(ref, base, owner, main_ref, rest_ref):
        for tile in range(sz.tiles):
            at = (base + tile) * LANES
            block = ref[:, at : at + LANES].astype(F32)
            if tile < sz.rows * w:
                row, m = divmod(tile, w)
                main_ref[m, pl.ds(pl.multiple_of((owner * sz.rows + row) * cd, 8), cd), :] = block
            else:
                row = owner * sz.rows + tile - sz.rows * w
                rest_ref[pl.ds(pl.multiple_of(row * cd, 8), cd), :] = block
                rest_ref[pl.ds(pl.multiple_of((row + half) * cd, 8), cd), :] = pltpu.roll(
                    block, sz.rest, 1
                )

    for r in range(sz.group):
        unpack(near[r], 0, me ^ r, lmain_ref, lrest_ref)
        unpack(near[r], sz.tiles, mine ^ r, rmain_ref, rrest_ref)
        unpack(far[r], 0, me ^ (sz.group + r), lmain_ref, lrest_ref)

    def matrix(c, size, main_ref, rest_ref):
        parts = [main_ref[m, pl.ds(c, size, stride=cd), :].astype(BF16) for m in range(w)]
        if sz.rest:
            parts.append(rest_ref[pl.ds(c, size, stride=cd), :].astype(BF16)[:, : sz.rest])
        return jnp.concatenate(parts, axis=1) if len(parts) > 1 else parts[0]

    for c in range(cd):
        outer = dot(
            matrix(c, sz.columns, rmain_ref, rrest_ref), matrix(c, n, lmain_ref, lrest_ref), 1, 1
        )
        for m in range(w):
            omain_ref[m, pl.ds(c, sz.columns, stride=cd), :] = outer[:, m * LANES : (m + 1) * LANES]
        if sz.rest:
            part = outer[:, w * LANES :]
            orest_ref[pl.ds(c, sz.columns, stride=cd), :] = jnp.concatenate([part, part], axis=1)
    low = lax.broadcasted_iota(jnp.int32, (cd, LANES), 1) < sz.rest
    for r in range(sz.group):
        start = (mine ^ r) * sz.rows
        for tile in range(sz.tiles):
            if tile < sz.rows * w:
                row, m = divmod(tile, w)
                block = omain_ref[m, pl.ds(pl.multiple_of((start + row) * cd, 8), cd), :]
            else:
                at = start + tile - sz.rows * w
                block = jnp.where(
                    low,
                    orest_ref[pl.ds(pl.multiple_of(at * cd, 8), cd), :],
                    orest_ref[pl.ds(pl.multiple_of((at + half) * cd, 8), cd), :],
                )
            outs[r][:, tile * LANES : (tile + 1) * LANES] = block.astype(BF16)


def update_kernel(sz, len_ref, lnp_ref, gate_ref, lnh_ref, tri_ref, lna_ref, biasw_ref, *refs):
    sums, near, pair = refs[: sz.group], refs[sz.group : 2 * sz.group], refs[2 * sz.group : -6]
    first_ref, col_ref, bias_ref, cols_ref, brow_ref, sums_ref = refs[-6:]
    n, w, half, ch, cd = sz.crop, sz.whole, sz.half, sz.channels, sz.chans
    me = len_ref[2]
    mine = me & (sz.group - 1)
    for r in range(sz.group):
        sums_ref[pl.ds(pl.multiple_of((mine ^ r) * cd, 8), cd), :] = sums[r][...].astype(F32)
        for ref, base, owner in (
            (near[r], 2 * sz.tiles, me ^ r),
            (pair[r], 0, me ^ (sz.group + r)),
        ):
            for t in range(sz.block_tiles):
                at = (base + t) * LANES
                row = pl.multiple_of(owner * sz.block + t * cd, 8)
                cols_ref[pl.ds(row, cd), :] = ref[:, at : at + LANES].astype(F32)
    gain_h = jnp.transpose(jnp.broadcast_to(lnh_ref[...], (ch, ch)))
    tri = tri_ref[...]

    def update(tile):
        block = sums_ref[:, tile * LANES : (tile + 1) * LANES]
        average = jnp.mean(block, axis=0, keepdims=True)
        centred = block - average
        variance = jnp.mean(centred * centred, axis=0, keepdims=True)
        hidden = (centred * lax.rsqrt(variance + EPS) * gain_h).astype(BF16)
        return dot(hidden, tri, 0, 0)

    rest = [update(sz.rows * w + q) for q in range(half)] if sz.rest else None
    for j in range(sz.rows):
        parts = [update(j * w + m) for m in range(w)]
        if sz.rest:
            h, q = divmod(j, half)
            parts.append(rest[q][h * sz.rest : (h + 1) * sz.rest])
        change = jnp.concatenate(parts, axis=0) if len(parts) > 1 else parts[0]
        x = cols_ref[pl.ds(j, n, stride=sz.rows), :]
        normed = norm_last(x, lnp_ref[...]).astype(BF16)
        gating = sigmoid(dot(normed, gate_ref[...], 1, 0))
        first = (x + gating * change).astype(BF16)
        first_ref[j] = first
        col = norm_last(first.astype(F32), lna_ref[...]).astype(BF16)
        col_ref[j] = col
        heads = biasw_ref.shape[1]
        brow_ref[pl.ds(j * heads, heads), :] = dot(biasw_ref[...], col, 0, 1)
    bias_ref[...] = brow_ref[...].astype(BF16)


def project_kernel(sz, col_ref, q_ref, k_ref, v_ref, g_ref, qo_ref, ko_ref, vo_ref, go_ref):
    n, ch = sz.crop, sz.channels
    qk = jnp.concatenate([q_ref[...], k_ref[...]], axis=1)
    vg = jnp.transpose(jnp.concatenate([v_ref[...], g_ref[...]], axis=1).astype(F32)).astype(BF16)
    width = q_ref.shape[1]
    for j in range(sz.rows):
        col = col_ref[j]
        both = dot(col, qk, 1, 0)
        qo_ref[j] = both[:, :width].astype(BF16)
        ko_ref[j] = both[:, width:].astype(BF16)
        other = dot(vg, col, 1, 1)
        vo_ref[j] = other[:width].astype(BF16)
        go_ref[j] = sigmoid(other[width:])


def attend_kernel(
    sz, heads, steps, len_ref, q_ref, k_ref, v_ref, g_ref, first_ref, aout_ref, *refs
):
    bias_refs, (out_ref, rows_ref, biasT_ref) = refs[:-3], refs[-3:]
    n, w, ch = sz.crop, sz.whole, sz.channels
    length, me = len_ref[0], len_ref[2]
    width = q_ref.shape[2]
    hd = width // heads
    per = sz.rows * heads
    for ref, offsets in zip(bias_refs, steps):
        for place, offset in enumerate(offsets):
            at = pl.ds(pl.multiple_of((me ^ offset) * per, 8), per)
            part = ref[place].astype(F32) * LOG2E
            for m in range(w):
                rows_ref[m, at, :] = part[:, m * LANES : (m + 1) * LANES]
            if sz.rest:
                rows_ref[w, at, : sz.rest] = part[:, w * LANES :]
    key = lax.broadcasted_iota(jnp.int32, (n, LANES), 0)
    dead = jnp.where(key < length, 0.0, -1e9 * LOG2E).astype(F32)
    halves = []
    for head in range(heads):
        b = [
            jnp.transpose(rows_ref[m, pl.ds(head, n, stride=heads), :])
            for m in range(w + (sz.rest > 0))
        ]
        if sz.rest:
            b[w] = b[w][: sz.rest]
        b = jnp.concatenate(b, axis=0) if len(b) > 1 else b[0]
        for m in range(w):
            biasT_ref[:, (head * w + m) * LANES : (head * w + m + 1) * LANES] = (
                b[:, m * LANES : (m + 1) * LANES] + dead
            )
        if sz.rest:
            halves.append(b[:, w * LANES :])
    per_tile = LANES // sz.rest if sz.rest else 1
    base = heads * w
    if sz.rest:
        for t in range(heads // per_tile):
            biasT_ref[:, (base + t) * LANES : (base + t + 1) * LANES] = (
                jnp.concatenate(halves[t * per_tile : (t + 1) * per_tile], axis=1) + dead
            )
    lane = lax.broadcasted_iota(jnp.int32, (1, width), 1)
    head_masks = [((lane >= h * hd) & (lane < (h + 1) * hd)).astype(BF16) for h in range(heads)]
    scale = (hd ** (-0.5)) * LOG2E
    for j in range(sz.rows):
        q = q_ref[j]
        masked = [q * head_masks[h] for h in range(heads)]
        pieces = [masked[h][: w * LANES] for h in range(heads)]
        if sz.rest:
            pieces += [masked[h][w * LANES :] for h in range(heads)]
        stacked = jnp.concatenate(pieces, axis=0)
        scores = dot(k_ref[j], stacked, 1, 1) * scale + biasT_ref[...]
        top = jnp.max(scores, axis=0, keepdims=True)
        weights = jnp.exp2(scores - top)
        total = jnp.sum(weights, axis=0, keepdims=True)
        mixed = dot(v_ref[j], weights.astype(BF16), 1, 0)
        inverse = 1.0 / total
        mains, rests = [], []
        for h in range(heads):
            sl = slice(h * w * LANES, (h + 1) * w * LANES)
            mains.append(mixed[h * hd : (h + 1) * hd, sl] * inverse[:, sl])
            if sz.rest:
                t, part = divmod(h, per_tile)
                sl = slice((base + t) * LANES, (base + t + 1) * LANES)
                piece = mixed[h * hd : (h + 1) * hd, sl] * inverse[:, sl]
                rests.append(piece[:, part * sz.rest : (part + 1) * sz.rest])
        attended = jnp.concatenate(mains, axis=0)
        if sz.rest:
            attended = jnp.concatenate([attended, jnp.concatenate(rests, axis=0)], axis=1)
        gated = (attended * g_ref[j]).astype(BF16)
        total_out = first_ref[j].astype(F32) + dot(gated, aout_ref[...], 0, 0)
        out_ref[j] = total_out.astype(BF16)


def spread(block, devices):
    pieces, offsets = [block[None]], [[0]]
    bit = devices // 2
    while bit:
        held = jnp.concatenate(pieces, axis=0) if len(pieces) > 1 else pieces[0]
        got = lax.ppermute(held, AXES, [(d, d ^ bit) for d in range(devices)])
        known = [o for part in offsets for o in part]
        pieces.append(got)
        offsets.append([o ^ bit for o in known])
        bit //= 2
    return pieces, offsets


def shards(
    devices,
    pair_rep, length, ln_pair, tri_in, tri_gate, ln_hidden, tri_out, ln_att,
    att_q, att_k, att_v, att_bias, att_gate, att_out,
):
    rows, crop, ch = pair_rep.shape
    heads = att_bias.shape[1]
    sz = Sizes(rows, crop, devices, ch)
    n, cd = crop, sz.chans
    me = lax.axis_index(AXES).astype(jnp.int32)
    info = jnp.stack([length[0], me * rows, me])

    def bound(kernel, *extra):
        def run(*refs):
            return kernel(sz, *extra, *refs)

        return run

    shape = jax.ShapeDtypeStruct
    g, t, bt = sz.group, sz.tiles, sz.block_tiles

    def slab(tiles):
        return shape((cd, tiles * LANES), BF16)

    def send(blocks, offset):
        return [
            block
            if not (offset ^ r)
            else lax.ppermute(block, AXES, [(d, d ^ offset ^ r) for d in range(devices)])
            for r, block in enumerate(blocks)
        ]

    made = call(
        bound(edges_kernel),
        [slab(2 * t + bt)] * g + [slab(t)] * g + [slab(bt)] * g,
        (info, pair_rep, ln_pair[None], tri_in),
        scratch=[
            pltpu.VMEM((rows * crop, ch), BF16),
            pltpu.VMEM((devices, bt * cd, ch), F32),
        ],
        smem=(0,),
        name="edges",
    )
    far = send(made[g : 2 * g], g)
    near = send(made[:g], 0)
    late, far, near = lax.optimization_barrier((made[2 * g :], far, near))
    pair = send(late, g)
    rest = sz.rest > 0
    outer = call(
        bound(outer_kernel),
        [slab(t)] * g,
        (info, *near, *far),
        scratch=[
            pltpu.VMEM((sz.whole, n * cd, LANES), F32),
            pltpu.VMEM((n * cd if rest else 8, LANES), F32),
            pltpu.VMEM((sz.whole, sz.columns * cd, LANES), F32),
            pltpu.VMEM((sz.columns * cd if rest else 8, LANES), F32),
            pltpu.VMEM((sz.whole, sz.columns * cd, LANES), F32),
            pltpu.VMEM((sz.columns * cd if rest else 8, LANES), F32),
        ],
        smem=(0,),
        name="outer",
    )
    sums = send(outer, 0)
    first, col, bias = call(
        bound(update_kernel),
        [
            shape((rows, n, ch), BF16),
            shape((rows, n, ch), BF16),
            shape((rows * heads, n), BF16),
        ],
        (
            info, ln_pair[None], tri_gate, ln_hidden[None], tri_out, ln_att[None], att_bias,
            *sums, *near, *pair,
        ),
        scratch=[
            pltpu.VMEM((devices * sz.block + cd, ch), F32),
            pltpu.VMEM((rows * heads, n), F32),
            pltpu.VMEM((ch, rows * n), F32),
        ],
        smem=(0,),
        name="update",
    )
    pieces, steps = spread(bias, devices)
    query, key, value, gate = call(
        bound(project_kernel),
        [
            shape((rows, n, att_q.shape[1]), BF16),
            shape((rows, n, att_q.shape[1]), BF16),
            shape((rows, att_q.shape[1], n), BF16),
            shape((rows, att_q.shape[1], n), F32),
        ],
        (col, att_q, att_k, att_v, att_gate),
        name="project",
    )
    out = call(
        bound(attend_kernel, heads, steps),
        shape((rows, n, ch), BF16),
        (info, query, key, value, gate, first, att_out, *pieces),
        scratch=[
            pltpu.VMEM((-(-n // LANES), n * heads, LANES), F32),
            pltpu.VMEM((n, heads * n), F32),
        ],
        smem=(0,),
        name="attend",
    )
    return jnp.swapaxes(out, 0, 1)


def solution(mesh):
    devices = mesh.shape["row"] * mesh.shape["node"]

    def body(*args):
        return shards(devices, *args)

    return jax.shard_map(
        body,
        mesh=mesh,
        in_specs=(P(("grp", "row", "node"), None, None), P("grp")) + (P(),) * 12,
        out_specs=P("grp", AXES, None),
        check_vma=False,
    )
```

```python
import jax
import jax.numpy as jnp
from jax import lax
from jax.experimental import pallas as pl
from jax.experimental.pallas import tpu as pltpu
from jax.sharding import PartitionSpec as P

EPS = 1e-05
LANES = 128
LOG2E = 1.4426950408889634
F32 = jnp.float32
BF16 = jnp.bfloat16
AXES = ("row", "node")
VMEM_BYTES = 48 * 1024 * 1024


def norm_last(values, gain):
    average = jnp.mean(values, axis=-1, keepdims=True)
    centred = values - average
    variance = jnp.mean(centred * centred, axis=-1, keepdims=True)
    return centred * lax.rsqrt(variance + EPS) * gain


def sigmoid(values):
    return 0.5 * jnp.tanh(0.5 * values) + 0.5


def dot(a, b, a_dim, b_dim):
    return lax.dot_general(a, b, (((a_dim,), (b_dim,)), ((), ())), preferred_element_type=F32)


def call(kernel, out_shape, args, scratch=(), smem=(), name=None):
    specs = [
        pl.BlockSpec(memory_space=pltpu.SMEM if n in smem else pltpu.VMEM) for n in range(len(args))
    ]
    single = not isinstance(out_shape, (list, tuple))
    vmem = pl.BlockSpec(memory_space=pltpu.VMEM)
    return pl.pallas_call(
        kernel,
        out_shape=out_shape,
        in_specs=specs,
        out_specs=vmem if single else [vmem] * len(out_shape),
        scratch_shapes=list(scratch),
        compiler_params=pltpu.CompilerParams(vmem_limit_bytes=VMEM_BYTES),
        name=name,
    )(*args)


class Sizes:
    def __init__(self, rows, crop, devices, channels):
        self.rows, self.crop, self.devices, self.channels = rows, crop, devices, channels
        self.half = rows // 2
        self.group = devices // 2
        self.columns = rows * self.group
        self.whole = crop // LANES
        self.rest = crop % LANES
        self.tiles = rows * crop // LANES
        self.chans = channels // self.group
        self.block = rows * rows
        self.block_tiles = -(-self.block // self.chans)


def project_edges(sz, info, norm_ref, gate_w, value_w, store):
    length, first = info[0], info[1]
    main = sz.whole * LANES
    lane = lax.broadcasted_iota(jnp.int32, (1, LANES), 1)

    def live(tile):
        if tile < sz.rows * sz.whole:
            row, m = divmod(tile, sz.whole)
            return ((first + row < length) & (m * LANES + lane < length)).astype(F32)
        q = tile - sz.rows * sz.whole
        second = lane >= sz.rest
        row = first + q + jnp.where(second, sz.half, 0)
        k = main + lane - jnp.where(second, sz.rest, 0)
        return ((row < length) & (k < length)).astype(F32)

    step = 2 if sz.tiles % 2 == 0 else 1
    for tile in range(0, sz.tiles, step):
        n = norm_ref[pl.ds(tile * LANES, step * LANES), :]
        mask = jnp.concatenate([live(tile + s) for s in range(step)], axis=1)
        edge = sigmoid(dot(gate_w, n, 1, 1)) * dot(value_w, n, 1, 1) * mask
        edge = edge.astype(BF16)
        for g in range(sz.group):
            store(g, tile, step, edge[g * sz.chans : (g + 1) * sz.chans])


def turned(w):
    return jnp.transpose(w.astype(F32)).astype(BF16)


def left_kernel(sz, len_ref, x_ref, ln_ref, w_ref, out_ref, norm_ref):
    gain = ln_ref[...]
    main = sz.whole * LANES
    for row in range(sz.rows):
        normed = norm_last(x_ref[row].astype(F32), gain).astype(BF16)
        norm_ref[pl.ds(row * main, main), :] = normed[:main]
        if sz.rest:
            h, q = divmod(row, sz.half)
            norm_ref[pl.ds(sz.rows * main + q * LANES + h * sz.rest, sz.rest), :] = normed[main:]

    def store(g, tile, step, edge):
        out_ref[g, :, tile * LANES : (tile + step) * LANES] = edge

    project_edges(sz, len_ref, norm_ref, turned(w_ref[0]), turned(w_ref[1]), store)


def right_kernel(sz, len_ref, x_ref, far_ref, norm_ref, w_ref, out_ref, pair_ref):
    cd = sz.chans
    upper = len_ref[3]
    for row in range(sz.rows):
        for h in range(2):
            x = x_ref[row, h * sz.columns : (h + 1) * sz.columns, :].astype(F32)
            if h:
                x = jnp.where(upper > 0, x, own)
            else:
                own = x
        for base, values in ((0, x), (1, far_ref[row].astype(F32))):
            for g in range(sz.group):
                pair_ref[base, g, row * sz.rows : (row + 1) * sz.rows, :] = values[
                    g * sz.rows : (g + 1) * sz.rows
                ]
    for base in range(2):
        for g in range(sz.group):
            for t in range(sz.block_tiles):
                at = (sz.tiles + base * sz.block_tiles + t) * LANES
                out_ref[g, :, at : at + LANES] = pair_ref[
                    base, g, t * cd : (t + 1) * cd, :
                ].astype(BF16)

    def store(g, tile, step, edge):
        out_ref[g, :, tile * LANES : (tile + step) * LANES] = edge

    project_edges(sz, len_ref, norm_ref, turned(w_ref[2]), turned(w_ref[3]), store)


def outer_kernel(
    sz, len_ref, own_ref, far_ref, right_ref, out_ref,
    lmain_ref, lrest_ref, rmain_ref, rrest_ref, omain_ref, orest_ref,
):
    upper = len_ref[3]
    cd, n, w, half = sz.chans, sz.crop, sz.whole, sz.half

    def unpack(ref, g, owner, main_ref, rest_ref):
        for tile in range(sz.tiles):
            block = ref[g, :, tile * LANES : (tile + 1) * LANES].astype(F32)
            if tile < sz.rows * w:
                row, m = divmod(tile, w)
                main_ref[m, pl.ds(pl.multiple_of((owner * sz.rows + row) * cd, 8), cd), :] = block
            else:
                row = owner * sz.rows + tile - sz.rows * w
                rest_ref[pl.ds(pl.multiple_of(row * cd, 8), cd), :] = block
                rest_ref[pl.ds(pl.multiple_of((row + half) * cd, 8), cd), :] = pltpu.roll(
                    block, sz.rest, 1
                )

    for g in range(sz.group):
        unpack(own_ref, g, upper * sz.group + g, lmain_ref, lrest_ref)
        unpack(right_ref, g, g, rmain_ref, rrest_ref)
        unpack(far_ref, g, (1 - upper) * sz.group + g, lmain_ref, lrest_ref)

    def matrix(c, size, main_ref, rest_ref):
        parts = [main_ref[m, pl.ds(c, size, stride=cd), :].astype(BF16) for m in range(w)]
        if sz.rest:
            parts.append(rest_ref[pl.ds(c, size, stride=cd), :].astype(BF16)[:, : sz.rest])
        return jnp.concatenate(parts, axis=1) if len(parts) > 1 else parts[0]

    for c in range(cd):
        outer = dot(
            matrix(c, sz.columns, rmain_ref, rrest_ref), matrix(c, n, lmain_ref, lrest_ref), 1, 1
        )
        for m in range(w):
            omain_ref[m, pl.ds(c, sz.columns, stride=cd), :] = outer[:, m * LANES : (m + 1) * LANES]
        if sz.rest:
            part = outer[:, w * LANES :]
            orest_ref[pl.ds(c, sz.columns, stride=cd), :] = jnp.concatenate([part, part], axis=1)
    low = lax.broadcasted_iota(jnp.int32, (cd, LANES), 1) < sz.rest
    for g in range(sz.group):
        start = g * sz.rows
        for tile in range(sz.tiles):
            if tile < sz.rows * w:
                row, m = divmod(tile, w)
                block = omain_ref[m, pl.ds((start + row) * cd, cd), :]
            else:
                at = start + tile - sz.rows * w
                block = jnp.where(
                    low,
                    orest_ref[pl.ds(at * cd, cd), :],
                    orest_ref[pl.ds((at + half) * cd, cd), :],
                )
            out_ref[g, :, tile * LANES : (tile + 1) * LANES] = block.astype(BF16)


def update_kernel(
    sz, len_ref, lnp_ref, gate_ref, lnh_ref, tri_ref, lna_ref, biasw_ref, sums_ref, pair_ref,
    first_ref, col_ref, bias_ref, cols_ref, brow_ref,
):
    n, w, half, ch, cd = sz.crop, sz.whole, sz.half, sz.channels, sz.chans
    upper = len_ref[3]
    for base, side in ((0, upper), (1, 1 - upper)):
        for g in range(sz.group):
            for t in range(sz.block_tiles):
                at = (sz.tiles + base * sz.block_tiles + t) * LANES
                row = pl.multiple_of((side * sz.group + g) * sz.block + t * cd, 8)
                cols_ref[pl.ds(row, cd), :] = pair_ref[g, :, at : at + LANES].astype(F32)
    gain_h = jnp.transpose(jnp.broadcast_to(lnh_ref[...], (ch, ch)))
    tri = tri_ref[...]

    def update(tile):
        block = sums_ref[:, :, tile * LANES : (tile + 1) * LANES].astype(F32).reshape(ch, LANES)
        average = jnp.mean(block, axis=0, keepdims=True)
        centred = block - average
        variance = jnp.mean(centred * centred, axis=0, keepdims=True)
        hidden = (centred * lax.rsqrt(variance + EPS) * gain_h).astype(BF16)
        return dot(hidden, tri, 0, 0)

    rest = [update(sz.rows * w + q) for q in range(half)] if sz.rest else None
    for j in range(sz.rows):
        parts = [update(j * w + m) for m in range(w)]
        if sz.rest:
            h, q = divmod(j, half)
            parts.append(rest[q][h * sz.rest : (h + 1) * sz.rest])
        change = jnp.concatenate(parts, axis=0) if len(parts) > 1 else parts[0]
        x = cols_ref[pl.ds(j, n, stride=sz.rows), :]
        normed = norm_last(x, lnp_ref[...]).astype(BF16)
        gating = sigmoid(dot(normed, gate_ref[...], 1, 0))
        first = (x + gating * change).astype(BF16)
        first_ref[j] = first
        col = norm_last(first.astype(F32), lna_ref[...]).astype(BF16)
        col_ref[j] = col
        heads = biasw_ref.shape[1]
        brow_ref[pl.ds(j * heads, heads), :] = dot(biasw_ref[...], col, 0, 1)
    bias_ref[...] = brow_ref[...].astype(BF16)


def project_kernel(sz, col_ref, q_ref, k_ref, v_ref, g_ref, qo_ref, ko_ref, vo_ref, go_ref):
    n, ch = sz.crop, sz.channels
    qk = jnp.concatenate([q_ref[...], k_ref[...]], axis=1)
    vg = jnp.transpose(jnp.concatenate([v_ref[...], g_ref[...]], axis=1).astype(F32)).astype(BF16)
    width = q_ref.shape[1]
    for j in range(sz.rows):
        col = col_ref[j]
        both = dot(col, qk, 1, 0)
        qo_ref[j] = both[:, :width].astype(BF16)
        ko_ref[j] = both[:, width:].astype(BF16)
        other = dot(vg, col, 1, 1)
        vo_ref[j] = other[:width].astype(BF16)
        go_ref[j] = sigmoid(other[width:])


def attend_kernel(
    sz, heads, steps, len_ref, q_ref, k_ref, v_ref, g_ref, first_ref, aout_ref, *refs
):
    bias_refs, (out_ref, rows_ref, biasT_ref) = refs[:-3], refs[-3:]
    n, w, ch = sz.crop, sz.whole, sz.channels
    length, me = len_ref[0], len_ref[2]
    width = q_ref.shape[2]
    hd = width // heads
    per = sz.rows * heads
    for ref, offsets in zip(bias_refs, steps):
        for place, offset in enumerate(offsets):
            at = pl.ds(pl.multiple_of((me ^ offset) * per, 8), per)
            part = ref[place].astype(F32) * LOG2E
            for m in range(w):
                rows_ref[m, at, :] = part[:, m * LANES : (m + 1) * LANES]
            if sz.rest:
                rows_ref[w, at, : sz.rest] = part[:, w * LANES :]
    key = lax.broadcasted_iota(jnp.int32, (n, LANES), 0)
    dead = jnp.where(key < length, 0.0, -1e9 * LOG2E).astype(F32)
    halves = []
    for head in range(heads):
        b = [
            jnp.transpose(rows_ref[m, pl.ds(head, n, stride=heads), :])
            for m in range(w + (sz.rest > 0))
        ]
        if sz.rest:
            b[w] = b[w][: sz.rest]
        b = jnp.concatenate(b, axis=0) if len(b) > 1 else b[0]
        for m in range(w):
            biasT_ref[:, (head * w + m) * LANES : (head * w + m + 1) * LANES] = (
                b[:, m * LANES : (m + 1) * LANES] + dead
            )
        if sz.rest:
            halves.append(b[:, w * LANES :])
    per_tile = LANES // sz.rest if sz.rest else 1
    base = heads * w
    if sz.rest:
        for t in range(heads // per_tile):
            biasT_ref[:, (base + t) * LANES : (base + t + 1) * LANES] = (
                jnp.concatenate(halves[t * per_tile : (t + 1) * per_tile], axis=1) + dead
            )
    lane = lax.broadcasted_iota(jnp.int32, (1, width), 1)
    head_masks = [((lane >= h * hd) & (lane < (h + 1) * hd)).astype(BF16) for h in range(heads)]
    scale = (hd ** (-0.5)) * LOG2E
    for j in range(sz.rows):
        q = q_ref[j]
        masked = [q * head_masks[h] for h in range(heads)]
        pieces = [masked[h][: w * LANES] for h in range(heads)]
        if sz.rest:
            pieces += [masked[h][w * LANES :] for h in range(heads)]
        stacked = jnp.concatenate(pieces, axis=0)
        scores = dot(k_ref[j], stacked, 1, 1) * scale + biasT_ref[...]
        top = jnp.max(scores, axis=0, keepdims=True)
        weights = jnp.exp2(scores - top)
        total = jnp.sum(weights, axis=0, keepdims=True)
        mixed = dot(v_ref[j], weights.astype(BF16), 1, 0)
        inverse = 1.0 / total
        mains, rests = [], []
        for h in range(heads):
            sl = slice(h * w * LANES, (h + 1) * w * LANES)
            mains.append(mixed[h * hd : (h + 1) * hd, sl] * inverse[:, sl])
            if sz.rest:
                t, part = divmod(h, per_tile)
                sl = slice((base + t) * LANES, (base + t + 1) * LANES)
                piece = mixed[h * hd : (h + 1) * hd, sl] * inverse[:, sl]
                rests.append(piece[:, part * sz.rest : (part + 1) * sz.rest])
        attended = jnp.concatenate(mains, axis=0)
        if sz.rest:
            attended = jnp.concatenate([attended, jnp.concatenate(rests, axis=0)], axis=1)
        gated = (attended * g_ref[j]).astype(BF16)
        total_out = first_ref[j].astype(F32) + dot(gated, aout_ref[...], 0, 0)
        out_ref[j] = total_out.astype(BF16)


def spread(block, devices):
    pieces, offsets = [block[None]], [[0]]
    bit = devices // 2
    while bit:
        held = jnp.concatenate(pieces, axis=0) if len(pieces) > 1 else pieces[0]
        got = lax.ppermute(held, AXES, [(d, d ^ bit) for d in range(devices)])
        known = [o for part in offsets for o in part]
        pieces.append(got)
        offsets.append([o ^ bit for o in known])
        bit //= 2
    return pieces, offsets


def shards(
    devices,
    pair_rep, length, ln_pair, tri_in, tri_gate, ln_hidden, tri_out, ln_att,
    att_q, att_k, att_v, att_bias, att_gate, att_out,
):
    rows, crop, ch = pair_rep.shape
    heads = att_bias.shape[1]
    sz = Sizes(rows, crop, devices, ch)
    n, cd = crop, sz.chans
    me = lax.axis_index(AXES).astype(jnp.int32)
    upper = me // sz.group
    info = jnp.stack([length[0], me * rows, me, upper])
    def bound(kernel, *extra):
        def run(*refs):
            return kernel(sz, *extra, *refs)

        return run

    shape = jax.ShapeDtypeStruct
    g, t, bt = sz.group, sz.tiles, sz.block_tiles

    def slab(tiles):
        return shape((g, cd, tiles * LANES), BF16)

    def mirror(block):
        return lax.ppermute(block, AXES, [(d, d ^ g) for d in range(devices)])

    def within(blocks):
        return lax.all_to_all(
            blocks, AXES, split_axis=0, concat_axis=0, tiled=True,
            axis_index_groups=[list(range(g)), list(range(g, devices))],
        )

    far_pair = mirror(lax.dynamic_slice_in_dim(pair_rep, (1 - upper) * sz.columns, sz.columns, 1))
    left, normed = call(
        bound(left_kernel),
        [slab(t), shape((rows * crop, ch), BF16)],
        (info, pair_rep, ln_pair[None], tri_in),
        smem=(0,),
        name="left",
    )
    left = within(left)
    far_left = mirror(left)
    right = within(
        call(
            bound(right_kernel),
            slab(t + 2 * bt),
            (info, pair_rep, far_pair, normed, tri_in),
            scratch=[pltpu.VMEM((2, g, bt * cd, ch), F32)],
            smem=(0,),
            name="right",
        )
    )
    rest = sz.rest > 0
    outer = call(
        bound(outer_kernel),
        slab(t),
        (info, left, far_left, right),
        scratch=[
            pltpu.VMEM((sz.whole, n * cd, LANES), F32),
            pltpu.VMEM((n * cd if rest else 8, LANES), F32),
            pltpu.VMEM((sz.whole, sz.columns * cd, LANES), F32),
            pltpu.VMEM((sz.columns * cd if rest else 8, LANES), F32),
            pltpu.VMEM((sz.whole, sz.columns * cd, LANES), F32),
            pltpu.VMEM((sz.columns * cd if rest else 8, LANES), F32),
        ],
        smem=(0,),
        name="outer",
    )
    sums = within(outer)
    first, col, bias = call(
        bound(update_kernel),
        [
            shape((rows, n, ch), BF16),
            shape((rows, n, ch), BF16),
            shape((rows * heads, n), BF16),
        ],
        (
            info, ln_pair[None], tri_gate, ln_hidden[None], tri_out, ln_att[None], att_bias,
            sums, right,
        ),
        scratch=[
            pltpu.VMEM((devices * sz.block + cd, ch), F32),
            pltpu.VMEM((rows * heads, n), F32),
        ],
        smem=(0,),
        name="update",
    )
    pieces, steps = spread(bias, devices)
    query, key, value, gate = call(
        bound(project_kernel),
        [
            shape((rows, n, att_q.shape[1]), BF16),
            shape((rows, n, att_q.shape[1]), BF16),
            shape((rows, att_q.shape[1], n), BF16),
            shape((rows, att_q.shape[1], n), F32),
        ],
        (col, att_q, att_k, att_v, att_gate),
        name="project",
    )
    out = call(
        bound(attend_kernel, heads, steps),
        shape((rows, n, ch), BF16),
        (info, query, key, value, gate, first, att_out, *pieces),
        scratch=[
            pltpu.VMEM((-(-n // LANES), n * heads, LANES), F32),
            pltpu.VMEM((n, heads * n), F32),
        ],
        smem=(0,),
        name="attend",
    )
    return jnp.swapaxes(out, 0, 1)


def solution(mesh):
    devices = mesh.shape["row"] * mesh.shape["node"]

    def body(*args):
        return shards(devices, *args)

    return jax.shard_map(
        body,
        mesh=mesh,
        in_specs=(P(("grp", "row", "node"), None, None), P("grp")) + (P(),) * 12,
        out_specs=P("grp", AXES, None),
        check_vma=False,
    )
```

```python
import jax
import jax.numpy as jnp
from jax import lax
from jax.experimental import pallas as pl
from jax.experimental.pallas import tpu as pltpu
from jax.sharding import PartitionSpec as P

EPS = 1e-05
LANES = 128
LOG2E = 1.4426950408889634
F32 = jnp.float32
BF16 = jnp.bfloat16
AXES = ("row", "node")
VMEM_BYTES = 48 * 1024 * 1024


def norm_last(values, gain):
    average = jnp.mean(values, axis=-1, keepdims=True)
    centred = values - average
    variance = jnp.mean(centred * centred, axis=-1, keepdims=True)
    return centred * lax.rsqrt(variance + EPS) * gain


def sigmoid(values):
    return 0.5 * jnp.tanh(0.5 * values) + 0.5


def dot(a, b, a_dim, b_dim):
    return lax.dot_general(a, b, (((a_dim,), (b_dim,)), ((), ())), preferred_element_type=F32)


def call(kernel, out_shape, args, scratch=(), smem=(), name=None):
    specs = [
        pl.BlockSpec(memory_space=pltpu.SMEM if n in smem else pltpu.VMEM) for n in range(len(args))
    ]
    single = not isinstance(out_shape, (list, tuple))
    vmem = pl.BlockSpec(memory_space=pltpu.VMEM)
    return pl.pallas_call(
        kernel,
        out_shape=out_shape,
        in_specs=specs,
        out_specs=vmem if single else [vmem] * len(out_shape),
        scratch_shapes=list(scratch),
        compiler_params=pltpu.CompilerParams(vmem_limit_bytes=VMEM_BYTES),
        name=name,
    )(*args)


class Sizes:
    def __init__(self, rows, crop, devices, channels):
        self.rows, self.crop, self.devices, self.channels = rows, crop, devices, channels
        self.half = rows // 2
        self.group = devices // 2
        self.columns = rows * self.group
        self.whole = crop // LANES
        self.rest = crop % LANES
        self.tiles = rows * crop // LANES
        self.chans = channels // self.group
        self.block = rows * rows
        self.block_tiles = -(-self.block // self.chans)


def edges_kernel(sz, len_ref, x_ref, ln_ref, w_ref, out_ref, *refs):
    near, pair = refs[: sz.group], refs[sz.group : 2 * sz.group]
    norm_ref, pair_ref = refs[2 * sz.group :]
    length, first, me = len_ref[0], len_ref[1], len_ref[2]
    cd, ch = sz.chans, sz.channels
    mine = me & (sz.group - 1)
    r = lax.broadcasted_iota(jnp.int32, (ch, ch), 0)
    e = lax.broadcasted_iota(jnp.int32, (ch, ch), 1)
    plain = (r == e).astype(BF16)
    slots = (((r // cd) ^ mine) * cd + r % cd == e).astype(BF16)
    picks = (plain, plain, slots, slots)
    weights = [dot(pick, w_ref[p], 1, 1).astype(BF16) for p, pick in enumerate(picks)]
    gate_w = jnp.concatenate([weights[0], weights[2]], axis=0)
    value_w = jnp.concatenate([weights[1], weights[3]], axis=0)
    gain = ln_ref[...]
    main = sz.whole * LANES
    for row in range(sz.rows):
        x = x_ref[row].astype(F32)
        for d in range(sz.devices):
            pair_ref[d, row * sz.rows : (row + 1) * sz.rows, :] = x[d * sz.rows : (d + 1) * sz.rows]
        normed = norm_last(x, gain).astype(BF16)
        norm_ref[pl.ds(row * main, main), :] = normed[:main]
        if sz.rest:
            h, q = divmod(row, sz.half)
            norm_ref[pl.ds(sz.rows * main + q * LANES + h * sz.rest, sz.rest), :] = normed[main:]
    for r in range(sz.group):
        for t in range(sz.block_tiles):
            at = (sz.tiles + t) * LANES
            rows = slice(t * cd, (t + 1) * cd)
            near[r][:, at : at + LANES] = pair_ref[me ^ r, rows, :].astype(BF16)
            pair[r][:, t * LANES : (t + 1) * LANES] = pair_ref[me ^ (sz.group + r), rows, :].astype(
                BF16
            )
    lane = lax.broadcasted_iota(jnp.int32, (1, LANES), 1)

    def live(tile):
        if tile < sz.rows * sz.whole:
            row, m = divmod(tile, sz.whole)
            return ((first + row < length) & (m * LANES + lane < length)).astype(F32)
        q = tile - sz.rows * sz.whole
        second = lane >= sz.rest
        row = first + q + jnp.where(second, sz.half, 0)
        k = main + lane - jnp.where(second, sz.rest, 0)
        return ((row < length) & (k < length)).astype(F32)

    step = 2 if sz.tiles % 2 == 0 else 1
    for tile in range(0, sz.tiles, step):
        n = norm_ref[pl.ds(tile * LANES, step * LANES), :]
        mask = jnp.concatenate([live(tile + s) for s in range(step)], axis=1)
        edge = sigmoid(dot(gate_w, n, 1, 1)) * dot(value_w, n, 1, 1) * mask
        edge = edge.astype(BF16)
        to = slice(tile * LANES, (tile + step) * LANES)
        for g in range(sz.group):
            left = edge[g * cd : (g + 1) * cd]
            out_ref[g, :, to] = left
            out_ref[sz.group + g, :, to] = left
            near[g][:, to] = edge[ch + g * cd : ch + (g + 1) * cd]


def outer_kernel(sz, len_ref, left_ref, *refs):
    near, out_ref = refs[: sz.group], refs[sz.group]
    lmain_ref, lrest_ref, rmain_ref, rrest_ref, omain_ref, orest_ref = refs[sz.group + 1 :]
    mine = len_ref[2] & (sz.group - 1)
    cd, n, w, half = sz.chans, sz.crop, sz.whole, sz.half

    def unpack(ref, owner, main_ref, rest_ref):
        for tile in range(sz.tiles):
            block = ref[:, tile * LANES : (tile + 1) * LANES].astype(F32)
            if tile < sz.rows * w:
                row, m = divmod(tile, w)
                main_ref[m, pl.ds(pl.multiple_of((owner * sz.rows + row) * cd, 8), cd), :] = block
            else:
                row = owner * sz.rows + tile - sz.rows * w
                rest_ref[pl.ds(pl.multiple_of(row * cd, 8), cd), :] = block
                rest_ref[pl.ds(pl.multiple_of((row + half) * cd, 8), cd), :] = pltpu.roll(
                    block, sz.rest, 1
                )

    for d in range(sz.devices):
        unpack(left_ref.at[d], jnp.int32(d), lmain_ref, lrest_ref)
    for r in range(sz.group):
        unpack(near[r], mine ^ r, rmain_ref, rrest_ref)

    def matrix(c, size, main_ref, rest_ref):
        parts = [main_ref[m, pl.ds(c, size, stride=cd), :].astype(BF16) for m in range(w)]
        if sz.rest:
            parts.append(rest_ref[pl.ds(c, size, stride=cd), :].astype(BF16)[:, : sz.rest])
        return jnp.concatenate(parts, axis=1) if len(parts) > 1 else parts[0]

    for c in range(cd):
        outer = dot(
            matrix(c, sz.columns, rmain_ref, rrest_ref), matrix(c, n, lmain_ref, lrest_ref), 1, 1
        )
        for m in range(w):
            omain_ref[m, pl.ds(c, sz.columns, stride=cd), :] = outer[:, m * LANES : (m + 1) * LANES]
        if sz.rest:
            part = outer[:, w * LANES :]
            orest_ref[pl.ds(c, sz.columns, stride=cd), :] = jnp.concatenate([part, part], axis=1)
    low = lax.broadcasted_iota(jnp.int32, (cd, LANES), 1) < sz.rest
    for g in range(sz.group):
        start = g * sz.rows
        for tile in range(sz.tiles):
            if tile < sz.rows * w:
                row, m = divmod(tile, w)
                block = omain_ref[m, pl.ds((start + row) * cd, cd), :]
            else:
                at = start + tile - sz.rows * w
                block = jnp.where(
                    low,
                    orest_ref[pl.ds(at * cd, cd), :],
                    orest_ref[pl.ds((at + half) * cd, cd), :],
                )
            out_ref[g, :, tile * LANES : (tile + 1) * LANES] = block.astype(BF16)


def update_kernel(
    sz, len_ref, lnp_ref, gate_ref, lnh_ref, tri_ref, lna_ref, biasw_ref, sums_ref, *refs
):
    near, pair = refs[: sz.group], refs[sz.group : 2 * sz.group]
    first_ref, col_ref, bias_ref, cols_ref, brow_ref = refs[2 * sz.group :]
    n, w, half, ch, cd = sz.crop, sz.whole, sz.half, sz.channels, sz.chans
    me = len_ref[2]
    for r in range(sz.group):
        for ref, base, owner in (
            (near[r], sz.tiles, me ^ r),
            (pair[r], 0, me ^ (sz.group + r)),
        ):
            for t in range(sz.block_tiles):
                at = (base + t) * LANES
                row = pl.multiple_of(owner * sz.block + t * cd, 8)
                cols_ref[pl.ds(row, cd), :] = ref[:, at : at + LANES].astype(F32)
    gain_h = jnp.transpose(jnp.broadcast_to(lnh_ref[...], (ch, ch)))
    tri = tri_ref[...]

    def update(tile):
        block = sums_ref[:, :, tile * LANES : (tile + 1) * LANES].astype(F32).reshape(ch, LANES)
        average = jnp.mean(block, axis=0, keepdims=True)
        centred = block - average
        variance = jnp.mean(centred * centred, axis=0, keepdims=True)
        hidden = (centred * lax.rsqrt(variance + EPS) * gain_h).astype(BF16)
        return dot(hidden, tri, 0, 0)

    rest = [update(sz.rows * w + q) for q in range(half)] if sz.rest else None
    for j in range(sz.rows):
        parts = [update(j * w + m) for m in range(w)]
        if sz.rest:
            h, q = divmod(j, half)
            parts.append(rest[q][h * sz.rest : (h + 1) * sz.rest])
        change = jnp.concatenate(parts, axis=0) if len(parts) > 1 else parts[0]
        x = cols_ref[pl.ds(j, n, stride=sz.rows), :]
        normed = norm_last(x, lnp_ref[...]).astype(BF16)
        gating = sigmoid(dot(normed, gate_ref[...], 1, 0))
        first = (x + gating * change).astype(BF16)
        first_ref[j] = first
        col = norm_last(first.astype(F32), lna_ref[...]).astype(BF16)
        col_ref[j] = col
        heads = biasw_ref.shape[1]
        brow_ref[pl.ds(j * heads, heads), :] = dot(biasw_ref[...], col, 0, 1)
    bias_ref[...] = brow_ref[...].astype(BF16)


def project_kernel(sz, col_ref, q_ref, k_ref, v_ref, g_ref, qo_ref, ko_ref, vo_ref, go_ref):
    n, ch = sz.crop, sz.channels
    qk = jnp.concatenate([q_ref[...], k_ref[...]], axis=1)
    vg = jnp.transpose(jnp.concatenate([v_ref[...], g_ref[...]], axis=1).astype(F32)).astype(BF16)
    width = q_ref.shape[1]
    for j in range(sz.rows):
        col = col_ref[j]
        both = dot(col, qk, 1, 0)
        qo_ref[j] = both[:, :width].astype(BF16)
        ko_ref[j] = both[:, width:].astype(BF16)
        other = dot(vg, col, 1, 1)
        vo_ref[j] = other[:width].astype(BF16)
        go_ref[j] = sigmoid(other[width:])


def attend_kernel(
    sz, heads, steps, len_ref, q_ref, k_ref, v_ref, g_ref, first_ref, aout_ref, *refs
):
    bias_refs, (out_ref, rows_ref, biasT_ref) = refs[:-3], refs[-3:]
    n, w, ch = sz.crop, sz.whole, sz.channels
    length, me = len_ref[0], len_ref[2]
    width = q_ref.shape[2]
    hd = width // heads
    per = sz.rows * heads
    for ref, offsets in zip(bias_refs, steps):
        for place, offset in enumerate(offsets):
            at = pl.ds(pl.multiple_of((me ^ offset) * per, 8), per)
            part = ref[place].astype(F32) * LOG2E
            for m in range(w):
                rows_ref[m, at, :] = part[:, m * LANES : (m + 1) * LANES]
            if sz.rest:
                rows_ref[w, at, : sz.rest] = part[:, w * LANES :]
    key = lax.broadcasted_iota(jnp.int32, (n, LANES), 0)
    dead = jnp.where(key < length, 0.0, -1e9 * LOG2E).astype(F32)
    halves = []
    for head in range(heads):
        b = [
            jnp.transpose(rows_ref[m, pl.ds(head, n, stride=heads), :])
            for m in range(w + (sz.rest > 0))
        ]
        if sz.rest:
            b[w] = b[w][: sz.rest]
        b = jnp.concatenate(b, axis=0) if len(b) > 1 else b[0]
        for m in range(w):
            biasT_ref[:, (head * w + m) * LANES : (head * w + m + 1) * LANES] = (
                b[:, m * LANES : (m + 1) * LANES] + dead
            )
        if sz.rest:
            halves.append(b[:, w * LANES :])
    per_tile = LANES // sz.rest if sz.rest else 1
    base = heads * w
    if sz.rest:
        for t in range(heads // per_tile):
            biasT_ref[:, (base + t) * LANES : (base + t + 1) * LANES] = (
                jnp.concatenate(halves[t * per_tile : (t + 1) * per_tile], axis=1) + dead
            )
    lane = lax.broadcasted_iota(jnp.int32, (1, width), 1)
    head_masks = [((lane >= h * hd) & (lane < (h + 1) * hd)).astype(BF16) for h in range(heads)]
    scale = (hd ** (-0.5)) * LOG2E
    for j in range(sz.rows):
        q = q_ref[j]
        masked = [q * head_masks[h] for h in range(heads)]
        pieces = [masked[h][: w * LANES] for h in range(heads)]
        if sz.rest:
            pieces += [masked[h][w * LANES :] for h in range(heads)]
        stacked = jnp.concatenate(pieces, axis=0)
        scores = dot(k_ref[j], stacked, 1, 1) * scale + biasT_ref[...]
        top = jnp.max(scores, axis=0, keepdims=True)
        weights = jnp.exp2(scores - top)
        total = jnp.sum(weights, axis=0, keepdims=True)
        mixed = dot(v_ref[j], weights.astype(BF16), 1, 0)
        inverse = 1.0 / total
        mains, rests = [], []
        for h in range(heads):
            sl = slice(h * w * LANES, (h + 1) * w * LANES)
            mains.append(mixed[h * hd : (h + 1) * hd, sl] * inverse[:, sl])
            if sz.rest:
                t, part = divmod(h, per_tile)
                sl = slice((base + t) * LANES, (base + t + 1) * LANES)
                piece = mixed[h * hd : (h + 1) * hd, sl] * inverse[:, sl]
                rests.append(piece[:, part * sz.rest : (part + 1) * sz.rest])
        attended = jnp.concatenate(mains, axis=0)
        if sz.rest:
            attended = jnp.concatenate([attended, jnp.concatenate(rests, axis=0)], axis=1)
        gated = (attended * g_ref[j]).astype(BF16)
        total_out = first_ref[j].astype(F32) + dot(gated, aout_ref[...], 0, 0)
        out_ref[j] = total_out.astype(BF16)


def spread(block, devices):
    pieces, offsets = [block[None]], [[0]]
    bit = devices // 2
    while bit:
        held = jnp.concatenate(pieces, axis=0) if len(pieces) > 1 else pieces[0]
        got = lax.ppermute(held, AXES, [(d, d ^ bit) for d in range(devices)])
        known = [o for part in offsets for o in part]
        pieces.append(got)
        offsets.append([o ^ bit for o in known])
        bit //= 2
    return pieces, offsets


def shards(
    devices,
    pair_rep, length, ln_pair, tri_in, tri_gate, ln_hidden, tri_out, ln_att,
    att_q, att_k, att_v, att_bias, att_gate, att_out,
):
    rows, crop, ch = pair_rep.shape
    heads = att_bias.shape[1]
    sz = Sizes(rows, crop, devices, ch)
    n, cd = crop, sz.chans
    me = lax.axis_index(AXES).astype(jnp.int32)
    info = jnp.stack([length[0], me * rows, me])
    def bound(kernel, *extra):
        def run(*refs):
            return kernel(sz, *extra, *refs)

        return run

    shape = jax.ShapeDtypeStruct
    g, t, bt = sz.group, sz.tiles, sz.block_tiles

    def slab(tiles, *lead):
        return shape((*lead, cd, tiles * LANES), BF16)

    def send(blocks, offset):
        return [
            block
            if not (offset ^ r)
            else lax.ppermute(block, AXES, [(d, d ^ offset ^ r) for d in range(devices)])
            for r, block in enumerate(blocks)
        ]

    left, *others = call(
        bound(edges_kernel),
        [slab(t, devices)] + [slab(t + bt)] * g + [slab(bt)] * g,
        (info, pair_rep, ln_pair[None], tri_in),
        scratch=[
            pltpu.VMEM((rows * crop, ch), BF16),
            pltpu.VMEM((devices, bt * cd, ch), F32),
        ],
        smem=(0,),
        name="edges",
    )
    left = lax.all_to_all(left, AXES, split_axis=0, concat_axis=0, tiled=True)
    near = send(others[:g], 0)
    rest = sz.rest > 0
    outer = call(
        bound(outer_kernel),
        slab(t, g),
        (info, left, *near),
        scratch=[
            pltpu.VMEM((sz.whole, n * cd, LANES), F32),
            pltpu.VMEM((n * cd if rest else 8, LANES), F32),
            pltpu.VMEM((sz.whole, sz.columns * cd, LANES), F32),
            pltpu.VMEM((sz.columns * cd if rest else 8, LANES), F32),
            pltpu.VMEM((sz.whole, sz.columns * cd, LANES), F32),
            pltpu.VMEM((sz.columns * cd if rest else 8, LANES), F32),
        ],
        smem=(0,),
        name="outer",
    )
    late, outer = lax.optimization_barrier((others[g:], outer))
    sums = lax.all_to_all(
        outer, AXES, split_axis=0, concat_axis=0, tiled=True,
        axis_index_groups=[list(range(g)), list(range(g, devices))],
    )
    pair = send(late, g)
    first, col, bias = call(
        bound(update_kernel),
        [
            shape((rows, n, ch), BF16),
            shape((rows, n, ch), BF16),
            shape((rows * heads, n), BF16),
        ],
        (
            info, ln_pair[None], tri_gate, ln_hidden[None], tri_out, ln_att[None], att_bias,
            sums, *near, *pair,
        ),
        scratch=[
            pltpu.VMEM((devices * sz.block + cd, ch), F32),
            pltpu.VMEM((rows * heads, n), F32),
        ],
        smem=(0,),
        name="update",
    )
    pieces, steps = spread(bias, devices)
    query, key, value, gate = call(
        bound(project_kernel),
        [
            shape((rows, n, att_q.shape[1]), BF16),
            shape((rows, n, att_q.shape[1]), BF16),
            shape((rows, att_q.shape[1], n), BF16),
            shape((rows, att_q.shape[1], n), F32),
        ],
        (col, att_q, att_k, att_v, att_gate),
        name="project",
    )
    out = call(
        bound(attend_kernel, heads, steps),
        shape((rows, n, ch), BF16),
        (info, query, key, value, gate, first, att_out, *pieces),
        scratch=[
            pltpu.VMEM((-(-n // LANES), n * heads, LANES), F32),
            pltpu.VMEM((n, heads * n), F32),
        ],
        smem=(0,),
        name="attend",
    )
    return jnp.swapaxes(out, 0, 1)


def solution(mesh):
    devices = mesh.shape["row"] * mesh.shape["node"]

    def body(*args):
        return shards(devices, *args)

    return jax.shard_map(
        body,
        mesh=mesh,
        in_specs=(P(("grp", "row", "node"), None, None), P("grp")) + (P(),) * 12,
        out_specs=P("grp", AXES, None),
        check_vma=False,
    )
```

```python
import jax
import jax.numpy as jnp
from jax import lax
from jax.experimental import pallas as pl
from jax.experimental.pallas import tpu as pltpu
from jax.sharding import PartitionSpec as P

EPS = 1e-05
LANES = 128
LOG2E = 1.4426950408889634
F32 = jnp.float32
BF16 = jnp.bfloat16
AXES = ("row", "node")
VMEM_BYTES = 48 * 1024 * 1024


def norm_last(values, gain):
    average = jnp.mean(values, axis=-1, keepdims=True)
    centred = values - average
    variance = jnp.mean(centred * centred, axis=-1, keepdims=True)
    return centred * lax.rsqrt(variance + EPS) * gain


def sigmoid(values):
    return 0.5 * jnp.tanh(0.5 * values) + 0.5


def dot(a, b, a_dim, b_dim):
    return lax.dot_general(a, b, (((a_dim,), (b_dim,)), ((), ())), preferred_element_type=F32)


def call(kernel, out_shape, args, scratch=(), smem=(), name=None):
    specs = [
        pl.BlockSpec(memory_space=pltpu.SMEM if n in smem else pltpu.VMEM) for n in range(len(args))
    ]
    single = not isinstance(out_shape, (list, tuple))
    vmem = pl.BlockSpec(memory_space=pltpu.VMEM)
    return pl.pallas_call(
        kernel,
        out_shape=out_shape,
        in_specs=specs,
        out_specs=vmem if single else [vmem] * len(out_shape),
        scratch_shapes=list(scratch),
        compiler_params=pltpu.CompilerParams(vmem_limit_bytes=VMEM_BYTES),
        name=name,
    )(*args)


class Sizes:
    def __init__(self, rows, crop, devices, channels):
        self.rows, self.crop, self.devices = rows, crop, devices
        self.half = rows // 2
        self.whole = crop // LANES
        self.rest = crop % LANES
        self.tiles = rows * crop // LANES
        self.chans = channels // devices
        self.fold = max(1, 16 // self.chans)
        while self.tiles % self.fold:
            self.fold //= 2
        self.fold_tiles = self.tiles // self.fold
        self.channels = channels

        self.block = rows * rows
        self.packed = self.fold * self.chans
        self.block_tiles = -(-self.block // self.packed)


def edges_kernel(sz, len_ref, x_ref, ln_ref, w_ref, out_ref, norm_ref):
    length, first = len_ref[0], len_ref[1]
    cd, two = sz.chans, 2 * sz.chans
    ch = sz.channels
    r = lax.broadcasted_iota(jnp.int32, (2 * ch, 2 * ch), 0)
    e = lax.broadcasted_iota(jnp.int32, (2 * ch, 2 * ch), 1)
    target = ((r // cd) % 2) * ch + (r // two) * cd + r % cd
    pick = (target == e).astype(BF16)
    gate_w = dot(pick, jnp.concatenate([w_ref[0], w_ref[2]], axis=1), 1, 1).astype(BF16)
    value_w = dot(pick, jnp.concatenate([w_ref[1], w_ref[3]], axis=1), 1, 1).astype(BF16)
    gain = ln_ref[...]
    main = sz.whole * LANES
    for row in range(sz.rows):
        x = x_ref[row].astype(F32)
        normed = norm_last(x, gain).astype(BF16)
        norm_ref[pl.ds(row * main, main), :] = normed[:main]
        if sz.rest:
            h, q = divmod(row, sz.half)
            norm_ref[pl.ds(sz.rows * main + q * LANES + h * sz.rest, sz.rest), :] = normed[main:]
    lane = lax.broadcasted_iota(jnp.int32, (1, LANES), 1)

    def live(tile):
        if tile < sz.rows * sz.whole:
            row, m = divmod(tile, sz.whole)
            return ((first + row < length) & (m * LANES + lane < length)).astype(F32)
        q = tile - sz.rows * sz.whole
        second = lane >= sz.rest
        row = first + q + jnp.where(second, sz.half, 0)
        k = main + lane - jnp.where(second, sz.rest, 0)
        return ((row < length) & (k < length)).astype(F32)

    step = 2 if sz.tiles % 2 == 0 else 1
    for tile in range(0, sz.tiles, step):
        n = norm_ref[pl.ds(tile * LANES, step * LANES), :]
        mask = jnp.concatenate([live(tile + s) for s in range(step)], axis=1)
        edge = sigmoid(dot(gate_w, n, 1, 1)) * dot(value_w, n, 1, 1) * mask
        out_ref[:, :, tile * LANES : (tile + step) * LANES] = edge.reshape(
            sz.devices, two, step * LANES
        ).astype(BF16)


def outer_kernel(sz, e_ref, x_ref, out_ref, main_ref, rest_ref, omain_ref, orest_ref, pair_ref):
    cd, two = sz.chans, 2 * sz.chans
    n, w, half = sz.crop, sz.whole, sz.half
    for s in range(sz.devices):
        for tile in range(sz.tiles):
            block = e_ref[s, :, tile * LANES : (tile + 1) * LANES].astype(F32)
            if tile < sz.rows * w:
                row, m = divmod(tile, w)
                main_ref[m, pl.ds((s * sz.rows + row) * two, two), :] = block
            else:
                at = s * sz.rows + tile - sz.rows * w
                rest_ref[pl.ds(at * two, two), :] = block
                rest_ref[pl.ds((at + half) * two, two), :] = pltpu.roll(block, sz.rest, 1)

    def matrix(index):
        parts = [main_ref[m, pl.ds(index, n, stride=two), :].astype(BF16) for m in range(w)]
        if sz.rest:
            parts.append(rest_ref[pl.ds(index, n, stride=two), :].astype(BF16)[:, : sz.rest])
        return jnp.concatenate(parts, axis=1) if len(parts) > 1 else parts[0]

    for c in range(cd):
        outer = dot(matrix(cd + c), matrix(c), 1, 1)
        for m in range(w):
            omain_ref[m, pl.ds(c, n, stride=cd), :] = outer[:, m * LANES : (m + 1) * LANES]
        if sz.rest:
            part = outer[:, w * LANES :]
            orest_ref[pl.ds(c, n, stride=cd), :] = jnp.concatenate([part, part], axis=1)
    low = lax.broadcasted_iota(jnp.int32, (cd, LANES), 1) < sz.rest
    for s in range(sz.devices):
        for t in range(sz.fold_tiles):
            blocks = []
            for f in range(sz.fold):
                tile = f * sz.fold_tiles + t
                if tile < sz.rows * w:
                    row, m = divmod(tile, w)
                    blocks.append(omain_ref[m, pl.ds((s * sz.rows + row) * cd, cd), :])
                else:
                    at = s * sz.rows + tile - sz.rows * w
                    one = orest_ref[pl.ds(at * cd, cd), :]
                    blocks.append(jnp.where(low, one, orest_ref[pl.ds((at + half) * cd, cd), :]))
            block = jnp.concatenate(blocks, axis=0) if len(blocks) > 1 else blocks[0]
            out_ref[s, :, t * LANES : (t + 1) * LANES] = block.astype(BF16)
    for row in range(sz.rows):
        x = x_ref[row].astype(F32)
        for d in range(sz.devices):
            pair_ref[d, row * sz.rows : (row + 1) * sz.rows, :] = x[d * sz.rows : (d + 1) * sz.rows]
    high = sz.packed
    for d in range(sz.devices):
        for t in range(sz.block_tiles):
            at = (sz.fold_tiles + t) * LANES
            out_ref[d, :, at : at + LANES] = pair_ref[d, t * high : (t + 1) * high, :].astype(BF16)


def update_kernel(
    sz, o_ref, lnp_ref, gate_ref, lnh_ref, tri_ref, lna_ref, biasw_ref,
    first_ref, col_ref, bias_ref, cols_ref, brow_ref,
):
    n, w, half, ch = sz.crop, sz.whole, sz.half, sz.channels
    high = sz.packed
    for s in range(sz.devices):
        for t in range(sz.block_tiles):
            at = (sz.fold_tiles + t) * LANES
            rows = pl.ds(s * sz.block + t * high, high)
            cols_ref[rows, :] = o_ref[s, :, at : at + LANES].astype(F32)
    gain_h = jnp.transpose(jnp.broadcast_to(lnh_ref[...], (ch, ch)))
    tri = tri_ref[...]

    def update(tile):
        f, t = divmod(tile, sz.fold_tiles)
        block = o_ref[:, :, t * LANES : (t + 1) * LANES].astype(F32)
        block = block[:, f * sz.chans : (f + 1) * sz.chans, :].reshape(ch, LANES)
        average = jnp.mean(block, axis=0, keepdims=True)
        centred = block - average
        variance = jnp.mean(centred * centred, axis=0, keepdims=True)
        hidden = (centred * lax.rsqrt(variance + EPS) * gain_h).astype(BF16)
        return dot(hidden, tri, 0, 0)

    rest = [update(sz.rows * w + q) for q in range(half)] if sz.rest else None
    for j in range(sz.rows):
        parts = [update(j * w + m) for m in range(w)]
        if sz.rest:
            h, q = divmod(j, half)
            parts.append(rest[q][h * sz.rest : (h + 1) * sz.rest])
        change = jnp.concatenate(parts, axis=0) if len(parts) > 1 else parts[0]
        x = cols_ref[pl.ds(j, n, stride=sz.rows), :]
        normed = norm_last(x, lnp_ref[...]).astype(BF16)
        gating = sigmoid(dot(normed, gate_ref[...], 1, 0))
        first = (x + gating * change).astype(BF16)
        first_ref[j] = first
        col = norm_last(first.astype(F32), lna_ref[...]).astype(BF16)
        col_ref[j] = col
        heads = biasw_ref.shape[1]
        brow_ref[pl.ds(j * heads, heads), :] = dot(biasw_ref[...], col, 0, 1)
    bias_ref[...] = brow_ref[...].astype(BF16)


def project_kernel(sz, col_ref, q_ref, k_ref, v_ref, g_ref, qo_ref, ko_ref, vo_ref, go_ref):
    n, ch = sz.crop, sz.channels
    qk = jnp.concatenate([q_ref[...], k_ref[...]], axis=1)
    vg = jnp.transpose(jnp.concatenate([v_ref[...], g_ref[...]], axis=1).astype(F32)).astype(BF16)
    width = q_ref.shape[1]
    for j in range(sz.rows):
        col = col_ref[j]
        both = dot(col, qk, 1, 0)
        qo_ref[j] = both[:, :width].astype(BF16)
        ko_ref[j] = both[:, width:].astype(BF16)
        other = dot(vg, col, 1, 1)
        vo_ref[j] = other[:width].astype(BF16)
        go_ref[j] = sigmoid(other[width:])


def attend_kernel(
    sz, heads, steps, len_ref, q_ref, k_ref, v_ref, g_ref, first_ref, aout_ref, *refs
):
    bias_refs, (out_ref, rows_ref, biasT_ref) = refs[:-3], refs[-3:]
    n, w, ch = sz.crop, sz.whole, sz.channels
    length, me = len_ref[0], len_ref[2]
    width = q_ref.shape[2]
    hd = width // heads
    per = sz.rows * heads
    for ref, offsets in zip(bias_refs, steps):
        for place, offset in enumerate(offsets):
            at = pl.ds(pl.multiple_of((me ^ offset) * per, 8), per)
            part = ref[place].astype(F32) * LOG2E
            for m in range(w):
                rows_ref[m, at, :] = part[:, m * LANES : (m + 1) * LANES]
            if sz.rest:
                rows_ref[w, at, : sz.rest] = part[:, w * LANES :]
    key = lax.broadcasted_iota(jnp.int32, (n, LANES), 0)
    dead = jnp.where(key < length, 0.0, -1e9 * LOG2E).astype(F32)
    halves = []
    for head in range(heads):
        b = [
            jnp.transpose(rows_ref[m, pl.ds(head, n, stride=heads), :])
            for m in range(w + (sz.rest > 0))
        ]
        if sz.rest:
            b[w] = b[w][: sz.rest]
        b = jnp.concatenate(b, axis=0) if len(b) > 1 else b[0]
        for m in range(w):
            biasT_ref[:, (head * w + m) * LANES : (head * w + m + 1) * LANES] = (
                b[:, m * LANES : (m + 1) * LANES] + dead
            )
        if sz.rest:
            halves.append(b[:, w * LANES :])
    per_tile = LANES // sz.rest if sz.rest else 1
    base = heads * w
    if sz.rest:
        for t in range(heads // per_tile):
            biasT_ref[:, (base + t) * LANES : (base + t + 1) * LANES] = (
                jnp.concatenate(halves[t * per_tile : (t + 1) * per_tile], axis=1) + dead
            )
    lane = lax.broadcasted_iota(jnp.int32, (1, width), 1)
    head_masks = [((lane >= h * hd) & (lane < (h + 1) * hd)).astype(BF16) for h in range(heads)]
    scale = (hd ** (-0.5)) * LOG2E
    for j in range(sz.rows):
        q = q_ref[j]
        masked = [q * head_masks[h] for h in range(heads)]
        pieces = [masked[h][: w * LANES] for h in range(heads)]
        if sz.rest:
            pieces += [masked[h][w * LANES :] for h in range(heads)]
        stacked = jnp.concatenate(pieces, axis=0)
        scores = dot(k_ref[j], stacked, 1, 1) * scale + biasT_ref[...]
        top = jnp.max(scores, axis=0, keepdims=True)
        weights = jnp.exp2(scores - top)
        total = jnp.sum(weights, axis=0, keepdims=True)
        mixed = dot(v_ref[j], weights.astype(BF16), 1, 0)
        inverse = 1.0 / total
        mains, rests = [], []
        for h in range(heads):
            sl = slice(h * w * LANES, (h + 1) * w * LANES)
            mains.append(mixed[h * hd : (h + 1) * hd, sl] * inverse[:, sl])
            if sz.rest:
                t, part = divmod(h, per_tile)
                sl = slice((base + t) * LANES, (base + t + 1) * LANES)
                piece = mixed[h * hd : (h + 1) * hd, sl] * inverse[:, sl]
                rests.append(piece[:, part * sz.rest : (part + 1) * sz.rest])
        attended = jnp.concatenate(mains, axis=0)
        if sz.rest:
            attended = jnp.concatenate([attended, jnp.concatenate(rests, axis=0)], axis=1)
        gated = (attended * g_ref[j]).astype(BF16)
        total_out = first_ref[j].astype(F32) + dot(gated, aout_ref[...], 0, 0)
        out_ref[j] = total_out.astype(BF16)


def spread(block, devices):
    pieces, offsets = [block[None]], [[0]]
    bit = devices // 2
    while bit:
        held = jnp.concatenate(pieces, axis=0) if len(pieces) > 1 else pieces[0]
        got = lax.ppermute(held, AXES, [(d, d ^ bit) for d in range(devices)])
        known = [o for part in offsets for o in part]
        pieces.append(got)
        offsets.append([o ^ bit for o in known])
        bit //= 2
    return pieces, offsets


def shards(
    devices,
    pair_rep, length, ln_pair, tri_in, tri_gate, ln_hidden, tri_out, ln_att,
    att_q, att_k, att_v, att_bias, att_gate, att_out,
):
    rows, crop, ch = pair_rep.shape
    heads = att_bias.shape[1]
    sz = Sizes(rows, crop, devices, ch)
    n, cd = crop, sz.chans
    me = lax.axis_index(AXES).astype(jnp.int32)
    info = jnp.stack([length[0], me * rows, me])

    def bound(kernel, *extra):
        def run(*refs):
            return kernel(sz, *extra, *refs)

        return run

    shape = jax.ShapeDtypeStruct
    edges = call(
        bound(edges_kernel),
        shape((devices, 2 * cd, sz.tiles * LANES), BF16),
        (info, pair_rep, ln_pair[None], tri_in),
        scratch=[
            pltpu.VMEM((rows * crop, ch), BF16),
        ],
        smem=(0,),
        name="edges",
    )
    edges = lax.all_to_all(edges, AXES, split_axis=0, concat_axis=0, tiled=True)
    rest_rows = n if sz.rest else 8
    outer = call(
        bound(outer_kernel),
        shape((devices, sz.packed, (sz.fold_tiles + sz.block_tiles) * LANES), BF16),
        (edges, pair_rep),
        scratch=[
            pltpu.VMEM((sz.whole, n * 2 * cd, LANES), F32),
            pltpu.VMEM((rest_rows * 2 * cd, LANES), F32),
            pltpu.VMEM((sz.whole, n * cd, LANES), F32),
            pltpu.VMEM((rest_rows * cd, LANES), F32),
            pltpu.VMEM((devices, sz.block_tiles * sz.packed, ch), F32),
        ],
        name="outer",
    )
    outer = lax.all_to_all(outer, AXES, split_axis=0, concat_axis=0, tiled=True)
    first, col, bias = call(
        bound(update_kernel),
        [
            shape((rows, n, ch), BF16),
            shape((rows, n, ch), BF16),
            shape((rows * heads, n), BF16),
        ],
        (outer, ln_pair[None], tri_gate, ln_hidden[None], tri_out, ln_att[None], att_bias),
        scratch=[
            pltpu.VMEM((devices * sz.block + sz.packed, ch), F32),
            pltpu.VMEM((rows * heads, n), F32),
        ],
        name="update",
    )
    pieces, steps = spread(bias, devices)
    query, key, value, gate = call(
        bound(project_kernel),
        [
            shape((rows, n, att_q.shape[1]), BF16),
            shape((rows, n, att_q.shape[1]), BF16),
            shape((rows, att_q.shape[1], n), BF16),
            shape((rows, att_q.shape[1], n), F32),
        ],
        (col, att_q, att_k, att_v, att_gate),
        name="project",
    )
    out = call(
        bound(attend_kernel, heads, steps),
        shape((rows, n, ch), BF16),
        (info, query, key, value, gate, first, att_out, *pieces),
        scratch=[
            pltpu.VMEM((-(-n // LANES), n * heads, LANES), F32),
            pltpu.VMEM((n, heads * n), F32),
        ],
        smem=(0,),
        name="attend",
    )
    return jnp.swapaxes(out, 0, 1)


def solution(mesh):
    devices = mesh.shape["row"] * mesh.shape["node"]

    def body(*args):
        return shards(devices, *args)

    return jax.shard_map(
        body,
        mesh=mesh,
        in_specs=(P(("grp", "row", "node"), None, None), P("grp")) + (P(),) * 12,
        out_specs=P("grp", AXES, None),
        check_vma=False,
    )
```

```python
import jax
import jax.numpy as jnp
from jax import lax
from jax.experimental import pallas as pl
from jax.experimental.pallas import tpu as pltpu
from jax.sharding import PartitionSpec as P

EPS = 1e-05
LANES = 128
LOG2E = 1.4426950408889634
F32 = jnp.float32
BF16 = jnp.bfloat16
AXES = ("row", "node")
VMEM_BYTES = 48 * 1024 * 1024
VMEM_MOST = 60 * 1024 * 1024


def norm_last(values, gain):
    average = jnp.mean(values, axis=-1, keepdims=True)
    centred = values - average
    variance = jnp.mean(centred * centred, axis=-1, keepdims=True)
    return centred * lax.rsqrt(variance + EPS) * gain


def sigmoid(values):
    return 0.5 * jnp.tanh(0.5 * values) + 0.5


def dot(a, b, a_dim, b_dim):
    return lax.dot_general(a, b, (((a_dim,), (b_dim,)), ((), ())), preferred_element_type=F32)


def call(kernel, out_shape, args, scratch=(), smem=(), name=None, vmem=VMEM_BYTES):
    specs = [
        pl.BlockSpec(memory_space=pltpu.SMEM if n in smem else pltpu.VMEM) for n in range(len(args))
    ]
    single = not isinstance(out_shape, (list, tuple))
    inside = pl.BlockSpec(memory_space=pltpu.VMEM)
    return pl.pallas_call(
        kernel,
        out_shape=out_shape,
        in_specs=specs,
        out_specs=inside if single else [inside] * len(out_shape),
        scratch_shapes=list(scratch),
        compiler_params=pltpu.CompilerParams(vmem_limit_bytes=vmem),
        name=name,
    )(*args)


class Sizes:
    def __init__(self, rows, crop, devices, channels):
        self.rows, self.crop, self.devices = rows, crop, devices
        self.half = rows // 2
        self.whole = crop // LANES
        self.rest = crop % LANES
        self.tiles = rows * crop // LANES
        self.chans = channels // devices
        self.fold = max(1, 16 // self.chans)
        while self.tiles % self.fold:
            self.fold //= 2
        self.fold_tiles = self.tiles // self.fold
        self.channels = channels

        self.block = rows * rows
        self.packed = self.fold * self.chans
        self.block_tiles = -(-self.block // self.packed)


def edges_kernel(sz, len_ref, x_ref, ln_ref, w_ref, out_ref, norm_ref):
    length, first = len_ref[0], len_ref[1]
    cd, two = sz.chans, 2 * sz.chans
    ch = sz.channels
    r = lax.broadcasted_iota(jnp.int32, (2 * ch, 2 * ch), 0)
    e = lax.broadcasted_iota(jnp.int32, (2 * ch, 2 * ch), 1)
    target = ((r // cd) % 2) * ch + (r // two) * cd + r % cd
    pick = (target == e).astype(BF16)
    gate_w = dot(pick, jnp.concatenate([w_ref[0], w_ref[2]], axis=1), 1, 1).astype(BF16)
    value_w = dot(pick, jnp.concatenate([w_ref[1], w_ref[3]], axis=1), 1, 1).astype(BF16)
    gain = ln_ref[...]
    main = sz.whole * LANES
    for row in range(sz.rows):
        x = x_ref[row].astype(F32)
        normed = norm_last(x, gain).astype(BF16)
        norm_ref[pl.ds(row * main, main), :] = normed[:main]
        if sz.rest:
            h, q = divmod(row, sz.half)
            norm_ref[pl.ds(sz.rows * main + q * LANES + h * sz.rest, sz.rest), :] = normed[main:]
    lane = lax.broadcasted_iota(jnp.int32, (1, LANES), 1)

    def live(tile):
        if tile < sz.rows * sz.whole:
            row, m = divmod(tile, sz.whole)
            return ((first + row < length) & (m * LANES + lane < length)).astype(F32)
        q = tile - sz.rows * sz.whole
        second = lane >= sz.rest
        row = first + q + jnp.where(second, sz.half, 0)
        k = main + lane - jnp.where(second, sz.rest, 0)
        return ((row < length) & (k < length)).astype(F32)

    step = 2 if sz.tiles % 2 == 0 else 1
    for tile in range(0, sz.tiles, step):
        n = norm_ref[pl.ds(tile * LANES, step * LANES), :]
        mask = jnp.concatenate([live(tile + s) for s in range(step)], axis=1)
        edge = sigmoid(dot(gate_w, n, 1, 1)) * dot(value_w, n, 1, 1) * mask
        out_ref[:, :, tile * LANES : (tile + step) * LANES] = edge.reshape(
            sz.devices, two, step * LANES
        ).astype(BF16)


def pack_kernel(sz, x_ref, out_ref, pair_ref):
    for row in range(sz.rows):
        x = x_ref[row].astype(F32)
        for d in range(sz.devices):
            pair_ref[d, row * sz.rows : (row + 1) * sz.rows, :] = x[d * sz.rows : (d + 1) * sz.rows]
    high = sz.packed
    for d in range(sz.devices):
        for t in range(sz.block_tiles):
            at = t * LANES
            out_ref[d, :, at : at + LANES] = pair_ref[d, t * high : (t + 1) * high, :].astype(BF16)


def outer_kernel(sz, e_ref, pair_ref, out_ref, main_ref, rest_ref, omain_ref, orest_ref):
    cd, two = sz.chans, 2 * sz.chans
    n, w, half = sz.crop, sz.whole, sz.half
    for s in range(sz.devices):
        for tile in range(sz.tiles):
            block = e_ref[s, :, tile * LANES : (tile + 1) * LANES].astype(F32)
            if tile < sz.rows * w:
                row, m = divmod(tile, w)
                main_ref[m, pl.ds((s * sz.rows + row) * two, two), :] = block
            else:
                at = s * sz.rows + tile - sz.rows * w
                rest_ref[pl.ds(at * two, two), :] = block
                rest_ref[pl.ds((at + half) * two, two), :] = pltpu.roll(block, sz.rest, 1)

    def matrix(index):
        parts = [main_ref[m, pl.ds(index, n, stride=two), :].astype(BF16) for m in range(w)]
        if sz.rest:
            parts.append(rest_ref[pl.ds(index, n, stride=two), :].astype(BF16)[:, : sz.rest])
        return jnp.concatenate(parts, axis=1) if len(parts) > 1 else parts[0]

    for c in range(cd):
        outer = dot(matrix(cd + c), matrix(c), 1, 1)
        for m in range(w):
            omain_ref[m, pl.ds(c, n, stride=cd), :] = outer[:, m * LANES : (m + 1) * LANES]
        if sz.rest:
            part = outer[:, w * LANES :]
            orest_ref[pl.ds(c, n, stride=cd), :] = jnp.concatenate([part, part], axis=1)
    low = lax.broadcasted_iota(jnp.int32, (cd, LANES), 1) < sz.rest
    for s in range(sz.devices):
        for t in range(sz.fold_tiles):
            blocks = []
            for f in range(sz.fold):
                tile = f * sz.fold_tiles + t
                if tile < sz.rows * w:
                    row, m = divmod(tile, w)
                    blocks.append(omain_ref[m, pl.ds((s * sz.rows + row) * cd, cd), :])
                else:
                    at = s * sz.rows + tile - sz.rows * w
                    one = orest_ref[pl.ds(at * cd, cd), :]
                    blocks.append(jnp.where(low, one, orest_ref[pl.ds((at + half) * cd, cd), :]))
            block = jnp.concatenate(blocks, axis=0) if len(blocks) > 1 else blocks[0]
            out_ref[s, :, t * LANES : (t + 1) * LANES] = block.astype(BF16)
        out_ref[s, :, sz.fold_tiles * LANES :] = pair_ref[s]


def update_kernel(
    sz, o_ref, lnp_ref, gate_ref, lnh_ref, tri_ref, lna_ref, biasw_ref,
    first_ref, col_ref, bias_ref, cols_ref, brow_ref,
):
    n, w, half, ch = sz.crop, sz.whole, sz.half, sz.channels
    high = sz.packed
    for s in range(sz.devices):
        for t in range(sz.block_tiles):
            at = (sz.fold_tiles + t) * LANES
            rows = pl.ds(s * sz.block + t * high, high)
            cols_ref[rows, :] = o_ref[s, :, at : at + LANES].astype(F32)
    gain_h = jnp.transpose(jnp.broadcast_to(lnh_ref[...], (ch, ch)))
    tri = tri_ref[...]

    def update(tile):
        f, t = divmod(tile, sz.fold_tiles)
        block = o_ref[:, :, t * LANES : (t + 1) * LANES].astype(F32)
        block = block[:, f * sz.chans : (f + 1) * sz.chans, :].reshape(ch, LANES)
        average = jnp.mean(block, axis=0, keepdims=True)
        centred = block - average
        variance = jnp.mean(centred * centred, axis=0, keepdims=True)
        hidden = (centred * lax.rsqrt(variance + EPS) * gain_h).astype(BF16)
        return dot(hidden, tri, 0, 0)

    rest = [update(sz.rows * w + q) for q in range(half)] if sz.rest else None
    for j in range(sz.rows):
        parts = [update(j * w + m) for m in range(w)]
        if sz.rest:
            h, q = divmod(j, half)
            parts.append(rest[q][h * sz.rest : (h + 1) * sz.rest])
        change = jnp.concatenate(parts, axis=0) if len(parts) > 1 else parts[0]
        x = cols_ref[pl.ds(j, n, stride=sz.rows), :]
        normed = norm_last(x, lnp_ref[...]).astype(BF16)
        gating = sigmoid(dot(normed, gate_ref[...], 1, 0))
        first = (x + gating * change).astype(BF16)
        first_ref[j] = first
        col = norm_last(first.astype(F32), lna_ref[...]).astype(BF16)
        col_ref[j] = col
        heads = biasw_ref.shape[1]
        brow_ref[pl.ds(j * heads, heads), :] = dot(biasw_ref[...], col, 0, 1)
    rows = brow_ref[...]
    part = rows.shape[0] // 2
    one, two = rows[:part], rows[part:]
    message = [one[:, : w * LANES], two[:, : w * LANES]]
    if sz.rest:
        message += [one[:, w * LANES :], two[:, w * LANES :]]
    message = jnp.concatenate(message, axis=1).astype(BF16)
    for d in range(sz.devices):
        bias_ref[d] = message


def project_kernel(sz, col_ref, q_ref, k_ref, v_ref, g_ref, qo_ref, ko_ref, vo_ref, go_ref):
    n, ch = sz.crop, sz.channels
    qk = jnp.concatenate([q_ref[...], k_ref[...]], axis=1)
    vg = jnp.transpose(jnp.concatenate([v_ref[...], g_ref[...]], axis=1).astype(F32)).astype(BF16)
    width = q_ref.shape[1]
    for j in range(sz.rows):
        col = col_ref[j]
        both = dot(col, qk, 1, 0)
        qo_ref[j] = both[:, :width].astype(BF16)
        ko_ref[j] = both[:, width:].astype(BF16)
        other = dot(vg, col, 1, 1)
        vo_ref[j] = other[:width].astype(BF16)
        go_ref[j] = sigmoid(other[width:])


def attend_kernel(
    sz, heads, len_ref, q_ref, k_ref, v_ref, g_ref, first_ref, aout_ref, bias_ref,
    out_ref, rows_ref, biasT_ref,
):
    n, w, ch = sz.crop, sz.whole, sz.channels
    length = len_ref[0]
    width = q_ref.shape[2]
    hd = width // heads
    per = sz.rows * heads // 2
    for s in range(sz.devices):
        block = bias_ref[s].astype(F32) * LOG2E
        for p in range(2):
            at = pl.ds((2 * s + p) * per, per)
            for m in range(w):
                rows_ref[m, at, :] = block[:, (p * w + m) * LANES : (p * w + m + 1) * LANES]
            if sz.rest:
                tail = block[:, 2 * w * LANES :]
                rows_ref[w, at, :] = pltpu.roll(tail, sz.rest, 1) if p else tail
    key = lax.broadcasted_iota(jnp.int32, (n, LANES), 0)
    dead = jnp.where(key < length, 0.0, -1e9 * LOG2E).astype(F32)
    halves = []
    for head in range(heads):
        b = [
            jnp.transpose(rows_ref[m, pl.ds(head, n, stride=heads), :])
            for m in range(w + (sz.rest > 0))
        ]
        if sz.rest:
            b[w] = b[w][: sz.rest]
        b = jnp.concatenate(b, axis=0) if len(b) > 1 else b[0]
        for m in range(w):
            biasT_ref[:, (head * w + m) * LANES : (head * w + m + 1) * LANES] = (
                b[:, m * LANES : (m + 1) * LANES] + dead
            )
        if sz.rest:
            halves.append(b[:, w * LANES :])
    per_tile = LANES // sz.rest if sz.rest else 1
    base = heads * w
    if sz.rest:
        for t in range(heads // per_tile):
            biasT_ref[:, (base + t) * LANES : (base + t + 1) * LANES] = (
                jnp.concatenate(halves[t * per_tile : (t + 1) * per_tile], axis=1) + dead
            )
    lane = lax.broadcasted_iota(jnp.int32, (1, width), 1)
    head_masks = [((lane >= h * hd) & (lane < (h + 1) * hd)).astype(BF16) for h in range(heads)]
    scale = (hd ** (-0.5)) * LOG2E
    for j in range(sz.rows):
        q = q_ref[j]
        masked = [q * head_masks[h] for h in range(heads)]
        pieces = [masked[h][: w * LANES] for h in range(heads)]
        if sz.rest:
            pieces += [masked[h][w * LANES :] for h in range(heads)]
        stacked = jnp.concatenate(pieces, axis=0)
        scores = dot(k_ref[j], stacked, 1, 1) * scale + biasT_ref[...]
        top = jnp.max(scores, axis=0, keepdims=True)
        weights = jnp.exp2(scores - top)
        total = jnp.sum(weights, axis=0, keepdims=True)
        mixed = dot(v_ref[j], weights.astype(BF16), 1, 0)
        inverse = 1.0 / total
        mains, rests = [], []
        for h in range(heads):
            sl = slice(h * w * LANES, (h + 1) * w * LANES)
            mains.append(mixed[h * hd : (h + 1) * hd, sl] * inverse[:, sl])
            if sz.rest:
                t, part = divmod(h, per_tile)
                sl = slice((base + t) * LANES, (base + t + 1) * LANES)
                piece = mixed[h * hd : (h + 1) * hd, sl] * inverse[:, sl]
                rests.append(piece[:, part * sz.rest : (part + 1) * sz.rest])
        attended = jnp.concatenate(mains, axis=0)
        if sz.rest:
            attended = jnp.concatenate([attended, jnp.concatenate(rests, axis=0)], axis=1)
        gated = (attended * g_ref[j]).astype(BF16)
        total_out = first_ref[j].astype(F32) + dot(gated, aout_ref[...], 0, 0)
        out_ref[j] = total_out.astype(BF16)


def shards(
    devices,
    pair_rep, length, ln_pair, tri_in, tri_gate, ln_hidden, tri_out, ln_att,
    att_q, att_k, att_v, att_bias, att_gate, att_out,
):
    rows, crop, ch = pair_rep.shape
    heads = att_bias.shape[1]
    sz = Sizes(rows, crop, devices, ch)
    n, cd = crop, sz.chans
    me = lax.axis_index(AXES).astype(jnp.int32)
    info = jnp.stack([length[0], me * rows])

    def bound(kernel, *extra):
        def run(*refs):
            return kernel(sz, *extra, *refs)

        return run

    shape = jax.ShapeDtypeStruct
    edges = call(
        bound(edges_kernel),
        shape((devices, 2 * cd, sz.tiles * LANES), BF16),
        (info, pair_rep, ln_pair[None], tri_in),
        scratch=[
            pltpu.VMEM((rows * crop, ch), BF16),
        ],
        smem=(0,),
        name="edges",
        vmem=VMEM_MOST,
    )
    packed = call(
        bound(pack_kernel),
        shape((devices, sz.packed, sz.block_tiles * LANES), BF16),
        (pair_rep,),
        scratch=[pltpu.VMEM((devices, sz.block_tiles * sz.packed, ch), F32)],
        name="pack",
    )
    edges = lax.all_to_all(edges, AXES, split_axis=0, concat_axis=0, tiled=True)
    rest_rows = n if sz.rest else 8
    outer = call(
        bound(outer_kernel),
        shape((devices, sz.packed, (sz.fold_tiles + sz.block_tiles) * LANES), BF16),
        (edges, packed),
        scratch=[
            pltpu.VMEM((sz.whole, n * 2 * cd, LANES), F32),
            pltpu.VMEM((rest_rows * 2 * cd, LANES), F32),
            pltpu.VMEM((sz.whole, n * cd, LANES), F32),
            pltpu.VMEM((rest_rows * cd, LANES), F32),
        ],
        name="outer",
    )
    outer = lax.all_to_all(outer, AXES, split_axis=0, concat_axis=0, tiled=True)
    first, col, bias = call(
        bound(update_kernel),
        [
            shape((rows, n, ch), BF16),
            shape((rows, n, ch), BF16),
            shape((devices, rows * heads // 2, 2 * n), BF16),
        ],
        (outer, ln_pair[None], tri_gate, ln_hidden[None], tri_out, ln_att[None], att_bias),
        scratch=[
            pltpu.VMEM((devices * sz.block + sz.packed, ch), F32),
            pltpu.VMEM((rows * heads, n), F32),
        ],
        name="update",
    )
    bias = lax.all_to_all(bias, AXES, split_axis=0, concat_axis=0, tiled=True)
    query, key, value, gate = call(
        bound(project_kernel),
        [
            shape((rows, n, att_q.shape[1]), BF16),
            shape((rows, n, att_q.shape[1]), BF16),
            shape((rows, att_q.shape[1], n), BF16),
            shape((rows, att_q.shape[1], n), F32),
        ],
        (col, att_q, att_k, att_v, att_gate),
        name="project",
    )
    out = call(
        bound(attend_kernel, heads),
        shape((rows, n, ch), BF16),
        (info, query, key, value, gate, first, att_out, bias),
        scratch=[
            pltpu.VMEM((-(-n // LANES), n * heads, LANES), F32),
            pltpu.VMEM((n, heads * n), F32),
        ],
        smem=(0,),
        name="attend",
    )
    return jnp.swapaxes(out, 0, 1)


def solution(mesh):
    devices = mesh.shape["row"] * mesh.shape["node"]

    def body(*args):
        return shards(devices, *args)

    return jax.shard_map(
        body,
        mesh=mesh,
        in_specs=(P(("grp", "row", "node"), None, None), P("grp")) + (P(),) * 12,
        out_specs=P("grp", AXES, None),
        check_vma=False,
    )
```

```python
import jax
import jax.numpy as jnp
from jax import lax
from jax.experimental import pallas as pl
from jax.experimental.pallas import tpu as pltpu
from jax.sharding import PartitionSpec as P

EPS = 1e-05
LANES = 128
LOG2E = 1.4426950408889634
F32 = jnp.float32
BF16 = jnp.bfloat16
AXES = ("row", "node")
VMEM_BYTES = 48 * 1024 * 1024
VMEM_MOST = 60 * 1024 * 1024


def norm_last(values, gain):
    average = jnp.mean(values, axis=-1, keepdims=True)
    centred = values - average
    variance = jnp.mean(centred * centred, axis=-1, keepdims=True)
    return centred * lax.rsqrt(variance + EPS) * gain


def sigmoid(values):
    return 0.5 * jnp.tanh(0.5 * values) + 0.5


def dot(a, b, a_dim, b_dim):
    return lax.dot_general(a, b, (((a_dim,), (b_dim,)), ((), ())), preferred_element_type=F32)


def call(kernel, out_shape, args, scratch=(), smem=(), name=None, vmem=VMEM_BYTES):
    specs = [
        pl.BlockSpec(memory_space=pltpu.SMEM if n in smem else pltpu.VMEM) for n in range(len(args))
    ]
    single = not isinstance(out_shape, (list, tuple))
    inside = pl.BlockSpec(memory_space=pltpu.VMEM)
    return pl.pallas_call(
        kernel,
        out_shape=out_shape,
        in_specs=specs,
        out_specs=inside if single else [inside] * len(out_shape),
        scratch_shapes=list(scratch),
        compiler_params=pltpu.CompilerParams(vmem_limit_bytes=vmem),
        name=name,
    )(*args)


class Sizes:
    def __init__(self, rows, crop, devices, channels):
        self.rows, self.crop, self.devices, self.channels = rows, crop, devices, channels
        self.half = rows // 2
        self.group = devices // 2
        self.columns = rows * self.group
        self.whole = crop // LANES
        self.rest = crop % LANES
        self.tiles = rows * crop // LANES
        self.chans = channels // self.group
        self.block = rows * rows
        self.block_tiles = -(-self.block // self.chans)


def edges_kernel(sz, len_ref, x_ref, ln_ref, w_ref, out_ref, *refs):
    near = refs[: sz.group]
    norm_ref, pair_ref = refs[sz.group :]
    length, first, me = len_ref[0], len_ref[1], len_ref[2]
    cd, ch = sz.chans, sz.channels
    mine = me & (sz.group - 1)
    r = lax.broadcasted_iota(jnp.int32, (ch, ch), 0)
    e = lax.broadcasted_iota(jnp.int32, (ch, ch), 1)
    plain = (r == e).astype(BF16)
    slots = (((r // cd) ^ mine) * cd + r % cd == e).astype(BF16)
    picks = (plain, plain, slots, slots)
    weights = [dot(pick, w_ref[p], 1, 1).astype(BF16) for p, pick in enumerate(picks)]
    gate_w = jnp.concatenate([weights[0], weights[2]], axis=0)
    value_w = jnp.concatenate([weights[1], weights[3]], axis=0)
    gain = ln_ref[...]
    main = sz.whole * LANES
    for row in range(sz.rows):
        x = x_ref[row].astype(F32)
        for d in range(sz.devices):
            pair_ref[d, row * sz.rows : (row + 1) * sz.rows, :] = x[d * sz.rows : (d + 1) * sz.rows]
        normed = norm_last(x, gain).astype(BF16)
        norm_ref[pl.ds(row * main, main), :] = normed[:main]
        if sz.rest:
            h, q = divmod(row, sz.half)
            norm_ref[pl.ds(sz.rows * main + q * LANES + h * sz.rest, sz.rest), :] = normed[main:]
    for d in range(sz.devices):
        for t in range(sz.block_tiles):
            at = (sz.tiles + t) * LANES
            out_ref[d, :, at : at + LANES] = pair_ref[d, t * cd : (t + 1) * cd, :].astype(BF16)
    lane = lax.broadcasted_iota(jnp.int32, (1, LANES), 1)

    def live(tile):
        if tile < sz.rows * sz.whole:
            row, m = divmod(tile, sz.whole)
            return ((first + row < length) & (m * LANES + lane < length)).astype(F32)
        q = tile - sz.rows * sz.whole
        second = lane >= sz.rest
        row = first + q + jnp.where(second, sz.half, 0)
        k = main + lane - jnp.where(second, sz.rest, 0)
        return ((row < length) & (k < length)).astype(F32)

    step = 2 if sz.tiles % 2 == 0 else 1
    for tile in range(0, sz.tiles, step):
        n = norm_ref[pl.ds(tile * LANES, step * LANES), :]
        mask = jnp.concatenate([live(tile + s) for s in range(step)], axis=1)
        edge = sigmoid(dot(gate_w, n, 1, 1)) * dot(value_w, n, 1, 1) * mask
        edge = edge.astype(BF16)
        to = slice(tile * LANES, (tile + step) * LANES)
        for g in range(sz.group):
            left = edge[g * cd : (g + 1) * cd]
            out_ref[g, :, to] = left
            out_ref[sz.group + g, :, to] = left
            near[g][:, to] = edge[ch + g * cd : ch + (g + 1) * cd]


def outer_kernel(sz, len_ref, left_ref, *refs):
    near, out_ref = refs[: sz.group], refs[sz.group]
    lmain_ref, lrest_ref, rmain_ref, rrest_ref, omain_ref, orest_ref = refs[sz.group + 1 :]
    mine = len_ref[2] & (sz.group - 1)
    cd, n, w, half = sz.chans, sz.crop, sz.whole, sz.half

    def unpack(ref, owner, main_ref, rest_ref):
        for tile in range(sz.tiles):
            block = ref[:, tile * LANES : (tile + 1) * LANES].astype(F32)
            if tile < sz.rows * w:
                row, m = divmod(tile, w)
                main_ref[m, pl.ds(pl.multiple_of((owner * sz.rows + row) * cd, 8), cd), :] = block
            else:
                row = owner * sz.rows + tile - sz.rows * w
                rest_ref[pl.ds(pl.multiple_of(row * cd, 8), cd), :] = block
                rest_ref[pl.ds(pl.multiple_of((row + half) * cd, 8), cd), :] = pltpu.roll(
                    block, sz.rest, 1
                )

    for d in range(sz.devices):
        unpack(left_ref.at[d], jnp.int32(d), lmain_ref, lrest_ref)
    for r in range(sz.group):
        unpack(near[r], mine ^ r, rmain_ref, rrest_ref)

    def matrix(c, size, main_ref, rest_ref):
        parts = [main_ref[m, pl.ds(c, size, stride=cd), :].astype(BF16) for m in range(w)]
        if sz.rest:
            parts.append(rest_ref[pl.ds(c, size, stride=cd), :].astype(BF16)[:, : sz.rest])
        return jnp.concatenate(parts, axis=1) if len(parts) > 1 else parts[0]

    for c in range(cd):
        outer = dot(
            matrix(c, sz.columns, rmain_ref, rrest_ref), matrix(c, n, lmain_ref, lrest_ref), 1, 1
        )
        for m in range(w):
            omain_ref[m, pl.ds(c, sz.columns, stride=cd), :] = outer[:, m * LANES : (m + 1) * LANES]
        if sz.rest:
            part = outer[:, w * LANES :]
            orest_ref[pl.ds(c, sz.columns, stride=cd), :] = jnp.concatenate([part, part], axis=1)
    low = lax.broadcasted_iota(jnp.int32, (cd, LANES), 1) < sz.rest
    for g in range(sz.group):
        start = g * sz.rows
        for tile in range(sz.tiles):
            if tile < sz.rows * w:
                row, m = divmod(tile, w)
                block = omain_ref[m, pl.ds((start + row) * cd, cd), :]
            else:
                at = start + tile - sz.rows * w
                block = jnp.where(
                    low,
                    orest_ref[pl.ds(at * cd, cd), :],
                    orest_ref[pl.ds((at + half) * cd, cd), :],
                )
            out_ref[g, :, tile * LANES : (tile + 1) * LANES] = block.astype(BF16)


def update_kernel(
    sz, lnp_ref, gate_ref, lnh_ref, tri_ref, lna_ref, biasw_ref, sums_ref, pair_ref,
    first_ref, col_ref, bias_ref, cols_ref, brow_ref,
):
    n, w, half, ch, cd = sz.crop, sz.whole, sz.half, sz.channels, sz.chans
    for s in range(sz.devices):
        for t in range(sz.block_tiles):
            at = (sz.tiles + t) * LANES
            rows = pl.ds(s * sz.block + t * cd, cd)
            cols_ref[rows, :] = pair_ref[s, :, at : at + LANES].astype(F32)
    gain_h = jnp.transpose(jnp.broadcast_to(lnh_ref[...], (ch, ch)))
    tri = tri_ref[...]

    def update(tile):
        block = sums_ref[:, :, tile * LANES : (tile + 1) * LANES].astype(F32).reshape(ch, LANES)
        average = jnp.mean(block, axis=0, keepdims=True)
        centred = block - average
        variance = jnp.mean(centred * centred, axis=0, keepdims=True)
        hidden = (centred * lax.rsqrt(variance + EPS) * gain_h).astype(BF16)
        return dot(hidden, tri, 0, 0)

    rest = [update(sz.rows * w + q) for q in range(half)] if sz.rest else None
    for j in range(sz.rows):
        parts = [update(j * w + m) for m in range(w)]
        if sz.rest:
            h, q = divmod(j, half)
            parts.append(rest[q][h * sz.rest : (h + 1) * sz.rest])
        change = jnp.concatenate(parts, axis=0) if len(parts) > 1 else parts[0]
        x = cols_ref[pl.ds(j, n, stride=sz.rows), :]
        normed = norm_last(x, lnp_ref[...]).astype(BF16)
        gating = sigmoid(dot(normed, gate_ref[...], 1, 0))
        first = (x + gating * change).astype(BF16)
        first_ref[j] = first
        col = norm_last(first.astype(F32), lna_ref[...]).astype(BF16)
        col_ref[j] = col
        heads = biasw_ref.shape[1]
        brow_ref[pl.ds(j * heads, heads), :] = dot(biasw_ref[...], col, 0, 1)
    bias_ref[...] = brow_ref[...].astype(BF16)


def project_kernel(sz, col_ref, q_ref, k_ref, v_ref, g_ref, qo_ref, ko_ref, vo_ref, go_ref):
    n, ch = sz.crop, sz.channels
    qk = jnp.concatenate([q_ref[...], k_ref[...]], axis=1)
    vg = jnp.transpose(jnp.concatenate([v_ref[...], g_ref[...]], axis=1).astype(F32)).astype(BF16)
    width = q_ref.shape[1]
    for j in range(sz.rows):
        col = col_ref[j]
        both = dot(col, qk, 1, 0)
        qo_ref[j] = both[:, :width].astype(BF16)
        ko_ref[j] = both[:, width:].astype(BF16)
        other = dot(vg, col, 1, 1)
        vo_ref[j] = other[:width].astype(BF16)
        go_ref[j] = sigmoid(other[width:])


def attend_kernel(
    sz, heads, steps, len_ref, q_ref, k_ref, v_ref, g_ref, first_ref, aout_ref, *refs
):
    bias_refs, (out_ref, rows_ref, biasT_ref) = refs[:-3], refs[-3:]
    n, w, ch = sz.crop, sz.whole, sz.channels
    length, me = len_ref[0], len_ref[2]
    width = q_ref.shape[2]
    hd = width // heads
    per = sz.rows * heads
    for ref, offsets in zip(bias_refs, steps):
        for place, offset in enumerate(offsets):
            at = pl.ds(pl.multiple_of((me ^ offset) * per, 8), per)
            part = ref[place].astype(F32) * LOG2E
            for m in range(w):
                rows_ref[m, at, :] = part[:, m * LANES : (m + 1) * LANES]
            if sz.rest:
                rows_ref[w, at, : sz.rest] = part[:, w * LANES :]
    key = lax.broadcasted_iota(jnp.int32, (n, LANES), 0)
    dead = jnp.where(key < length, 0.0, -1e9 * LOG2E).astype(F32)
    halves = []
    for head in range(heads):
        b = [
            jnp.transpose(rows_ref[m, pl.ds(head, n, stride=heads), :])
            for m in range(w + (sz.rest > 0))
        ]
        if sz.rest:
            b[w] = b[w][: sz.rest]
        b = jnp.concatenate(b, axis=0) if len(b) > 1 else b[0]
        for m in range(w):
            biasT_ref[:, (head * w + m) * LANES : (head * w + m + 1) * LANES] = (
                b[:, m * LANES : (m + 1) * LANES] + dead
            )
        if sz.rest:
            halves.append(b[:, w * LANES :])
    per_tile = LANES // sz.rest if sz.rest else 1
    base = heads * w
    if sz.rest:
        for t in range(heads // per_tile):
            biasT_ref[:, (base + t) * LANES : (base + t + 1) * LANES] = (
                jnp.concatenate(halves[t * per_tile : (t + 1) * per_tile], axis=1) + dead
            )
    lane = lax.broadcasted_iota(jnp.int32, (1, width), 1)
    head_masks = [((lane >= h * hd) & (lane < (h + 1) * hd)).astype(BF16) for h in range(heads)]
    scale = (hd ** (-0.5)) * LOG2E
    for j in range(sz.rows):
        q = q_ref[j]
        masked = [q * head_masks[h] for h in range(heads)]
        pieces = [masked[h][: w * LANES] for h in range(heads)]
        if sz.rest:
            pieces += [masked[h][w * LANES :] for h in range(heads)]
        stacked = jnp.concatenate(pieces, axis=0)
        scores = dot(k_ref[j], stacked, 1, 1) * scale + biasT_ref[...]
        top = jnp.max(scores, axis=0, keepdims=True)
        weights = jnp.exp2(scores - top)
        total = jnp.sum(weights, axis=0, keepdims=True)
        mixed = dot(v_ref[j], weights.astype(BF16), 1, 0)
        inverse = 1.0 / total
        mains, rests = [], []
        for h in range(heads):
            sl = slice(h * w * LANES, (h + 1) * w * LANES)
            mains.append(mixed[h * hd : (h + 1) * hd, sl] * inverse[:, sl])
            if sz.rest:
                t, part = divmod(h, per_tile)
                sl = slice((base + t) * LANES, (base + t + 1) * LANES)
                piece = mixed[h * hd : (h + 1) * hd, sl] * inverse[:, sl]
                rests.append(piece[:, part * sz.rest : (part + 1) * sz.rest])
        attended = jnp.concatenate(mains, axis=0)
        if sz.rest:
            attended = jnp.concatenate([attended, jnp.concatenate(rests, axis=0)], axis=1)
        gated = (attended * g_ref[j]).astype(BF16)
        total_out = first_ref[j].astype(F32) + dot(gated, aout_ref[...], 0, 0)
        out_ref[j] = total_out.astype(BF16)


def spread(block, devices):
    pieces, offsets = [block[None]], [[0]]
    bit = devices // 2
    while bit:
        held = jnp.concatenate(pieces, axis=0) if len(pieces) > 1 else pieces[0]
        got = lax.ppermute(held, AXES, [(d, d ^ bit) for d in range(devices)])
        known = [o for part in offsets for o in part]
        pieces.append(got)
        offsets.append([o ^ bit for o in known])
        bit //= 2
    return pieces, offsets


def shards(
    devices,
    pair_rep, length, ln_pair, tri_in, tri_gate, ln_hidden, tri_out, ln_att,
    att_q, att_k, att_v, att_bias, att_gate, att_out,
):
    rows, crop, ch = pair_rep.shape
    heads = att_bias.shape[1]
    sz = Sizes(rows, crop, devices, ch)
    n, cd = crop, sz.chans
    me = lax.axis_index(AXES).astype(jnp.int32)
    info = jnp.stack([length[0], me * rows, me])
    def bound(kernel, *extra):
        def run(*refs):
            return kernel(sz, *extra, *refs)

        return run

    shape = jax.ShapeDtypeStruct
    g, t, bt = sz.group, sz.tiles, sz.block_tiles

    def slab(tiles, *lead):
        return shape((*lead, cd, tiles * LANES), BF16)

    def send(blocks, offset):
        return [
            block
            if not (offset ^ r)
            else lax.ppermute(block, AXES, [(d, d ^ offset ^ r) for d in range(devices)])
            for r, block in enumerate(blocks)
        ]

    left, *others = call(
        bound(edges_kernel),
        [slab(t + bt, devices)] + [slab(t)] * g,
        (info, pair_rep, ln_pair[None], tri_in),
        scratch=[
            pltpu.VMEM((rows * crop, ch), BF16),
            pltpu.VMEM((devices, bt * cd, ch), F32),
        ],
        smem=(0,),
        name="edges",
        vmem=VMEM_MOST,
    )
    left = lax.all_to_all(left, AXES, split_axis=0, concat_axis=0, tiled=True)
    near = send(others, 0)
    rest = sz.rest > 0
    outer = call(
        bound(outer_kernel),
        slab(t, g),
        (info, left, *near),
        scratch=[
            pltpu.VMEM((sz.whole, n * cd, LANES), F32),
            pltpu.VMEM((n * cd if rest else 8, LANES), F32),
            pltpu.VMEM((sz.whole, sz.columns * cd, LANES), F32),
            pltpu.VMEM((sz.columns * cd if rest else 8, LANES), F32),
            pltpu.VMEM((sz.whole, sz.columns * cd, LANES), F32),
            pltpu.VMEM((sz.columns * cd if rest else 8, LANES), F32),
        ],
        smem=(0,),
        name="outer",
    )
    sums = lax.all_to_all(
        outer, AXES, split_axis=0, concat_axis=0, tiled=True,
        axis_index_groups=[list(range(g)), list(range(g, devices))],
    )
    first, col, bias = call(
        bound(update_kernel),
        [
            shape((rows, n, ch), BF16),
            shape((rows, n, ch), BF16),
            shape((rows * heads, n), BF16),
        ],
        (
            ln_pair[None], tri_gate, ln_hidden[None], tri_out, ln_att[None], att_bias,
            sums, left,
        ),
        scratch=[
            pltpu.VMEM((devices * sz.block + cd, ch), F32),
            pltpu.VMEM((rows * heads, n), F32),
        ],
        name="update",
    )
    pieces, steps = spread(bias, devices)
    query, key, value, gate = call(
        bound(project_kernel),
        [
            shape((rows, n, att_q.shape[1]), BF16),
            shape((rows, n, att_q.shape[1]), BF16),
            shape((rows, att_q.shape[1], n), BF16),
            shape((rows, att_q.shape[1], n), F32),
        ],
        (col, att_q, att_k, att_v, att_gate),
        name="project",
    )
    out = call(
        bound(attend_kernel, heads, steps),
        shape((rows, n, ch), BF16),
        (info, query, key, value, gate, first, att_out, *pieces),
        scratch=[
            pltpu.VMEM((-(-n // LANES), n * heads, LANES), F32),
            pltpu.VMEM((n, heads * n), F32),
        ],
        smem=(0,),
        name="attend",
    )
    return jnp.swapaxes(out, 0, 1)


def solution(mesh):
    devices = mesh.shape["row"] * mesh.shape["node"]

    def body(*args):
        return shards(devices, *args)

    return jax.shard_map(
        body,
        mesh=mesh,
        in_specs=(P(("grp", "row", "node"), None, None), P("grp")) + (P(),) * 12,
        out_specs=P("grp", AXES, None),
        check_vma=False,
    )
```

```python
import jax
import jax.numpy as jnp
from jax import lax
from jax.experimental import pallas as pl
from jax.experimental.pallas import tpu as pltpu
from jax.sharding import PartitionSpec as P

EPS = 1e-05
LANES = 128
LOG2E = 1.4426950408889634
F32 = jnp.float32
BF16 = jnp.bfloat16
AXES = ("row", "node")
VMEM_BYTES = 48 * 1024 * 1024
VMEM_MOST = 60 * 1024 * 1024


def norm_last(values, gain):
    average = jnp.mean(values, axis=-1, keepdims=True)
    centred = values - average
    variance = jnp.mean(centred * centred, axis=-1, keepdims=True)
    return centred * lax.rsqrt(variance + EPS) * gain


def sigmoid(values):
    return 0.5 * jnp.tanh(0.5 * values) + 0.5


def dot(a, b, a_dim, b_dim):
    return lax.dot_general(a, b, (((a_dim,), (b_dim,)), ((), ())), preferred_element_type=F32)


def position():
    return lax.axis_index("row") * lax.axis_size("node") + lax.axis_index("node")


def call(kernel, out_shape, args, scratch=(), smem=(), name=None, vmem=VMEM_BYTES, away=0):
    specs = [
        pl.BlockSpec(memory_space=pltpu.SMEM if n in smem else pltpu.VMEM) for n in range(len(args))
    ]
    single = not isinstance(out_shape, (list, tuple))
    inside = pl.BlockSpec(memory_space=pltpu.VMEM)
    if away:
        outs = [pl.BlockSpec(memory_space=pl.ANY)] * away + [inside] * (len(out_shape) - away)
    else:
        outs = inside if single else [inside] * len(out_shape)
    return pl.pallas_call(
        kernel,
        out_shape=out_shape,
        in_specs=specs,
        out_specs=outs,
        scratch_shapes=list(scratch),
        compiler_params=pltpu.CompilerParams(vmem_limit_bytes=vmem),
        name=name,
    )(*args)


class Sizes:
    def __init__(self, rows, crop, devices, channels):
        self.rows, self.crop, self.devices, self.channels = rows, crop, devices, channels
        self.half = rows // 2
        self.group = devices // 2
        self.columns = rows * self.group
        self.whole = crop // LANES
        self.rest = crop % LANES
        self.tiles = rows * crop // LANES
        self.chans = channels // self.group
        self.block = rows * rows
        self.block_tiles = -(-self.block // self.chans)


def edges_kernel(sz, len_ref, x_ref, ln_ref, w_ref, away_ref, *refs):
    near = refs[: sz.group]
    norm_ref, pair_ref, out_ref, sems = refs[sz.group :]
    length, me = len_ref[0], position()
    first = me * sz.rows
    copies = []

    def leave(start, stop):
        lanes = pl.ds(start * LANES, (stop - start) * LANES)
        copy = pltpu.make_async_copy(
            out_ref.at[:, :, lanes], away_ref.at[:, :, lanes], sems.at[len(copies)]
        )
        copy.start()
        copies.append(copy)

    cd, ch = sz.chans, sz.channels
    mine = me & (sz.group - 1)
    r = lax.broadcasted_iota(jnp.int32, (ch, ch), 0)
    e = lax.broadcasted_iota(jnp.int32, (ch, ch), 1)
    plain = (r == e).astype(BF16)
    slots = (((r // cd) ^ mine) * cd + r % cd == e).astype(BF16)
    picks = (plain, plain, slots, slots)
    weights = [dot(pick, w_ref[p], 1, 1).astype(BF16) for p, pick in enumerate(picks)]
    gate_w = jnp.concatenate([weights[0], weights[2]], axis=0)
    value_w = jnp.concatenate([weights[1], weights[3]], axis=0)
    gain = ln_ref[...]
    main = sz.whole * LANES
    for row in range(sz.rows):
        x = x_ref[row].astype(F32)
        for d in range(sz.devices):
            pair_ref[d, row * sz.rows : (row + 1) * sz.rows, :] = x[d * sz.rows : (d + 1) * sz.rows]
        normed = norm_last(x, gain).astype(BF16)
        norm_ref[pl.ds(row * main, main), :] = normed[:main]
        if sz.rest:
            h, q = divmod(row, sz.half)
            norm_ref[pl.ds(sz.rows * main + q * LANES + h * sz.rest, sz.rest), :] = normed[main:]
    for d in range(sz.devices):
        for t in range(sz.block_tiles):
            at = (sz.tiles + t) * LANES
            out_ref[d, :, at : at + LANES] = pair_ref[d, t * cd : (t + 1) * cd, :].astype(BF16)
    leave(sz.tiles, sz.tiles + sz.block_tiles)
    lane = lax.broadcasted_iota(jnp.int32, (1, LANES), 1)

    def live(tile):
        if tile < sz.rows * sz.whole:
            row, m = divmod(tile, sz.whole)
            return ((first + row < length) & (m * LANES + lane < length)).astype(F32)
        q = tile - sz.rows * sz.whole
        second = lane >= sz.rest
        row = first + q + jnp.where(second, sz.half, 0)
        k = main + lane - jnp.where(second, sz.rest, 0)
        return ((row < length) & (k < length)).astype(F32)

    step = 2 if sz.tiles % 2 == 0 else 1
    for tile in range(0, sz.tiles, step):
        n = norm_ref[pl.ds(tile * LANES, step * LANES), :]
        mask = jnp.concatenate([live(tile + s) for s in range(step)], axis=1)
        edge = sigmoid(dot(gate_w, n, 1, 1)) * dot(value_w, n, 1, 1) * mask
        edge = edge.astype(BF16)
        to = slice(tile * LANES, (tile + step) * LANES)
        for g in range(sz.group):
            left = edge[g * cd : (g + 1) * cd]
            out_ref[g, :, to] = left
            out_ref[sz.group + g, :, to] = left
            near[g][:, to] = edge[ch + g * cd : ch + (g + 1) * cd]
        leave(tile, tile + step)
    for copy in copies:
        copy.wait()


def unpack(sz, ref, owner, main_ref, rest_ref):
    cd, w = sz.chans, sz.whole
    for tile in range(sz.tiles):
        block = ref[:, tile * LANES : (tile + 1) * LANES].astype(F32)
        if tile < sz.rows * w:
            row, m = divmod(tile, w)
            main_ref[m, pl.ds(pl.multiple_of((owner * sz.rows + row) * cd, 8), cd), :] = block
        else:
            row = owner * sz.rows + tile - sz.rows * w
            rest_ref[pl.ds(pl.multiple_of(row * cd, 8), cd), :] = block
            rest_ref[pl.ds(pl.multiple_of((row + sz.half) * cd, 8), cd), :] = pltpu.roll(
                block, sz.rest, 1
            )


def matrix(sz, c, size, main_ref, rest_ref):
    cd, w = sz.chans, sz.whole
    parts = [main_ref[m, pl.ds(c, size, stride=cd), :].astype(BF16) for m in range(w)]
    if sz.rest:
        parts.append(rest_ref[pl.ds(c, size, stride=cd), :].astype(BF16)[:, : sz.rest])
    return jnp.concatenate(parts, axis=1) if len(parts) > 1 else parts[0]


def right_kernel(sz, *refs):
    near, (out_ref, main_ref, rest_ref) = refs[: sz.group], refs[sz.group :]
    mine = position() & (sz.group - 1)
    for r in range(sz.group):
        unpack(sz, near[r], mine ^ r, main_ref, rest_ref)
    for c in range(sz.chans):
        out_ref[c] = matrix(sz, c, sz.columns, main_ref, rest_ref)


def outer_kernel(
    sz, left_ref, right_ref, out_ref, lmain_ref, lrest_ref, omain_ref, orest_ref
):
    cd, n, w, half = sz.chans, sz.crop, sz.whole, sz.half
    for d in range(sz.devices):
        unpack(sz, left_ref.at[d], jnp.int32(d), lmain_ref, lrest_ref)
    for c in range(cd):
        outer = dot(right_ref[c], matrix(sz, c, n, lmain_ref, lrest_ref), 1, 1)
        for m in range(w):
            omain_ref[m, pl.ds(c, sz.columns, stride=cd), :] = outer[:, m * LANES : (m + 1) * LANES]
        if sz.rest:
            part = outer[:, w * LANES :]
            orest_ref[pl.ds(c, sz.columns, stride=cd), :] = jnp.concatenate([part, part], axis=1)
    low = lax.broadcasted_iota(jnp.int32, (cd, LANES), 1) < sz.rest
    for g in range(sz.group):
        start = g * sz.rows
        for tile in range(sz.tiles):
            if tile < sz.rows * w:
                row, m = divmod(tile, w)
                block = omain_ref[m, pl.ds((start + row) * cd, cd), :]
            else:
                at = start + tile - sz.rows * w
                block = jnp.where(
                    low,
                    orest_ref[pl.ds(at * cd, cd), :],
                    orest_ref[pl.ds((at + half) * cd, cd), :],
                )
            out_ref[g, :, tile * LANES : (tile + 1) * LANES] = block.astype(BF16)


def columns_kernel(sz, pair_ref, lnp_ref, gate_ref, x_ref, gating_ref, cols_ref):
    cd = sz.chans
    for s in range(sz.devices):
        for t in range(sz.block_tiles):
            at = (sz.tiles + t) * LANES
            rows = pl.ds(s * sz.block + t * cd, cd)
            cols_ref[rows, :] = pair_ref[s, :, at : at + LANES].astype(F32)
    for j in range(sz.rows):
        x = cols_ref[pl.ds(j, sz.crop, stride=sz.rows), :]
        x_ref[j] = x.astype(BF16)
        normed = norm_last(x, lnp_ref[...]).astype(BF16)
        gating_ref[j] = sigmoid(dot(normed, gate_ref[...], 1, 0))


def update_kernel(
    sz, x_ref, gating_ref, lnh_ref, tri_ref, lna_ref, biasw_ref, sums_ref,
    first_ref, col_ref, bias_ref, brow_ref,
):
    n, w, half, ch = sz.crop, sz.whole, sz.half, sz.channels
    gain_h = jnp.transpose(jnp.broadcast_to(lnh_ref[...], (ch, ch)))
    tri = tri_ref[...]

    def update(tile):
        block = sums_ref[:, :, tile * LANES : (tile + 1) * LANES].astype(F32).reshape(ch, LANES)
        average = jnp.mean(block, axis=0, keepdims=True)
        centred = block - average
        variance = jnp.mean(centred * centred, axis=0, keepdims=True)
        hidden = (centred * lax.rsqrt(variance + EPS) * gain_h).astype(BF16)
        return dot(hidden, tri, 0, 0)

    rest = [update(sz.rows * w + q) for q in range(half)] if sz.rest else None
    for j in range(sz.rows):
        parts = [update(j * w + m) for m in range(w)]
        if sz.rest:
            h, q = divmod(j, half)
            parts.append(rest[q][h * sz.rest : (h + 1) * sz.rest])
        change = jnp.concatenate(parts, axis=0) if len(parts) > 1 else parts[0]
        first = (x_ref[j].astype(F32) + gating_ref[j] * change).astype(BF16)
        first_ref[j] = first
        col = norm_last(first.astype(F32), lna_ref[...]).astype(BF16)
        col_ref[j] = col
        heads = biasw_ref.shape[1]
        brow_ref[pl.ds(j * heads, heads), :] = dot(biasw_ref[...], col, 0, 1)
    rows = brow_ref[...]
    part = rows.shape[0] // 2
    one, two = rows[:part], rows[part:]
    message = [one[:, : w * LANES], two[:, : w * LANES]]
    if sz.rest:
        message += [one[:, w * LANES :], two[:, w * LANES :]]
    bias_ref[...] = jnp.concatenate(message, axis=1).astype(BF16)


def project_kernel(sz, col_ref, q_ref, k_ref, v_ref, g_ref, qo_ref, ko_ref, vo_ref, go_ref):
    n, ch = sz.crop, sz.channels
    qk = jnp.concatenate([q_ref[...], k_ref[...]], axis=1)
    vg = jnp.transpose(jnp.concatenate([v_ref[...], g_ref[...]], axis=1).astype(F32)).astype(BF16)
    width = q_ref.shape[1]
    for j in range(sz.rows):
        col = col_ref[j]
        both = dot(col, qk, 1, 0)
        qo_ref[j] = both[:, :width].astype(BF16)
        ko_ref[j] = both[:, width:].astype(BF16)
        other = dot(vg, col, 1, 1)
        vo_ref[j] = other[:width].astype(BF16)
        go_ref[j] = sigmoid(other[width:])


def attend_kernel(
    sz, heads, steps, len_ref, q_ref, k_ref, v_ref, g_ref, first_ref, aout_ref, *refs
):
    bias_refs, (out_ref, rows_ref, biasT_ref) = refs[:-3], refs[-3:]
    n, w, ch = sz.crop, sz.whole, sz.channels
    length, me = len_ref[0], position()
    width = q_ref.shape[2]
    hd = width // heads
    per = sz.rows * heads // 2
    for ref, offsets in zip(bias_refs, steps):
        for place, offset in enumerate(offsets):
            block = ref[place].astype(F32) * LOG2E
            for p in range(2):
                at = pl.ds(pl.multiple_of(((me ^ offset) * 2 + p) * per, 8), per)
                for m in range(w):
                    rows_ref[m, at, :] = block[:, (p * w + m) * LANES : (p * w + m + 1) * LANES]
                if sz.rest:
                    tail = block[:, 2 * w * LANES :]
                    rows_ref[w, at, :] = pltpu.roll(tail, sz.rest, 1) if p else tail
    key = lax.broadcasted_iota(jnp.int32, (n, LANES), 0)
    dead = jnp.where(key < length, 0.0, -1e9 * LOG2E).astype(F32)
    halves = []
    for head in range(heads):
        b = [
            jnp.transpose(rows_ref[m, pl.ds(head, n, stride=heads), :])
            for m in range(w + (sz.rest > 0))
        ]
        if sz.rest:
            b[w] = b[w][: sz.rest]
        b = jnp.concatenate(b, axis=0) if len(b) > 1 else b[0]
        for m in range(w):
            biasT_ref[:, (head * w + m) * LANES : (head * w + m + 1) * LANES] = (
                b[:, m * LANES : (m + 1) * LANES] + dead
            )
        if sz.rest:
            halves.append(b[:, w * LANES :])
    per_tile = LANES // sz.rest if sz.rest else 1
    base = heads * w
    if sz.rest:
        for t in range(heads // per_tile):
            biasT_ref[:, (base + t) * LANES : (base + t + 1) * LANES] = (
                jnp.concatenate(halves[t * per_tile : (t + 1) * per_tile], axis=1) + dead
            )
    lane = lax.broadcasted_iota(jnp.int32, (1, width), 1)
    head_masks = [((lane >= h * hd) & (lane < (h + 1) * hd)).astype(BF16) for h in range(heads)]
    scale = (hd ** (-0.5)) * LOG2E
    for j in range(sz.rows):
        q = q_ref[j]
        masked = [q * head_masks[h] for h in range(heads)]
        pieces = [masked[h][: w * LANES] for h in range(heads)]
        if sz.rest:
            pieces += [masked[h][w * LANES :] for h in range(heads)]
        stacked = jnp.concatenate(pieces, axis=0)
        scores = dot(k_ref[j], stacked, 1, 1) * scale + biasT_ref[...]
        top = jnp.max(scores, axis=0, keepdims=True)
        weights = jnp.exp2(scores - top)
        total = jnp.sum(weights, axis=0, keepdims=True)
        mixed = dot(v_ref[j], weights.astype(BF16), 1, 0)
        inverse = 1.0 / total
        mains, rests = [], []
        for h in range(heads):
            sl = slice(h * w * LANES, (h + 1) * w * LANES)
            mains.append(mixed[h * hd : (h + 1) * hd, sl] * inverse[:, sl])
            if sz.rest:
                t, part = divmod(h, per_tile)
                sl = slice((base + t) * LANES, (base + t + 1) * LANES)
                piece = mixed[h * hd : (h + 1) * hd, sl] * inverse[:, sl]
                rests.append(piece[:, part * sz.rest : (part + 1) * sz.rest])
        attended = jnp.concatenate(mains, axis=0)
        if sz.rest:
            attended = jnp.concatenate([attended, jnp.concatenate(rests, axis=0)], axis=1)
        gated = (attended * g_ref[j]).astype(BF16)
        total_out = first_ref[j].astype(F32) + dot(gated, aout_ref[...], 0, 0)
        out_ref[j] = total_out.astype(BF16)


def spread(block, devices):
    pieces, offsets = [block[None]], [[0]]
    first = [devices // 2, devices // 4, devices // 2 + devices // 4]
    for partners in [first] + [[devices >> s] for s in range(3, devices.bit_length())]:
        held = jnp.concatenate(pieces, axis=0) if len(pieces) > 1 else pieces[0]
        known = [o for part in offsets for o in part]
        for bit in partners:
            pieces.append(lax.ppermute(held, AXES, [(d, d ^ bit) for d in range(devices)]))
            offsets.append([o ^ bit for o in known])
    return pieces, offsets


def shards(
    devices,
    pair_rep, length, ln_pair, tri_in, tri_gate, ln_hidden, tri_out, ln_att,
    att_q, att_k, att_v, att_bias, att_gate, att_out,
):
    rows, crop, ch = pair_rep.shape
    heads = att_bias.shape[1]
    sz = Sizes(rows, crop, devices, ch)
    n, cd = crop, sz.chans
    def bound(kernel, *extra):
        def run(*refs):
            return kernel(sz, *extra, *refs)

        return run

    shape = jax.ShapeDtypeStruct
    g, t, bt = sz.group, sz.tiles, sz.block_tiles

    def slab(tiles, *lead):
        return shape((*lead, cd, tiles * LANES), BF16)

    def send(blocks, offset):
        return [
            block
            if not (offset ^ r)
            else lax.ppermute(block, AXES, [(d, d ^ offset ^ r) for d in range(devices)])
            for r, block in enumerate(blocks)
        ]

    left, *others = call(
        bound(edges_kernel),
        [slab(t + bt, devices)] + [slab(t)] * g,
        (length, pair_rep, ln_pair[None], tri_in),
        scratch=[
            pltpu.VMEM((rows * crop, ch), BF16),
            pltpu.VMEM((devices, bt * cd, ch), F32),
            pltpu.VMEM((devices, cd, (t + bt) * LANES), BF16),
            pltpu.SemaphoreType.DMA((t + 1,)),
        ],
        smem=(0,),
        away=1,
        name="edges",
        vmem=VMEM_MOST,
    )
    left = lax.all_to_all(left, AXES, split_axis=0, concat_axis=0, tiled=True)
    near = send(others, 0)
    rest = sz.rest > 0
    column_rows = sz.columns * cd
    right = call(
        bound(right_kernel),
        shape((cd, sz.columns, n), BF16),
        tuple(near),
        scratch=[
            pltpu.VMEM((sz.whole, column_rows, LANES), F32),
            pltpu.VMEM((column_rows if rest else 8, LANES), F32),
        ],
        name="right",
    )
    outer = call(
        bound(outer_kernel),
        slab(t, g),
        (left, right),
        scratch=[
            pltpu.VMEM((sz.whole, n * cd, LANES), F32),
            pltpu.VMEM((n * cd if rest else 8, LANES), F32),
            pltpu.VMEM((sz.whole, column_rows, LANES), F32),
            pltpu.VMEM((column_rows if rest else 8, LANES), F32),
        ],
        name="outer",
    )
    sums = lax.all_to_all(
        outer, AXES, split_axis=0, concat_axis=0, tiled=True,
        axis_index_groups=[list(range(g)), list(range(g, devices))],
    )
    columns, gating = call(
        bound(columns_kernel),
        [shape((rows, n, ch), BF16), shape((rows, n, ch), F32)],
        (left, ln_pair[None], tri_gate),
        scratch=[pltpu.VMEM((devices * sz.block + cd, ch), F32)],
        name="columns",
    )
    first, col, bias = call(
        bound(update_kernel),
        [
            shape((rows, n, ch), BF16),
            shape((rows, n, ch), BF16),
            shape((rows * heads // 2, 2 * n), BF16),
        ],
        (columns, gating, ln_hidden[None], tri_out, ln_att[None], att_bias, sums),
        scratch=[pltpu.VMEM((rows * heads, n), F32)],
        name="update",
    )
    pieces, steps = spread(bias, devices)
    query, key, value, gate = call(
        bound(project_kernel),
        [
            shape((rows, n, att_q.shape[1]), BF16),
            shape((rows, n, att_q.shape[1]), BF16),
            shape((rows, att_q.shape[1], n), BF16),
            shape((rows, att_q.shape[1], n), F32),
        ],
        (col, att_q, att_k, att_v, att_gate),
        name="project",
    )
    out = call(
        bound(attend_kernel, heads, steps),
        shape((rows, n, ch), BF16),
        (length, query, key, value, gate, first, att_out, *pieces),
        scratch=[
            pltpu.VMEM((-(-n // LANES), n * heads, LANES), F32),
            pltpu.VMEM((n, heads * n), F32),
        ],
        smem=(0,),
        name="attend",
    )
    return jnp.swapaxes(out, 0, 1)


def solution(mesh):
    devices = mesh.shape["row"] * mesh.shape["node"]

    def body(*args):
        return shards(devices, *args)

    return jax.shard_map(
        body,
        mesh=mesh,
        in_specs=(P(("grp", "row", "node"), None, None), P("grp")) + (P(),) * 12,
        out_specs=P("grp", AXES, None),
        check_vma=False,
    )
```

```python
import jax
import jax.numpy as jnp
from jax import lax
from jax.experimental import pallas as pl
from jax.experimental.pallas import tpu as pltpu
from jax.sharding import PartitionSpec as P

EPS = 1e-05
LANES = 128
LOG2E = 1.4426950408889634
F32 = jnp.float32
BF16 = jnp.bfloat16
AXES = ("row", "node")
VMEM_BYTES = 48 * 1024 * 1024
VMEM_MOST = 60 * 1024 * 1024


def norm_last(values, gain):
    average = jnp.mean(values, axis=-1, keepdims=True)
    centred = values - average
    variance = jnp.mean(centred * centred, axis=-1, keepdims=True)
    return centred * lax.rsqrt(variance + EPS) * gain


def sigmoid(values):
    return 0.5 * jnp.tanh(0.5 * values) + 0.5


def dot(a, b, a_dim, b_dim):
    return lax.dot_general(a, b, (((a_dim,), (b_dim,)), ((), ())), preferred_element_type=F32)


def position():
    return lax.axis_index("row") * lax.axis_size("node") + lax.axis_index("node")


def call(kernel, out_shape, args, scratch=(), smem=(), name=None, vmem=VMEM_BYTES, far=(), away=0):
    specs = [
        pl.BlockSpec(
            memory_space=pltpu.SMEM if n in smem else pl.ANY if n in far else pltpu.VMEM
        )
        for n in range(len(args))
    ]
    single = not isinstance(out_shape, (list, tuple))
    inside = pl.BlockSpec(memory_space=pltpu.VMEM)
    if away:
        outs = [pl.BlockSpec(memory_space=pl.ANY)] * away + [inside] * (len(out_shape) - away)
    else:
        outs = inside if single else [inside] * len(out_shape)
    return pl.pallas_call(
        kernel,
        out_shape=out_shape,
        in_specs=specs,
        out_specs=outs,
        scratch_shapes=list(scratch),
        compiler_params=pltpu.CompilerParams(vmem_limit_bytes=vmem),
        name=name,
    )(*args)


class Sizes:
    def __init__(self, rows, crop, devices, channels):
        self.rows, self.crop, self.devices, self.channels = rows, crop, devices, channels
        self.half = rows // 2
        self.group = devices // 2
        self.columns = rows * self.group
        self.whole = crop // LANES
        self.rest = crop % LANES
        self.tiles = rows * crop // LANES
        self.chans = channels // self.group
        self.block = rows * rows
        self.block_tiles = -(-self.block // self.chans)


def edges_kernel(sz, len_ref, x_ref, ln_ref, w_ref, away_ref, *refs):
    near_refs = refs[: sz.group]
    x_buf, w_buf, norm_ref, pair_ref, out_ref, near_ref, in_sems, out_sems = refs[sz.group :]
    length, me = len_ref[0], position()
    first = me * sz.rows
    arriving = [
        pltpu.make_async_copy(x_ref.at[row], x_buf.at[row], in_sems.at[row])
        for row in range(sz.rows)
    ]
    weights_in = pltpu.make_async_copy(w_ref, w_buf, in_sems.at[sz.rows])
    for copy in arriving:
        copy.start()
    weights_in.start()
    leaving = []

    def leave(source, target):
        copy = pltpu.make_async_copy(source, target, out_sems.at[len(leaving)])
        copy.start()
        leaving.append(copy)

    cd, ch = sz.chans, sz.channels
    mine = me & (sz.group - 1)
    gain = ln_ref[...]
    main = sz.whole * LANES
    for row in range(sz.rows):
        arriving[row].wait()
        x = x_buf[row].astype(F32)
        for d in range(sz.devices):
            pair_ref[d, row * sz.rows : (row + 1) * sz.rows, :] = x[d * sz.rows : (d + 1) * sz.rows]
        normed = norm_last(x, gain).astype(BF16)
        norm_ref[pl.ds(row * main, main), :] = normed[:main]
        if sz.rest:
            h, q = divmod(row, sz.half)
            norm_ref[pl.ds(sz.rows * main + q * LANES + h * sz.rest, sz.rest), :] = normed[main:]
    r = lax.broadcasted_iota(jnp.int32, (ch, ch), 0)
    e = lax.broadcasted_iota(jnp.int32, (ch, ch), 1)
    plain = (r == e).astype(BF16)
    slots = (((r // cd) ^ mine) * cd + r % cd == e).astype(BF16)
    weights_in.wait()
    weights = [
        dot(pick, w_buf[p], 1, 1).astype(BF16) for p, pick in enumerate((plain, plain, slots, slots))
    ]
    lane = lax.broadcasted_iota(jnp.int32, (1, LANES), 1)

    def live(tile):
        if tile < sz.rows * sz.whole:
            row, m = divmod(tile, sz.whole)
            return ((first + row < length) & (m * LANES + lane < length)).astype(F32)
        q = tile - sz.rows * sz.whole
        second = lane >= sz.rest
        row = first + q + jnp.where(second, sz.half, 0)
        k = main + lane - jnp.where(second, sz.rest, 0)
        return ((row < length) & (k < length)).astype(F32)

    step = 2 if sz.tiles % 2 == 0 else 1

    def edge(gate_w, value_w, tile):
        n = norm_ref[pl.ds(tile * LANES, step * LANES), :]
        mask = jnp.concatenate([live(tile + s) for s in range(step)], axis=1)
        return (sigmoid(dot(gate_w, n, 1, 1)) * (dot(value_w, n, 1, 1) * mask)).astype(BF16)

    for tile in range(0, sz.tiles, step):
        to = slice(tile * LANES, (tile + step) * LANES)
        right = edge(weights[2], weights[3], tile)
        for g in range(sz.group):
            near_ref[g, :, to] = right[g * cd : (g + 1) * cd]
    for g in range(sz.group):
        leave(near_ref.at[g], near_refs[g])
    for d in range(sz.devices):
        for t in range(sz.block_tiles):
            at = (sz.tiles + t) * LANES
            out_ref[d, :, at : at + LANES] = pair_ref[d, t * cd : (t + 1) * cd, :].astype(BF16)
    lanes = pl.ds(sz.tiles * LANES, sz.block_tiles * LANES)
    leave(out_ref.at[:, :, lanes], away_ref.at[:, :, lanes])
    for tile in range(0, sz.tiles, step):
        to = slice(tile * LANES, (tile + step) * LANES)
        left = edge(weights[0], weights[1], tile)
        for g in range(sz.group):
            part = left[g * cd : (g + 1) * cd]
            out_ref[g, :, to] = part
            out_ref[sz.group + g, :, to] = part
        lanes = pl.ds(tile * LANES, step * LANES)
        leave(out_ref.at[:, :, lanes], away_ref.at[:, :, lanes])
    for copy in leaving:
        copy.wait()


def unpack(sz, ref, owner, main_ref, rest_ref):
    cd, w = sz.chans, sz.whole
    for tile in range(sz.tiles):
        block = ref[:, tile * LANES : (tile + 1) * LANES].astype(F32)
        if tile < sz.rows * w:
            row, m = divmod(tile, w)
            main_ref[m, pl.ds(pl.multiple_of((owner * sz.rows + row) * cd, 8), cd), :] = block
        else:
            row = owner * sz.rows + tile - sz.rows * w
            rest_ref[pl.ds(pl.multiple_of(row * cd, 8), cd), :] = block
            rest_ref[pl.ds(pl.multiple_of((row + sz.half) * cd, 8), cd), :] = pltpu.roll(
                block, sz.rest, 1
            )


def matrix(sz, c, size, main_ref, rest_ref):
    cd, w = sz.chans, sz.whole
    parts = [main_ref[m, pl.ds(c, size, stride=cd), :].astype(BF16) for m in range(w)]
    if sz.rest:
        parts.append(rest_ref[pl.ds(c, size, stride=cd), :].astype(BF16)[:, : sz.rest])
    return jnp.concatenate(parts, axis=1) if len(parts) > 1 else parts[0]


def right_kernel(sz, *refs):
    near, (out_ref, main_ref, rest_ref) = refs[: sz.group], refs[sz.group :]
    mine = position() & (sz.group - 1)
    for r in range(sz.group):
        unpack(sz, near[r], mine ^ r, main_ref, rest_ref)
    for c in range(sz.chans):
        out_ref[c] = matrix(sz, c, sz.columns, main_ref, rest_ref)


def outer_kernel(
    sz, left_ref, right_ref, out_ref, lmain_ref, lrest_ref, omain_ref, orest_ref
):
    cd, n, w, half = sz.chans, sz.crop, sz.whole, sz.half
    for d in range(sz.devices):
        unpack(sz, left_ref.at[d], jnp.int32(d), lmain_ref, lrest_ref)
    for c in range(cd):
        outer = dot(right_ref[c], matrix(sz, c, n, lmain_ref, lrest_ref), 1, 1)
        for m in range(w):
            omain_ref[m, pl.ds(c, sz.columns, stride=cd), :] = outer[:, m * LANES : (m + 1) * LANES]
        if sz.rest:
            part = outer[:, w * LANES :]
            orest_ref[pl.ds(c, sz.columns, stride=cd), :] = jnp.concatenate([part, part], axis=1)
    low = lax.broadcasted_iota(jnp.int32, (cd, LANES), 1) < sz.rest
    for g in range(sz.group):
        start = g * sz.rows
        for tile in range(sz.tiles):
            if tile < sz.rows * w:
                row, m = divmod(tile, w)
                block = omain_ref[m, pl.ds((start + row) * cd, cd), :]
            else:
                at = start + tile - sz.rows * w
                block = jnp.where(
                    low,
                    orest_ref[pl.ds(at * cd, cd), :],
                    orest_ref[pl.ds((at + half) * cd, cd), :],
                )
            out_ref[g, :, tile * LANES : (tile + 1) * LANES] = block.astype(BF16)


def update_kernel(
    sz, lnp_ref, gate_ref, lnh_ref, tri_ref, lna_ref, biasw_ref, sums_ref, pair_ref,
    first_ref, col_ref, bias_ref, cols_ref, brow_ref,
):
    n, w, half, ch, cd = sz.crop, sz.whole, sz.half, sz.channels, sz.chans
    for s in range(sz.devices):
        for t in range(sz.block_tiles):
            at = (sz.tiles + t) * LANES
            rows = pl.ds(s * sz.block + t * cd, cd)
            cols_ref[rows, :] = pair_ref[s, :, at : at + LANES].astype(F32)
    gain_h = jnp.transpose(jnp.broadcast_to(lnh_ref[...], (ch, ch)))
    tri = tri_ref[...]

    def update(tile):
        block = sums_ref[:, :, tile * LANES : (tile + 1) * LANES].astype(F32).reshape(ch, LANES)
        average = jnp.mean(block, axis=0, keepdims=True)
        centred = block - average
        variance = jnp.mean(centred * centred, axis=0, keepdims=True)
        hidden = (centred * lax.rsqrt(variance + EPS) * gain_h).astype(BF16)
        return dot(hidden, tri, 0, 0)

    rest = [update(sz.rows * w + q) for q in range(half)] if sz.rest else None
    for j in range(sz.rows):
        parts = [update(j * w + m) for m in range(w)]
        if sz.rest:
            h, q = divmod(j, half)
            parts.append(rest[q][h * sz.rest : (h + 1) * sz.rest])
        change = jnp.concatenate(parts, axis=0) if len(parts) > 1 else parts[0]
        x = cols_ref[pl.ds(j, n, stride=sz.rows), :]
        normed = norm_last(x, lnp_ref[...]).astype(BF16)
        gating = sigmoid(dot(normed, gate_ref[...], 1, 0))
        first = (x + gating * change).astype(BF16)
        first_ref[j] = first
        col = norm_last(first.astype(F32), lna_ref[...]).astype(BF16)
        col_ref[j] = col
        heads = biasw_ref.shape[1]
        brow_ref[pl.ds(j * heads, heads), :] = dot(biasw_ref[...], col, 0, 1)
    rows = brow_ref[...]
    part = rows.shape[0] // 2
    one, two = rows[:part], rows[part:]
    message = [one[:, : w * LANES], two[:, : w * LANES]]
    if sz.rest:
        message += [one[:, w * LANES :], two[:, w * LANES :]]
    bias_ref[...] = jnp.concatenate(message, axis=1).astype(BF16)


def project_kernel(sz, col_ref, q_ref, k_ref, v_ref, g_ref, qo_ref, ko_ref, vo_ref, go_ref):
    n, ch = sz.crop, sz.channels
    qk = jnp.concatenate([q_ref[...], k_ref[...]], axis=1)
    vg = jnp.transpose(jnp.concatenate([v_ref[...], g_ref[...]], axis=1).astype(F32)).astype(BF16)
    width = q_ref.shape[1]
    for j in range(sz.rows):
        col = col_ref[j]
        both = dot(col, qk, 1, 0)
        qo_ref[j] = both[:, :width].astype(BF16)
        ko_ref[j] = both[:, width:].astype(BF16)
        other = dot(vg, col, 1, 1)
        vo_ref[j] = other[:width].astype(BF16)
        go_ref[j] = sigmoid(other[width:])


def attend_kernel(
    sz, heads, steps, len_ref, q_ref, k_ref, v_ref, g_ref, first_ref, aout_ref, *refs
):
    bias_refs, (out_ref, rows_ref, biasT_ref) = refs[:-3], refs[-3:]
    n, w, ch = sz.crop, sz.whole, sz.channels
    length, me = len_ref[0], position()
    width = q_ref.shape[2]
    hd = width // heads
    per = sz.rows * heads // 2
    for ref, offsets in zip(bias_refs, steps):
        for place, offset in enumerate(offsets):
            block = ref[place].astype(F32) * LOG2E
            for p in range(2):
                at = pl.ds(pl.multiple_of(((me ^ offset) * 2 + p) * per, 8), per)
                for m in range(w):
                    rows_ref[m, at, :] = block[:, (p * w + m) * LANES : (p * w + m + 1) * LANES]
                if sz.rest:
                    tail = block[:, 2 * w * LANES :]
                    rows_ref[w, at, :] = pltpu.roll(tail, sz.rest, 1) if p else tail
    key = lax.broadcasted_iota(jnp.int32, (n, LANES), 0)
    dead = jnp.where(key < length, 0.0, -1e9 * LOG2E).astype(F32)
    halves = []
    for head in range(heads):
        b = [
            jnp.transpose(rows_ref[m, pl.ds(head, n, stride=heads), :])
            for m in range(w + (sz.rest > 0))
        ]
        if sz.rest:
            b[w] = b[w][: sz.rest]
        b = jnp.concatenate(b, axis=0) if len(b) > 1 else b[0]
        for m in range(w):
            biasT_ref[:, (head * w + m) * LANES : (head * w + m + 1) * LANES] = (
                b[:, m * LANES : (m + 1) * LANES] + dead
            )
        if sz.rest:
            halves.append(b[:, w * LANES :])
    per_tile = LANES // sz.rest if sz.rest else 1
    base = heads * w
    if sz.rest:
        for t in range(heads // per_tile):
            biasT_ref[:, (base + t) * LANES : (base + t + 1) * LANES] = (
                jnp.concatenate(halves[t * per_tile : (t + 1) * per_tile], axis=1) + dead
            )
    lane = lax.broadcasted_iota(jnp.int32, (1, width), 1)
    head_masks = [((lane >= h * hd) & (lane < (h + 1) * hd)).astype(BF16) for h in range(heads)]
    scale = (hd ** (-0.5)) * LOG2E
    tiles = [[(h, m * LANES, LANES)] for h in range(heads) for m in range(w)]
    if sz.rest:
        tiles += [
            [(h, w * LANES, sz.rest) for h in range(t * per_tile, (t + 1) * per_tile)]
            for t in range(heads // per_tile)
        ]
    units = [list(range(u, min(u + 2, len(tiles)))) for u in range(0, len(tiles), 2)]

    def score(j, unit):
        stacked = [
            q_ref[j, start : start + count, :] * head_masks[h]
            for t in unit
            for h, start, count in tiles[t]
        ]
        lanes = slice(unit[0] * LANES, (unit[-1] + 1) * LANES)
        return dot(k_ref[j], jnp.concatenate(stacked, axis=0), 1, 1) * scale + biasT_ref[:, lanes]

    def mix(j, unit, scores, mains, rests):
        weights = jnp.exp2(scores - jnp.max(scores, axis=0, keepdims=True))
        total = jnp.sum(weights, axis=0, keepdims=True)
        held = sorted({h for t in unit for h, _, _ in tiles[t]})
        values = v_ref[j, held[0] * hd : (held[-1] + 1) * hd, :]
        mixed = dot(values, weights.astype(BF16), 1, 0)
        inverse = 1.0 / total
        for place, t in enumerate(unit):
            lanes = slice(place * LANES, (place + 1) * LANES)
            for part, (h, start, count) in enumerate(tiles[t]):
                rows = slice((h - held[0]) * hd, (h - held[0] + 1) * hd)
                piece = mixed[rows, lanes] * inverse[:, lanes]
                if count == LANES:
                    mains[h].append(piece)
                else:
                    rests[h] = piece[:, part * sz.rest : (part + 1) * sz.rest]

    order = [(j, u) for j in range(sz.rows) for u in range(len(units))]
    scores = score(order[0][0], units[order[0][1]])
    for at, (j, u) in enumerate(order):
        if u == 0:
            mains, rests = [[] for _ in range(heads)], [None] * heads
        now = scores
        if at + 1 < len(order):
            scores = score(order[at + 1][0], units[order[at + 1][1]])
        mix(j, units[u], now, mains, rests)
        if u == len(units) - 1:
            attended = jnp.concatenate(
                [
                    jnp.concatenate(mains[h] + ([rests[h]] if sz.rest else []), axis=1)
                    if w + (sz.rest > 0) > 1
                    else mains[h][0]
                    for h in range(heads)
                ],
                axis=0,
            )
            gated = (attended * g_ref[j]).astype(BF16)
            total_out = first_ref[j].astype(F32) + dot(gated, aout_ref[...], 0, 0)
            out_ref[j] = total_out.astype(BF16)


def spread(block, devices):
    pieces, offsets = [block[None]], [[0]]
    bit = devices // 2
    while bit:
        held = jnp.concatenate(pieces, axis=0) if len(pieces) > 1 else pieces[0]
        known = [o for part in offsets for o in part]
        pieces.append(lax.ppermute(held, AXES, [(d, d ^ bit) for d in range(devices)]))
        offsets.append([o ^ bit for o in known])
        bit //= 2
    return pieces, offsets


def shards(
    devices,
    pair_rep, length, ln_pair, tri_in, tri_gate, ln_hidden, tri_out, ln_att,
    att_q, att_k, att_v, att_bias, att_gate, att_out,
):
    rows, crop, ch = pair_rep.shape
    heads = att_bias.shape[1]
    sz = Sizes(rows, crop, devices, ch)
    n, cd = crop, sz.chans
    def bound(kernel, *extra):
        def run(*refs):
            return kernel(sz, *extra, *refs)

        return run

    shape = jax.ShapeDtypeStruct
    g, t, bt = sz.group, sz.tiles, sz.block_tiles

    def slab(tiles, *lead):
        return shape((*lead, cd, tiles * LANES), BF16)

    def send(blocks, offset):
        return [
            block
            if not (offset ^ r)
            else lax.ppermute(block, AXES, [(d, d ^ offset ^ r) for d in range(devices)])
            for r, block in enumerate(blocks)
        ]

    left, *others = call(
        bound(edges_kernel),
        [slab(t + bt, devices)] + [slab(t)] * g,
        (length, pair_rep, ln_pair[None], tri_in),
        scratch=[
            pltpu.VMEM(pair_rep.shape, BF16),
            pltpu.VMEM(tri_in.shape, BF16),
            pltpu.VMEM((rows * crop, ch), BF16),
            pltpu.VMEM((devices, bt * cd, ch), F32),
            pltpu.VMEM((devices, cd, (t + bt) * LANES), BF16),
            pltpu.VMEM((g, cd, t * LANES), BF16),
            pltpu.SemaphoreType.DMA((rows + 1,)),
            pltpu.SemaphoreType.DMA((t + 1 + g,)),
        ],
        smem=(0,),
        far=(1, 3),
        away=1 + g,
        name="edges",
        vmem=VMEM_MOST,
    )
    left = lax.all_to_all(left, AXES, split_axis=0, concat_axis=0, tiled=True)
    near = send(others, 0)
    rest = sz.rest > 0
    column_rows = sz.columns * cd
    right = call(
        bound(right_kernel),
        shape((cd, sz.columns, n), BF16),
        tuple(near),
        scratch=[
            pltpu.VMEM((sz.whole, column_rows, LANES), F32),
            pltpu.VMEM((column_rows if rest else 8, LANES), F32),
        ],
        name="right",
    )
    outer = call(
        bound(outer_kernel),
        slab(t, g),
        (left, right),
        scratch=[
            pltpu.VMEM((sz.whole, n * cd, LANES), F32),
            pltpu.VMEM((n * cd if rest else 8, LANES), F32),
            pltpu.VMEM((sz.whole, column_rows, LANES), F32),
            pltpu.VMEM((column_rows if rest else 8, LANES), F32),
        ],
        name="outer",
    )
    sums = lax.all_to_all(
        outer, AXES, split_axis=0, concat_axis=0, tiled=True,
        axis_index_groups=[list(range(g)), list(range(g, devices))],
    )
    first, col, bias = call(
        bound(update_kernel),
        [
            shape((rows, n, ch), BF16),
            shape((rows, n, ch), BF16),
            shape((rows * heads // 2, 2 * n), BF16),
        ],
        (
            ln_pair[None], tri_gate, ln_hidden[None], tri_out, ln_att[None], att_bias,
            sums, left,
        ),
        scratch=[
            pltpu.VMEM((devices * sz.block + cd, ch), F32),
            pltpu.VMEM((rows * heads, n), F32),
        ],
        name="update",
    )
    pieces, steps = spread(bias, devices)
    query, key, value, gate = call(
        bound(project_kernel),
        [
            shape((rows, n, att_q.shape[1]), BF16),
            shape((rows, n, att_q.shape[1]), BF16),
            shape((rows, att_q.shape[1], n), BF16),
            shape((rows, att_q.shape[1], n), F32),
        ],
        (col, att_q, att_k, att_v, att_gate),
        name="project",
    )
    out = call(
        bound(attend_kernel, heads, steps),
        shape((rows, n, ch), BF16),
        (length, query, key, value, gate, first, att_out, *pieces),
        scratch=[
            pltpu.VMEM((-(-n // LANES), n * heads, LANES), F32),
            pltpu.VMEM((n, heads * n), F32),
        ],
        smem=(0,),
        name="attend",
    )
    return jnp.swapaxes(out, 0, 1)


def solution(mesh):
    devices = mesh.shape["row"] * mesh.shape["node"]

    def body(*args):
        return shards(devices, *args)

    return jax.shard_map(
        body,
        mesh=mesh,
        in_specs=(P(("grp", "row", "node"), None, None), P("grp")) + (P(),) * 12,
        out_specs=P("grp", AXES, None),
        check_vma=False,
    )
```

```python
import jax
import jax.numpy as jnp
from jax import lax
from jax.experimental import pallas as pl
from jax.experimental.pallas import tpu as pltpu
from jax.sharding import PartitionSpec as P

EPS = 1e-05
LANES = 128
LOG2E = 1.4426950408889634
F32 = jnp.float32
BF16 = jnp.bfloat16
AXES = ("row", "node")
VMEM_BYTES = 48 * 1024 * 1024
VMEM_MOST = 60 * 1024 * 1024


def norm_last(values, gain):
    average = jnp.mean(values, axis=-1, keepdims=True)
    centred = values - average
    variance = jnp.mean(centred * centred, axis=-1, keepdims=True)
    return centred * lax.rsqrt(variance + EPS) * gain


def sigmoid(values):
    return 0.5 * jnp.tanh(0.5 * values) + 0.5


def dot(a, b, a_dim, b_dim):
    return lax.dot_general(a, b, (((a_dim,), (b_dim,)), ((), ())), preferred_element_type=F32)


def position():
    return lax.axis_index("row") * lax.axis_size("node") + lax.axis_index("node")


def call(kernel, out_shape, args, scratch=(), smem=(), name=None, vmem=VMEM_BYTES):
    specs = [
        pl.BlockSpec(memory_space=pltpu.SMEM if n in smem else pltpu.VMEM) for n in range(len(args))
    ]
    single = not isinstance(out_shape, (list, tuple))
    inside = pl.BlockSpec(memory_space=pltpu.VMEM)
    return pl.pallas_call(
        kernel,
        out_shape=out_shape,
        in_specs=specs,
        out_specs=inside if single else [inside] * len(out_shape),
        scratch_shapes=list(scratch),
        compiler_params=pltpu.CompilerParams(vmem_limit_bytes=vmem),
        name=name,
    )(*args)


class Sizes:
    def __init__(self, rows, crop, devices, channels):
        self.rows, self.crop, self.devices, self.channels = rows, crop, devices, channels
        self.half = rows // 2
        self.group = devices // 2
        self.columns = rows * self.group
        self.whole = crop // LANES
        self.rest = crop % LANES
        self.tiles = rows * crop // LANES
        self.chans = channels // self.group
        self.block = rows * rows
        self.block_tiles = -(-self.block // self.chans)


def edges_kernel(sz, len_ref, x_ref, ln_ref, w_ref, out_ref, *refs):
    near = refs[: sz.group]
    norm_ref, pair_ref = refs[sz.group :]
    length, me = len_ref[0], position()
    first = me * sz.rows
    cd, ch = sz.chans, sz.channels
    mine = me & (sz.group - 1)
    r = lax.broadcasted_iota(jnp.int32, (ch, ch), 0)
    e = lax.broadcasted_iota(jnp.int32, (ch, ch), 1)
    plain = (r == e).astype(BF16)
    slots = (((r // cd) ^ mine) * cd + r % cd == e).astype(BF16)
    picks = (plain, plain, slots, slots)
    weights = [dot(pick, w_ref[p], 1, 1).astype(BF16) for p, pick in enumerate(picks)]
    stacked = jnp.concatenate([weights[p] for p in (0, 2, 1, 3)], axis=0)
    gain = ln_ref[...]
    main = sz.whole * LANES
    for row in range(sz.rows):
        x = x_ref[row].astype(F32)
        for d in range(sz.devices):
            pair_ref[d, row * sz.rows : (row + 1) * sz.rows, :] = x[d * sz.rows : (d + 1) * sz.rows]
        normed = norm_last(x, gain).astype(BF16)
        norm_ref[pl.ds(row * main, main), :] = normed[:main]
        if sz.rest:
            h, q = divmod(row, sz.half)
            norm_ref[pl.ds(sz.rows * main + q * LANES + h * sz.rest, sz.rest), :] = normed[main:]
    for d in range(sz.devices):
        for t in range(sz.block_tiles):
            at = (sz.tiles + t) * LANES
            out_ref[d, :, at : at + LANES] = pair_ref[d, t * cd : (t + 1) * cd, :].astype(BF16)
    lane = lax.broadcasted_iota(jnp.int32, (1, LANES), 1)

    def live(tile):
        if tile < sz.rows * sz.whole:
            row, m = divmod(tile, sz.whole)
            return ((first + row < length) & (m * LANES + lane < length)).astype(F32)
        q = tile - sz.rows * sz.whole
        second = lane >= sz.rest
        row = first + q + jnp.where(second, sz.half, 0)
        k = main + lane - jnp.where(second, sz.rest, 0)
        return ((row < length) & (k < length)).astype(F32)

    step = 2 if sz.tiles % 2 == 0 else 1
    for tile in range(0, sz.tiles, step):
        n = norm_ref[pl.ds(tile * LANES, step * LANES), :]
        mask = jnp.concatenate([live(tile + s) for s in range(step)], axis=1)
        both = dot(stacked, n, 1, 1)
        edge = (sigmoid(both[: 2 * ch]) * (both[2 * ch :] * mask)).astype(BF16)
        to = slice(tile * LANES, (tile + step) * LANES)
        for g in range(sz.group):
            left = edge[g * cd : (g + 1) * cd]
            out_ref[g, :, to] = left
            out_ref[sz.group + g, :, to] = left
            near[g][:, to] = edge[ch + g * cd : ch + (g + 1) * cd]


def unpack(sz, ref, owner, main_ref, rest_ref):
    cd, w = sz.chans, sz.whole
    for tile in range(sz.tiles):
        block = ref[:, tile * LANES : (tile + 1) * LANES].astype(F32)
        if tile < sz.rows * w:
            row, m = divmod(tile, w)
            main_ref[m, pl.ds(pl.multiple_of((owner * sz.rows + row) * cd, 8), cd), :] = block
        else:
            row = owner * sz.rows + tile - sz.rows * w
            rest_ref[pl.ds(pl.multiple_of(row * cd, 8), cd), :] = block
            rest_ref[pl.ds(pl.multiple_of((row + sz.half) * cd, 8), cd), :] = pltpu.roll(
                block, sz.rest, 1
            )


def matrix(sz, c, size, main_ref, rest_ref):
    cd, w = sz.chans, sz.whole
    parts = [main_ref[m, pl.ds(c, size, stride=cd), :].astype(BF16) for m in range(w)]
    if sz.rest:
        parts.append(rest_ref[pl.ds(c, size, stride=cd), :].astype(BF16)[:, : sz.rest])
    return jnp.concatenate(parts, axis=1) if len(parts) > 1 else parts[0]


def right_kernel(sz, *refs):
    near, (out_ref, main_ref, rest_ref) = refs[: sz.group], refs[sz.group :]
    mine = position() & (sz.group - 1)
    for r in range(sz.group):
        unpack(sz, near[r], mine ^ r, main_ref, rest_ref)
    for c in range(sz.chans):
        out_ref[c] = matrix(sz, c, sz.columns, main_ref, rest_ref)


def outer_kernel(
    sz, left_ref, right_ref, out_ref, lmain_ref, lrest_ref, omain_ref, orest_ref
):
    cd, n, w, half = sz.chans, sz.crop, sz.whole, sz.half
    for d in range(sz.devices):
        unpack(sz, left_ref.at[d], jnp.int32(d), lmain_ref, lrest_ref)
    for c in range(cd):
        outer = dot(right_ref[c], matrix(sz, c, n, lmain_ref, lrest_ref), 1, 1)
        for m in range(w):
            omain_ref[m, pl.ds(c, sz.columns, stride=cd), :] = outer[:, m * LANES : (m + 1) * LANES]
        if sz.rest:
            part = outer[:, w * LANES :]
            orest_ref[pl.ds(c, sz.columns, stride=cd), :] = jnp.concatenate([part, part], axis=1)
    low = lax.broadcasted_iota(jnp.int32, (cd, LANES), 1) < sz.rest
    for g in range(sz.group):
        start = g * sz.rows
        for tile in range(sz.tiles):
            if tile < sz.rows * w:
                row, m = divmod(tile, w)
                block = omain_ref[m, pl.ds((start + row) * cd, cd), :]
            else:
                at = start + tile - sz.rows * w
                block = jnp.where(
                    low,
                    orest_ref[pl.ds(at * cd, cd), :],
                    orest_ref[pl.ds((at + half) * cd, cd), :],
                )
            out_ref[g, :, tile * LANES : (tile + 1) * LANES] = block.astype(BF16)


def update_kernel(
    sz, lnp_ref, gate_ref, lnh_ref, tri_ref, lna_ref, biasw_ref, sums_ref, pair_ref,
    first_ref, col_ref, bias_ref, cols_ref, brow_ref,
):
    n, w, half, ch, cd = sz.crop, sz.whole, sz.half, sz.channels, sz.chans
    for s in range(sz.devices):
        for t in range(sz.block_tiles):
            at = (sz.tiles + t) * LANES
            rows = pl.ds(s * sz.block + t * cd, cd)
            cols_ref[rows, :] = pair_ref[s, :, at : at + LANES].astype(F32)
    gain_h = jnp.transpose(jnp.broadcast_to(lnh_ref[...], (ch, ch)))
    tri = tri_ref[...]

    def update(tile):
        block = sums_ref[:, :, tile * LANES : (tile + 1) * LANES].astype(F32).reshape(ch, LANES)
        average = jnp.mean(block, axis=0, keepdims=True)
        centred = block - average
        variance = jnp.mean(centred * centred, axis=0, keepdims=True)
        hidden = (centred * lax.rsqrt(variance + EPS) * gain_h).astype(BF16)
        return dot(hidden, tri, 0, 0)

    rest = [update(sz.rows * w + q) for q in range(half)] if sz.rest else None
    for j in range(sz.rows):
        parts = [update(j * w + m) for m in range(w)]
        if sz.rest:
            h, q = divmod(j, half)
            parts.append(rest[q][h * sz.rest : (h + 1) * sz.rest])
        change = jnp.concatenate(parts, axis=0) if len(parts) > 1 else parts[0]
        x = cols_ref[pl.ds(j, n, stride=sz.rows), :]
        normed = norm_last(x, lnp_ref[...]).astype(BF16)
        gating = sigmoid(dot(normed, gate_ref[...], 1, 0))
        first = (x + gating * change).astype(BF16)
        first_ref[j] = first
        col = norm_last(first.astype(F32), lna_ref[...]).astype(BF16)
        col_ref[j] = col
        heads = biasw_ref.shape[1]
        brow_ref[pl.ds(j * heads, heads), :] = dot(biasw_ref[...], col, 0, 1)
    rows = brow_ref[...]
    part = rows.shape[0] // 2
    one, two = rows[:part], rows[part:]
    message = [one[:, : w * LANES], two[:, : w * LANES]]
    if sz.rest:
        message += [one[:, w * LANES :], two[:, w * LANES :]]
    bias_ref[...] = jnp.concatenate(message, axis=1).astype(BF16)


def project_kernel(sz, col_ref, q_ref, k_ref, v_ref, g_ref, qo_ref, ko_ref, vo_ref, go_ref):
    joined = jnp.concatenate([ref[...] for ref in (q_ref, k_ref, v_ref, g_ref)], axis=1)
    width = q_ref.shape[1]
    for j in range(sz.rows):
        made = dot(col_ref[j], joined, 1, 0)
        qo_ref[j] = made[:, :width].astype(BF16)
        ko_ref[j] = made[:, width : 2 * width].astype(BF16)
        vo_ref[j] = made[:, 2 * width : 3 * width].astype(BF16)
        go_ref[j] = sigmoid(made[:, 3 * width :])


def attend_kernel(
    sz, heads, steps, len_ref, q_ref, k_ref, v_ref, g_ref, first_ref, aout_ref, *refs
):
    bias_refs, (out_ref, rows_ref, bias_ref) = refs[:-3], refs[-3:]
    n, w, ch = sz.crop, sz.whole, sz.channels
    length, me = len_ref[0], position()
    width = q_ref.shape[2]
    hd = width // heads
    per = sz.rows * heads // 2
    for ref, offsets in zip(bias_refs, steps):
        for place, offset in enumerate(offsets):
            block = ref[place].astype(F32) * LOG2E
            for p in range(2):
                at = pl.ds(pl.multiple_of(((me ^ offset) * 2 + p) * per, 8), per)
                for m in range(w):
                    rows_ref[m, at, :] = block[:, (p * w + m) * LANES : (p * w + m + 1) * LANES]
                if sz.rest:
                    tail = block[:, 2 * w * LANES :]
                    rows_ref[w, at, :] = pltpu.roll(tail, sz.rest, 1) if p else tail
    lane = lax.broadcasted_iota(jnp.int32, (1, LANES), 1)
    for m in range(w + (sz.rest > 0)):
        lanes = slice(m * LANES, min((m + 1) * LANES, n))
        dead = jnp.where(m * LANES + lane < length, 0.0, -1e9 * LOG2E).astype(F32)
        for head in range(heads):
            rows = rows_ref[m, pl.ds(head, n, stride=heads), :] + dead
            bias_ref[head, :, lanes] = rows[:, : lanes.stop - lanes.start]
    column = lax.broadcasted_iota(jnp.int32, (1, width), 1)
    head_masks = [(column >= h * hd) & (column < (h + 1) * hd) for h in range(heads)]
    scale = (hd ** (-0.5)) * LOG2E
    ones = jnp.ones((n, width), BF16)

    def score(j, h):
        query = q_ref[j] * head_masks[h].astype(BF16)
        return dot(query, k_ref[j], 1, 1) * scale + bias_ref[h]

    order = [(j, h) for j in range(sz.rows) for h in range(heads)]
    scores = score(*order[0])
    for at, (j, h) in enumerate(order):
        now = scores
        if at + 1 < len(order):
            scores = score(*order[at + 1])
        weights = jnp.exp2(now - jnp.max(now, axis=1, keepdims=True)).astype(BF16)
        if h == 0:
            values = jnp.concatenate([v_ref[j], ones], axis=1)
        mixed = dot(weights, values, 1, 0)
        if h == 0:
            attended, total = mixed[:, :width], mixed[:, width:]
        else:
            attended = jnp.where(head_masks[h], mixed[:, :width], attended)
            total = jnp.where(head_masks[h], mixed[:, width:], total)
        if h == heads - 1:
            gated = (attended / total * g_ref[j]).astype(BF16)
            out_ref[j] = (first_ref[j].astype(F32) + dot(gated, aout_ref[...], 1, 0)).astype(BF16)


def spread(block, devices):
    pieces, offsets = [block[None]], [[0]]
    bit = devices // 2
    while bit:
        held = jnp.concatenate(pieces, axis=0) if len(pieces) > 1 else pieces[0]
        known = [o for part in offsets for o in part]
        pieces.append(lax.ppermute(held, AXES, [(d, d ^ bit) for d in range(devices)]))
        offsets.append([o ^ bit for o in known])
        bit //= 2
    return pieces, offsets


def shards(
    devices,
    pair_rep, length, ln_pair, tri_in, tri_gate, ln_hidden, tri_out, ln_att,
    att_q, att_k, att_v, att_bias, att_gate, att_out,
):
    rows, crop, ch = pair_rep.shape
    heads = att_bias.shape[1]
    sz = Sizes(rows, crop, devices, ch)
    n, cd = crop, sz.chans
    def bound(kernel, *extra):
        def run(*refs):
            return kernel(sz, *extra, *refs)

        return run

    shape = jax.ShapeDtypeStruct
    g, t, bt = sz.group, sz.tiles, sz.block_tiles

    def slab(tiles, *lead):
        return shape((*lead, cd, tiles * LANES), BF16)

    def send(blocks, offset):
        return [
            block
            if not (offset ^ r)
            else lax.ppermute(block, AXES, [(d, d ^ offset ^ r) for d in range(devices)])
            for r, block in enumerate(blocks)
        ]

    left, *others = call(
        bound(edges_kernel),
        [slab(t + bt, devices)] + [slab(t)] * g,
        (length, pair_rep, ln_pair[None], tri_in),
        scratch=[
            pltpu.VMEM((rows * crop, ch), BF16),
            pltpu.VMEM((devices, bt * cd, ch), F32),
        ],
        smem=(0,),
        name="edges",
        vmem=VMEM_MOST,
    )
    left = lax.all_to_all(left, AXES, split_axis=0, concat_axis=0, tiled=True)
    near = send(others, 0)
    rest = sz.rest > 0
    column_rows = sz.columns * cd
    right = call(
        bound(right_kernel),
        shape((cd, sz.columns, n), BF16),
        tuple(near),
        scratch=[
            pltpu.VMEM((sz.whole, column_rows, LANES), F32),
            pltpu.VMEM((column_rows if rest else 8, LANES), F32),
        ],
        name="right",
    )
    outer = call(
        bound(outer_kernel),
        slab(t, g),
        (left, right),
        scratch=[
            pltpu.VMEM((sz.whole, n * cd, LANES), F32),
            pltpu.VMEM((n * cd if rest else 8, LANES), F32),
            pltpu.VMEM((sz.whole, column_rows, LANES), F32),
            pltpu.VMEM((column_rows if rest else 8, LANES), F32),
        ],
        name="outer",
    )
    sums = lax.all_to_all(
        outer, AXES, split_axis=0, concat_axis=0, tiled=True,
        axis_index_groups=[list(range(g)), list(range(g, devices))],
    )
    first, col, bias = call(
        bound(update_kernel),
        [
            shape((rows, n, ch), BF16),
            shape((rows, n, ch), BF16),
            shape((rows * heads // 2, 2 * n), BF16),
        ],
        (
            ln_pair[None], tri_gate, ln_hidden[None], tri_out, ln_att[None], att_bias,
            sums, left,
        ),
        scratch=[
            pltpu.VMEM((devices * sz.block + cd, ch), F32),
            pltpu.VMEM((rows * heads, n), F32),
        ],
        name="update",
    )
    pieces, steps = spread(bias, devices)
    query, key, value, gate = call(
        bound(project_kernel),
        [
            shape((rows, n, att_q.shape[1]), BF16),
            shape((rows, n, att_q.shape[1]), BF16),
            shape((rows, n, att_q.shape[1]), BF16),
            shape((rows, n, att_q.shape[1]), F32),
        ],
        (col, att_q, att_k, att_v, att_gate),
        name="project",
    )
    out = call(
        bound(attend_kernel, heads, steps),
        shape((rows, n, ch), BF16),
        (length, query, key, value, gate, first, att_out, *pieces),
        scratch=[
            pltpu.VMEM((-(-n // LANES), n * heads, LANES), F32),
            pltpu.VMEM((heads, n, n), F32),
        ],
        smem=(0,),
        name="attend",
    )
    return jnp.swapaxes(out, 0, 1)


def solution(mesh):
    devices = mesh.shape["row"] * mesh.shape["node"]

    def body(*args):
        return shards(devices, *args)

    return jax.shard_map(
        body,
        mesh=mesh,
        in_specs=(P(("grp", "row", "node"), None, None), P("grp")) + (P(),) * 12,
        out_specs=P("grp", AXES, None),
        check_vma=False,
    )
```

```python
import jax
import jax.numpy as jnp
from jax import lax
from jax.experimental import pallas as pl
from jax.experimental.pallas import tpu as pltpu
from jax.sharding import PartitionSpec as P

EPS = 1e-05
LANES = 128
LOG2E = 1.4426950408889634
F32 = jnp.float32
BF16 = jnp.bfloat16
AXES = ("row", "node")
VMEM_BYTES = 48 * 1024 * 1024
VMEM_MOST = 60 * 1024 * 1024


def norm_last(values, gain):
    average = jnp.mean(values, axis=-1, keepdims=True)
    centred = values - average
    variance = jnp.mean(centred * centred, axis=-1, keepdims=True)
    return centred * lax.rsqrt(variance + EPS) * gain


def sigmoid(values):
    return 0.5 * jnp.tanh(0.5 * values) + 0.5


def dot(a, b, a_dim, b_dim):
    return lax.dot_general(a, b, (((a_dim,), (b_dim,)), ((), ())), preferred_element_type=F32)


def position():
    return lax.axis_index("row") * lax.axis_size("node") + lax.axis_index("node")


def call(kernel, out_shape, args, scratch=(), smem=(), name=None, vmem=VMEM_BYTES):
    specs = [
        pl.BlockSpec(memory_space=pltpu.SMEM if n in smem else pltpu.VMEM) for n in range(len(args))
    ]
    single = not isinstance(out_shape, (list, tuple))
    inside = pl.BlockSpec(memory_space=pltpu.VMEM)
    return pl.pallas_call(
        kernel,
        out_shape=out_shape,
        in_specs=specs,
        out_specs=inside if single else [inside] * len(out_shape),
        scratch_shapes=list(scratch),
        compiler_params=pltpu.CompilerParams(vmem_limit_bytes=vmem),
        name=name,
    )(*args)


class Sizes:
    def __init__(self, rows, crop, devices, channels):
        self.rows, self.crop, self.devices, self.channels = rows, crop, devices, channels
        self.half = rows // 2
        self.group = devices // 2
        self.columns = rows * self.group
        self.whole = crop // LANES
        self.rest = crop % LANES
        self.tiles = rows * crop // LANES
        self.chans = channels // self.group
        self.block = rows * rows
        self.block_tiles = -(-self.block // self.chans)


def edges_kernel(sz, len_ref, x_ref, ln_ref, w_ref, out_ref, *refs):
    near = refs[: sz.group]
    norm_ref, pair_ref = refs[sz.group :]
    length, me = len_ref[0], position()
    first = me * sz.rows
    cd, ch = sz.chans, sz.channels
    mine = me & (sz.group - 1)
    r = lax.broadcasted_iota(jnp.int32, (ch, ch), 0)
    e = lax.broadcasted_iota(jnp.int32, (ch, ch), 1)
    plain = (r == e).astype(BF16)
    slots = (((r // cd) ^ mine) * cd + r % cd == e).astype(BF16)
    picks = (plain, plain, slots, slots)
    weights = [dot(pick, w_ref[p], 1, 1).astype(BF16) for p, pick in enumerate(picks)]
    stacked = jnp.concatenate([weights[p] for p in (0, 2, 1, 3)], axis=0)
    gain = ln_ref[...]
    main = sz.whole * LANES
    for row in range(sz.rows):
        x = x_ref[row].astype(F32)
        for d in range(sz.devices):
            pair_ref[d, row * sz.rows : (row + 1) * sz.rows, :] = x[d * sz.rows : (d + 1) * sz.rows]
        normed = norm_last(x, gain).astype(BF16)
        norm_ref[pl.ds(row * main, main), :] = normed[:main]
        if sz.rest:
            h, q = divmod(row, sz.half)
            norm_ref[pl.ds(sz.rows * main + q * LANES + h * sz.rest, sz.rest), :] = normed[main:]
    for d in range(sz.devices):
        for t in range(sz.block_tiles):
            at = (sz.tiles + t) * LANES
            out_ref[d, :, at : at + LANES] = pair_ref[d, t * cd : (t + 1) * cd, :].astype(BF16)
    lane = lax.broadcasted_iota(jnp.int32, (1, LANES), 1)

    def live(tile):
        if tile < sz.rows * sz.whole:
            row, m = divmod(tile, sz.whole)
            return ((first + row < length) & (m * LANES + lane < length)).astype(F32)
        q = tile - sz.rows * sz.whole
        second = lane >= sz.rest
        row = first + q + jnp.where(second, sz.half, 0)
        k = main + lane - jnp.where(second, sz.rest, 0)
        return ((row < length) & (k < length)).astype(F32)

    step = 2 if sz.tiles % 2 == 0 else 1
    for tile in range(0, sz.tiles, step):
        n = norm_ref[pl.ds(tile * LANES, step * LANES), :]
        mask = jnp.concatenate([live(tile + s) for s in range(step)], axis=1)
        both = dot(stacked, n, 1, 1)
        edge = (sigmoid(both[: 2 * ch]) * (both[2 * ch :] * mask)).astype(BF16)
        to = slice(tile * LANES, (tile + step) * LANES)
        for g in range(sz.group):
            left = edge[g * cd : (g + 1) * cd]
            out_ref[g, :, to] = left
            out_ref[sz.group + g, :, to] = left
            near[g][:, to] = edge[ch + g * cd : ch + (g + 1) * cd]


def unpack(sz, ref, owner, main_ref, rest_ref):
    cd, w = sz.chans, sz.whole
    for tile in range(sz.tiles):
        block = ref[:, tile * LANES : (tile + 1) * LANES].astype(F32)
        if tile < sz.rows * w:
            row, m = divmod(tile, w)
            main_ref[m, pl.ds(pl.multiple_of((owner * sz.rows + row) * cd, 8), cd), :] = block
        else:
            row = owner * sz.rows + tile - sz.rows * w
            rest_ref[pl.ds(pl.multiple_of(row * cd, 8), cd), :] = block
            rest_ref[pl.ds(pl.multiple_of((row + sz.half) * cd, 8), cd), :] = pltpu.roll(
                block, sz.rest, 1
            )


def matrix(sz, c, size, main_ref, rest_ref):
    cd, w = sz.chans, sz.whole
    parts = [main_ref[m, pl.ds(c, size, stride=cd), :].astype(BF16) for m in range(w)]
    if sz.rest:
        parts.append(rest_ref[pl.ds(c, size, stride=cd), :].astype(BF16)[:, : sz.rest])
    return jnp.concatenate(parts, axis=1) if len(parts) > 1 else parts[0]


def right_kernel(sz, *refs):
    near, (out_ref, main_ref, rest_ref) = refs[: sz.group], refs[sz.group :]
    mine = position() & (sz.group - 1)
    for r in range(sz.group):
        unpack(sz, near[r], mine ^ r, main_ref, rest_ref)
    for c in range(sz.chans):
        out_ref[c] = matrix(sz, c, sz.columns, main_ref, rest_ref)


def outer_kernel(
    sz, left_ref, right_ref, out_ref, lmain_ref, lrest_ref, omain_ref, orest_ref
):
    cd, n, w, half = sz.chans, sz.crop, sz.whole, sz.half
    for d in range(sz.devices):
        unpack(sz, left_ref.at[d], jnp.int32(d), lmain_ref, lrest_ref)
    for c in range(cd):
        outer = dot(right_ref[c], matrix(sz, c, n, lmain_ref, lrest_ref), 1, 1)
        for m in range(w):
            omain_ref[m, pl.ds(c, sz.columns, stride=cd), :] = outer[:, m * LANES : (m + 1) * LANES]
        if sz.rest:
            part = outer[:, w * LANES :]
            orest_ref[pl.ds(c, sz.columns, stride=cd), :] = jnp.concatenate([part, part], axis=1)
    low = lax.broadcasted_iota(jnp.int32, (cd, LANES), 1) < sz.rest
    for g in range(sz.group):
        start = g * sz.rows
        for tile in range(sz.tiles):
            if tile < sz.rows * w:
                row, m = divmod(tile, w)
                block = omain_ref[m, pl.ds((start + row) * cd, cd), :]
            else:
                at = start + tile - sz.rows * w
                block = jnp.where(
                    low,
                    orest_ref[pl.ds(at * cd, cd), :],
                    orest_ref[pl.ds((at + half) * cd, cd), :],
                )
            out_ref[g, :, tile * LANES : (tile + 1) * LANES] = block.astype(BF16)


def columns_kernel(sz, pair_ref, lnp_ref, gate_ref, x_ref, gating_ref, cols_ref):
    cd = sz.chans
    for s in range(sz.devices):
        for t in range(sz.block_tiles):
            at = (sz.tiles + t) * LANES
            rows = pl.ds(s * sz.block + t * cd, cd)
            cols_ref[rows, :] = pair_ref[s, :, at : at + LANES].astype(F32)
    for j in range(sz.rows):
        x = cols_ref[pl.ds(j, sz.crop, stride=sz.rows), :]
        x_ref[j] = x.astype(BF16)
        normed = norm_last(x, lnp_ref[...]).astype(BF16)
        gating_ref[j] = sigmoid(dot(normed, gate_ref[...], 1, 0)).astype(BF16)


def update_kernel(
    sz, x_ref, gating_ref, lnh_ref, tri_ref, lna_ref, biasw_ref, sums_ref,
    first_ref, col_ref, bias_ref, brow_ref,
):
    n, w, half, ch = sz.crop, sz.whole, sz.half, sz.channels
    gain_h = jnp.transpose(jnp.broadcast_to(lnh_ref[...], (ch, ch)))
    tri = tri_ref[...]

    def update(tile):
        block = sums_ref[:, :, tile * LANES : (tile + 1) * LANES].astype(F32).reshape(ch, LANES)
        average = jnp.mean(block, axis=0, keepdims=True)
        centred = block - average
        variance = jnp.mean(centred * centred, axis=0, keepdims=True)
        hidden = (centred * lax.rsqrt(variance + EPS) * gain_h).astype(BF16)
        return dot(hidden, tri, 0, 0)

    rest = [update(sz.rows * w + q) for q in range(half)] if sz.rest else None
    for j in range(sz.rows):
        parts = [update(j * w + m) for m in range(w)]
        if sz.rest:
            h, q = divmod(j, half)
            parts.append(rest[q][h * sz.rest : (h + 1) * sz.rest])
        change = jnp.concatenate(parts, axis=0) if len(parts) > 1 else parts[0]
        first = (x_ref[j].astype(F32) + gating_ref[j].astype(F32) * change).astype(BF16)
        first_ref[j] = first
        col = norm_last(first.astype(F32), lna_ref[...]).astype(BF16)
        col_ref[j] = col
        heads = biasw_ref.shape[1]
        brow_ref[pl.ds(j * heads, heads), :] = dot(biasw_ref[...], col, 0, 1)
    rows = brow_ref[...]
    part = rows.shape[0] // 2
    one, two = rows[:part], rows[part:]
    message = [one[:, : w * LANES], two[:, : w * LANES]]
    if sz.rest:
        message += [one[:, w * LANES :], two[:, w * LANES :]]
    bias_ref[...] = jnp.concatenate(message, axis=1).astype(BF16)


def project_kernel(sz, col_ref, q_ref, k_ref, v_ref, g_ref, qo_ref, ko_ref, vo_ref, go_ref):
    joined = jnp.concatenate([ref[...] for ref in (q_ref, k_ref, v_ref, g_ref)], axis=1)
    width = q_ref.shape[1]
    for j in range(sz.rows):
        made = dot(col_ref[j], joined, 1, 0)
        qo_ref[j] = made[:, :width].astype(BF16)
        ko_ref[j] = made[:, width : 2 * width].astype(BF16)
        vo_ref[j] = made[:, 2 * width : 3 * width].astype(BF16)
        go_ref[j] = sigmoid(made[:, 3 * width :])


def attend_kernel(
    sz, heads, steps, len_ref, q_ref, k_ref, v_ref, g_ref, first_ref, aout_ref, *refs
):
    bias_refs, (out_ref, rows_ref, bias_ref) = refs[:-3], refs[-3:]
    n, w, ch = sz.crop, sz.whole, sz.channels
    length, me = len_ref[0], position()
    width = q_ref.shape[2]
    hd = width // heads
    per = sz.rows * heads // 2
    for ref, offsets in zip(bias_refs, steps):
        for place, offset in enumerate(offsets):
            block = ref[place].astype(F32) * LOG2E
            for p in range(2):
                at = pl.ds(pl.multiple_of(((me ^ offset) * 2 + p) * per, 8), per)
                for m in range(w):
                    rows_ref[m, at, :] = block[:, (p * w + m) * LANES : (p * w + m + 1) * LANES]
                if sz.rest:
                    tail = block[:, 2 * w * LANES :]
                    rows_ref[w, at, :] = pltpu.roll(tail, sz.rest, 1) if p else tail
    lane = lax.broadcasted_iota(jnp.int32, (1, LANES), 1)
    for m in range(w + (sz.rest > 0)):
        lanes = slice(m * LANES, min((m + 1) * LANES, n))
        dead = jnp.where(m * LANES + lane < length, 0.0, -1e9 * LOG2E).astype(F32)
        for head in range(heads):
            rows = rows_ref[m, pl.ds(head, n, stride=heads), :] + dead
            bias_ref[head, :, lanes] = rows[:, : lanes.stop - lanes.start]
    column = lax.broadcasted_iota(jnp.int32, (1, width), 1)
    head_masks = [(column >= h * hd) & (column < (h + 1) * hd) for h in range(heads)]
    scale = (hd ** (-0.5)) * LOG2E
    ones = jnp.ones((n, width), BF16)

    def score(j):
        query = [q_ref[j] * head_masks[h].astype(BF16) for h in range(heads)]
        return dot(jnp.concatenate(query, axis=0), k_ref[j], 1, 1)

    scores = score(0)
    for j in range(sz.rows):
        now = scores
        if j + 1 < sz.rows:
            scores = score(j + 1)
        weights = []
        for h in range(heads):
            part = now[h * n : (h + 1) * n] * scale + bias_ref[h]
            weights.append(jnp.exp2(part - jnp.max(part, axis=1, keepdims=True)).astype(BF16))
        values = jnp.concatenate([v_ref[j], ones], axis=1)
        mixed = dot(jnp.concatenate(weights, axis=0), values, 1, 0)
        attended, total = mixed[:n, :width], mixed[:n, width:]
        for h in range(1, heads):
            rows = slice(h * n, (h + 1) * n)
            attended = jnp.where(head_masks[h], mixed[rows, :width], attended)
            total = jnp.where(head_masks[h], mixed[rows, width:], total)
        gated = (attended / total * g_ref[j]).astype(BF16)
        out_ref[j] = (first_ref[j].astype(F32) + dot(gated, aout_ref[...], 1, 0)).astype(BF16)


def spread(block, devices):
    pieces, offsets = [block[None]], [[0]]
    bit = devices // 2
    while bit:
        held = jnp.concatenate(pieces, axis=0) if len(pieces) > 1 else pieces[0]
        known = [o for part in offsets for o in part]
        pieces.append(lax.ppermute(held, AXES, [(d, d ^ bit) for d in range(devices)]))
        offsets.append([o ^ bit for o in known])
        bit //= 2
    return pieces, offsets


def shards(
    devices,
    pair_rep, length, ln_pair, tri_in, tri_gate, ln_hidden, tri_out, ln_att,
    att_q, att_k, att_v, att_bias, att_gate, att_out,
):
    rows, crop, ch = pair_rep.shape
    heads = att_bias.shape[1]
    sz = Sizes(rows, crop, devices, ch)
    n, cd = crop, sz.chans
    def bound(kernel, *extra):
        def run(*refs):
            return kernel(sz, *extra, *refs)

        return run

    shape = jax.ShapeDtypeStruct
    g, t, bt = sz.group, sz.tiles, sz.block_tiles

    def slab(tiles, *lead):
        return shape((*lead, cd, tiles * LANES), BF16)

    def send(blocks, offset):
        return [
            block
            if not (offset ^ r)
            else lax.ppermute(block, AXES, [(d, d ^ offset ^ r) for d in range(devices)])
            for r, block in enumerate(blocks)
        ]

    left, *others = call(
        bound(edges_kernel),
        [slab(t + bt, devices)] + [slab(t)] * g,
        (length, pair_rep, ln_pair[None], tri_in),
        scratch=[
            pltpu.VMEM((rows * crop, ch), BF16),
            pltpu.VMEM((devices, bt * cd, ch), F32),
        ],
        smem=(0,),
        name="edges",
        vmem=VMEM_MOST,
    )
    left = lax.all_to_all(left, AXES, split_axis=0, concat_axis=0, tiled=True)
    near = send(others, 0)
    rest = sz.rest > 0
    column_rows = sz.columns * cd
    right = call(
        bound(right_kernel),
        shape((cd, sz.columns, n), BF16),
        tuple(near),
        scratch=[
            pltpu.VMEM((sz.whole, column_rows, LANES), F32),
            pltpu.VMEM((column_rows if rest else 8, LANES), F32),
        ],
        name="right",
    )
    outer = call(
        bound(outer_kernel),
        slab(t, g),
        (left, right),
        scratch=[
            pltpu.VMEM((sz.whole, n * cd, LANES), F32),
            pltpu.VMEM((n * cd if rest else 8, LANES), F32),
            pltpu.VMEM((sz.whole, column_rows, LANES), F32),
            pltpu.VMEM((column_rows if rest else 8, LANES), F32),
        ],
        name="outer",
    )
    sums = lax.all_to_all(
        outer, AXES, split_axis=0, concat_axis=0, tiled=True,
        axis_index_groups=[list(range(g)), list(range(g, devices))],
    )
    columns, gating = call(
        bound(columns_kernel),
        [shape((rows, n, ch), BF16), shape((rows, n, ch), BF16)],
        (left, ln_pair[None], tri_gate),
        scratch=[pltpu.VMEM((devices * sz.block + cd, ch), F32)],
        name="columns",
    )
    first, col, bias = call(
        bound(update_kernel),
        [
            shape((rows, n, ch), BF16),
            shape((rows, n, ch), BF16),
            shape((rows * heads // 2, 2 * n), BF16),
        ],
        (columns, gating, ln_hidden[None], tri_out, ln_att[None], att_bias, sums),
        scratch=[pltpu.VMEM((rows * heads, n), F32)],
        name="update",
    )
    pieces, steps = spread(bias, devices)
    query, key, value, gate = call(
        bound(project_kernel),
        [
            shape((rows, n, att_q.shape[1]), BF16),
            shape((rows, n, att_q.shape[1]), BF16),
            shape((rows, n, att_q.shape[1]), BF16),
            shape((rows, n, att_q.shape[1]), F32),
        ],
        (col, att_q, att_k, att_v, att_gate),
        name="project",
    )
    out = call(
        bound(attend_kernel, heads, steps),
        shape((rows, n, ch), BF16),
        (length, query, key, value, gate, first, att_out, *pieces),
        scratch=[
            pltpu.VMEM((-(-n // LANES), n * heads, LANES), F32),
            pltpu.VMEM((heads, n, n), F32),
        ],
        smem=(0,),
        name="attend",
    )
    return jnp.swapaxes(out, 0, 1)


def solution(mesh):
    devices = mesh.shape["row"] * mesh.shape["node"]

    def body(*args):
        return shards(devices, *args)

    return jax.shard_map(
        body,
        mesh=mesh,
        in_specs=(P(("grp", "row", "node"), None, None), P("grp")) + (P(),) * 12,
        out_specs=P("grp", AXES, None),
        check_vma=False,
    )
```

```python
import jax
import jax.numpy as jnp
from jax import lax
from jax.experimental import pallas as pl
from jax.experimental.pallas import tpu as pltpu
from jax.sharding import PartitionSpec as P

EPS = 1e-05
LANES = 128
LOG2E = 1.4426950408889634
F32 = jnp.float32
BF16 = jnp.bfloat16
AXES = ("row", "node")
VMEM_BYTES = 48 * 1024 * 1024
VMEM_MOST = 60 * 1024 * 1024


def norm_last(values, gain):
    average = jnp.mean(values, axis=-1, keepdims=True)
    centred = values - average
    variance = jnp.mean(centred * centred, axis=-1, keepdims=True)
    return centred * lax.rsqrt(variance + EPS) * gain


def sigmoid(values):
    return 0.5 * jnp.tanh(0.5 * values) + 0.5


def dot(a, b, a_dim, b_dim):
    return lax.dot_general(a, b, (((a_dim,), (b_dim,)), ((), ())), preferred_element_type=F32)


def position():
    return lax.axis_index("row") * lax.axis_size("node") + lax.axis_index("node")


def call(kernel, out_shape, args, scratch=(), smem=(), name=None, vmem=VMEM_BYTES):
    specs = [
        pl.BlockSpec(memory_space=pltpu.SMEM if n in smem else pltpu.VMEM) for n in range(len(args))
    ]
    single = not isinstance(out_shape, (list, tuple))
    inside = pl.BlockSpec(memory_space=pltpu.VMEM)
    return pl.pallas_call(
        kernel,
        out_shape=out_shape,
        in_specs=specs,
        out_specs=inside if single else [inside] * len(out_shape),
        scratch_shapes=list(scratch),
        compiler_params=pltpu.CompilerParams(vmem_limit_bytes=vmem),
        name=name,
    )(*args)


class Sizes:
    def __init__(self, rows, crop, devices, channels):
        self.rows, self.crop, self.devices, self.channels = rows, crop, devices, channels
        self.half = rows // 2
        self.group = devices // 2
        self.columns = rows * self.group
        self.whole = crop // LANES
        self.rest = crop % LANES
        self.tiles = rows * crop // LANES
        self.chans = channels // self.group
        self.block = rows * rows
        self.block_tiles = -(-self.block // self.chans)


def edges_kernel(sz, len_ref, x_ref, ln_ref, w_ref, out_ref, *refs):
    near = refs[: sz.group]
    norm_ref, pair_ref = refs[sz.group :]
    length, me = len_ref[0], position()
    first = me * sz.rows
    cd, ch = sz.chans, sz.channels
    mine = me & (sz.group - 1)
    r = lax.broadcasted_iota(jnp.int32, (ch, ch), 0)
    e = lax.broadcasted_iota(jnp.int32, (ch, ch), 1)
    plain = (r == e).astype(BF16)
    slots = (((r // cd) ^ mine) * cd + r % cd == e).astype(BF16)
    picks = (plain, plain, slots, slots)
    weights = [dot(pick, w_ref[p], 1, 1).astype(BF16) for p, pick in enumerate(picks)]
    stacked = jnp.concatenate([weights[p] for p in (0, 2, 1, 3)], axis=0)
    gain = ln_ref[...]
    main = sz.whole * LANES
    for row in range(sz.rows):
        x = x_ref[row].astype(F32)
        for d in range(sz.devices):
            pair_ref[d, row * sz.rows : (row + 1) * sz.rows, :] = x[d * sz.rows : (d + 1) * sz.rows]
        normed = norm_last(x, gain).astype(BF16)
        norm_ref[pl.ds(row * main, main), :] = normed[:main]
        if sz.rest:
            h, q = divmod(row, sz.half)
            norm_ref[pl.ds(sz.rows * main + q * LANES + h * sz.rest, sz.rest), :] = normed[main:]
    for d in range(sz.devices):
        for t in range(sz.block_tiles):
            at = (sz.tiles + t) * LANES
            out_ref[d, :, at : at + LANES] = pair_ref[d, t * cd : (t + 1) * cd, :].astype(BF16)
    lane = lax.broadcasted_iota(jnp.int32, (1, LANES), 1)

    def live(tile):
        if tile < sz.rows * sz.whole:
            row, m = divmod(tile, sz.whole)
            return ((first + row < length) & (m * LANES + lane < length)).astype(F32)
        q = tile - sz.rows * sz.whole
        second = lane >= sz.rest
        row = first + q + jnp.where(second, sz.half, 0)
        k = main + lane - jnp.where(second, sz.rest, 0)
        return ((row < length) & (k < length)).astype(F32)

    step = 2 if sz.tiles % 2 == 0 else 1
    for tile in range(0, sz.tiles, step):
        n = norm_ref[pl.ds(tile * LANES, step * LANES), :]
        mask = jnp.concatenate([live(tile + s) for s in range(step)], axis=1)
        both = dot(stacked, n, 1, 1)
        edge = (sigmoid(both[: 2 * ch]) * (both[2 * ch :] * mask)).astype(BF16)
        to = slice(tile * LANES, (tile + step) * LANES)
        for g in range(sz.group):
            left = edge[g * cd : (g + 1) * cd]
            out_ref[g, :, to] = left
            out_ref[sz.group + g, :, to] = left
            near[g][:, to] = edge[ch + g * cd : ch + (g + 1) * cd]


def unpack(sz, ref, owner, main_ref, rest_ref):
    cd, w = sz.chans, sz.whole
    for tile in range(sz.tiles):
        block = ref[:, tile * LANES : (tile + 1) * LANES].astype(F32)
        if tile < sz.rows * w:
            row, m = divmod(tile, w)
            main_ref[m, pl.ds(pl.multiple_of((owner * sz.rows + row) * cd, 8), cd), :] = block
        else:
            row = owner * sz.rows + tile - sz.rows * w
            rest_ref[pl.ds(pl.multiple_of(row * cd, 8), cd), :] = block
            rest_ref[pl.ds(pl.multiple_of((row + sz.half) * cd, 8), cd), :] = pltpu.roll(
                block, sz.rest, 1
            )


def matrix(sz, c, size, main_ref, rest_ref):
    cd, w = sz.chans, sz.whole
    parts = [main_ref[m, pl.ds(c, size, stride=cd), :].astype(BF16) for m in range(w)]
    if sz.rest:
        parts.append(rest_ref[pl.ds(c, size, stride=cd), :].astype(BF16)[:, : sz.rest])
    return jnp.concatenate(parts, axis=1) if len(parts) > 1 else parts[0]


def right_kernel(sz, *refs):
    near, (out_ref, main_ref, rest_ref) = refs[: sz.group], refs[sz.group :]
    mine = position() & (sz.group - 1)
    for r in range(sz.group):
        unpack(sz, near[r], mine ^ r, main_ref, rest_ref)
    for c in range(sz.chans):
        out_ref[c] = matrix(sz, c, sz.columns, main_ref, rest_ref)


def outer_kernel(
    sz, left_ref, right_ref, out_ref, lmain_ref, lrest_ref, omain_ref, orest_ref
):
    cd, n, w, half = sz.chans, sz.crop, sz.whole, sz.half
    for d in range(sz.devices):
        unpack(sz, left_ref.at[d], jnp.int32(d), lmain_ref, lrest_ref)
    for c in range(cd):
        outer = dot(right_ref[c], matrix(sz, c, n, lmain_ref, lrest_ref), 1, 1)
        for m in range(w):
            omain_ref[m, pl.ds(c, sz.columns, stride=cd), :] = outer[:, m * LANES : (m + 1) * LANES]
        if sz.rest:
            part = outer[:, w * LANES :]
            orest_ref[pl.ds(c, sz.columns, stride=cd), :] = jnp.concatenate([part, part], axis=1)
    low = lax.broadcasted_iota(jnp.int32, (cd, LANES), 1) < sz.rest
    for g in range(sz.group):
        start = g * sz.rows
        for tile in range(sz.tiles):
            if tile < sz.rows * w:
                row, m = divmod(tile, w)
                block = omain_ref[m, pl.ds((start + row) * cd, cd), :]
            else:
                at = start + tile - sz.rows * w
                block = jnp.where(
                    low,
                    orest_ref[pl.ds(at * cd, cd), :],
                    orest_ref[pl.ds((at + half) * cd, cd), :],
                )
            out_ref[g, :, tile * LANES : (tile + 1) * LANES] = block.astype(BF16)


def update_kernel(
    sz, lnp_ref, gate_ref, lnh_ref, tri_ref, lna_ref, biasw_ref, sums_ref, pair_ref,
    first_ref, col_ref, bias_ref, cols_ref, brow_ref,
):
    n, w, half, ch, cd = sz.crop, sz.whole, sz.half, sz.channels, sz.chans
    for s in range(sz.devices):
        for t in range(sz.block_tiles):
            at = (sz.tiles + t) * LANES
            rows = pl.ds(s * sz.block + t * cd, cd)
            cols_ref[rows, :] = pair_ref[s, :, at : at + LANES].astype(F32)
    gain_h = jnp.transpose(jnp.broadcast_to(lnh_ref[...], (ch, ch)))
    tri = tri_ref[...]

    def update(tile):
        block = sums_ref[:, :, tile * LANES : (tile + 1) * LANES].astype(F32).reshape(ch, LANES)
        average = jnp.mean(block, axis=0, keepdims=True)
        centred = block - average
        variance = jnp.mean(centred * centred, axis=0, keepdims=True)
        hidden = (centred * lax.rsqrt(variance + EPS) * gain_h).astype(BF16)
        return dot(hidden, tri, 0, 0)

    rest = [update(sz.rows * w + q) for q in range(half)] if sz.rest else None
    for j in range(sz.rows):
        parts = [update(j * w + m) for m in range(w)]
        if sz.rest:
            h, q = divmod(j, half)
            parts.append(rest[q][h * sz.rest : (h + 1) * sz.rest])
        change = jnp.concatenate(parts, axis=0) if len(parts) > 1 else parts[0]
        x = cols_ref[pl.ds(j, n, stride=sz.rows), :]
        normed = norm_last(x, lnp_ref[...]).astype(BF16)
        gating = sigmoid(dot(normed, gate_ref[...], 1, 0))
        first = (x + gating * change).astype(BF16)
        first_ref[j] = first
        col = norm_last(first.astype(F32), lna_ref[...]).astype(BF16)
        col_ref[j] = col
        heads = biasw_ref.shape[1]
        brow_ref[pl.ds(j * heads, heads), :] = dot(biasw_ref[...], col, 0, 1)
    rows = brow_ref[...]
    part = rows.shape[0] // 2
    one, two = rows[:part], rows[part:]
    message = [one[:, : w * LANES], two[:, : w * LANES]]
    if sz.rest:
        message += [one[:, w * LANES :], two[:, w * LANES :]]
    bias_ref[...] = jnp.concatenate(message, axis=1).astype(BF16)


def project_kernel(sz, col_ref, q_ref, k_ref, v_ref, g_ref, qo_ref, ko_ref, vo_ref, go_ref):
    joined = jnp.concatenate([ref[...] for ref in (q_ref, k_ref, v_ref, g_ref)], axis=1)
    width = q_ref.shape[1]
    for j in range(sz.rows):
        made = dot(col_ref[j], joined, 1, 0)
        qo_ref[j] = made[:, :width].astype(BF16)
        ko_ref[j] = made[:, width : 2 * width].astype(BF16)
        vo_ref[j] = made[:, 2 * width : 3 * width].astype(BF16)
        go_ref[j] = sigmoid(made[:, 3 * width :])


def attend_kernel(
    sz, heads, len_ref, q_ref, k_ref, v_ref, g_ref, first_ref, aout_ref, *refs
):
    bias_refs, (out_ref, rows_ref, bias_ref) = refs[:-3], refs[-3:]
    n, w, ch = sz.crop, sz.whole, sz.channels
    length, core = len_ref[0], lax.axis_index("node")
    width = q_ref.shape[2]
    hd = width // heads
    per = sz.rows * heads // 2
    for other, ref in enumerate(bias_refs):
        for chip in range(ref.shape[0]):
            block = ref[chip].astype(F32) * LOG2E
            owner = 2 * chip + (core ^ other)
            for p in range(2):
                at = pl.ds(pl.multiple_of((owner * 2 + p) * per, 8), per)
                for m in range(w):
                    rows_ref[m, at, :] = block[:, (p * w + m) * LANES : (p * w + m + 1) * LANES]
                if sz.rest:
                    tail = block[:, 2 * w * LANES :]
                    rows_ref[w, at, :] = pltpu.roll(tail, sz.rest, 1) if p else tail
    lane = lax.broadcasted_iota(jnp.int32, (1, LANES), 1)
    for m in range(w + (sz.rest > 0)):
        lanes = slice(m * LANES, min((m + 1) * LANES, n))
        dead = jnp.where(m * LANES + lane < length, 0.0, -1e9 * LOG2E).astype(F32)
        for head in range(heads):
            rows = rows_ref[m, pl.ds(head, n, stride=heads), :] + dead
            bias_ref[head, :, lanes] = rows[:, : lanes.stop - lanes.start]
    column = lax.broadcasted_iota(jnp.int32, (1, width), 1)
    head_masks = [(column >= h * hd) & (column < (h + 1) * hd) for h in range(heads)]
    scale = (hd ** (-0.5)) * LOG2E
    ones = jnp.ones((n, width), BF16)

    def score(j):
        query = [q_ref[j] * head_masks[h].astype(BF16) for h in range(heads)]
        return dot(jnp.concatenate(query, axis=0), k_ref[j], 1, 1)

    scores = score(0)
    for j in range(sz.rows):
        now = scores
        if j + 1 < sz.rows:
            scores = score(j + 1)
        weights = []
        for h in range(heads):
            part = now[h * n : (h + 1) * n] * scale + bias_ref[h]
            weights.append(jnp.exp2(part - jnp.max(part, axis=1, keepdims=True)).astype(BF16))
        values = jnp.concatenate([v_ref[j], ones], axis=1)
        mixed = dot(jnp.concatenate(weights, axis=0), values, 1, 0)
        attended, total = mixed[:n, :width], mixed[:n, width:]
        for h in range(1, heads):
            rows = slice(h * n, (h + 1) * n)
            attended = jnp.where(head_masks[h], mixed[rows, :width], attended)
            total = jnp.where(head_masks[h], mixed[rows, width:], total)
        gated = (attended / total * g_ref[j]).astype(BF16)
        out_ref[j] = (first_ref[j].astype(F32) + dot(gated, aout_ref[...], 1, 0)).astype(BF16)


def shards(
    devices,
    pair_rep, length, ln_pair, tri_in, tri_gate, ln_hidden, tri_out, ln_att,
    att_q, att_k, att_v, att_bias, att_gate, att_out,
):
    rows, crop, ch = pair_rep.shape
    heads = att_bias.shape[1]
    sz = Sizes(rows, crop, devices, ch)
    n, cd = crop, sz.chans
    def bound(kernel, *extra):
        def run(*refs):
            return kernel(sz, *extra, *refs)

        return run

    shape = jax.ShapeDtypeStruct
    g, t, bt = sz.group, sz.tiles, sz.block_tiles

    def slab(tiles, *lead):
        return shape((*lead, cd, tiles * LANES), BF16)

    def send(blocks, offset):
        return [
            block
            if not (offset ^ r)
            else lax.ppermute(block, AXES, [(d, d ^ offset ^ r) for d in range(devices)])
            for r, block in enumerate(blocks)
        ]

    left, *others = call(
        bound(edges_kernel),
        [slab(t + bt, devices)] + [slab(t)] * g,
        (length, pair_rep, ln_pair[None], tri_in),
        scratch=[
            pltpu.VMEM((rows * crop, ch), BF16),
            pltpu.VMEM((devices, bt * cd, ch), F32),
        ],
        smem=(0,),
        name="edges",
        vmem=VMEM_MOST,
    )
    left = lax.all_to_all(left, AXES, split_axis=0, concat_axis=0, tiled=True)
    near = send(others, 0)
    rest = sz.rest > 0
    column_rows = sz.columns * cd
    right = call(
        bound(right_kernel),
        shape((cd, sz.columns, n), BF16),
        tuple(near),
        scratch=[
            pltpu.VMEM((sz.whole, column_rows, LANES), F32),
            pltpu.VMEM((column_rows if rest else 8, LANES), F32),
        ],
        name="right",
    )
    outer = call(
        bound(outer_kernel),
        slab(t, g),
        (left, right),
        scratch=[
            pltpu.VMEM((sz.whole, n * cd, LANES), F32),
            pltpu.VMEM((n * cd if rest else 8, LANES), F32),
            pltpu.VMEM((sz.whole, column_rows, LANES), F32),
            pltpu.VMEM((column_rows if rest else 8, LANES), F32),
        ],
        name="outer",
    )
    sums = lax.all_to_all(
        outer, AXES, split_axis=0, concat_axis=0, tiled=True,
        axis_index_groups=[list(range(g)), list(range(g, devices))],
    )
    first, col, bias = call(
        bound(update_kernel),
        [
            shape((rows, n, ch), BF16),
            shape((rows, n, ch), BF16),
            shape((rows * heads // 2, 2 * n), BF16),
        ],
        (
            ln_pair[None], tri_gate, ln_hidden[None], tri_out, ln_att[None], att_bias,
            sums, left,
        ),
        scratch=[
            pltpu.VMEM((devices * sz.block + cd, ch), F32),
            pltpu.VMEM((rows * heads, n), F32),
        ],
        name="update",
    )
    same = lax.all_gather(bias, "row", axis=0, tiled=False)
    other = lax.ppermute(same, "node", [(0, 1), (1, 0)])
    query, key, value, gate = call(
        bound(project_kernel),
        [
            shape((rows, n, att_q.shape[1]), BF16),
            shape((rows, n, att_q.shape[1]), BF16),
            shape((rows, n, att_q.shape[1]), BF16),
            shape((rows, n, att_q.shape[1]), F32),
        ],
        (col, att_q, att_k, att_v, att_gate),
        name="project",
    )
    out = call(
        bound(attend_kernel, heads),
        shape((rows, n, ch), BF16),
        (length, query, key, value, gate, first, att_out, same, other),
        scratch=[
            pltpu.VMEM((-(-n // LANES), n * heads, LANES), F32),
            pltpu.VMEM((heads, n, n), F32),
        ],
        smem=(0,),
        name="attend",
    )
    return jnp.swapaxes(out, 0, 1)


def solution(mesh):
    devices = mesh.shape["row"] * mesh.shape["node"]

    def body(*args):
        return shards(devices, *args)

    return jax.shard_map(
        body,
        mesh=mesh,
        in_specs=(P(("grp", "row", "node"), None, None), P("grp")) + (P(),) * 12,
        out_specs=P("grp", AXES, None),
        check_vma=False,
    )
```

```python
import jax
import jax.numpy as jnp
from jax import lax
from jax.experimental import pallas as pl
from jax.experimental.pallas import tpu as pltpu
from jax.sharding import PartitionSpec as P

EPS = 1e-05
LANES = 128
LOG2E = 1.4426950408889634
F32 = jnp.float32
BF16 = jnp.bfloat16
AXES = ("row", "node")
VMEM_BYTES = 48 * 1024 * 1024
VMEM_MOST = 60 * 1024 * 1024


def norm_last(values, gain):
    average = jnp.mean(values, axis=-1, keepdims=True)
    centred = values - average
    variance = jnp.mean(centred * centred, axis=-1, keepdims=True)
    return centred * lax.rsqrt(variance + EPS) * gain


def sigmoid(values):
    return 0.5 * jnp.tanh(0.5 * values) + 0.5


def dot(a, b, a_dim, b_dim):
    return lax.dot_general(a, b, (((a_dim,), (b_dim,)), ((), ())), preferred_element_type=F32)


def position():
    return lax.axis_index("row") * lax.axis_size("node") + lax.axis_index("node")


def call(kernel, out_shape, args, scratch=(), smem=(), name=None, vmem=VMEM_BYTES):
    specs = [
        pl.BlockSpec(memory_space=pltpu.SMEM if n in smem else pltpu.VMEM) for n in range(len(args))
    ]
    single = not isinstance(out_shape, (list, tuple))
    inside = pl.BlockSpec(memory_space=pltpu.VMEM)
    return pl.pallas_call(
        kernel,
        out_shape=out_shape,
        in_specs=specs,
        out_specs=inside if single else [inside] * len(out_shape),
        scratch_shapes=list(scratch),
        compiler_params=pltpu.CompilerParams(vmem_limit_bytes=vmem),
        name=name,
    )(*args)


class Sizes:
    def __init__(self, rows, crop, devices, channels):
        self.rows, self.crop, self.devices, self.channels = rows, crop, devices, channels
        self.half = rows // 2
        self.group = devices // 2
        self.columns = rows * self.group
        self.whole = crop // LANES
        self.rest = crop % LANES
        self.tiles = rows * crop // LANES
        self.chans = channels // self.group
        self.block = rows * rows
        self.block_tiles = -(-self.block // self.chans)


def normalise(sz, row, x, gain, norm_ref):
    main = sz.whole * LANES
    normed = norm_last(x, gain).astype(BF16)
    norm_ref[pl.ds(row * main, main), :] = normed[:main]
    if sz.rest:
        h, q = divmod(row, sz.half)
        norm_ref[pl.ds(sz.rows * main + q * LANES + h * sz.rest, sz.rest), :] = normed[main:]


def project_edges(sz, length, first, gate, value, pick, norm_ref, store):
    main, ch = sz.whole * LANES, sz.channels
    lane = lax.broadcasted_iota(jnp.int32, (1, LANES), 1)

    def live(tile):
        if tile < sz.rows * sz.whole:
            row, m = divmod(tile, sz.whole)
            return ((first + row < length) & (m * LANES + lane < length)).astype(F32)
        q = tile - sz.rows * sz.whole
        second = lane >= sz.rest
        row = first + q + jnp.where(second, sz.half, 0)
        k = main + lane - jnp.where(second, sz.rest, 0)
        return ((row < length) & (k < length)).astype(F32)

    weights = jnp.concatenate([dot(pick, w, 1, 1).astype(BF16) for w in (gate, value)], axis=0)
    step = 2 if sz.tiles % 2 == 0 else 1
    for tile in range(0, sz.tiles, step):
        n = norm_ref[pl.ds(tile * LANES, step * LANES), :]
        mask = jnp.concatenate([live(tile + s) for s in range(step)], axis=1)
        both = dot(weights, n, 1, 1)
        edge = (sigmoid(both[:ch]) * (both[ch:] * mask)).astype(BF16)
        for g in range(sz.group):
            store(
                g,
                slice(tile * LANES, (tile + step) * LANES),
                edge[g * sz.chans : (g + 1) * sz.chans],
            )


def left_kernel(sz, len_ref, x_ref, ln_ref, w_ref, out_ref, norm_ref, pair_ref):
    cd, ch = sz.chans, sz.channels
    gain = ln_ref[...]
    for row in range(sz.rows):
        x = x_ref[row].astype(F32)
        for d in range(sz.devices):
            pair_ref[d, row * sz.rows : (row + 1) * sz.rows, :] = x[d * sz.rows : (d + 1) * sz.rows]
        normalise(sz, row, x, gain, norm_ref)
    for d in range(sz.devices):
        for t in range(sz.block_tiles):
            at = (sz.tiles + t) * LANES
            out_ref[d, :, at : at + LANES] = pair_ref[d, t * cd : (t + 1) * cd, :].astype(BF16)
    r = lax.broadcasted_iota(jnp.int32, (ch, ch), 0)
    e = lax.broadcasted_iota(jnp.int32, (ch, ch), 1)

    def store(g, lanes, edge):
        out_ref[g, :, lanes] = edge
        out_ref[sz.group + g, :, lanes] = edge

    first = position() * sz.rows
    pick = (r == e).astype(BF16)
    project_edges(sz, len_ref[0], first, w_ref[0], w_ref[1], pick, norm_ref, store)


def right_kernel(sz, len_ref, x_ref, ln_ref, w_ref, *refs):
    near, norm_ref = refs[: sz.group], refs[sz.group]
    cd, ch = sz.chans, sz.channels
    gain = ln_ref[...]
    for row in range(sz.rows):
        normalise(sz, row, x_ref[row].astype(F32), gain, norm_ref)
    me = position()
    r = lax.broadcasted_iota(jnp.int32, (ch, ch), 0)
    e = lax.broadcasted_iota(jnp.int32, (ch, ch), 1)
    pick = (((r // cd) ^ (me & (sz.group - 1))) * cd + r % cd == e).astype(BF16)

    def store(g, lanes, edge):
        near[g][:, lanes] = edge

    project_edges(sz, len_ref[0], me * sz.rows, w_ref[2], w_ref[3], pick, norm_ref, store)


def unpack(sz, ref, owner, main_ref, rest_ref):
    cd, w = sz.chans, sz.whole
    for tile in range(sz.tiles):
        block = ref[:, tile * LANES : (tile + 1) * LANES].astype(F32)
        if tile < sz.rows * w:
            row, m = divmod(tile, w)
            main_ref[m, pl.ds(pl.multiple_of((owner * sz.rows + row) * cd, 8), cd), :] = block
        else:
            row = owner * sz.rows + tile - sz.rows * w
            rest_ref[pl.ds(pl.multiple_of(row * cd, 8), cd), :] = block
            rest_ref[pl.ds(pl.multiple_of((row + sz.half) * cd, 8), cd), :] = pltpu.roll(
                block, sz.rest, 1
            )


def matrix(sz, c, size, main_ref, rest_ref):
    cd, w = sz.chans, sz.whole
    parts = [main_ref[m, pl.ds(c, size, stride=cd), :].astype(BF16) for m in range(w)]
    if sz.rest:
        parts.append(rest_ref[pl.ds(c, size, stride=cd), :].astype(BF16)[:, : sz.rest])
    return jnp.concatenate(parts, axis=1) if len(parts) > 1 else parts[0]


def arrange_kernel(sz, *refs):
    near, (out_ref, main_ref, rest_ref) = refs[: sz.group], refs[sz.group :]
    mine = position() & (sz.group - 1)
    for r in range(sz.group):
        unpack(sz, near[r], mine ^ r, main_ref, rest_ref)
    for c in range(sz.chans):
        out_ref[c] = matrix(sz, c, sz.columns, main_ref, rest_ref)


def outer_kernel(
    sz, left_ref, right_ref, out_ref, lmain_ref, lrest_ref, omain_ref, orest_ref
):
    cd, n, w, half = sz.chans, sz.crop, sz.whole, sz.half
    for d in range(sz.devices):
        unpack(sz, left_ref.at[d], jnp.int32(d), lmain_ref, lrest_ref)
    for c in range(cd):
        outer = dot(right_ref[c], matrix(sz, c, n, lmain_ref, lrest_ref), 1, 1)
        for m in range(w):
            omain_ref[m, pl.ds(c, sz.columns, stride=cd), :] = outer[:, m * LANES : (m + 1) * LANES]
        if sz.rest:
            part = outer[:, w * LANES :]
            orest_ref[pl.ds(c, sz.columns, stride=cd), :] = jnp.concatenate([part, part], axis=1)
    low = lax.broadcasted_iota(jnp.int32, (cd, LANES), 1) < sz.rest
    for g in range(sz.group):
        start = g * sz.rows
        for tile in range(sz.tiles):
            if tile < sz.rows * w:
                row, m = divmod(tile, w)
                block = omain_ref[m, pl.ds((start + row) * cd, cd), :]
            else:
                at = start + tile - sz.rows * w
                block = jnp.where(
                    low,
                    orest_ref[pl.ds(at * cd, cd), :],
                    orest_ref[pl.ds((at + half) * cd, cd), :],
                )
            out_ref[g, :, tile * LANES : (tile + 1) * LANES] = block.astype(BF16)


def update_kernel(
    sz, lnp_ref, gate_ref, lnh_ref, tri_ref, lna_ref, biasw_ref, sums_ref, pair_ref,
    first_ref, col_ref, bias_ref, cols_ref, brow_ref,
):
    n, w, half, ch, cd = sz.crop, sz.whole, sz.half, sz.channels, sz.chans
    for s in range(sz.devices):
        for t in range(sz.block_tiles):
            at = (sz.tiles + t) * LANES
            rows = pl.ds(s * sz.block + t * cd, cd)
            cols_ref[rows, :] = pair_ref[s, :, at : at + LANES].astype(F32)
    gain_h = jnp.transpose(jnp.broadcast_to(lnh_ref[...], (ch, ch)))
    tri = tri_ref[...]

    def update(tile):
        block = sums_ref[:, :, tile * LANES : (tile + 1) * LANES].astype(F32).reshape(ch, LANES)
        average = jnp.mean(block, axis=0, keepdims=True)
        centred = block - average
        variance = jnp.mean(centred * centred, axis=0, keepdims=True)
        hidden = (centred * lax.rsqrt(variance + EPS) * gain_h).astype(BF16)
        return dot(hidden, tri, 0, 0)

    rest = [update(sz.rows * w + q) for q in range(half)] if sz.rest else None
    for j in range(sz.rows):
        parts = [update(j * w + m) for m in range(w)]
        if sz.rest:
            h, q = divmod(j, half)
            parts.append(rest[q][h * sz.rest : (h + 1) * sz.rest])
        change = jnp.concatenate(parts, axis=0) if len(parts) > 1 else parts[0]
        x = cols_ref[pl.ds(j, n, stride=sz.rows), :]
        normed = norm_last(x, lnp_ref[...]).astype(BF16)
        gating = sigmoid(dot(normed, gate_ref[...], 1, 0))
        first = (x + gating * change).astype(BF16)
        first_ref[j] = first
        col = norm_last(first.astype(F32), lna_ref[...]).astype(BF16)
        col_ref[j] = col
        heads = biasw_ref.shape[1]
        brow_ref[pl.ds(j * heads, heads), :] = dot(biasw_ref[...], col, 0, 1)
    rows = brow_ref[...]
    part = rows.shape[0] // 2
    one, two = rows[:part], rows[part:]
    message = [one[:, : w * LANES], two[:, : w * LANES]]
    if sz.rest:
        message += [one[:, w * LANES :], two[:, w * LANES :]]
    bias_ref[...] = jnp.concatenate(message, axis=1).astype(BF16)


def project_kernel(sz, col_ref, q_ref, k_ref, v_ref, g_ref, qo_ref, ko_ref, vo_ref, go_ref):
    joined = jnp.concatenate([ref[...] for ref in (q_ref, k_ref, v_ref, g_ref)], axis=1)
    width = q_ref.shape[1]
    for j in range(sz.rows):
        made = dot(col_ref[j], joined, 1, 0)
        qo_ref[j] = made[:, :width].astype(BF16)
        ko_ref[j] = made[:, width : 2 * width].astype(BF16)
        vo_ref[j] = made[:, 2 * width : 3 * width].astype(BF16)
        go_ref[j] = sigmoid(made[:, 3 * width :])


def attend_kernel(
    sz, heads, steps, len_ref, q_ref, k_ref, v_ref, g_ref, first_ref, aout_ref, *refs
):
    bias_refs, (out_ref, rows_ref, bias_ref) = refs[:-3], refs[-3:]
    n, w, ch = sz.crop, sz.whole, sz.channels
    length, me = len_ref[0], position()
    width = q_ref.shape[2]
    hd = width // heads
    per = sz.rows * heads // 2
    for ref, offsets in zip(bias_refs, steps):
        for place, offset in enumerate(offsets):
            block = ref[place].astype(F32) * LOG2E
            for p in range(2):
                at = pl.ds(pl.multiple_of(((me ^ offset) * 2 + p) * per, 8), per)
                for m in range(w):
                    rows_ref[m, at, :] = block[:, (p * w + m) * LANES : (p * w + m + 1) * LANES]
                if sz.rest:
                    tail = block[:, 2 * w * LANES :]
                    rows_ref[w, at, :] = pltpu.roll(tail, sz.rest, 1) if p else tail
    lane = lax.broadcasted_iota(jnp.int32, (1, LANES), 1)
    for m in range(w + (sz.rest > 0)):
        lanes = slice(m * LANES, min((m + 1) * LANES, n))
        dead = jnp.where(m * LANES + lane < length, 0.0, -1e9 * LOG2E).astype(F32)
        for head in range(heads):
            rows = rows_ref[m, pl.ds(head, n, stride=heads), :] + dead
            bias_ref[head, :, lanes] = rows[:, : lanes.stop - lanes.start]
    column = lax.broadcasted_iota(jnp.int32, (1, width), 1)
    head_masks = [(column >= h * hd) & (column < (h + 1) * hd) for h in range(heads)]
    scale = (hd ** (-0.5)) * LOG2E
    ones = jnp.ones((n, width), BF16)

    def score(j):
        query = [q_ref[j] * head_masks[h].astype(BF16) for h in range(heads)]
        return dot(jnp.concatenate(query, axis=0), k_ref[j], 1, 1)

    scores = score(0)
    for j in range(sz.rows):
        now = scores
        if j + 1 < sz.rows:
            scores = score(j + 1)
        weights = []
        for h in range(heads):
            part = now[h * n : (h + 1) * n] * scale + bias_ref[h]
            weights.append(jnp.exp2(part - jnp.max(part, axis=1, keepdims=True)).astype(BF16))
        values = jnp.concatenate([v_ref[j], ones], axis=1)
        mixed = dot(jnp.concatenate(weights, axis=0), values, 1, 0)
        attended, total = mixed[:n, :width], mixed[:n, width:]
        for h in range(1, heads):
            rows = slice(h * n, (h + 1) * n)
            attended = jnp.where(head_masks[h], mixed[rows, :width], attended)
            total = jnp.where(head_masks[h], mixed[rows, width:], total)
        gated = (attended / total * g_ref[j]).astype(BF16)
        out_ref[j] = (first_ref[j].astype(F32) + dot(gated, aout_ref[...], 1, 0)).astype(BF16)


def spread(block, devices):
    pieces, offsets = [block[None]], [[0]]
    bit = devices // 2
    while bit:
        held = jnp.concatenate(pieces, axis=0) if len(pieces) > 1 else pieces[0]
        known = [o for part in offsets for o in part]
        pieces.append(lax.ppermute(held, AXES, [(d, d ^ bit) for d in range(devices)]))
        offsets.append([o ^ bit for o in known])
        bit //= 2
    return pieces, offsets


def shards(
    devices,
    pair_rep, length, ln_pair, tri_in, tri_gate, ln_hidden, tri_out, ln_att,
    att_q, att_k, att_v, att_bias, att_gate, att_out,
):
    rows, crop, ch = pair_rep.shape
    heads = att_bias.shape[1]
    sz = Sizes(rows, crop, devices, ch)
    n, cd = crop, sz.chans
    def bound(kernel, *extra):
        def run(*refs):
            return kernel(sz, *extra, *refs)

        return run

    shape = jax.ShapeDtypeStruct
    g, t, bt = sz.group, sz.tiles, sz.block_tiles

    def slab(tiles, *lead):
        return shape((*lead, cd, tiles * LANES), BF16)

    def send(blocks, offset):
        return [
            block
            if not (offset ^ r)
            else lax.ppermute(block, AXES, [(d, d ^ offset ^ r) for d in range(devices)])
            for r, block in enumerate(blocks)
        ]

    left = call(
        bound(left_kernel),
        slab(t + bt, devices),
        (length, pair_rep, ln_pair[None], tri_in),
        scratch=[
            pltpu.VMEM((rows * crop, ch), BF16),
            pltpu.VMEM((devices, bt * cd, ch), F32),
        ],
        smem=(0,),
        name="left",
        vmem=VMEM_MOST,
    )
    others = call(
        bound(right_kernel),
        [slab(t)] * g,
        (length, pair_rep, ln_pair[None], tri_in),
        scratch=[pltpu.VMEM((rows * crop, ch), BF16)],
        smem=(0,),
        name="right",
        vmem=VMEM_MOST,
    )
    left = lax.all_to_all(left, AXES, split_axis=0, concat_axis=0, tiled=True)
    near = send(others, 0)
    rest = sz.rest > 0
    column_rows = sz.columns * cd
    right = call(
        bound(arrange_kernel),
        shape((cd, sz.columns, n), BF16),
        tuple(near),
        scratch=[
            pltpu.VMEM((sz.whole, column_rows, LANES), F32),
            pltpu.VMEM((column_rows if rest else 8, LANES), F32),
        ],
        name="arrange",
    )
    outer = call(
        bound(outer_kernel),
        slab(t, g),
        (left, right),
        scratch=[
            pltpu.VMEM((sz.whole, n * cd, LANES), F32),
            pltpu.VMEM((n * cd if rest else 8, LANES), F32),
            pltpu.VMEM((sz.whole, column_rows, LANES), F32),
            pltpu.VMEM((column_rows if rest else 8, LANES), F32),
        ],
        name="outer",
    )
    sums = lax.all_to_all(
        outer, AXES, split_axis=0, concat_axis=0, tiled=True,
        axis_index_groups=[list(range(g)), list(range(g, devices))],
    )
    first, col, bias = call(
        bound(update_kernel),
        [
            shape((rows, n, ch), BF16),
            shape((rows, n, ch), BF16),
            shape((rows * heads // 2, 2 * n), BF16),
        ],
        (
            ln_pair[None], tri_gate, ln_hidden[None], tri_out, ln_att[None], att_bias,
            sums, left,
        ),
        scratch=[
            pltpu.VMEM((devices * sz.block + cd, ch), F32),
            pltpu.VMEM((rows * heads, n), F32),
        ],
        name="update",
    )
    pieces, steps = spread(bias, devices)
    query, key, value, gate = call(
        bound(project_kernel),
        [
            shape((rows, n, att_q.shape[1]), BF16),
            shape((rows, n, att_q.shape[1]), BF16),
            shape((rows, n, att_q.shape[1]), BF16),
            shape((rows, n, att_q.shape[1]), F32),
        ],
        (col, att_q, att_k, att_v, att_gate),
        name="project",
    )
    out = call(
        bound(attend_kernel, heads, steps),
        shape((rows, n, ch), BF16),
        (length, query, key, value, gate, first, att_out, *pieces),
        scratch=[
            pltpu.VMEM((-(-n // LANES), n * heads, LANES), F32),
            pltpu.VMEM((heads, n, n), F32),
        ],
        smem=(0,),
        name="attend",
    )
    return jnp.swapaxes(out, 0, 1)


def solution(mesh):
    devices = mesh.shape["row"] * mesh.shape["node"]

    def body(*args):
        return shards(devices, *args)

    return jax.shard_map(
        body,
        mesh=mesh,
        in_specs=(P(("grp", "row", "node"), None, None), P("grp")) + (P(),) * 12,
        out_specs=P("grp", AXES, None),
        check_vma=False,
    )
```

```python
import jax
import jax.numpy as jnp
from jax import lax
from jax.experimental import pallas as pl
from jax.experimental.pallas import tpu as pltpu
from jax.sharding import PartitionSpec as P

EPS = 1e-05
LANES = 128
LOG2E = 1.4426950408889634
F32 = jnp.float32
BF16 = jnp.bfloat16
AXES = ("row", "node")
VMEM_BYTES = 48 * 1024 * 1024
VMEM_MOST = 60 * 1024 * 1024


def norm_last(values, gain):
    average = jnp.mean(values, axis=-1, keepdims=True)
    centred = values - average
    variance = jnp.mean(centred * centred, axis=-1, keepdims=True)
    return centred * lax.rsqrt(variance + EPS) * gain


def sigmoid(values):
    return 0.5 * jnp.tanh(0.5 * values) + 0.5


def dot(a, b, a_dim, b_dim):
    return lax.dot_general(a, b, (((a_dim,), (b_dim,)), ((), ())), preferred_element_type=F32)


def position():
    return lax.axis_index("row") * lax.axis_size("node") + lax.axis_index("node")


def call(kernel, out_shape, args, scratch=(), smem=(), name=None, vmem=VMEM_BYTES, away=False):
    specs = [
        pl.BlockSpec(memory_space=pltpu.SMEM if n in smem else pltpu.VMEM) for n in range(len(args))
    ]
    single = not isinstance(out_shape, (list, tuple))
    inside = pl.BlockSpec(memory_space=pl.ANY if away else pltpu.VMEM)
    return pl.pallas_call(
        kernel,
        out_shape=out_shape,
        in_specs=specs,
        out_specs=inside if single else [inside] * len(out_shape),
        scratch_shapes=list(scratch),
        compiler_params=pltpu.CompilerParams(vmem_limit_bytes=vmem),
        name=name,
    )(*args)


class Sizes:
    def __init__(self, rows, crop, devices, channels):
        self.rows, self.crop, self.devices, self.channels = rows, crop, devices, channels
        self.half = rows // 2
        self.group = devices // 2
        self.columns = rows * self.group
        self.whole = crop // LANES
        self.rest = crop % LANES
        self.tiles = rows * crop // LANES
        self.chans = channels // self.group
        self.block = rows * rows
        self.block_tiles = -(-self.block // self.chans)


def normalise(sz, row, x, gain, norm_ref):
    main = sz.whole * LANES
    normed = norm_last(x, gain).astype(BF16)
    norm_ref[pl.ds(row * main, main), :] = normed[:main]
    if sz.rest:
        h, q = divmod(row, sz.half)
        norm_ref[pl.ds(sz.rows * main + q * LANES + h * sz.rest, sz.rest), :] = normed[main:]


def project_edges(sz, length, first, gate, value, pick, norm_ref, store):
    main, ch = sz.whole * LANES, sz.channels
    lane = lax.broadcasted_iota(jnp.int32, (1, LANES), 1)

    def live(tile):
        if tile < sz.rows * sz.whole:
            row, m = divmod(tile, sz.whole)
            return ((first + row < length) & (m * LANES + lane < length)).astype(F32)
        q = tile - sz.rows * sz.whole
        second = lane >= sz.rest
        row = first + q + jnp.where(second, sz.half, 0)
        k = main + lane - jnp.where(second, sz.rest, 0)
        return ((row < length) & (k < length)).astype(F32)

    weights = jnp.concatenate([dot(pick, w, 1, 1).astype(BF16) for w in (gate, value)], axis=0)
    step = 2 if sz.tiles % 2 == 0 else 1
    for tile in range(0, sz.tiles, step):
        n = norm_ref[pl.ds(tile * LANES, step * LANES), :]
        mask = jnp.concatenate([live(tile + s) for s in range(step)], axis=1)
        both = dot(weights, n, 1, 1)
        edge = (sigmoid(both[:ch]) * (both[ch:] * mask)).astype(BF16)
        for g in range(sz.group):
            store(
                g,
                slice(tile * LANES, (tile + step) * LANES),
                edge[g * sz.chans : (g + 1) * sz.chans],
            )


def left_kernel(
    sz, len_ref, x_ref, ln_ref, w_ref, away_ref, out_ref, norm_ref, wide_ref, pair_ref, sems
):
    cd, ch = sz.chans, sz.channels
    gain = ln_ref[...]
    for row in range(sz.rows):
        x = x_ref[row].astype(F32)
        wide_ref[pl.ds(row * sz.crop, sz.crop), :] = x
        normalise(sz, row, x, gain, norm_ref)
    for d in range(sz.devices):
        for row in range(sz.rows):
            block = wide_ref[pl.ds(row * sz.crop + d * sz.rows, sz.rows), :]
            pair_ref[pl.ds(d * sz.block + row * sz.rows, sz.rows), :] = block
        for t in range(sz.block_tiles):
            at = (sz.tiles + t) * LANES
            block = pair_ref[pl.ds(d * sz.block + t * cd, cd), :]
            out_ref[d, :, at : at + LANES] = block.astype(BF16)

    def leave(start, stop, sem):
        lanes = pl.ds(start * LANES, (stop - start) * LANES)
        copy = pltpu.make_async_copy(
            out_ref.at[:, :, lanes], away_ref.at[:, :, lanes], sems.at[sem]
        )
        copy.start()
        return copy

    pairs_out = leave(sz.tiles, sz.tiles + sz.block_tiles, 0)
    r = lax.broadcasted_iota(jnp.int32, (ch, ch), 0)
    e = lax.broadcasted_iota(jnp.int32, (ch, ch), 1)

    def store(g, lanes, edge):
        out_ref[g, :, lanes] = edge
        out_ref[sz.group + g, :, lanes] = edge

    first = position() * sz.rows
    pick = (r == e).astype(BF16)
    project_edges(sz, len_ref[0], first, w_ref[0], w_ref[1], pick, norm_ref, store)
    edges_out = leave(0, sz.tiles, 1)
    pairs_out.wait()
    edges_out.wait()


def right_kernel(sz, len_ref, x_ref, ln_ref, w_ref, *refs):
    near, norm_ref = refs[: sz.group], refs[sz.group]
    cd, ch = sz.chans, sz.channels
    gain = ln_ref[...]
    for row in range(sz.rows):
        normalise(sz, row, x_ref[row].astype(F32), gain, norm_ref)
    me = position()
    r = lax.broadcasted_iota(jnp.int32, (ch, ch), 0)
    e = lax.broadcasted_iota(jnp.int32, (ch, ch), 1)
    pick = (((r // cd) ^ (me & (sz.group - 1))) * cd + r % cd == e).astype(BF16)

    def store(g, lanes, edge):
        near[g][:, lanes] = edge

    project_edges(sz, len_ref[0], me * sz.rows, w_ref[2], w_ref[3], pick, norm_ref, store)


def unpack(sz, ref, owner, main_ref, rest_ref):
    cd, w = sz.chans, sz.whole
    for tile in range(sz.tiles):
        block = ref[:, tile * LANES : (tile + 1) * LANES].astype(F32)
        if tile < sz.rows * w:
            row, m = divmod(tile, w)
            main_ref[m, pl.ds(pl.multiple_of((owner * sz.rows + row) * cd, 8), cd), :] = block
        else:
            row = owner * sz.rows + tile - sz.rows * w
            rest_ref[pl.ds(pl.multiple_of(row * cd, 8), cd), :] = block
            rest_ref[pl.ds(pl.multiple_of((row + sz.half) * cd, 8), cd), :] = pltpu.roll(
                block, sz.rest, 1
            )


def matrix(sz, c, size, main_ref, rest_ref):
    cd, w = sz.chans, sz.whole
    parts = [main_ref[m, pl.ds(c, size, stride=cd), :].astype(BF16) for m in range(w)]
    if sz.rest:
        parts.append(rest_ref[pl.ds(c, size, stride=cd), :].astype(BF16)[:, : sz.rest])
    return jnp.concatenate(parts, axis=1) if len(parts) > 1 else parts[0]


def arrange_kernel(sz, *refs):
    near, (out_ref, main_ref, rest_ref) = refs[: sz.group], refs[sz.group :]
    mine = position() & (sz.group - 1)
    for r in range(sz.group):
        unpack(sz, near[r], mine ^ r, main_ref, rest_ref)
    for c in range(sz.chans):
        out_ref[c] = matrix(sz, c, sz.columns, main_ref, rest_ref)


def outer_kernel(
    sz, left_ref, right_ref, out_ref, lmain_ref, lrest_ref, omain_ref, orest_ref
):
    cd, n, w, half = sz.chans, sz.crop, sz.whole, sz.half
    for d in range(sz.devices):
        unpack(sz, left_ref.at[d], jnp.int32(d), lmain_ref, lrest_ref)
    for c in range(cd):
        outer = dot(right_ref[c], matrix(sz, c, n, lmain_ref, lrest_ref), 1, 1)
        for m in range(w):
            omain_ref[m, pl.ds(c, sz.columns, stride=cd), :] = outer[:, m * LANES : (m + 1) * LANES]
        if sz.rest:
            part = outer[:, w * LANES :]
            orest_ref[pl.ds(c, sz.columns, stride=cd), :] = jnp.concatenate([part, part], axis=1)
    low = lax.broadcasted_iota(jnp.int32, (cd, LANES), 1) < sz.rest
    for g in range(sz.group):
        start = g * sz.rows
        for tile in range(sz.tiles):
            if tile < sz.rows * w:
                row, m = divmod(tile, w)
                block = omain_ref[m, pl.ds((start + row) * cd, cd), :]
            else:
                at = start + tile - sz.rows * w
                block = jnp.where(
                    low,
                    orest_ref[pl.ds(at * cd, cd), :],
                    orest_ref[pl.ds((at + half) * cd, cd), :],
                )
            out_ref[g, :, tile * LANES : (tile + 1) * LANES] = block.astype(BF16)


def take_columns(sz, pair_ref, cols_ref):
    cd = sz.chans
    for s in range(sz.devices):
        for t in range(sz.block_tiles):
            at = (sz.tiles + t) * LANES
            rows = pl.ds(s * sz.block + t * cd, cd)
            cols_ref[rows, :] = pair_ref[s, :, at : at + LANES].astype(F32)


def gating_kernel(sz, pair_ref, lnp_ref, gate_ref, gating_ref, cols_ref):
    take_columns(sz, pair_ref, cols_ref)
    for j in range(sz.rows):
        x = cols_ref[pl.ds(j, sz.crop, stride=sz.rows), :]
        normed = norm_last(x, lnp_ref[...]).astype(BF16)
        gating_ref[j] = sigmoid(dot(normed, gate_ref[...], 1, 0)).astype(BF16)


def update_kernel(
    sz, gating_ref, lnh_ref, tri_ref, lna_ref, biasw_ref, sums_ref, pair_ref,
    first_ref, col_ref, bias_ref, cols_ref, brow_ref,
):
    n, w, half, ch = sz.crop, sz.whole, sz.half, sz.channels
    take_columns(sz, pair_ref, cols_ref)
    gain_h = jnp.transpose(jnp.broadcast_to(lnh_ref[...], (ch, ch)))
    tri = tri_ref[...]

    def update(tile):
        block = sums_ref[:, :, tile * LANES : (tile + 1) * LANES].astype(F32).reshape(ch, LANES)
        average = jnp.mean(block, axis=0, keepdims=True)
        centred = block - average
        variance = jnp.mean(centred * centred, axis=0, keepdims=True)
        hidden = (centred * lax.rsqrt(variance + EPS) * gain_h).astype(BF16)
        return dot(hidden, tri, 0, 0)

    rest = [update(sz.rows * w + q) for q in range(half)] if sz.rest else None
    for j in range(sz.rows):
        parts = [update(j * w + m) for m in range(w)]
        if sz.rest:
            h, q = divmod(j, half)
            parts.append(rest[q][h * sz.rest : (h + 1) * sz.rest])
        change = jnp.concatenate(parts, axis=0) if len(parts) > 1 else parts[0]
        x = cols_ref[pl.ds(j, n, stride=sz.rows), :]
        first = (x + gating_ref[j].astype(F32) * change).astype(BF16)
        first_ref[j] = first
        col = norm_last(first.astype(F32), lna_ref[...]).astype(BF16)
        col_ref[j] = col
        heads = biasw_ref.shape[1]
        brow_ref[pl.ds(j * heads, heads), :] = dot(biasw_ref[...], col, 0, 1)
    rows = brow_ref[...]
    part = rows.shape[0] // 2
    one, two = rows[:part], rows[part:]
    message = [one[:, : w * LANES], two[:, : w * LANES]]
    if sz.rest:
        message += [one[:, w * LANES :], two[:, w * LANES :]]
    bias_ref[...] = jnp.concatenate(message, axis=1).astype(BF16)


def project_kernel(sz, col_ref, q_ref, k_ref, v_ref, g_ref, qo_ref, ko_ref, vo_ref, go_ref):
    joined = jnp.concatenate([ref[...] for ref in (q_ref, k_ref, v_ref, g_ref)], axis=1)
    width = q_ref.shape[1]
    for j in range(sz.rows):
        made = dot(col_ref[j], joined, 1, 0)
        qo_ref[j] = made[:, :width].astype(BF16)
        ko_ref[j] = made[:, width : 2 * width].astype(BF16)
        vo_ref[j] = made[:, 2 * width : 3 * width].astype(BF16)
        go_ref[j] = sigmoid(made[:, 3 * width :])


def attend_kernel(
    sz, heads, steps, len_ref, q_ref, k_ref, v_ref, g_ref, first_ref, aout_ref, *refs
):
    bias_refs, (out_ref, rows_ref, bias_ref) = refs[:-3], refs[-3:]
    n, w, ch = sz.crop, sz.whole, sz.channels
    length, me = len_ref[0], position()
    width = q_ref.shape[2]
    hd = width // heads
    per = sz.rows * heads // 2
    for ref, offsets in zip(bias_refs, steps):
        for place, offset in enumerate(offsets):
            block = ref[place].astype(F32) * LOG2E
            for p in range(2):
                at = pl.ds(pl.multiple_of(((me ^ offset) * 2 + p) * per, 8), per)
                for m in range(w):
                    rows_ref[m, at, :] = block[:, (p * w + m) * LANES : (p * w + m + 1) * LANES]
                if sz.rest:
                    tail = block[:, 2 * w * LANES :]
                    rows_ref[w, at, :] = pltpu.roll(tail, sz.rest, 1) if p else tail
    lane = lax.broadcasted_iota(jnp.int32, (1, LANES), 1)
    for m in range(w + (sz.rest > 0)):
        lanes = slice(m * LANES, min((m + 1) * LANES, n))
        dead = jnp.where(m * LANES + lane < length, 0.0, -1e9 * LOG2E).astype(F32)
        for head in range(heads):
            rows = rows_ref[m, pl.ds(head, n, stride=heads), :] + dead
            bias_ref[head, :, lanes] = rows[:, : lanes.stop - lanes.start]
    column = lax.broadcasted_iota(jnp.int32, (1, width), 1)
    head_masks = [(column >= h * hd) & (column < (h + 1) * hd) for h in range(heads)]
    scale = (hd ** (-0.5)) * LOG2E
    ones = jnp.ones((n, width), BF16)

    def score(j):
        query = [q_ref[j] * head_masks[h].astype(BF16) for h in range(heads)]
        return dot(jnp.concatenate(query, axis=0), k_ref[j], 1, 1)

    scores = score(0)
    for j in range(sz.rows):
        now = scores
        if j + 1 < sz.rows:
            scores = score(j + 1)
        weights = []
        for h in range(heads):
            part = now[h * n : (h + 1) * n] * scale + bias_ref[h]
            weights.append(jnp.exp2(part - jnp.max(part, axis=1, keepdims=True)).astype(BF16))
        values = jnp.concatenate([v_ref[j], ones], axis=1)
        mixed = dot(jnp.concatenate(weights, axis=0), values, 1, 0)
        attended, total = mixed[:n, :width], mixed[:n, width:]
        for h in range(1, heads):
            rows = slice(h * n, (h + 1) * n)
            attended = jnp.where(head_masks[h], mixed[rows, :width], attended)
            total = jnp.where(head_masks[h], mixed[rows, width:], total)
        gated = (attended / total * g_ref[j]).astype(BF16)
        out_ref[j] = (first_ref[j].astype(F32) + dot(gated, aout_ref[...], 1, 0)).astype(BF16)


def spread(block, devices):
    pieces, offsets = [block[None]], [[0]]
    bit = devices // 2
    while bit:
        held = jnp.concatenate(pieces, axis=0) if len(pieces) > 1 else pieces[0]
        known = [o for part in offsets for o in part]
        pieces.append(lax.ppermute(held, AXES, [(d, d ^ bit) for d in range(devices)]))
        offsets.append([o ^ bit for o in known])
        bit //= 2
    return pieces, offsets


def shards(
    devices,
    pair_rep, length, ln_pair, tri_in, tri_gate, ln_hidden, tri_out, ln_att,
    att_q, att_k, att_v, att_bias, att_gate, att_out,
):
    rows, crop, ch = pair_rep.shape
    heads = att_bias.shape[1]
    sz = Sizes(rows, crop, devices, ch)
    n, cd = crop, sz.chans
    def bound(kernel, *extra):
        def run(*refs):
            return kernel(sz, *extra, *refs)

        return run

    shape = jax.ShapeDtypeStruct
    g, t, bt = sz.group, sz.tiles, sz.block_tiles

    def slab(tiles, *lead):
        return shape((*lead, cd, tiles * LANES), BF16)

    def send(blocks, offset):
        return [
            block
            if not (offset ^ r)
            else lax.ppermute(block, AXES, [(d, d ^ offset ^ r) for d in range(devices)])
            for r, block in enumerate(blocks)
        ]

    left = call(
        bound(left_kernel),
        slab(t + bt, devices),
        (length, pair_rep, ln_pair[None], tri_in),
        scratch=[
            pltpu.VMEM((devices, cd, (t + bt) * LANES), BF16),
            pltpu.VMEM((rows * crop, ch), BF16),
            pltpu.VMEM((rows * crop, ch), F32),
            pltpu.VMEM((devices * sz.block + cd, ch), F32),
            pltpu.SemaphoreType.DMA((2,)),
        ],
        smem=(0,),
        away=True,
        name="left",
        vmem=VMEM_MOST,
    )
    others = call(
        bound(right_kernel),
        [slab(t)] * g,
        (length, pair_rep, ln_pair[None], tri_in),
        scratch=[pltpu.VMEM((rows * crop, ch), BF16)],
        smem=(0,),
        name="right",
    )
    left = lax.all_to_all(left, AXES, split_axis=0, concat_axis=0, tiled=True)
    near = send(others, 0)
    rest = sz.rest > 0
    column_rows = sz.columns * cd
    right = call(
        bound(arrange_kernel),
        shape((cd, sz.columns, n), BF16),
        tuple(near),
        scratch=[
            pltpu.VMEM((sz.whole, column_rows, LANES), F32),
            pltpu.VMEM((column_rows if rest else 8, LANES), F32),
        ],
        name="arrange",
    )
    outer = call(
        bound(outer_kernel),
        slab(t, g),
        (left, right),
        scratch=[
            pltpu.VMEM((sz.whole, n * cd, LANES), F32),
            pltpu.VMEM((n * cd if rest else 8, LANES), F32),
            pltpu.VMEM((sz.whole, column_rows, LANES), F32),
            pltpu.VMEM((column_rows if rest else 8, LANES), F32),
        ],
        name="outer",
    )
    sums = lax.all_to_all(
        outer, AXES, split_axis=0, concat_axis=0, tiled=True,
        axis_index_groups=[list(range(g)), list(range(g, devices))],
    )
    gating = call(
        bound(gating_kernel),
        shape((rows, n, ch), BF16),
        (left, ln_pair[None], tri_gate),
        scratch=[pltpu.VMEM((devices * sz.block + cd, ch), F32)],
        name="gating",
    )
    first, col, bias = call(
        bound(update_kernel),
        [
            shape((rows, n, ch), BF16),
            shape((rows, n, ch), BF16),
            shape((rows * heads // 2, 2 * n), BF16),
        ],
        (
            gating, ln_hidden[None], tri_out, ln_att[None], att_bias, sums, left,
        ),
        scratch=[
            pltpu.VMEM((devices * sz.block + cd, ch), F32),
            pltpu.VMEM((rows * heads, n), F32),
        ],
        name="update",
    )
    pieces, steps = spread(bias, devices)
    query, key, value, gate = call(
        bound(project_kernel),
        [
            shape((rows, n, att_q.shape[1]), BF16),
            shape((rows, n, att_q.shape[1]), BF16),
            shape((rows, n, att_q.shape[1]), BF16),
            shape((rows, n, att_q.shape[1]), F32),
        ],
        (col, att_q, att_k, att_v, att_gate),
        name="project",
    )
    out = call(
        bound(attend_kernel, heads, steps),
        shape((rows, n, ch), BF16),
        (length, query, key, value, gate, first, att_out, *pieces),
        scratch=[
            pltpu.VMEM((-(-n // LANES), n * heads, LANES), F32),
            pltpu.VMEM((heads, n, n), F32),
        ],
        smem=(0,),
        name="attend",
    )
    return jnp.swapaxes(out, 0, 1)


def solution(mesh):
    devices = mesh.shape["row"] * mesh.shape["node"]

    def body(*args):
        return shards(devices, *args)

    return jax.shard_map(
        body,
        mesh=mesh,
        in_specs=(P(("grp", "row", "node"), None, None), P("grp")) + (P(),) * 12,
        out_specs=P("grp", AXES, None),
        check_vma=False,
    )
```

```python
import jax
import jax.numpy as jnp
from jax import lax
from jax.experimental import pallas as pl
from jax.experimental.pallas import tpu as pltpu
from jax.sharding import PartitionSpec as P

EPS = 1e-05
LANES = 128
LOG2E = 1.4426950408889634
F32 = jnp.float32
BF16 = jnp.bfloat16
AXES = ("row", "node")
VMEM_BYTES = 48 * 1024 * 1024
VMEM_MOST = 60 * 1024 * 1024


def norm_last(values, gain):
    average = jnp.mean(values, axis=-1, keepdims=True)
    centred = values - average
    variance = jnp.mean(centred * centred, axis=-1, keepdims=True)
    return centred * lax.rsqrt(variance + EPS) * gain


def sigmoid(values):
    return 0.5 * jnp.tanh(0.5 * values) + 0.5


def dot(a, b, a_dim, b_dim):
    return lax.dot_general(a, b, (((a_dim,), (b_dim,)), ((), ())), preferred_element_type=F32)


def position():
    return lax.axis_index("row") * lax.axis_size("node") + lax.axis_index("node")


def call(kernel, out_shape, args, scratch=(), smem=(), name=None, vmem=VMEM_BYTES, away=False, cost=None):
    specs = [
        pl.BlockSpec(memory_space=pltpu.SMEM if n in smem else pltpu.VMEM) for n in range(len(args))
    ]
    single = not isinstance(out_shape, (list, tuple))
    inside = pl.BlockSpec(memory_space=pl.ANY if away else pltpu.VMEM)
    return pl.pallas_call(
        kernel,
        out_shape=out_shape,
        in_specs=specs,
        out_specs=inside if single else [inside] * len(out_shape),
        scratch_shapes=list(scratch),
        compiler_params=pltpu.CompilerParams(vmem_limit_bytes=vmem),
        name=name,
        cost_estimate=cost,
    )(*args)


class Sizes:
    def __init__(self, rows, crop, devices, channels):
        self.rows, self.crop, self.devices, self.channels = rows, crop, devices, channels
        self.half = rows // 2
        self.group = devices // 2
        self.columns = rows * self.group
        self.whole = crop // LANES
        self.rest = crop % LANES
        self.tiles = rows * crop // LANES
        self.chans = channels // self.group
        self.block = rows * rows
        self.block_tiles = -(-self.block // self.chans)


def normalise(sz, row, x, gain, norm_ref):
    main = sz.whole * LANES
    normed = norm_last(x, gain).astype(BF16)
    norm_ref[pl.ds(row * main, main), :] = normed[:main]
    if sz.rest:
        h, q = divmod(row, sz.half)
        norm_ref[pl.ds(sz.rows * main + q * LANES + h * sz.rest, sz.rest), :] = normed[main:]


def project_edges(sz, length, first, gate, value, pick, norm_ref, store):
    main, ch = sz.whole * LANES, sz.channels
    lane = lax.broadcasted_iota(jnp.int32, (1, LANES), 1)

    def live(tile):
        if tile < sz.rows * sz.whole:
            row, m = divmod(tile, sz.whole)
            return ((first + row < length) & (m * LANES + lane < length)).astype(F32)
        q = tile - sz.rows * sz.whole
        second = lane >= sz.rest
        row = first + q + jnp.where(second, sz.half, 0)
        k = main + lane - jnp.where(second, sz.rest, 0)
        return ((row < length) & (k < length)).astype(F32)

    weights = jnp.concatenate([dot(pick, w, 1, 1).astype(BF16) for w in (gate, value)], axis=0)
    step = 2 if sz.tiles % 2 == 0 else 1
    for tile in range(0, sz.tiles, step):
        n = norm_ref[pl.ds(tile * LANES, step * LANES), :]
        mask = jnp.concatenate([live(tile + s) for s in range(step)], axis=1)
        both = dot(weights, n, 1, 1)
        edge = (sigmoid(both[:ch]) * (both[ch:] * mask)).astype(BF16)
        for g in range(sz.group):
            store(
                g,
                slice(tile * LANES, (tile + step) * LANES),
                edge[g * sz.chans : (g + 1) * sz.chans],
            )


def left_kernel(sz, len_ref, x_ref, ln_ref, w_ref, out_ref, norm_ref):
    ch = sz.channels
    gain = ln_ref[...]
    for row in range(sz.rows):
        normalise(sz, row, x_ref[row].astype(F32), gain, norm_ref)
    r = lax.broadcasted_iota(jnp.int32, (ch, ch), 0)
    e = lax.broadcasted_iota(jnp.int32, (ch, ch), 1)

    def store(g, lanes, edge):
        out_ref[g, :, lanes] = edge
        out_ref[sz.group + g, :, lanes] = edge

    first = position() * sz.rows
    pick = (r == e).astype(BF16)
    project_edges(sz, len_ref[0], first, w_ref[0], w_ref[1], pick, norm_ref, store)


def right_kernel(sz, len_ref, x_ref, far_ref, ln_ref, w_ref, *refs):
    near, (norm_ref, own_ref, far_rows_ref, pair_ref) = refs[: sz.group], refs[sz.group :]
    cd, ch = sz.chans, sz.channels
    gain = ln_ref[...]
    me = position()
    mine = me & (sz.group - 1)
    upper = me >= sz.group
    for row in range(sz.rows):
        x = x_ref[row].astype(F32)
        normalise(sz, row, x, gain, norm_ref)
        rows = pl.ds(row * sz.columns, sz.columns)
        own_ref[rows, :] = jnp.where(upper, x[sz.columns :], x[: sz.columns])
        far_rows_ref[rows, :] = far_ref[row].astype(F32)
    for base, wide_ref in enumerate((own_ref, far_rows_ref)):
        for g in range(sz.group):
            for row in range(sz.rows):
                block = wide_ref[pl.ds(row * sz.columns + g * sz.rows, sz.rows), :]
                pair_ref[base, g, row * sz.rows : (row + 1) * sz.rows, :] = block
    for r in range(sz.group):
        for base in range(2):
            for t in range(sz.block_tiles):
                at = (sz.tiles + base * sz.block_tiles + t) * LANES
                block = pair_ref[base, mine ^ r, t * cd : (t + 1) * cd, :]
                near[r][:, at : at + LANES] = block.astype(BF16)
    r = lax.broadcasted_iota(jnp.int32, (ch, ch), 0)
    e = lax.broadcasted_iota(jnp.int32, (ch, ch), 1)
    pick = (((r // cd) ^ mine) * cd + r % cd == e).astype(BF16)

    def store(g, lanes, edge):
        near[g][:, lanes] = edge

    project_edges(sz, len_ref[0], me * sz.rows, w_ref[2], w_ref[3], pick, norm_ref, store)


def unpack(sz, ref, owner, main_ref, rest_ref):
    cd, w = sz.chans, sz.whole
    for tile in range(sz.tiles):
        block = ref[:, tile * LANES : (tile + 1) * LANES].astype(F32)
        if tile < sz.rows * w:
            row, m = divmod(tile, w)
            main_ref[m, pl.ds(pl.multiple_of((owner * sz.rows + row) * cd, 8), cd), :] = block
        else:
            row = owner * sz.rows + tile - sz.rows * w
            rest_ref[pl.ds(pl.multiple_of(row * cd, 8), cd), :] = block
            rest_ref[pl.ds(pl.multiple_of((row + sz.half) * cd, 8), cd), :] = pltpu.roll(
                block, sz.rest, 1
            )


def matrix(sz, c, size, main_ref, rest_ref):
    cd, w = sz.chans, sz.whole
    parts = [main_ref[m, pl.ds(c, size, stride=cd), :].astype(BF16) for m in range(w)]
    if sz.rest:
        parts.append(rest_ref[pl.ds(c, size, stride=cd), :].astype(BF16)[:, : sz.rest])
    return jnp.concatenate(parts, axis=1) if len(parts) > 1 else parts[0]


def arrange_kernel(sz, *refs):
    near, (out_ref, main_ref, rest_ref) = refs[: sz.group], refs[sz.group :]
    mine = position() & (sz.group - 1)
    for r in range(sz.group):
        unpack(sz, near[r], mine ^ r, main_ref, rest_ref)
    for c in range(sz.chans):
        out_ref[c] = matrix(sz, c, sz.columns, main_ref, rest_ref)


def outer_kernel(
    sz, left_ref, right_ref, out_ref, lmain_ref, lrest_ref, omain_ref, orest_ref
):
    cd, n, w, half = sz.chans, sz.crop, sz.whole, sz.half
    for d in range(sz.devices):
        unpack(sz, left_ref.at[d], jnp.int32(d), lmain_ref, lrest_ref)
    for c in range(cd):
        outer = dot(right_ref[c], matrix(sz, c, n, lmain_ref, lrest_ref), 1, 1)
        for m in range(w):
            omain_ref[m, pl.ds(c, sz.columns, stride=cd), :] = outer[:, m * LANES : (m + 1) * LANES]
        if sz.rest:
            part = outer[:, w * LANES :]
            orest_ref[pl.ds(c, sz.columns, stride=cd), :] = jnp.concatenate([part, part], axis=1)
    low = lax.broadcasted_iota(jnp.int32, (cd, LANES), 1) < sz.rest
    for g in range(sz.group):
        start = g * sz.rows
        for tile in range(sz.tiles):
            if tile < sz.rows * w:
                row, m = divmod(tile, w)
                block = omain_ref[m, pl.ds((start + row) * cd, cd), :]
            else:
                at = start + tile - sz.rows * w
                block = jnp.where(
                    low,
                    orest_ref[pl.ds(at * cd, cd), :],
                    orest_ref[pl.ds((at + half) * cd, cd), :],
                )
            out_ref[g, :, tile * LANES : (tile + 1) * LANES] = block.astype(BF16)


def take_columns(sz, near, cols_ref):
    cd, me = sz.chans, position()
    for r in range(sz.group):
        for base, owner in ((0, me ^ r), (1, me ^ (sz.group + r))):
            for t in range(sz.block_tiles):
                at = (sz.tiles + base * sz.block_tiles + t) * LANES
                rows = pl.ds(pl.multiple_of(owner * sz.block + t * cd, 8), cd)
                cols_ref[rows, :] = near[r][:, at : at + LANES].astype(F32)


def gating_kernel(sz, lnp_ref, gate_ref, *refs):
    near, (gating_ref, cols_ref) = refs[: sz.group], refs[sz.group :]
    take_columns(sz, near, cols_ref)
    for j in range(sz.rows):
        x = cols_ref[pl.ds(j, sz.crop, stride=sz.rows), :]
        normed = norm_last(x, lnp_ref[...]).astype(BF16)
        gating_ref[j] = sigmoid(dot(normed, gate_ref[...], 1, 0)).astype(BF16)


def update_kernel(sz, gating_ref, lnh_ref, tri_ref, lna_ref, biasw_ref, sums_ref, *refs):
    near, (first_ref, col_ref, bias_ref, cols_ref, brow_ref) = refs[: sz.group], refs[sz.group :]
    n, w, half, ch = sz.crop, sz.whole, sz.half, sz.channels
    take_columns(sz, near, cols_ref)
    gain_h = jnp.transpose(jnp.broadcast_to(lnh_ref[...], (ch, ch)))
    tri = tri_ref[...]

    def update(tile):
        block = sums_ref[:, :, tile * LANES : (tile + 1) * LANES].astype(F32).reshape(ch, LANES)
        average = jnp.mean(block, axis=0, keepdims=True)
        centred = block - average
        variance = jnp.mean(centred * centred, axis=0, keepdims=True)
        hidden = (centred * lax.rsqrt(variance + EPS) * gain_h).astype(BF16)
        return dot(hidden, tri, 0, 0)

    rest = [update(sz.rows * w + q) for q in range(half)] if sz.rest else None
    for j in range(sz.rows):
        parts = [update(j * w + m) for m in range(w)]
        if sz.rest:
            h, q = divmod(j, half)
            parts.append(rest[q][h * sz.rest : (h + 1) * sz.rest])
        change = jnp.concatenate(parts, axis=0) if len(parts) > 1 else parts[0]
        x = cols_ref[pl.ds(j, n, stride=sz.rows), :]
        first = (x + gating_ref[j].astype(F32) * change).astype(BF16)
        first_ref[j] = first
        col = norm_last(first.astype(F32), lna_ref[...]).astype(BF16)
        col_ref[j] = col
        heads = biasw_ref.shape[1]
        brow_ref[pl.ds(j * heads, heads), :] = dot(biasw_ref[...], col, 0, 1)
    rows = brow_ref[...]
    part = rows.shape[0] // 2
    one, two = rows[:part], rows[part:]
    message = [one[:, : w * LANES], two[:, : w * LANES]]
    if sz.rest:
        message += [one[:, w * LANES :], two[:, w * LANES :]]
    bias_ref[...] = jnp.concatenate(message, axis=1).astype(BF16)


def project_kernel(sz, col_ref, q_ref, k_ref, v_ref, g_ref, qo_ref, ko_ref, vo_ref, go_ref):
    joined = jnp.concatenate([ref[...] for ref in (q_ref, k_ref, v_ref, g_ref)], axis=1)
    width = q_ref.shape[1]
    for j in range(sz.rows):
        made = dot(col_ref[j], joined, 1, 0)
        qo_ref[j] = made[:, :width].astype(BF16)
        ko_ref[j] = made[:, width : 2 * width].astype(BF16)
        vo_ref[j] = made[:, 2 * width : 3 * width].astype(BF16)
        go_ref[j] = sigmoid(made[:, 3 * width :])


def attend_kernel(
    sz, heads, steps, len_ref, q_ref, k_ref, v_ref, g_ref, first_ref, aout_ref, *refs
):
    bias_refs, (out_ref, rows_ref, bias_ref) = refs[:-3], refs[-3:]
    n, w, ch = sz.crop, sz.whole, sz.channels
    length, me = len_ref[0], position()
    width = q_ref.shape[2]
    hd = width // heads
    per = sz.rows * heads // 2
    for ref, offsets in zip(bias_refs, steps):
        for place, offset in enumerate(offsets):
            block = ref[place].astype(F32) * LOG2E
            for p in range(2):
                at = pl.ds(pl.multiple_of(((me ^ offset) * 2 + p) * per, 8), per)
                for m in range(w):
                    rows_ref[m, at, :] = block[:, (p * w + m) * LANES : (p * w + m + 1) * LANES]
                if sz.rest:
                    tail = block[:, 2 * w * LANES :]
                    rows_ref[w, at, :] = pltpu.roll(tail, sz.rest, 1) if p else tail
    lane = lax.broadcasted_iota(jnp.int32, (1, LANES), 1)
    for m in range(w + (sz.rest > 0)):
        lanes = slice(m * LANES, min((m + 1) * LANES, n))
        dead = jnp.where(m * LANES + lane < length, 0.0, -1e9 * LOG2E).astype(F32)
        for head in range(heads):
            rows = rows_ref[m, pl.ds(head, n, stride=heads), :] + dead
            bias_ref[head, :, lanes] = rows[:, : lanes.stop - lanes.start]
    column = lax.broadcasted_iota(jnp.int32, (1, width), 1)
    head_masks = [(column >= h * hd) & (column < (h + 1) * hd) for h in range(heads)]
    scale = (hd ** (-0.5)) * LOG2E
    ones = jnp.ones((n, width), BF16)

    def score(j):
        query = [q_ref[j] * head_masks[h].astype(BF16) for h in range(heads)]
        return dot(jnp.concatenate(query, axis=0), k_ref[j], 1, 1)

    scores = score(0)
    for j in range(sz.rows):
        now = scores
        if j + 1 < sz.rows:
            scores = score(j + 1)
        weights = []
        for h in range(heads):
            part = now[h * n : (h + 1) * n] * scale + bias_ref[h]
            weights.append(jnp.exp2(part - jnp.max(part, axis=1, keepdims=True)).astype(BF16))
        values = jnp.concatenate([v_ref[j], ones], axis=1)
        mixed = dot(jnp.concatenate(weights, axis=0), values, 1, 0)
        attended, total = mixed[:n, :width], mixed[:n, width:]
        for h in range(1, heads):
            rows = slice(h * n, (h + 1) * n)
            attended = jnp.where(head_masks[h], mixed[rows, :width], attended)
            total = jnp.where(head_masks[h], mixed[rows, width:], total)
        gated = (attended / total * g_ref[j]).astype(BF16)
        out_ref[j] = (first_ref[j].astype(F32) + dot(gated, aout_ref[...], 1, 0)).astype(BF16)


def spread(block, devices):
    pieces, offsets = [block[None]], [[0]]
    bit = devices // 2
    while bit:
        held = jnp.concatenate(pieces, axis=0) if len(pieces) > 1 else pieces[0]
        known = [o for part in offsets for o in part]
        pieces.append(lax.ppermute(held, AXES, [(d, d ^ bit) for d in range(devices)]))
        offsets.append([o ^ bit for o in known])
        bit //= 2
    return pieces, offsets


def shards(
    devices,
    pair_rep, length, ln_pair, tri_in, tri_gate, ln_hidden, tri_out, ln_att,
    att_q, att_k, att_v, att_bias, att_gate, att_out,
):
    rows, crop, ch = pair_rep.shape
    heads = att_bias.shape[1]
    sz = Sizes(rows, crop, devices, ch)
    n, cd = crop, sz.chans
    def bound(kernel, *extra):
        def run(*refs):
            return kernel(sz, *extra, *refs)

        return run

    shape = jax.ShapeDtypeStruct
    g, t, bt = sz.group, sz.tiles, sz.block_tiles

    def slab(tiles, *lead):
        return shape((*lead, cd, tiles * LANES), BF16)

    def send(blocks, offset):
        return [
            block
            if not (offset ^ r)
            else lax.ppermute(block, AXES, [(d, d ^ offset ^ r) for d in range(devices)])
            for r, block in enumerate(blocks)
        ]

    upper = (lax.axis_index(AXES) >= g).astype(jnp.int32)
    far = lax.ppermute(
        lax.dynamic_slice_in_dim(pair_rep, (1 - upper) * sz.columns, sz.columns, 1),
        AXES,
        [(d, d ^ g) for d in range(devices)],
    )
    left = call(
        bound(left_kernel),
        slab(t, devices),
        (length, pair_rep, ln_pair[None], tri_in),
        scratch=[pltpu.VMEM((rows * crop, ch), BF16)],
        smem=(0,),
        name="left",
        vmem=VMEM_MOST,
    )
    others = call(
        bound(right_kernel),
        [slab(t + 2 * bt)] * g,
        (length, pair_rep, far, ln_pair[None], tri_in),
        scratch=[
            pltpu.VMEM((rows * crop, ch), BF16),
            pltpu.VMEM((rows * sz.columns, ch), F32),
            pltpu.VMEM((rows * sz.columns, ch), F32),
            pltpu.VMEM((2, g, bt * cd, ch), F32),
        ],
        smem=(0,),
        name="right",
        cost=pl.CostEstimate(flops=10**11, bytes_accessed=10**6, transcendentals=0),
    )
    left = lax.all_to_all(left, AXES, split_axis=0, concat_axis=0, tiled=True)
    near = send(others, 0)
    rest = sz.rest > 0
    column_rows = sz.columns * cd
    right = call(
        bound(arrange_kernel),
        shape((cd, sz.columns, n), BF16),
        tuple(near),
        scratch=[
            pltpu.VMEM((sz.whole, column_rows, LANES), F32),
            pltpu.VMEM((column_rows if rest else 8, LANES), F32),
        ],
        name="arrange",
    )
    outer = call(
        bound(outer_kernel),
        slab(t, g),
        (left, right),
        scratch=[
            pltpu.VMEM((sz.whole, n * cd, LANES), F32),
            pltpu.VMEM((n * cd if rest else 8, LANES), F32),
            pltpu.VMEM((sz.whole, column_rows, LANES), F32),
            pltpu.VMEM((column_rows if rest else 8, LANES), F32),
        ],
        name="outer",
    )
    sums = lax.all_to_all(
        outer, AXES, split_axis=0, concat_axis=0, tiled=True,
        axis_index_groups=[list(range(g)), list(range(g, devices))],
    )
    gating = call(
        bound(gating_kernel),
        shape((rows, n, ch), BF16),
        (ln_pair[None], tri_gate, *near),
        scratch=[pltpu.VMEM((devices * sz.block + cd, ch), F32)],
        name="gating",
    )
    first, col, bias = call(
        bound(update_kernel),
        [
            shape((rows, n, ch), BF16),
            shape((rows, n, ch), BF16),
            shape((rows * heads // 2, 2 * n), BF16),
        ],
        (
            gating, ln_hidden[None], tri_out, ln_att[None], att_bias, sums, *near,
        ),
        scratch=[
            pltpu.VMEM((devices * sz.block + cd, ch), F32),
            pltpu.VMEM((rows * heads, n), F32),
        ],
        name="update",
    )
    pieces, steps = spread(bias, devices)
    query, key, value, gate = call(
        bound(project_kernel),
        [
            shape((rows, n, att_q.shape[1]), BF16),
            shape((rows, n, att_q.shape[1]), BF16),
            shape((rows, n, att_q.shape[1]), BF16),
            shape((rows, n, att_q.shape[1]), F32),
        ],
        (col, att_q, att_k, att_v, att_gate),
        name="project",
    )
    out = call(
        bound(attend_kernel, heads, steps),
        shape((rows, n, ch), BF16),
        (length, query, key, value, gate, first, att_out, *pieces),
        scratch=[
            pltpu.VMEM((-(-n // LANES), n * heads, LANES), F32),
            pltpu.VMEM((heads, n, n), F32),
        ],
        smem=(0,),
        name="attend",
    )
    return jnp.swapaxes(out, 0, 1)


def solution(mesh):
    devices = mesh.shape["row"] * mesh.shape["node"]

    def body(*args):
        return shards(devices, *args)

    return jax.shard_map(
        body,
        mesh=mesh,
        in_specs=(P(("grp", "row", "node"), None, None), P("grp")) + (P(),) * 12,
        out_specs=P("grp", AXES, None),
        check_vma=False,
    )
```

```python
import jax
import jax.numpy as jnp
from jax import lax
from jax.experimental import pallas as pl
from jax.experimental.pallas import tpu as pltpu
from jax.sharding import PartitionSpec as P

EPS = 1e-05
LANES = 128
LOG2E = 1.4426950408889634
F32 = jnp.float32
BF16 = jnp.bfloat16
AXES = ("row", "node")
VMEM_BYTES = 48 * 1024 * 1024
VMEM_MOST = 60 * 1024 * 1024


def norm_last(values, gain):
    average = jnp.mean(values, axis=-1, keepdims=True)
    centred = values - average
    variance = jnp.mean(centred * centred, axis=-1, keepdims=True)
    return centred * lax.rsqrt(variance + EPS) * gain


def sigmoid(values):
    return 0.5 * jnp.tanh(0.5 * values) + 0.5


def dot(a, b, a_dim, b_dim):
    return lax.dot_general(a, b, (((a_dim,), (b_dim,)), ((), ())), preferred_element_type=F32)


def position():
    return lax.axis_index("row") * lax.axis_size("node") + lax.axis_index("node")


def call(kernel, out_shape, args, scratch=(), smem=(), name=None, vmem=VMEM_BYTES, away=False, cost=None):
    specs = [
        pl.BlockSpec(memory_space=pltpu.SMEM if n in smem else pltpu.VMEM) for n in range(len(args))
    ]
    single = not isinstance(out_shape, (list, tuple))
    inside = pl.BlockSpec(memory_space=pl.ANY if away else pltpu.VMEM)
    return pl.pallas_call(
        kernel,
        out_shape=out_shape,
        in_specs=specs,
        out_specs=inside if single else [inside] * len(out_shape),
        scratch_shapes=list(scratch),
        compiler_params=pltpu.CompilerParams(vmem_limit_bytes=vmem),
        name=name,
        cost_estimate=cost,
    )(*args)


class Sizes:
    def __init__(self, rows, crop, devices, channels):
        self.rows, self.crop, self.devices, self.channels = rows, crop, devices, channels
        self.half = rows // 2
        self.group = devices // 2
        self.partners = [-s % self.group for s in range(self.group)]
        self.columns = rows * self.group
        self.whole = crop // LANES
        self.rest = crop % LANES
        self.tiles = rows * crop // LANES
        self.chans = channels // self.group
        self.block = rows * rows
        self.block_tiles = -(-self.block // self.chans)


def normalise(sz, row, x, gain, norm_ref):
    main = sz.whole * LANES
    normed = norm_last(x, gain).astype(BF16)
    norm_ref[pl.ds(row * main, main), :] = normed[:main]
    if sz.rest:
        h, q = divmod(row, sz.half)
        norm_ref[pl.ds(sz.rows * main + q * LANES + h * sz.rest, sz.rest), :] = normed[main:]


def project_edges(sz, length, first, gate, value, pick, norm_ref, store):
    main, ch = sz.whole * LANES, sz.channels
    lane = lax.broadcasted_iota(jnp.int32, (1, LANES), 1)

    def live(tile):
        if tile < sz.rows * sz.whole:
            row, m = divmod(tile, sz.whole)
            return ((first + row < length) & (m * LANES + lane < length)).astype(F32)
        q = tile - sz.rows * sz.whole
        second = lane >= sz.rest
        row = first + q + jnp.where(second, sz.half, 0)
        k = main + lane - jnp.where(second, sz.rest, 0)
        return ((row < length) & (k < length)).astype(F32)

    weights = jnp.concatenate([dot(pick, w, 1, 1).astype(BF16) for w in (gate, value)], axis=0)
    step = 2 if sz.tiles % 2 == 0 else 1
    for tile in range(0, sz.tiles, step):
        n = norm_ref[pl.ds(tile * LANES, step * LANES), :]
        mask = jnp.concatenate([live(tile + s) for s in range(step)], axis=1)
        both = dot(weights, n, 1, 1)
        edge = (sigmoid(both[:ch]) * (both[ch:] * mask)).astype(BF16)
        for g in range(sz.group):
            store(
                g,
                slice(tile * LANES, (tile + step) * LANES),
                edge[g * sz.chans : (g + 1) * sz.chans],
            )


def left_kernel(sz, len_ref, x_ref, ln_ref, w_ref, out_ref, norm_ref):
    ch = sz.channels
    gain = ln_ref[...]
    for row in range(sz.rows):
        normalise(sz, row, x_ref[row].astype(F32), gain, norm_ref)
    r = lax.broadcasted_iota(jnp.int32, (ch, ch), 0)
    e = lax.broadcasted_iota(jnp.int32, (ch, ch), 1)

    def store(g, lanes, edge):
        out_ref[g, :, lanes] = edge
        out_ref[sz.group + g, :, lanes] = edge

    first = position() * sz.rows
    pick = (r == e).astype(BF16)
    project_edges(sz, len_ref[0], first, w_ref[0], w_ref[1], pick, norm_ref, store)


def right_kernel(sz, len_ref, x_ref, far_ref, ln_ref, w_ref, *refs):
    near, (norm_ref, own_ref, far_rows_ref, pair_ref) = refs[: sz.group], refs[sz.group :]
    cd, ch = sz.chans, sz.channels
    gain = ln_ref[...]
    me = position()
    mine = me & (sz.group - 1)
    upper = me >= sz.group
    for row in range(sz.rows):
        x = x_ref[row].astype(F32)
        normalise(sz, row, x, gain, norm_ref)
        rows = pl.ds(row * sz.columns, sz.columns)
        own_ref[rows, :] = jnp.where(upper, x[sz.columns :], x[: sz.columns])
        far_rows_ref[rows, :] = far_ref[row].astype(F32)
    for base, wide_ref in enumerate((own_ref, far_rows_ref)):
        for g in range(sz.group):
            for row in range(sz.rows):
                block = wide_ref[pl.ds(row * sz.columns + g * sz.rows, sz.rows), :]
                pair_ref[base, g, row * sz.rows : (row + 1) * sz.rows, :] = block
    for slot, partner in enumerate(sz.partners):
        for base in range(2):
            for t in range(sz.block_tiles):
                at = (sz.tiles + base * sz.block_tiles + t) * LANES
                block = pair_ref[base, mine ^ partner, t * cd : (t + 1) * cd, :]
                near[slot][:, at : at + LANES] = block.astype(BF16)
    r = lax.broadcasted_iota(jnp.int32, (ch, ch), 0)
    e = lax.broadcasted_iota(jnp.int32, (ch, ch), 1)
    partner = (sz.group - r // cd) & (sz.group - 1)
    pick = ((partner ^ mine) * cd + r % cd == e).astype(BF16)

    def store(g, lanes, edge):
        near[g][:, lanes] = edge

    project_edges(sz, len_ref[0], me * sz.rows, w_ref[2], w_ref[3], pick, norm_ref, store)


def unpack(sz, ref, owner, main_ref, rest_ref):
    cd, w = sz.chans, sz.whole
    for tile in range(sz.tiles):
        block = ref[:, tile * LANES : (tile + 1) * LANES].astype(F32)
        if tile < sz.rows * w:
            row, m = divmod(tile, w)
            main_ref[m, pl.ds(pl.multiple_of((owner * sz.rows + row) * cd, 8), cd), :] = block
        else:
            row = owner * sz.rows + tile - sz.rows * w
            rest_ref[pl.ds(pl.multiple_of(row * cd, 8), cd), :] = block
            rest_ref[pl.ds(pl.multiple_of((row + sz.half) * cd, 8), cd), :] = pltpu.roll(
                block, sz.rest, 1
            )


def matrix(sz, c, size, main_ref, rest_ref):
    cd, w = sz.chans, sz.whole
    parts = [main_ref[m, pl.ds(c, size, stride=cd), :].astype(BF16) for m in range(w)]
    if sz.rest:
        parts.append(rest_ref[pl.ds(c, size, stride=cd), :].astype(BF16)[:, : sz.rest])
    return jnp.concatenate(parts, axis=1) if len(parts) > 1 else parts[0]


def arrange_kernel(sz, *refs):
    near, (out_ref, main_ref, rest_ref) = refs[: sz.group], refs[sz.group :]
    mine = position() & (sz.group - 1)
    for slot, partner in enumerate(sz.partners):
        unpack(sz, near[slot], mine ^ partner, main_ref, rest_ref)
    for c in range(sz.chans):
        out_ref[c] = matrix(sz, c, sz.columns, main_ref, rest_ref)


def outer_kernel(
    sz, left_ref, right_ref, out_ref, lmain_ref, lrest_ref, omain_ref, orest_ref
):
    cd, n, w, half = sz.chans, sz.crop, sz.whole, sz.half
    for d in range(sz.devices):
        unpack(sz, left_ref.at[d], jnp.int32(d), lmain_ref, lrest_ref)
    for c in range(cd):
        outer = dot(right_ref[c], matrix(sz, c, n, lmain_ref, lrest_ref), 1, 1)
        for m in range(w):
            omain_ref[m, pl.ds(c, sz.columns, stride=cd), :] = outer[:, m * LANES : (m + 1) * LANES]
        if sz.rest:
            part = outer[:, w * LANES :]
            orest_ref[pl.ds(c, sz.columns, stride=cd), :] = jnp.concatenate([part, part], axis=1)
    low = lax.broadcasted_iota(jnp.int32, (cd, LANES), 1) < sz.rest
    for g in range(sz.group):
        start = g * sz.rows
        for tile in range(sz.tiles):
            if tile < sz.rows * w:
                row, m = divmod(tile, w)
                block = omain_ref[m, pl.ds((start + row) * cd, cd), :]
            else:
                at = start + tile - sz.rows * w
                block = jnp.where(
                    low,
                    orest_ref[pl.ds(at * cd, cd), :],
                    orest_ref[pl.ds((at + half) * cd, cd), :],
                )
            out_ref[g, :, tile * LANES : (tile + 1) * LANES] = block.astype(BF16)


def take_columns(sz, near, cols_ref):
    cd, me = sz.chans, position()
    for slot, partner in enumerate(sz.partners):
        for base, owner in ((0, me ^ partner), (1, me ^ (sz.group + partner))):
            for t in range(sz.block_tiles):
                at = (sz.tiles + base * sz.block_tiles + t) * LANES
                rows = pl.ds(pl.multiple_of(owner * sz.block + t * cd, 8), cd)
                cols_ref[rows, :] = near[slot][:, at : at + LANES].astype(F32)


def gating_kernel(sz, lnp_ref, gate_ref, *refs):
    near, (gating_ref, cols_ref) = refs[: sz.group], refs[sz.group :]
    take_columns(sz, near, cols_ref)
    for j in range(sz.rows):
        x = cols_ref[pl.ds(j, sz.crop, stride=sz.rows), :]
        normed = norm_last(x, lnp_ref[...]).astype(BF16)
        gating_ref[j] = sigmoid(dot(normed, gate_ref[...], 1, 0)).astype(BF16)


def update_kernel(sz, gating_ref, lnh_ref, tri_ref, lna_ref, biasw_ref, sums_ref, *refs):
    near, (first_ref, col_ref, bias_ref, cols_ref, brow_ref) = refs[: sz.group], refs[sz.group :]
    n, w, half, ch = sz.crop, sz.whole, sz.half, sz.channels
    take_columns(sz, near, cols_ref)
    gain_h = jnp.transpose(jnp.broadcast_to(lnh_ref[...], (ch, ch)))
    tri = tri_ref[...]

    def update(tile):
        block = sums_ref[:, :, tile * LANES : (tile + 1) * LANES].astype(F32).reshape(ch, LANES)
        average = jnp.mean(block, axis=0, keepdims=True)
        centred = block - average
        variance = jnp.mean(centred * centred, axis=0, keepdims=True)
        hidden = (centred * lax.rsqrt(variance + EPS) * gain_h).astype(BF16)
        return dot(hidden, tri, 0, 0)

    rest = [update(sz.rows * w + q) for q in range(half)] if sz.rest else None
    for j in range(sz.rows):
        parts = [update(j * w + m) for m in range(w)]
        if sz.rest:
            h, q = divmod(j, half)
            parts.append(rest[q][h * sz.rest : (h + 1) * sz.rest])
        change = jnp.concatenate(parts, axis=0) if len(parts) > 1 else parts[0]
        x = cols_ref[pl.ds(j, n, stride=sz.rows), :]
        first = (x + gating_ref[j].astype(F32) * change).astype(BF16)
        first_ref[j] = first
        col = norm_last(first.astype(F32), lna_ref[...]).astype(BF16)
        col_ref[j] = col
        heads = biasw_ref.shape[1]
        brow_ref[pl.ds(j * heads, heads), :] = dot(biasw_ref[...], col, 0, 1)
    rows = brow_ref[...]
    part = rows.shape[0] // 2
    one, two = rows[:part], rows[part:]
    message = [one[:, : w * LANES], two[:, : w * LANES]]
    if sz.rest:
        message += [one[:, w * LANES :], two[:, w * LANES :]]
    bias_ref[...] = jnp.concatenate(message, axis=1).astype(BF16)


def project_kernel(sz, col_ref, q_ref, k_ref, v_ref, g_ref, qo_ref, ko_ref, vo_ref, go_ref):
    joined = jnp.concatenate([ref[...] for ref in (q_ref, k_ref, v_ref, g_ref)], axis=1)
    width = q_ref.shape[1]
    for j in range(sz.rows):
        made = dot(col_ref[j], joined, 1, 0)
        qo_ref[j] = made[:, :width].astype(BF16)
        ko_ref[j] = made[:, width : 2 * width].astype(BF16)
        vo_ref[j] = made[:, 2 * width : 3 * width].astype(BF16)
        go_ref[j] = sigmoid(made[:, 3 * width :])


def attend_kernel(
    sz, heads, steps, len_ref, q_ref, k_ref, v_ref, g_ref, first_ref, aout_ref, *refs
):
    bias_refs, (out_ref, rows_ref, bias_ref) = refs[:-3], refs[-3:]
    n, w, ch = sz.crop, sz.whole, sz.channels
    length, me = len_ref[0], position()
    width = q_ref.shape[2]
    hd = width // heads
    per = sz.rows * heads // 2
    for ref, offsets in zip(bias_refs, steps):
        for place, offset in enumerate(offsets):
            block = ref[place].astype(F32) * LOG2E
            for p in range(2):
                at = pl.ds(pl.multiple_of(((me ^ offset) * 2 + p) * per, 8), per)
                for m in range(w):
                    rows_ref[m, at, :] = block[:, (p * w + m) * LANES : (p * w + m + 1) * LANES]
                if sz.rest:
                    tail = block[:, 2 * w * LANES :]
                    rows_ref[w, at, :] = pltpu.roll(tail, sz.rest, 1) if p else tail
    lane = lax.broadcasted_iota(jnp.int32, (1, LANES), 1)
    for m in range(w + (sz.rest > 0)):
        lanes = slice(m * LANES, min((m + 1) * LANES, n))
        dead = jnp.where(m * LANES + lane < length, 0.0, -1e9 * LOG2E).astype(F32)
        for head in range(heads):
            rows = rows_ref[m, pl.ds(head, n, stride=heads), :] + dead
            bias_ref[head, :, lanes] = rows[:, : lanes.stop - lanes.start]
    column = lax.broadcasted_iota(jnp.int32, (1, width), 1)
    head_masks = [(column >= h * hd) & (column < (h + 1) * hd) for h in range(heads)]
    scale = (hd ** (-0.5)) * LOG2E
    ones = jnp.ones((n, width), BF16)

    def score(j):
        query = [q_ref[j] * head_masks[h].astype(BF16) for h in range(heads)]
        return dot(jnp.concatenate(query, axis=0), k_ref[j], 1, 1)

    scores = score(0)
    for j in range(sz.rows):
        now = scores
        if j + 1 < sz.rows:
            scores = score(j + 1)
        weights = []
        for h in range(heads):
            part = now[h * n : (h + 1) * n] * scale + bias_ref[h]
            weights.append(jnp.exp2(part - jnp.max(part, axis=1, keepdims=True)).astype(BF16))
        values = jnp.concatenate([v_ref[j], ones], axis=1)
        mixed = dot(jnp.concatenate(weights, axis=0), values, 1, 0)
        attended, total = mixed[:n, :width], mixed[:n, width:]
        for h in range(1, heads):
            rows = slice(h * n, (h + 1) * n)
            attended = jnp.where(head_masks[h], mixed[rows, :width], attended)
            total = jnp.where(head_masks[h], mixed[rows, width:], total)
        gated = (attended / total * g_ref[j]).astype(BF16)
        out_ref[j] = (first_ref[j].astype(F32) + dot(gated, aout_ref[...], 1, 0)).astype(BF16)


def spread(block, devices):
    pieces, offsets = [block[None]], [[0]]
    bit = devices // 2
    while bit:
        held = jnp.concatenate(pieces, axis=0) if len(pieces) > 1 else pieces[0]
        known = [o for part in offsets for o in part]
        pieces.append(lax.ppermute(held, AXES, [(d, d ^ bit) for d in range(devices)]))
        offsets.append([o ^ bit for o in known])
        bit //= 2
    return pieces, offsets


def shards(
    devices,
    pair_rep, length, ln_pair, tri_in, tri_gate, ln_hidden, tri_out, ln_att,
    att_q, att_k, att_v, att_bias, att_gate, att_out,
):
    rows, crop, ch = pair_rep.shape
    heads = att_bias.shape[1]
    sz = Sizes(rows, crop, devices, ch)
    n, cd = crop, sz.chans
    def bound(kernel, *extra):
        def run(*refs):
            return kernel(sz, *extra, *refs)

        return run

    shape = jax.ShapeDtypeStruct
    g, t, bt = sz.group, sz.tiles, sz.block_tiles

    def slab(tiles, *lead):
        return shape((*lead, cd, tiles * LANES), BF16)

    def send(blocks):
        return [
            lax.ppermute(block, AXES, [(d, d ^ partner) for d in range(devices)])
            if partner
            else block
            for partner, block in zip(sz.partners, blocks)
        ]

    upper = (lax.axis_index(AXES) >= g).astype(jnp.int32)
    far = lax.ppermute(
        lax.dynamic_slice_in_dim(pair_rep, (1 - upper) * sz.columns, sz.columns, 1),
        AXES,
        [(d, d ^ g) for d in range(devices)],
    )
    left = call(
        bound(left_kernel),
        slab(t, devices),
        (length, pair_rep, ln_pair[None], tri_in),
        scratch=[pltpu.VMEM((rows * crop, ch), BF16)],
        smem=(0,),
        name="left",
        vmem=VMEM_MOST,
    )
    others = call(
        bound(right_kernel),
        [slab(t + 2 * bt)] * g,
        (length, pair_rep, far, ln_pair[None], tri_in),
        scratch=[
            pltpu.VMEM((rows * crop, ch), BF16),
            pltpu.VMEM((rows * sz.columns, ch), F32),
            pltpu.VMEM((rows * sz.columns, ch), F32),
            pltpu.VMEM((2, g, bt * cd, ch), F32),
        ],
        smem=(0,),
        name="right",
        cost=pl.CostEstimate(flops=10**11, bytes_accessed=10**6, transcendentals=0),
    )
    left = lax.all_to_all(left, AXES, split_axis=0, concat_axis=0, tiled=True)
    near = send(others)
    rest = sz.rest > 0
    column_rows = sz.columns * cd
    right = call(
        bound(arrange_kernel),
        shape((cd, sz.columns, n), BF16),
        tuple(near),
        scratch=[
            pltpu.VMEM((sz.whole, column_rows, LANES), F32),
            pltpu.VMEM((column_rows if rest else 8, LANES), F32),
        ],
        name="arrange",
    )
    outer = call(
        bound(outer_kernel),
        slab(t, g),
        (left, right),
        scratch=[
            pltpu.VMEM((sz.whole, n * cd, LANES), F32),
            pltpu.VMEM((n * cd if rest else 8, LANES), F32),
            pltpu.VMEM((sz.whole, column_rows, LANES), F32),
            pltpu.VMEM((column_rows if rest else 8, LANES), F32),
        ],
        name="outer",
    )
    sums = lax.all_to_all(
        outer, AXES, split_axis=0, concat_axis=0, tiled=True,
        axis_index_groups=[list(range(g)), list(range(g, devices))],
    )
    gating = call(
        bound(gating_kernel),
        shape((rows, n, ch), BF16),
        (ln_pair[None], tri_gate, *near),
        scratch=[pltpu.VMEM((devices * sz.block + cd, ch), F32)],
        name="gating",
    )
    first, col, bias = call(
        bound(update_kernel),
        [
            shape((rows, n, ch), BF16),
            shape((rows, n, ch), BF16),
            shape((rows * heads // 2, 2 * n), BF16),
        ],
        (
            gating, ln_hidden[None], tri_out, ln_att[None], att_bias, sums, *near,
        ),
        scratch=[
            pltpu.VMEM((devices * sz.block + cd, ch), F32),
            pltpu.VMEM((rows * heads, n), F32),
        ],
        name="update",
    )
    pieces, steps = spread(bias, devices)
    query, key, value, gate = call(
        bound(project_kernel),
        [
            shape((rows, n, att_q.shape[1]), BF16),
            shape((rows, n, att_q.shape[1]), BF16),
            shape((rows, n, att_q.shape[1]), BF16),
            shape((rows, n, att_q.shape[1]), F32),
        ],
        (col, att_q, att_k, att_v, att_gate),
        name="project",
    )
    out = call(
        bound(attend_kernel, heads, steps),
        shape((rows, n, ch), BF16),
        (length, query, key, value, gate, first, att_out, *pieces),
        scratch=[
            pltpu.VMEM((-(-n // LANES), n * heads, LANES), F32),
            pltpu.VMEM((heads, n, n), F32),
        ],
        smem=(0,),
        name="attend",
    )
    return jnp.swapaxes(out, 0, 1)


def solution(mesh):
    devices = mesh.shape["row"] * mesh.shape["node"]

    def body(*args):
        return shards(devices, *args)

    return jax.shard_map(
        body,
        mesh=mesh,
        in_specs=(P(("grp", "row", "node"), None, None), P("grp")) + (P(),) * 12,
        out_specs=P("grp", AXES, None),
        check_vma=False,
    )
```

```python
import jax
import jax.numpy as jnp
from jax import lax
from jax.experimental import pallas as pl
from jax.experimental.pallas import tpu as pltpu
from jax.sharding import PartitionSpec as P

EPS = 1e-05
LANES = 128
LOG2E = 1.4426950408889634
F32 = jnp.float32
BF16 = jnp.bfloat16
AXES = ("row", "node")
VMEM_BYTES = 48 * 1024 * 1024


def norm_last(values, gain):
    average = jnp.mean(values, axis=-1, keepdims=True)
    centred = values - average
    variance = jnp.mean(centred * centred, axis=-1, keepdims=True)
    return centred * lax.rsqrt(variance + EPS) * gain


def sigmoid(values):
    return 0.5 * jnp.tanh(0.5 * values) + 0.5


def dot(a, b, a_dim, b_dim):
    return lax.dot_general(a, b, (((a_dim,), (b_dim,)), ((), ())), preferred_element_type=F32)


def position():
    return lax.axis_index("row") * lax.axis_size("node") + lax.axis_index("node")


def call(kernel, out_shape, args, scratch=(), smem=(), name=None, vmem=VMEM_BYTES, away=False, cost=None):
    specs = [
        pl.BlockSpec(memory_space=pltpu.SMEM if n in smem else pltpu.VMEM) for n in range(len(args))
    ]
    single = not isinstance(out_shape, (list, tuple))
    inside = pl.BlockSpec(memory_space=pl.ANY if away else pltpu.VMEM)
    return pl.pallas_call(
        kernel,
        out_shape=out_shape,
        in_specs=specs,
        out_specs=inside if single else [inside] * len(out_shape),
        scratch_shapes=list(scratch),
        compiler_params=pltpu.CompilerParams(vmem_limit_bytes=vmem),
        name=name,
        cost_estimate=cost,
    )(*args)


class Sizes:
    def __init__(self, rows, crop, devices, channels):
        self.rows, self.crop, self.devices, self.channels = rows, crop, devices, channels
        self.half = rows // 2
        self.group = devices // 2
        self.partners = [-s % self.group for s in range(self.group)]
        self.columns = rows * self.group
        self.whole = crop // LANES
        self.rest = crop % LANES
        self.tiles = rows * crop // LANES
        self.chans = channels // self.group
        self.block = rows * rows
        self.block_tiles = -(-self.block // self.chans)


def normalise(sz, row, x, gain, norm_ref):
    main = sz.whole * LANES
    normed = norm_last(x, gain).astype(BF16)
    norm_ref[pl.ds(row * main, main), :] = normed[:main]
    if sz.rest:
        h, q = divmod(row, sz.half)
        norm_ref[pl.ds(sz.rows * main + q * LANES + h * sz.rest, sz.rest), :] = normed[main:]


def project_edges(sz, length, first, gate, value, pick, norm_ref, store):
    main, ch = sz.whole * LANES, sz.channels
    lane = lax.broadcasted_iota(jnp.int32, (1, LANES), 1)

    def live(tile):
        if tile < sz.rows * sz.whole:
            row, m = divmod(tile, sz.whole)
            return ((first + row < length) & (m * LANES + lane < length)).astype(F32)
        q = tile - sz.rows * sz.whole
        second = lane >= sz.rest
        row = first + q + jnp.where(second, sz.half, 0)
        k = main + lane - jnp.where(second, sz.rest, 0)
        return ((row < length) & (k < length)).astype(F32)

    weights = jnp.concatenate([dot(pick, w, 1, 1).astype(BF16) for w in (gate, value)], axis=0)
    step = 2 if sz.tiles % 2 == 0 else 1
    for tile in range(0, sz.tiles, step):
        n = norm_ref[pl.ds(tile * LANES, step * LANES), :]
        mask = jnp.concatenate([live(tile + s) for s in range(step)], axis=1)
        both = dot(weights, n, 1, 1)
        edge = (sigmoid(both[:ch]) * (both[ch:] * mask)).astype(BF16)
        for g in range(sz.group):
            store(
                g,
                slice(tile * LANES, (tile + step) * LANES),
                edge[g * sz.chans : (g + 1) * sz.chans],
            )


def left_kernel(sz, len_ref, x_ref, ln_ref, w_ref, out_ref, norm_ref):
    ch = sz.channels
    gain = ln_ref[...]
    for row in range(sz.rows):
        normalise(sz, row, x_ref[row].astype(F32), gain, norm_ref)
    r = lax.broadcasted_iota(jnp.int32, (ch, ch), 0)
    e = lax.broadcasted_iota(jnp.int32, (ch, ch), 1)

    def store(g, lanes, edge):
        out_ref[g, :, lanes] = edge
        out_ref[sz.group + g, :, lanes] = edge

    first = position() * sz.rows
    pick = (r == e).astype(BF16)
    project_edges(sz, len_ref[0], first, w_ref[0], w_ref[1], pick, norm_ref, store)


def right_kernel(sz, len_ref, x_ref, far_ref, ln_ref, w_ref, *refs):
    near, (norm_ref, own_ref, far_rows_ref, pair_ref) = refs[: sz.group], refs[sz.group :]
    cd, ch = sz.chans, sz.channels
    gain = ln_ref[...]
    me = position()
    mine = me & (sz.group - 1)
    upper = me >= sz.group
    for row in range(sz.rows):
        x = x_ref[row].astype(F32)
        normalise(sz, row, x, gain, norm_ref)
        rows = pl.ds(row * sz.columns, sz.columns)
        own_ref[rows, :] = jnp.where(upper, x[sz.columns :], x[: sz.columns])
        far_rows_ref[rows, :] = far_ref[row].astype(F32)
    for base, wide_ref in enumerate((own_ref, far_rows_ref)):
        for g in range(sz.group):
            for row in range(sz.rows):
                block = wide_ref[pl.ds(row * sz.columns + g * sz.rows, sz.rows), :]
                pair_ref[base, g, row * sz.rows : (row + 1) * sz.rows, :] = block
    for slot, partner in enumerate(sz.partners):
        for base in range(2):
            for t in range(sz.block_tiles):
                at = (sz.tiles + base * sz.block_tiles + t) * LANES
                block = pair_ref[base, mine ^ partner, t * cd : (t + 1) * cd, :]
                near[slot][:, at : at + LANES] = block.astype(BF16)
    r = lax.broadcasted_iota(jnp.int32, (ch, ch), 0)
    e = lax.broadcasted_iota(jnp.int32, (ch, ch), 1)
    partner = (sz.group - r // cd) & (sz.group - 1)
    pick = ((partner ^ mine) * cd + r % cd == e).astype(BF16)

    def store(g, lanes, edge):
        near[g][:, lanes] = edge

    project_edges(sz, len_ref[0], me * sz.rows, w_ref[2], w_ref[3], pick, norm_ref, store)


def unpack(sz, ref, owner, main_ref, rest_ref):
    cd, w = sz.chans, sz.whole
    for tile in range(sz.tiles):
        block = ref[:, tile * LANES : (tile + 1) * LANES].astype(F32)
        if tile < sz.rows * w:
            row, m = divmod(tile, w)
            main_ref[m, pl.ds(pl.multiple_of((owner * sz.rows + row) * cd, 8), cd), :] = block
        else:
            row = owner * sz.rows + tile - sz.rows * w
            rest_ref[pl.ds(pl.multiple_of(row * cd, 8), cd), :] = block
            rest_ref[pl.ds(pl.multiple_of((row + sz.half) * cd, 8), cd), :] = pltpu.roll(
                block, sz.rest, 1
            )


def matrix(sz, c, size, main_ref, rest_ref):
    cd, w = sz.chans, sz.whole
    parts = [main_ref[m, pl.ds(c, size, stride=cd), :].astype(BF16) for m in range(w)]
    if sz.rest:
        parts.append(rest_ref[pl.ds(c, size, stride=cd), :].astype(BF16)[:, : sz.rest])
    return jnp.concatenate(parts, axis=1) if len(parts) > 1 else parts[0]


def arrange_kernel(sz, *refs):
    near, (out_ref, main_ref, rest_ref) = refs[: sz.group], refs[sz.group :]
    mine = position() & (sz.group - 1)
    for slot, partner in enumerate(sz.partners):
        unpack(sz, near[slot], mine ^ partner, main_ref, rest_ref)
    for c in range(sz.chans):
        out_ref[c] = matrix(sz, c, sz.columns, main_ref, rest_ref)


def outer_kernel(
    sz, left_ref, right_ref, out_ref, lmain_ref, lrest_ref, omain_ref, orest_ref
):
    cd, n, w, half = sz.chans, sz.crop, sz.whole, sz.half
    for d in range(sz.devices):
        unpack(sz, left_ref.at[d], jnp.int32(d), lmain_ref, lrest_ref)
    for c in range(cd):
        outer = dot(right_ref[c], matrix(sz, c, n, lmain_ref, lrest_ref), 1, 1)
        for m in range(w):
            omain_ref[m, pl.ds(c, sz.columns, stride=cd), :] = outer[:, m * LANES : (m + 1) * LANES]
        if sz.rest:
            part = outer[:, w * LANES :]
            orest_ref[pl.ds(c, sz.columns, stride=cd), :] = jnp.concatenate([part, part], axis=1)
    low = lax.broadcasted_iota(jnp.int32, (cd, LANES), 1) < sz.rest
    for g in range(sz.group):
        start = g * sz.rows
        for tile in range(sz.tiles):
            if tile < sz.rows * w:
                row, m = divmod(tile, w)
                block = omain_ref[m, pl.ds((start + row) * cd, cd), :]
            else:
                at = start + tile - sz.rows * w
                block = jnp.where(
                    low,
                    orest_ref[pl.ds(at * cd, cd), :],
                    orest_ref[pl.ds((at + half) * cd, cd), :],
                )
            out_ref[g, :, tile * LANES : (tile + 1) * LANES] = block.astype(BF16)


def take_columns(sz, near, cols_ref):
    cd, me = sz.chans, position()
    for slot, partner in enumerate(sz.partners):
        for base, owner in ((0, me ^ partner), (1, me ^ (sz.group + partner))):
            for t in range(sz.block_tiles):
                at = (sz.tiles + base * sz.block_tiles + t) * LANES
                rows = pl.ds(pl.multiple_of(owner * sz.block + t * cd, 8), cd)
                cols_ref[rows, :] = near[slot][:, at : at + LANES].astype(F32)


def gating_kernel(sz, lnp_ref, gate_ref, *refs):
    near, (x_ref, gating_ref, cols_ref) = refs[: sz.group], refs[sz.group :]
    take_columns(sz, near, cols_ref)
    for j in range(sz.rows):
        x = cols_ref[pl.ds(j, sz.crop, stride=sz.rows), :]
        x_ref[j] = x.astype(BF16)
        normed = norm_last(x, lnp_ref[...]).astype(BF16)
        gating_ref[j] = sigmoid(dot(normed, gate_ref[...], 1, 0)).astype(BF16)


def update_kernel(
    sz, x_ref, gating_ref, lnh_ref, tri_ref, lna_ref, biasw_ref, sums_ref,
    first_ref, col_ref, bias_ref, brow_ref,
):
    n, w, half, ch = sz.crop, sz.whole, sz.half, sz.channels
    gain_h = jnp.transpose(jnp.broadcast_to(lnh_ref[...], (ch, ch)))
    tri = tri_ref[...]

    def update(tile):
        block = sums_ref[:, :, tile * LANES : (tile + 1) * LANES].astype(F32).reshape(ch, LANES)
        average = jnp.mean(block, axis=0, keepdims=True)
        centred = block - average
        variance = jnp.mean(centred * centred, axis=0, keepdims=True)
        hidden = (centred * lax.rsqrt(variance + EPS) * gain_h).astype(BF16)
        return dot(hidden, tri, 0, 0)

    rest = [update(sz.rows * w + q) for q in range(half)] if sz.rest else None
    for j in range(sz.rows):
        parts = [update(j * w + m) for m in range(w)]
        if sz.rest:
            h, q = divmod(j, half)
            parts.append(rest[q][h * sz.rest : (h + 1) * sz.rest])
        change = jnp.concatenate(parts, axis=0) if len(parts) > 1 else parts[0]
        first = (x_ref[j].astype(F32) + gating_ref[j].astype(F32) * change).astype(BF16)
        first_ref[j] = first
        col = norm_last(first.astype(F32), lna_ref[...]).astype(BF16)
        col_ref[j] = col
        heads = biasw_ref.shape[1]
        brow_ref[pl.ds(j * heads, heads), :] = dot(biasw_ref[...], col, 0, 1)
    rows = brow_ref[...]
    part = rows.shape[0] // 2
    one, two = rows[:part], rows[part:]
    message = [one[:, : w * LANES], two[:, : w * LANES]]
    if sz.rest:
        message += [one[:, w * LANES :], two[:, w * LANES :]]
    bias_ref[...] = jnp.concatenate(message, axis=1).astype(BF16)


def project_kernel(sz, col_ref, q_ref, k_ref, v_ref, g_ref, qo_ref, ko_ref, vo_ref, go_ref):
    joined = jnp.concatenate([ref[...] for ref in (q_ref, k_ref, v_ref, g_ref)], axis=1)
    width = q_ref.shape[1]
    for j in range(sz.rows):
        made = dot(col_ref[j], joined, 1, 0)
        qo_ref[j] = made[:, :width].astype(BF16)
        ko_ref[j] = made[:, width : 2 * width].astype(BF16)
        vo_ref[j] = made[:, 2 * width : 3 * width].astype(BF16)
        go_ref[j] = sigmoid(made[:, 3 * width :])


def attend_kernel(
    sz, heads, steps, len_ref, q_ref, k_ref, v_ref, g_ref, first_ref, aout_ref, *refs
):
    bias_refs, (out_ref, rows_ref, bias_ref) = refs[:-3], refs[-3:]
    n, w, ch = sz.crop, sz.whole, sz.channels
    length, me = len_ref[0], position()
    width = q_ref.shape[2]
    hd = width // heads
    per = sz.rows * heads // 2
    for ref, offsets in zip(bias_refs, steps):
        for place, offset in enumerate(offsets):
            block = ref[place].astype(F32) * LOG2E
            for p in range(2):
                at = pl.ds(pl.multiple_of(((me ^ offset) * 2 + p) * per, 8), per)
                for m in range(w):
                    rows_ref[m, at, :] = block[:, (p * w + m) * LANES : (p * w + m + 1) * LANES]
                if sz.rest:
                    tail = block[:, 2 * w * LANES :]
                    rows_ref[w, at, :] = pltpu.roll(tail, sz.rest, 1) if p else tail
    lane = lax.broadcasted_iota(jnp.int32, (1, LANES), 1)
    for m in range(w + (sz.rest > 0)):
        lanes = slice(m * LANES, min((m + 1) * LANES, n))
        dead = jnp.where(m * LANES + lane < length, 0.0, -1e9 * LOG2E).astype(F32)
        for head in range(heads):
            rows = rows_ref[m, pl.ds(head, n, stride=heads), :] + dead
            bias_ref[head, :, lanes] = rows[:, : lanes.stop - lanes.start]
    column = lax.broadcasted_iota(jnp.int32, (1, width), 1)
    head_masks = [(column >= h * hd) & (column < (h + 1) * hd) for h in range(heads)]
    scale = (hd ** (-0.5)) * LOG2E
    ones = jnp.ones((n, width), BF16)

    def score(j):
        query = [q_ref[j] * head_masks[h].astype(BF16) for h in range(heads)]
        return dot(jnp.concatenate(query, axis=0), k_ref[j], 1, 1)

    scores = score(0)
    for j in range(sz.rows):
        now = scores
        if j + 1 < sz.rows:
            scores = score(j + 1)
        weights = []
        for h in range(heads):
            part = now[h * n : (h + 1) * n] * scale + bias_ref[h]
            weights.append(jnp.exp2(part - jnp.max(part, axis=1, keepdims=True)).astype(BF16))
        values = jnp.concatenate([v_ref[j], ones], axis=1)
        mixed = dot(jnp.concatenate(weights, axis=0), values, 1, 0)
        attended, total = mixed[:n, :width], mixed[:n, width:]
        for h in range(1, heads):
            rows = slice(h * n, (h + 1) * n)
            attended = jnp.where(head_masks[h], mixed[rows, :width], attended)
            total = jnp.where(head_masks[h], mixed[rows, width:], total)
        gated = (attended / total * g_ref[j]).astype(BF16)
        out_ref[j] = (first_ref[j].astype(F32) + dot(gated, aout_ref[...], 1, 0)).astype(BF16)


def spread(block, devices):
    pieces, offsets = [block[None]], [[0]]
    bit = devices // 2
    while bit:
        held = jnp.concatenate(pieces, axis=0) if len(pieces) > 1 else pieces[0]
        known = [o for part in offsets for o in part]
        pieces.append(lax.ppermute(held, AXES, [(d, d ^ bit) for d in range(devices)]))
        offsets.append([o ^ bit for o in known])
        bit //= 2
    return pieces, offsets


def shards(
    devices,
    pair_rep, length, ln_pair, tri_in, tri_gate, ln_hidden, tri_out, ln_att,
    att_q, att_k, att_v, att_bias, att_gate, att_out,
):
    rows, crop, ch = pair_rep.shape
    heads = att_bias.shape[1]
    sz = Sizes(rows, crop, devices, ch)
    n, cd = crop, sz.chans
    def bound(kernel, *extra):
        def run(*refs):
            return kernel(sz, *extra, *refs)

        return run

    shape = jax.ShapeDtypeStruct
    g, t, bt = sz.group, sz.tiles, sz.block_tiles

    def slab(tiles, *lead):
        return shape((*lead, cd, tiles * LANES), BF16)

    def send(blocks):
        return [
            lax.ppermute(block, AXES, [(d, d ^ partner) for d in range(devices)])
            if partner
            else block
            for partner, block in zip(sz.partners, blocks)
        ]

    upper = (lax.axis_index(AXES) >= g).astype(jnp.int32)
    far = lax.ppermute(
        lax.dynamic_slice_in_dim(pair_rep, (1 - upper) * sz.columns, sz.columns, 1),
        AXES,
        [(d, d ^ g) for d in range(devices)],
    )
    left = call(
        bound(left_kernel),
        slab(t, devices),
        (length, pair_rep, ln_pair[None], tri_in),
        scratch=[pltpu.VMEM((rows * crop, ch), BF16)],
        smem=(0,),
        name="left",
    )
    others = call(
        bound(right_kernel),
        [slab(t + 2 * bt)] * g,
        (length, pair_rep, far, ln_pair[None], tri_in),
        scratch=[
            pltpu.VMEM((rows * crop, ch), BF16),
            pltpu.VMEM((rows * sz.columns, ch), F32),
            pltpu.VMEM((rows * sz.columns, ch), F32),
            pltpu.VMEM((2, g, bt * cd, ch), F32),
        ],
        smem=(0,),
        name="right",
        cost=pl.CostEstimate(flops=10**11, bytes_accessed=10**6, transcendentals=0),
    )
    left = lax.all_to_all(left, AXES, split_axis=0, concat_axis=0, tiled=True)
    near = send(others)
    rest = sz.rest > 0
    column_rows = sz.columns * cd
    right = call(
        bound(arrange_kernel),
        shape((cd, sz.columns, n), BF16),
        tuple(near),
        scratch=[
            pltpu.VMEM((sz.whole, column_rows, LANES), F32),
            pltpu.VMEM((column_rows if rest else 8, LANES), F32),
        ],
        name="arrange",
    )
    outer = call(
        bound(outer_kernel),
        slab(t, g),
        (left, right),
        scratch=[
            pltpu.VMEM((sz.whole, n * cd, LANES), F32),
            pltpu.VMEM((n * cd if rest else 8, LANES), F32),
            pltpu.VMEM((sz.whole, column_rows, LANES), F32),
            pltpu.VMEM((column_rows if rest else 8, LANES), F32),
        ],
        name="outer",
    )
    sums = lax.all_to_all(
        outer, AXES, split_axis=0, concat_axis=0, tiled=True,
        axis_index_groups=[list(range(g)), list(range(g, devices))],
    )
    columns, gating = call(
        bound(gating_kernel),
        [shape((rows, n, ch), BF16)] * 2,
        (ln_pair[None], tri_gate, *near),
        scratch=[pltpu.VMEM((devices * sz.block + cd, ch), F32)],
        name="gating",
    )
    first, col, bias = call(
        bound(update_kernel),
        [
            shape((rows, n, ch), BF16),
            shape((rows, n, ch), BF16),
            shape((rows * heads // 2, 2 * n), BF16),
        ],
        (
            columns, gating, ln_hidden[None], tri_out, ln_att[None], att_bias, sums,
        ),
        scratch=[pltpu.VMEM((rows * heads, n), F32)],
        name="update",
    )
    pieces, steps = spread(bias, devices)
    query, key, value, gate = call(
        bound(project_kernel),
        [
            shape((rows, n, att_q.shape[1]), BF16),
            shape((rows, n, att_q.shape[1]), BF16),
            shape((rows, n, att_q.shape[1]), BF16),
            shape((rows, n, att_q.shape[1]), F32),
        ],
        (col, att_q, att_k, att_v, att_gate),
        name="project",
    )
    out = call(
        bound(attend_kernel, heads, steps),
        shape((rows, n, ch), BF16),
        (length, query, key, value, gate, first, att_out, *pieces),
        scratch=[
            pltpu.VMEM((-(-n // LANES), n * heads, LANES), F32),
            pltpu.VMEM((heads, n, n), F32),
        ],
        smem=(0,),
        name="attend",
    )
    return jnp.swapaxes(out, 0, 1)


def solution(mesh):
    devices = mesh.shape["row"] * mesh.shape["node"]

    def body(*args):
        return shards(devices, *args)

    return jax.shard_map(
        body,
        mesh=mesh,
        in_specs=(P(("grp", "row", "node"), None, None), P("grp")) + (P(),) * 12,
        out_specs=P("grp", AXES, None),
        check_vma=False,
    )
```

```python
import jax
import jax.numpy as jnp
from jax import lax
from jax.experimental import pallas as pl
from jax.experimental.pallas import tpu as pltpu
from jax.sharding import PartitionSpec as P

EPS = 1e-05
LANES = 128
LOG2E = 1.4426950408889634
F32 = jnp.float32
BF16 = jnp.bfloat16
AXES = ("row", "node")
VMEM_BYTES = 48 * 1024 * 1024


def norm_last(values, gain):
    average = jnp.mean(values, axis=-1, keepdims=True)
    centred = values - average
    variance = jnp.mean(centred * centred, axis=-1, keepdims=True)
    return centred * lax.rsqrt(variance + EPS) * gain


def sigmoid(values):
    return 0.5 * jnp.tanh(0.5 * values) + 0.5


def dot(a, b, a_dim, b_dim):
    return lax.dot_general(a, b, (((a_dim,), (b_dim,)), ((), ())), preferred_element_type=F32)


def position():
    return lax.axis_index("row") * lax.axis_size("node") + lax.axis_index("node")


def call(kernel, out_shape, args, scratch=(), smem=(), name=None, vmem=VMEM_BYTES, away=False, cost=None):
    specs = [
        pl.BlockSpec(memory_space=pltpu.SMEM if n in smem else pltpu.VMEM) for n in range(len(args))
    ]
    single = not isinstance(out_shape, (list, tuple))
    inside = pl.BlockSpec(memory_space=pl.ANY if away else pltpu.VMEM)
    return pl.pallas_call(
        kernel,
        out_shape=out_shape,
        in_specs=specs,
        out_specs=inside if single else [inside] * len(out_shape),
        scratch_shapes=list(scratch),
        compiler_params=pltpu.CompilerParams(vmem_limit_bytes=vmem),
        name=name,
        cost_estimate=cost,
    )(*args)


class Sizes:
    def __init__(self, rows, crop, devices, channels):
        self.rows, self.crop, self.devices, self.channels = rows, crop, devices, channels
        self.half = rows // 2
        self.group = devices // 2
        self.partners = [-s % self.group for s in range(self.group)]
        self.columns = rows * self.group
        self.whole = crop // LANES
        self.rest = crop % LANES
        self.tiles = rows * crop // LANES
        self.chans = channels // self.group
        self.block = rows * rows
        self.block_tiles = -(-self.block // self.chans)


def normalise(sz, row, x, gain, norm_ref):
    main = sz.whole * LANES
    normed = norm_last(x, gain).astype(BF16)
    norm_ref[pl.ds(row * main, main), :] = normed[:main]
    if sz.rest:
        h, q = divmod(row, sz.half)
        norm_ref[pl.ds(sz.rows * main + q * LANES + h * sz.rest, sz.rest), :] = normed[main:]


def project_edges(sz, length, first, gate, value, pick, norm_ref, store):
    main, ch = sz.whole * LANES, sz.channels
    lane = lax.broadcasted_iota(jnp.int32, (1, LANES), 1)

    def live(tile):
        if tile < sz.rows * sz.whole:
            row, m = divmod(tile, sz.whole)
            return ((first + row < length) & (m * LANES + lane < length)).astype(F32)
        q = tile - sz.rows * sz.whole
        second = lane >= sz.rest
        row = first + q + jnp.where(second, sz.half, 0)
        k = main + lane - jnp.where(second, sz.rest, 0)
        return ((row < length) & (k < length)).astype(F32)

    weights = jnp.concatenate([dot(pick, w, 1, 1).astype(BF16) for w in (gate, value)], axis=0)
    step = 2 if sz.tiles % 2 == 0 else 1
    for tile in range(0, sz.tiles, step):
        n = norm_ref[pl.ds(tile * LANES, step * LANES), :]
        mask = jnp.concatenate([live(tile + s) for s in range(step)], axis=1)
        both = dot(weights, n, 1, 1)
        edge = (sigmoid(both[:ch]) * (both[ch:] * mask)).astype(BF16)
        for g in range(sz.group):
            store(
                g,
                slice(tile * LANES, (tile + step) * LANES),
                edge[g * sz.chans : (g + 1) * sz.chans],
            )


def left_kernel(sz, len_ref, x_ref, ln_ref, w_ref, out_ref, norm_ref):
    ch = sz.channels
    gain = ln_ref[...]
    for row in range(sz.rows):
        normalise(sz, row, x_ref[row].astype(F32), gain, norm_ref)
    r = lax.broadcasted_iota(jnp.int32, (ch, ch), 0)
    e = lax.broadcasted_iota(jnp.int32, (ch, ch), 1)

    def store(g, lanes, edge):
        out_ref[g, :, lanes] = edge
        out_ref[sz.group + g, :, lanes] = edge

    first = position() * sz.rows
    pick = (r == e).astype(BF16)
    project_edges(sz, len_ref[0], first, w_ref[0], w_ref[1], pick, norm_ref, store)


def right_kernel(sz, len_ref, x_ref, far_ref, ln_ref, w_ref, *refs):
    near, (norm_ref, own_ref, far_rows_ref, pair_ref) = refs[: sz.group], refs[sz.group :]
    cd, ch = sz.chans, sz.channels
    gain = ln_ref[...]
    me = position()
    mine = me & (sz.group - 1)
    upper = me >= sz.group
    for row in range(sz.rows):
        x = x_ref[row].astype(F32)
        normalise(sz, row, x, gain, norm_ref)
        rows = pl.ds(row * sz.columns, sz.columns)
        own_ref[rows, :] = jnp.where(upper, x[sz.columns :], x[: sz.columns])
        far_rows_ref[rows, :] = far_ref[row].astype(F32)
    for base, wide_ref in enumerate((own_ref, far_rows_ref)):
        for g in range(sz.group):
            for row in range(sz.rows):
                block = wide_ref[pl.ds(row * sz.columns + g * sz.rows, sz.rows), :]
                pair_ref[base, g, row * sz.rows : (row + 1) * sz.rows, :] = block
    for slot, partner in enumerate(sz.partners):
        for base in range(2):
            for t in range(sz.block_tiles):
                at = (sz.tiles + base * sz.block_tiles + t) * LANES
                block = pair_ref[base, mine ^ partner, t * cd : (t + 1) * cd, :]
                near[slot][:, at : at + LANES] = block.astype(BF16)
    r = lax.broadcasted_iota(jnp.int32, (ch, ch), 0)
    e = lax.broadcasted_iota(jnp.int32, (ch, ch), 1)
    partner = (sz.group - r // cd) & (sz.group - 1)
    pick = ((partner ^ mine) * cd + r % cd == e).astype(BF16)

    def store(g, lanes, edge):
        near[g][:, lanes] = edge

    project_edges(sz, len_ref[0], me * sz.rows, w_ref[2], w_ref[3], pick, norm_ref, store)


def unpack(sz, ref, owner, main_ref, rest_ref):
    cd, w = sz.chans, sz.whole
    for tile in range(sz.tiles):
        block = ref[:, tile * LANES : (tile + 1) * LANES].astype(F32)
        if tile < sz.rows * w:
            row, m = divmod(tile, w)
            main_ref[m, pl.ds(pl.multiple_of((owner * sz.rows + row) * cd, 8), cd), :] = block
        else:
            row = owner * sz.rows + tile - sz.rows * w
            rest_ref[pl.ds(pl.multiple_of(row * cd, 8), cd), :] = block
            rest_ref[pl.ds(pl.multiple_of((row + sz.half) * cd, 8), cd), :] = pltpu.roll(
                block, sz.rest, 1
            )


def matrix(sz, c, size, main_ref, rest_ref):
    cd, w = sz.chans, sz.whole
    parts = [main_ref[m, pl.ds(c, size, stride=cd), :].astype(BF16) for m in range(w)]
    if sz.rest:
        parts.append(rest_ref[pl.ds(c, size, stride=cd), :].astype(BF16)[:, : sz.rest])
    return jnp.concatenate(parts, axis=1) if len(parts) > 1 else parts[0]


def arrange_kernel(sz, *refs):
    near, (out_ref, main_ref, rest_ref) = refs[: sz.group], refs[sz.group :]
    mine = position() & (sz.group - 1)
    for slot, partner in enumerate(sz.partners):
        unpack(sz, near[slot], mine ^ partner, main_ref, rest_ref)
    for c in range(sz.chans):
        out_ref[c] = matrix(sz, c, sz.columns, main_ref, rest_ref)


def outer_kernel(
    sz, left_ref, right_ref, away_ref, out_ref, lmain_ref, lrest_ref, omain_ref, orest_ref, sems
):
    cd, n, w, half = sz.chans, sz.crop, sz.whole, sz.half
    for d in range(sz.devices):
        unpack(sz, left_ref.at[d], jnp.int32(d), lmain_ref, lrest_ref)
    for c in range(cd):
        outer = dot(right_ref[c], matrix(sz, c, n, lmain_ref, lrest_ref), 1, 1)
        for m in range(w):
            omain_ref[m, pl.ds(c, sz.columns, stride=cd), :] = outer[:, m * LANES : (m + 1) * LANES]
        if sz.rest:
            part = outer[:, w * LANES :]
            orest_ref[pl.ds(c, sz.columns, stride=cd), :] = jnp.concatenate([part, part], axis=1)
    low = lax.broadcasted_iota(jnp.int32, (cd, LANES), 1) < sz.rest
    copies = [
        pltpu.make_async_copy(out_ref.at[g], away_ref.at[g], sems.at[g]) for g in range(sz.group)
    ]
    for g in range(sz.group):
        start = g * sz.rows
        for tile in range(sz.tiles):
            if tile < sz.rows * w:
                row, m = divmod(tile, w)
                block = omain_ref[m, pl.ds((start + row) * cd, cd), :]
            else:
                at = start + tile - sz.rows * w
                block = jnp.where(
                    low,
                    orest_ref[pl.ds(at * cd, cd), :],
                    orest_ref[pl.ds((at + half) * cd, cd), :],
                )
            out_ref[g, :, tile * LANES : (tile + 1) * LANES] = block.astype(BF16)
        copies[g].start()
    for copy in copies:
        copy.wait()


def take_columns(sz, near, cols_ref):
    cd, me = sz.chans, position()
    for slot, partner in enumerate(sz.partners):
        for base, owner in ((0, me ^ partner), (1, me ^ (sz.group + partner))):
            for t in range(sz.block_tiles):
                at = (sz.tiles + base * sz.block_tiles + t) * LANES
                rows = pl.ds(pl.multiple_of(owner * sz.block + t * cd, 8), cd)
                cols_ref[rows, :] = near[slot][:, at : at + LANES].astype(F32)


def gating_kernel(sz, lnp_ref, gate_ref, *refs):
    near, (x_ref, gating_ref, cols_ref) = refs[: sz.group], refs[sz.group :]
    take_columns(sz, near, cols_ref)
    for j in range(sz.rows):
        x = cols_ref[pl.ds(j, sz.crop, stride=sz.rows), :]
        x_ref[j] = x.astype(BF16)
        normed = norm_last(x, lnp_ref[...]).astype(BF16)
        gating_ref[j] = sigmoid(dot(normed, gate_ref[...], 1, 0)).astype(BF16)


def update_kernel(
    sz, x_ref, gating_ref, lnh_ref, tri_ref, lna_ref, biasw_ref, sums_ref,
    first_ref, col_ref, bias_ref, brow_ref,
):
    n, w, half, ch = sz.crop, sz.whole, sz.half, sz.channels
    gain_h = jnp.transpose(jnp.broadcast_to(lnh_ref[...], (ch, ch)))
    tri = tri_ref[...]

    def update(tile):
        block = sums_ref[:, :, tile * LANES : (tile + 1) * LANES].astype(F32).reshape(ch, LANES)
        average = jnp.mean(block, axis=0, keepdims=True)
        centred = block - average
        variance = jnp.mean(centred * centred, axis=0, keepdims=True)
        hidden = (centred * lax.rsqrt(variance + EPS) * gain_h).astype(BF16)
        return dot(hidden, tri, 0, 0)

    rest = [update(sz.rows * w + q) for q in range(half)] if sz.rest else None
    for j in range(sz.rows):
        parts = [update(j * w + m) for m in range(w)]
        if sz.rest:
            h, q = divmod(j, half)
            parts.append(rest[q][h * sz.rest : (h + 1) * sz.rest])
        change = jnp.concatenate(parts, axis=0) if len(parts) > 1 else parts[0]
        first = (x_ref[j].astype(F32) + gating_ref[j].astype(F32) * change).astype(BF16)
        first_ref[j] = first
        col = norm_last(first.astype(F32), lna_ref[...]).astype(BF16)
        col_ref[j] = col
        heads = biasw_ref.shape[1]
        brow_ref[pl.ds(j * heads, heads), :] = dot(biasw_ref[...], col, 0, 1)
    rows = brow_ref[...]
    part = rows.shape[0] // 2
    one, two = rows[:part], rows[part:]
    message = [one[:, : w * LANES], two[:, : w * LANES]]
    if sz.rest:
        message += [one[:, w * LANES :], two[:, w * LANES :]]
    bias_ref[...] = jnp.concatenate(message, axis=1).astype(BF16)


def project_kernel(sz, col_ref, q_ref, k_ref, v_ref, g_ref, qo_ref, ko_ref, vo_ref, go_ref):
    joined = jnp.concatenate([ref[...] for ref in (q_ref, k_ref, v_ref, g_ref)], axis=1)
    width = q_ref.shape[1]
    for j in range(sz.rows):
        made = dot(col_ref[j], joined, 1, 0)
        qo_ref[j] = made[:, :width].astype(BF16)
        ko_ref[j] = made[:, width : 2 * width].astype(BF16)
        vo_ref[j] = made[:, 2 * width : 3 * width].astype(BF16)
        go_ref[j] = sigmoid(made[:, 3 * width :])


def attend_kernel(
    sz, heads, steps, len_ref, q_ref, k_ref, v_ref, g_ref, first_ref, aout_ref, *refs
):
    bias_refs, (away_ref, out_ref, rows_ref, bias_ref, sems) = refs[:-5], refs[-5:]
    n, w, ch = sz.crop, sz.whole, sz.channels
    length, me = len_ref[0], position()
    width = q_ref.shape[2]
    hd = width // heads
    per = sz.rows * heads // 2
    for ref, offsets in zip(bias_refs, steps):
        for place, offset in enumerate(offsets):
            block = ref[place].astype(F32) * LOG2E
            for p in range(2):
                at = pl.ds(pl.multiple_of(((me ^ offset) * 2 + p) * per, 8), per)
                for m in range(w):
                    rows_ref[m, at, :] = block[:, (p * w + m) * LANES : (p * w + m + 1) * LANES]
                if sz.rest:
                    tail = block[:, 2 * w * LANES :]
                    rows_ref[w, at, :] = pltpu.roll(tail, sz.rest, 1) if p else tail
    lane = lax.broadcasted_iota(jnp.int32, (1, LANES), 1)
    for m in range(w + (sz.rest > 0)):
        lanes = slice(m * LANES, min((m + 1) * LANES, n))
        dead = jnp.where(m * LANES + lane < length, 0.0, -1e9 * LOG2E).astype(F32)
        for head in range(heads):
            rows = rows_ref[m, pl.ds(head, n, stride=heads), :] + dead
            bias_ref[head, :, lanes] = rows[:, : lanes.stop - lanes.start]
    column = lax.broadcasted_iota(jnp.int32, (1, width), 1)
    head_masks = [(column >= h * hd) & (column < (h + 1) * hd) for h in range(heads)]
    scale = (hd ** (-0.5)) * LOG2E
    ones = jnp.ones((n, width), BF16)

    def score(j):
        query = [q_ref[j] * head_masks[h].astype(BF16) for h in range(heads)]
        return dot(jnp.concatenate(query, axis=0), k_ref[j], 1, 1)

    copies = [
        pltpu.make_async_copy(out_ref.at[j], away_ref.at[j], sems.at[j]) for j in range(sz.rows)
    ]
    scores = score(0)
    for j in range(sz.rows):
        now = scores
        if j + 1 < sz.rows:
            scores = score(j + 1)
        weights = []
        for h in range(heads):
            part = now[h * n : (h + 1) * n] * scale + bias_ref[h]
            weights.append(jnp.exp2(part - jnp.max(part, axis=1, keepdims=True)).astype(BF16))
        values = jnp.concatenate([v_ref[j], ones], axis=1)
        mixed = dot(jnp.concatenate(weights, axis=0), values, 1, 0)
        attended, total = mixed[:n, :width], mixed[:n, width:]
        for h in range(1, heads):
            rows = slice(h * n, (h + 1) * n)
            attended = jnp.where(head_masks[h], mixed[rows, :width], attended)
            total = jnp.where(head_masks[h], mixed[rows, width:], total)
        gated = (attended / total * g_ref[j]).astype(BF16)
        out_ref[j] = (first_ref[j].astype(F32) + dot(gated, aout_ref[...], 1, 0)).astype(BF16)
        copies[j].start()
    for copy in copies:
        copy.wait()


def spread(block, devices):
    pieces, offsets = [block[None]], [[0]]
    bit = devices // 2
    while bit:
        held = jnp.concatenate(pieces, axis=0) if len(pieces) > 1 else pieces[0]
        known = [o for part in offsets for o in part]
        pieces.append(lax.ppermute(held, AXES, [(d, d ^ bit) for d in range(devices)]))
        offsets.append([o ^ bit for o in known])
        bit //= 2
    return pieces, offsets


def shards(
    devices,
    pair_rep, length, ln_pair, tri_in, tri_gate, ln_hidden, tri_out, ln_att,
    att_q, att_k, att_v, att_bias, att_gate, att_out,
):
    rows, crop, ch = pair_rep.shape
    heads = att_bias.shape[1]
    sz = Sizes(rows, crop, devices, ch)
    n, cd = crop, sz.chans
    def bound(kernel, *extra):
        def run(*refs):
            return kernel(sz, *extra, *refs)

        return run

    shape = jax.ShapeDtypeStruct
    g, t, bt = sz.group, sz.tiles, sz.block_tiles

    def slab(tiles, *lead):
        return shape((*lead, cd, tiles * LANES), BF16)

    def send(blocks):
        return [
            lax.ppermute(block, AXES, [(d, d ^ partner) for d in range(devices)])
            if partner
            else block
            for partner, block in zip(sz.partners, blocks)
        ]

    upper = (lax.axis_index(AXES) >= g).astype(jnp.int32)
    far = lax.ppermute(
        lax.dynamic_slice_in_dim(pair_rep, (1 - upper) * sz.columns, sz.columns, 1),
        AXES,
        [(d, d ^ g) for d in range(devices)],
    )
    left = call(
        bound(left_kernel),
        slab(t, devices),
        (length, pair_rep, ln_pair[None], tri_in),
        scratch=[pltpu.VMEM((rows * crop, ch), BF16)],
        smem=(0,),
        name="left",
    )
    others = call(
        bound(right_kernel),
        [slab(t + 2 * bt)] * g,
        (length, pair_rep, far, ln_pair[None], tri_in),
        scratch=[
            pltpu.VMEM((rows * crop, ch), BF16),
            pltpu.VMEM((rows * sz.columns, ch), F32),
            pltpu.VMEM((rows * sz.columns, ch), F32),
            pltpu.VMEM((2, g, bt * cd, ch), F32),
        ],
        smem=(0,),
        name="right",
        cost=pl.CostEstimate(flops=10**11, bytes_accessed=10**6, transcendentals=0),
    )
    left = lax.all_to_all(left, AXES, split_axis=0, concat_axis=0, tiled=True)
    near = send(others)
    rest = sz.rest > 0
    column_rows = sz.columns * cd
    right = call(
        bound(arrange_kernel),
        shape((cd, sz.columns, n), BF16),
        tuple(near),
        scratch=[
            pltpu.VMEM((sz.whole, column_rows, LANES), F32),
            pltpu.VMEM((column_rows if rest else 8, LANES), F32),
        ],
        name="arrange",
    )
    outer = call(
        bound(outer_kernel),
        slab(t, g),
        (left, right),
        scratch=[
            pltpu.VMEM((g, cd, t * LANES), BF16),
            pltpu.VMEM((sz.whole, n * cd, LANES), F32),
            pltpu.VMEM((n * cd if rest else 8, LANES), F32),
            pltpu.VMEM((sz.whole, column_rows, LANES), F32),
            pltpu.VMEM((column_rows if rest else 8, LANES), F32),
            pltpu.SemaphoreType.DMA((g,)),
        ],
        away=True,
        name="outer",
    )
    sums = lax.all_to_all(
        outer, AXES, split_axis=0, concat_axis=0, tiled=True,
        axis_index_groups=[list(range(g)), list(range(g, devices))],
    )
    columns, gating = call(
        bound(gating_kernel),
        [shape((rows, n, ch), BF16)] * 2,
        (ln_pair[None], tri_gate, *near),
        scratch=[pltpu.VMEM((devices * sz.block + cd, ch), F32)],
        name="gating",
    )
    first, col, bias = call(
        bound(update_kernel),
        [
            shape((rows, n, ch), BF16),
            shape((rows, n, ch), BF16),
            shape((rows * heads // 2, 2 * n), BF16),
        ],
        (
            columns, gating, ln_hidden[None], tri_out, ln_att[None], att_bias, sums,
        ),
        scratch=[pltpu.VMEM((rows * heads, n), F32)],
        name="update",
    )
    pieces, steps = spread(bias, devices)
    query, key, value, gate = call(
        bound(project_kernel),
        [
            shape((rows, n, att_q.shape[1]), BF16),
            shape((rows, n, att_q.shape[1]), BF16),
            shape((rows, n, att_q.shape[1]), BF16),
            shape((rows, n, att_q.shape[1]), F32),
        ],
        (col, att_q, att_k, att_v, att_gate),
        name="project",
    )
    out = call(
        bound(attend_kernel, heads, steps),
        shape((rows, n, ch), BF16),
        (length, query, key, value, gate, first, att_out, *pieces),
        scratch=[
            pltpu.VMEM((rows, n, ch), BF16),
            pltpu.VMEM((-(-n // LANES), n * heads, LANES), F32),
            pltpu.VMEM((heads, n, n), F32),
            pltpu.SemaphoreType.DMA((rows,)),
        ],
        smem=(0,),
        away=True,
        name="attend",
    )
    return jnp.swapaxes(out, 0, 1)


def solution(mesh):
    devices = mesh.shape["row"] * mesh.shape["node"]

    def body(*args):
        return shards(devices, *args)

    return jax.shard_map(
        body,
        mesh=mesh,
        in_specs=(P(("grp", "row", "node"), None, None), P("grp")) + (P(),) * 12,
        out_specs=P("grp", AXES, None),
        check_vma=False,
    )
```

```python
import jax
import jax.numpy as jnp
from jax import lax
from jax.experimental import pallas as pl
from jax.experimental.pallas import tpu as pltpu
from jax.sharding import PartitionSpec as P

EPS = 1e-05
LANES = 128
LOG2E = 1.4426950408889634
F32 = jnp.float32
BF16 = jnp.bfloat16
AXES = ("row", "node")
VMEM_BYTES = 48 * 1024 * 1024


def norm_last(values, gain):
    average = jnp.mean(values, axis=-1, keepdims=True)
    centred = values - average
    variance = jnp.mean(centred * centred, axis=-1, keepdims=True)
    return centred * lax.rsqrt(variance + EPS) * gain


def sigmoid(values):
    return 0.5 * jnp.tanh(0.5 * values) + 0.5


def dot(a, b, a_dim, b_dim):
    return lax.dot_general(a, b, (((a_dim,), (b_dim,)), ((), ())), preferred_element_type=F32)


def position():
    return lax.axis_index("row") * lax.axis_size("node") + lax.axis_index("node")


def call(kernel, out_shape, args, scratch=(), smem=(), name=None, vmem=VMEM_BYTES, away=False, cost=None):
    specs = [
        pl.BlockSpec(memory_space=pltpu.SMEM if n in smem else pltpu.VMEM) for n in range(len(args))
    ]
    single = not isinstance(out_shape, (list, tuple))
    inside = pl.BlockSpec(memory_space=pl.ANY if away else pltpu.VMEM)
    return pl.pallas_call(
        kernel,
        out_shape=out_shape,
        in_specs=specs,
        out_specs=inside if single else [inside] * len(out_shape),
        scratch_shapes=list(scratch),
        compiler_params=pltpu.CompilerParams(vmem_limit_bytes=vmem),
        name=name,
        cost_estimate=cost,
    )(*args)


class Sizes:
    def __init__(self, rows, crop, devices, channels):
        self.rows, self.crop, self.devices, self.channels = rows, crop, devices, channels
        self.half = rows // 2
        self.group = devices // 2
        self.partners = [-s % self.group for s in range(self.group)]
        self.columns = rows * self.group
        self.whole = crop // LANES
        self.rest = crop % LANES
        self.tiles = rows * crop // LANES
        self.chans = channels // self.group
        self.block = rows * rows
        self.block_tiles = -(-self.block // self.chans)


def normalise(sz, row, x, gain, norm_ref):
    main = sz.whole * LANES
    normed = norm_last(x, gain).astype(BF16)
    norm_ref[pl.ds(row * main, main), :] = normed[:main]
    if sz.rest:
        h, q = divmod(row, sz.half)
        norm_ref[pl.ds(sz.rows * main + q * LANES + h * sz.rest, sz.rest), :] = normed[main:]


def project_edges(sz, length, first, gate, value, pick, norm_ref, store):
    main, ch = sz.whole * LANES, sz.channels
    lane = lax.broadcasted_iota(jnp.int32, (1, LANES), 1)

    def live(tile):
        if tile < sz.rows * sz.whole:
            row, m = divmod(tile, sz.whole)
            return ((first + row < length) & (m * LANES + lane < length)).astype(F32)
        q = tile - sz.rows * sz.whole
        second = lane >= sz.rest
        row = first + q + jnp.where(second, sz.half, 0)
        k = main + lane - jnp.where(second, sz.rest, 0)
        return ((row < length) & (k < length)).astype(F32)

    weights = jnp.concatenate([dot(pick, w, 1, 1).astype(BF16) for w in (gate, value)], axis=0)
    step = 2 if sz.tiles % 2 == 0 else 1
    for tile in range(0, sz.tiles, step):
        n = norm_ref[pl.ds(tile * LANES, step * LANES), :]
        mask = jnp.concatenate([live(tile + s) for s in range(step)], axis=1)
        both = dot(weights, n, 1, 1)
        edge = (sigmoid(both[:ch]) * (both[ch:] * mask)).astype(BF16)
        for g in range(sz.group):
            store(
                g,
                slice(tile * LANES, (tile + step) * LANES),
                edge[g * sz.chans : (g + 1) * sz.chans],
            )


def left_kernel(sz, len_ref, x_ref, ln_ref, w_ref, out_ref, norm_ref):
    ch = sz.channels
    gain = ln_ref[...]
    for row in range(sz.rows):
        normalise(sz, row, x_ref[row].astype(F32), gain, norm_ref)
    r = lax.broadcasted_iota(jnp.int32, (ch, ch), 0)
    e = lax.broadcasted_iota(jnp.int32, (ch, ch), 1)

    def store(g, lanes, edge):
        out_ref[g, :, lanes] = edge
        out_ref[sz.group + g, :, lanes] = edge

    first = position() * sz.rows
    pick = (r == e).astype(BF16)
    project_edges(sz, len_ref[0], first, w_ref[0], w_ref[1], pick, norm_ref, store)


def right_kernel(sz, len_ref, x_ref, ln_ref, w_ref, *refs):
    near, norm_ref = refs[: sz.group], refs[sz.group]
    cd, ch = sz.chans, sz.channels
    gain = ln_ref[...]
    for row in range(sz.rows):
        normalise(sz, row, x_ref[row].astype(F32), gain, norm_ref)
    me = position()
    mine = me & (sz.group - 1)
    r = lax.broadcasted_iota(jnp.int32, (ch, ch), 0)
    e = lax.broadcasted_iota(jnp.int32, (ch, ch), 1)
    partner = (sz.group - r // cd) & (sz.group - 1)
    pick = ((partner ^ mine) * cd + r % cd == e).astype(BF16)

    def store(g, lanes, edge):
        near[g][:, lanes] = edge

    project_edges(sz, len_ref[0], me * sz.rows, w_ref[2], w_ref[3], pick, norm_ref, store)


def relay_kernel(sz, x_ref, far_ref, *refs):
    near, (own_ref, far_rows_ref, pair_ref) = refs[: sz.group], refs[sz.group :]
    cd, me = sz.chans, position()
    mine = me & (sz.group - 1)
    upper = me >= sz.group
    for row in range(sz.rows):
        x = x_ref[row].astype(F32)
        rows = pl.ds(row * sz.columns, sz.columns)
        own_ref[rows, :] = jnp.where(upper, x[sz.columns :], x[: sz.columns])
        far_rows_ref[rows, :] = far_ref[row].astype(F32)
    for base, wide_ref in enumerate((own_ref, far_rows_ref)):
        for g in range(sz.group):
            for row in range(sz.rows):
                block = wide_ref[pl.ds(row * sz.columns + g * sz.rows, sz.rows), :]
                pair_ref[base, g, row * sz.rows : (row + 1) * sz.rows, :] = block
    for slot, partner in enumerate(sz.partners):
        for base in range(2):
            for t in range(sz.block_tiles):
                at = (base * sz.block_tiles + t) * LANES
                block = pair_ref[base, mine ^ partner, t * cd : (t + 1) * cd, :]
                near[slot][:, at : at + LANES] = block.astype(BF16)


def unpack(sz, ref, owner, main_ref, rest_ref):
    cd, w = sz.chans, sz.whole
    for tile in range(sz.tiles):
        block = ref[:, tile * LANES : (tile + 1) * LANES].astype(F32)
        if tile < sz.rows * w:
            row, m = divmod(tile, w)
            main_ref[m, pl.ds(pl.multiple_of((owner * sz.rows + row) * cd, 8), cd), :] = block
        else:
            row = owner * sz.rows + tile - sz.rows * w
            rest_ref[pl.ds(pl.multiple_of(row * cd, 8), cd), :] = block
            rest_ref[pl.ds(pl.multiple_of((row + sz.half) * cd, 8), cd), :] = pltpu.roll(
                block, sz.rest, 1
            )


def matrix(sz, c, size, main_ref, rest_ref):
    cd, w = sz.chans, sz.whole
    parts = [main_ref[m, pl.ds(c, size, stride=cd), :].astype(BF16) for m in range(w)]
    if sz.rest:
        parts.append(rest_ref[pl.ds(c, size, stride=cd), :].astype(BF16)[:, : sz.rest])
    return jnp.concatenate(parts, axis=1) if len(parts) > 1 else parts[0]


def arrange_kernel(sz, *refs):
    near, (out_ref, main_ref, rest_ref) = refs[: sz.group], refs[sz.group :]
    mine = position() & (sz.group - 1)
    for slot, partner in enumerate(sz.partners):
        unpack(sz, near[slot], mine ^ partner, main_ref, rest_ref)
    for c in range(sz.chans):
        out_ref[c] = matrix(sz, c, sz.columns, main_ref, rest_ref)


def outer_kernel(
    sz, left_ref, right_ref, away_ref, out_ref, lmain_ref, lrest_ref, omain_ref, orest_ref, sems
):
    cd, n, w, half = sz.chans, sz.crop, sz.whole, sz.half
    for d in range(sz.devices):
        unpack(sz, left_ref.at[d], jnp.int32(d), lmain_ref, lrest_ref)
    for c in range(cd):
        outer = dot(right_ref[c], matrix(sz, c, n, lmain_ref, lrest_ref), 1, 1)
        for m in range(w):
            omain_ref[m, pl.ds(c, sz.columns, stride=cd), :] = outer[:, m * LANES : (m + 1) * LANES]
        if sz.rest:
            part = outer[:, w * LANES :]
            orest_ref[pl.ds(c, sz.columns, stride=cd), :] = jnp.concatenate([part, part], axis=1)
    low = lax.broadcasted_iota(jnp.int32, (cd, LANES), 1) < sz.rest
    copies = [
        pltpu.make_async_copy(out_ref.at[g], away_ref.at[g], sems.at[g]) for g in range(sz.group)
    ]
    for g in range(sz.group):
        start = g * sz.rows
        for tile in range(sz.tiles):
            if tile < sz.rows * w:
                row, m = divmod(tile, w)
                block = omain_ref[m, pl.ds((start + row) * cd, cd), :]
            else:
                at = start + tile - sz.rows * w
                block = jnp.where(
                    low,
                    orest_ref[pl.ds(at * cd, cd), :],
                    orest_ref[pl.ds((at + half) * cd, cd), :],
                )
            out_ref[g, :, tile * LANES : (tile + 1) * LANES] = block.astype(BF16)
        copies[g].start()
    for copy in copies:
        copy.wait()


def take_columns(sz, near, cols_ref):
    cd, me = sz.chans, position()
    for slot, partner in enumerate(sz.partners):
        for base, owner in ((0, me ^ partner), (1, me ^ (sz.group + partner))):
            for t in range(sz.block_tiles):
                at = (base * sz.block_tiles + t) * LANES
                rows = pl.ds(pl.multiple_of(owner * sz.block + t * cd, 8), cd)
                cols_ref[rows, :] = near[slot][:, at : at + LANES].astype(F32)


def gating_kernel(sz, lnp_ref, gate_ref, *refs):
    near, (x_ref, gating_ref, cols_ref) = refs[: sz.group], refs[sz.group :]
    take_columns(sz, near, cols_ref)
    for j in range(sz.rows):
        x = cols_ref[pl.ds(j, sz.crop, stride=sz.rows), :]
        x_ref[j] = x.astype(BF16)
        normed = norm_last(x, lnp_ref[...]).astype(BF16)
        gating_ref[j] = sigmoid(dot(normed, gate_ref[...], 1, 0)).astype(BF16)


def update_kernel(
    sz, x_ref, gating_ref, lnh_ref, tri_ref, lna_ref, biasw_ref, sums_ref,
    first_ref, col_ref, bias_ref, brow_ref,
):
    n, w, half, ch = sz.crop, sz.whole, sz.half, sz.channels
    gain_h = jnp.transpose(jnp.broadcast_to(lnh_ref[...], (ch, ch)))
    tri = tri_ref[...]

    def update(tile):
        block = sums_ref[:, :, tile * LANES : (tile + 1) * LANES].astype(F32).reshape(ch, LANES)
        average = jnp.mean(block, axis=0, keepdims=True)
        centred = block - average
        variance = jnp.mean(centred * centred, axis=0, keepdims=True)
        hidden = (centred * lax.rsqrt(variance + EPS) * gain_h).astype(BF16)
        return dot(hidden, tri, 0, 0)

    rest = [update(sz.rows * w + q) for q in range(half)] if sz.rest else None
    for j in range(sz.rows):
        parts = [update(j * w + m) for m in range(w)]
        if sz.rest:
            h, q = divmod(j, half)
            parts.append(rest[q][h * sz.rest : (h + 1) * sz.rest])
        change = jnp.concatenate(parts, axis=0) if len(parts) > 1 else parts[0]
        first = (x_ref[j].astype(F32) + gating_ref[j].astype(F32) * change).astype(BF16)
        first_ref[j] = first
        col = norm_last(first.astype(F32), lna_ref[...]).astype(BF16)
        col_ref[j] = col
        heads = biasw_ref.shape[1]
        brow_ref[pl.ds(j * heads, heads), :] = dot(biasw_ref[...], col, 0, 1)
    rows = brow_ref[...]
    part = rows.shape[0] // 2
    one, two = rows[:part], rows[part:]
    message = [one[:, : w * LANES], two[:, : w * LANES]]
    if sz.rest:
        message += [one[:, w * LANES :], two[:, w * LANES :]]
    bias_ref[...] = jnp.concatenate(message, axis=1).astype(BF16)


def project_kernel(sz, col_ref, q_ref, k_ref, v_ref, g_ref, qo_ref, ko_ref, vo_ref, go_ref):
    joined = jnp.concatenate([ref[...] for ref in (q_ref, k_ref, v_ref, g_ref)], axis=1)
    width = q_ref.shape[1]
    for j in range(sz.rows):
        made = dot(col_ref[j], joined, 1, 0)
        qo_ref[j] = made[:, :width].astype(BF16)
        ko_ref[j] = made[:, width : 2 * width].astype(BF16)
        vo_ref[j] = made[:, 2 * width : 3 * width].astype(BF16)
        go_ref[j] = sigmoid(made[:, 3 * width :])


def attend_kernel(
    sz, heads, steps, len_ref, q_ref, k_ref, v_ref, g_ref, first_ref, aout_ref, *refs
):
    bias_refs, (away_ref, out_ref, rows_ref, bias_ref, sems) = refs[:-5], refs[-5:]
    n, w, ch = sz.crop, sz.whole, sz.channels
    length, me = len_ref[0], position()
    width = q_ref.shape[2]
    hd = width // heads
    per = sz.rows * heads // 2
    for ref, offsets in zip(bias_refs, steps):
        for place, offset in enumerate(offsets):
            block = ref[place].astype(F32) * LOG2E
            for p in range(2):
                at = pl.ds(pl.multiple_of(((me ^ offset) * 2 + p) * per, 8), per)
                for m in range(w):
                    rows_ref[m, at, :] = block[:, (p * w + m) * LANES : (p * w + m + 1) * LANES]
                if sz.rest:
                    tail = block[:, 2 * w * LANES :]
                    rows_ref[w, at, :] = pltpu.roll(tail, sz.rest, 1) if p else tail
    lane = lax.broadcasted_iota(jnp.int32, (1, LANES), 1)
    for m in range(w + (sz.rest > 0)):
        lanes = slice(m * LANES, min((m + 1) * LANES, n))
        dead = jnp.where(m * LANES + lane < length, 0.0, -1e9 * LOG2E).astype(F32)
        for head in range(heads):
            rows = rows_ref[m, pl.ds(head, n, stride=heads), :] + dead
            bias_ref[head, :, lanes] = rows[:, : lanes.stop - lanes.start]
    column = lax.broadcasted_iota(jnp.int32, (1, width), 1)
    head_masks = [(column >= h * hd) & (column < (h + 1) * hd) for h in range(heads)]
    scale = (hd ** (-0.5)) * LOG2E
    ones = jnp.ones((n, width), BF16)

    def score(j):
        query = [q_ref[j] * head_masks[h].astype(BF16) for h in range(heads)]
        return dot(jnp.concatenate(query, axis=0), k_ref[j], 1, 1)

    copies = [
        pltpu.make_async_copy(out_ref.at[j], away_ref.at[j], sems.at[j]) for j in range(sz.rows)
    ]
    scores = score(0)
    for j in range(sz.rows):
        now = scores
        if j + 1 < sz.rows:
            scores = score(j + 1)
        weights = []
        for h in range(heads):
            part = now[h * n : (h + 1) * n] * scale + bias_ref[h]
            weights.append(jnp.exp2(part - jnp.max(part, axis=1, keepdims=True)).astype(BF16))
        values = jnp.concatenate([v_ref[j], ones], axis=1)
        mixed = dot(jnp.concatenate(weights, axis=0), values, 1, 0)
        attended, total = mixed[:n, :width], mixed[:n, width:]
        for h in range(1, heads):
            rows = slice(h * n, (h + 1) * n)
            attended = jnp.where(head_masks[h], mixed[rows, :width], attended)
            total = jnp.where(head_masks[h], mixed[rows, width:], total)
        gated = (attended / total * g_ref[j]).astype(BF16)
        out_ref[j] = (first_ref[j].astype(F32) + dot(gated, aout_ref[...], 1, 0)).astype(BF16)
        copies[j].start()
    for copy in copies:
        copy.wait()


def spread(block, devices):
    pieces, offsets = [block[None]], [[0]]
    bit = devices // 2
    while bit:
        held = jnp.concatenate(pieces, axis=0) if len(pieces) > 1 else pieces[0]
        known = [o for part in offsets for o in part]
        pieces.append(lax.ppermute(held, AXES, [(d, d ^ bit) for d in range(devices)]))
        offsets.append([o ^ bit for o in known])
        bit //= 2
    return pieces, offsets


def shards(
    devices,
    pair_rep, length, ln_pair, tri_in, tri_gate, ln_hidden, tri_out, ln_att,
    att_q, att_k, att_v, att_bias, att_gate, att_out,
):
    rows, crop, ch = pair_rep.shape
    heads = att_bias.shape[1]
    sz = Sizes(rows, crop, devices, ch)
    n, cd = crop, sz.chans
    def bound(kernel, *extra):
        def run(*refs):
            return kernel(sz, *extra, *refs)

        return run

    shape = jax.ShapeDtypeStruct
    g, t, bt = sz.group, sz.tiles, sz.block_tiles

    def slab(tiles, *lead):
        return shape((*lead, cd, tiles * LANES), BF16)

    def send(blocks):
        return [
            lax.ppermute(block, AXES, [(d, d ^ partner) for d in range(devices)])
            if partner
            else block
            for partner, block in zip(sz.partners, blocks)
        ]

    upper = (lax.axis_index(AXES) >= g).astype(jnp.int32)
    far = lax.ppermute(
        lax.dynamic_slice_in_dim(pair_rep, (1 - upper) * sz.columns, sz.columns, 1),
        AXES,
        [(d, d ^ g) for d in range(devices)],
    )
    left = call(
        bound(left_kernel),
        slab(t, devices),
        (length, pair_rep, ln_pair[None], tri_in),
        scratch=[pltpu.VMEM((rows * crop, ch), BF16)],
        smem=(0,),
        name="left",
    )
    rights = call(
        bound(right_kernel),
        [slab(t)] * g,
        (length, pair_rep, ln_pair[None], tri_in),
        scratch=[pltpu.VMEM((rows * crop, ch), BF16)],
        smem=(0,),
        name="right",
    )
    pairs = call(
        bound(relay_kernel),
        [slab(2 * bt)] * g,
        (pair_rep, far),
        scratch=[
            pltpu.VMEM((rows * sz.columns, ch), F32),
            pltpu.VMEM((rows * sz.columns, ch), F32),
            pltpu.VMEM((2, g, bt * cd, ch), F32),
        ],
        name="relay",
        cost=pl.CostEstimate(flops=10**11, bytes_accessed=10**6, transcendentals=0),
    )
    left = lax.all_to_all(left, AXES, split_axis=0, concat_axis=0, tiled=True)
    near = send(rights)
    pairs = send(pairs)
    rest = sz.rest > 0
    left, pairs = lax.optimization_barrier((left, pairs))
    column_rows = sz.columns * cd
    right = call(
        bound(arrange_kernel),
        shape((cd, sz.columns, n), BF16),
        tuple(near),
        scratch=[
            pltpu.VMEM((sz.whole, column_rows, LANES), F32),
            pltpu.VMEM((column_rows if rest else 8, LANES), F32),
        ],
        name="arrange",
    )
    outer = call(
        bound(outer_kernel),
        slab(t, g),
        (left, right),
        scratch=[
            pltpu.VMEM((g, cd, t * LANES), BF16),
            pltpu.VMEM((sz.whole, n * cd, LANES), F32),
            pltpu.VMEM((n * cd if rest else 8, LANES), F32),
            pltpu.VMEM((sz.whole, column_rows, LANES), F32),
            pltpu.VMEM((column_rows if rest else 8, LANES), F32),
            pltpu.SemaphoreType.DMA((g,)),
        ],
        away=True,
        name="outer",
    )
    sums = lax.all_to_all(
        outer, AXES, split_axis=0, concat_axis=0, tiled=True,
        axis_index_groups=[list(range(g)), list(range(g, devices))],
    )
    columns, gating = call(
        bound(gating_kernel),
        [shape((rows, n, ch), BF16)] * 2,
        (ln_pair[None], tri_gate, *pairs),
        scratch=[pltpu.VMEM((devices * sz.block + cd, ch), F32)],
        name="gating",
    )
    first, col, bias = call(
        bound(update_kernel),
        [
            shape((rows, n, ch), BF16),
            shape((rows, n, ch), BF16),
            shape((rows * heads // 2, 2 * n), BF16),
        ],
        (
            columns, gating, ln_hidden[None], tri_out, ln_att[None], att_bias, sums,
        ),
        scratch=[pltpu.VMEM((rows * heads, n), F32)],
        name="update",
    )
    pieces, steps = spread(bias, devices)
    query, key, value, gate = call(
        bound(project_kernel),
        [
            shape((rows, n, att_q.shape[1]), BF16),
            shape((rows, n, att_q.shape[1]), BF16),
            shape((rows, n, att_q.shape[1]), BF16),
            shape((rows, n, att_q.shape[1]), F32),
        ],
        (col, att_q, att_k, att_v, att_gate),
        name="project",
    )
    out = call(
        bound(attend_kernel, heads, steps),
        shape((rows, n, ch), BF16),
        (length, query, key, value, gate, first, att_out, *pieces),
        scratch=[
            pltpu.VMEM((rows, n, ch), BF16),
            pltpu.VMEM((-(-n // LANES), n * heads, LANES), F32),
            pltpu.VMEM((heads, n, n), F32),
            pltpu.SemaphoreType.DMA((rows,)),
        ],
        smem=(0,),
        away=True,
        name="attend",
    )
    return jnp.swapaxes(out, 0, 1)


def solution(mesh):
    devices = mesh.shape["row"] * mesh.shape["node"]

    def body(*args):
        return shards(devices, *args)

    return jax.shard_map(
        body,
        mesh=mesh,
        in_specs=(P(("grp", "row", "node"), None, None), P("grp")) + (P(),) * 12,
        out_specs=P("grp", AXES, None),
        check_vma=False,
    )
```

```python
import jax
import jax.numpy as jnp
from jax import lax
from jax.experimental import pallas as pl
from jax.experimental.pallas import tpu as pltpu
from jax.sharding import PartitionSpec as P

EPS = 1e-05
LANES = 128
LOG2E = 1.4426950408889634
F32 = jnp.float32
BF16 = jnp.bfloat16
AXES = ("row", "node")
VMEM_BYTES = 48 * 1024 * 1024


def norm_last(values, gain):
    average = jnp.mean(values, axis=-1, keepdims=True)
    centred = values - average
    variance = jnp.mean(centred * centred, axis=-1, keepdims=True)
    return centred * lax.rsqrt(variance + EPS) * gain


def sigmoid(values):
    return 0.5 * jnp.tanh(0.5 * values) + 0.5


def dot(a, b, a_dim, b_dim):
    return lax.dot_general(a, b, (((a_dim,), (b_dim,)), ((), ())), preferred_element_type=F32)


def position():
    return lax.axis_index("row") * lax.axis_size("node") + lax.axis_index("node")


def call(kernel, out_shape, args, scratch=(), smem=(), name=None, vmem=VMEM_BYTES, away=False, cost=None):
    specs = [
        pl.BlockSpec(memory_space=pltpu.SMEM if n in smem else pltpu.VMEM) for n in range(len(args))
    ]
    single = not isinstance(out_shape, (list, tuple))
    inside = pl.BlockSpec(memory_space=pl.ANY if away else pltpu.VMEM)
    return pl.pallas_call(
        kernel,
        out_shape=out_shape,
        in_specs=specs,
        out_specs=inside if single else [inside] * len(out_shape),
        scratch_shapes=list(scratch),
        compiler_params=pltpu.CompilerParams(vmem_limit_bytes=vmem),
        name=name,
        cost_estimate=cost,
    )(*args)


class Sizes:
    def __init__(self, rows, crop, devices, channels):
        self.rows, self.crop, self.devices, self.channels = rows, crop, devices, channels
        self.half = rows // 2
        self.group = devices // 2
        self.partners = [-s % self.group for s in range(self.group)]
        self.columns = rows * self.group
        self.whole = crop // LANES
        self.rest = crop % LANES
        self.tiles = rows * crop // LANES
        self.chans = channels // self.group
        self.block = rows * rows
        self.block_tiles = -(-self.block // self.chans)


def normalise(sz, row, x, gain, norm_ref):
    main = sz.whole * LANES
    normed = norm_last(x, gain).astype(BF16)
    norm_ref[pl.ds(row * main, main), :] = normed[:main]
    if sz.rest:
        h, q = divmod(row, sz.half)
        norm_ref[pl.ds(sz.rows * main + q * LANES + h * sz.rest, sz.rest), :] = normed[main:]


def project_edges(sz, length, first, gate, value, pick, norm_ref, store):
    main, ch = sz.whole * LANES, sz.channels
    lane = lax.broadcasted_iota(jnp.int32, (1, LANES), 1)

    def live(tile):
        if tile < sz.rows * sz.whole:
            row, m = divmod(tile, sz.whole)
            return ((first + row < length) & (m * LANES + lane < length)).astype(F32)
        q = tile - sz.rows * sz.whole
        second = lane >= sz.rest
        row = first + q + jnp.where(second, sz.half, 0)
        k = main + lane - jnp.where(second, sz.rest, 0)
        return ((row < length) & (k < length)).astype(F32)

    weights = jnp.concatenate([dot(pick, w, 1, 1).astype(BF16) for w in (gate, value)], axis=0)
    step = 2 if sz.tiles % 2 == 0 else 1
    for tile in range(0, sz.tiles, step):
        n = norm_ref[pl.ds(tile * LANES, step * LANES), :]
        mask = jnp.concatenate([live(tile + s) for s in range(step)], axis=1)
        both = dot(weights, n, 1, 1)
        edge = (sigmoid(both[:ch]) * (both[ch:] * mask)).astype(BF16)
        for g in range(sz.group):
            store(
                g,
                slice(tile * LANES, (tile + step) * LANES),
                edge[g * sz.chans : (g + 1) * sz.chans],
            )


def left_kernel(sz, len_ref, x_ref, ln_ref, w_ref, out_ref, norm_ref):
    ch = sz.channels
    gain = ln_ref[...]
    for row in range(sz.rows):
        normalise(sz, row, x_ref[row].astype(F32), gain, norm_ref)
    r = lax.broadcasted_iota(jnp.int32, (ch, ch), 0)
    e = lax.broadcasted_iota(jnp.int32, (ch, ch), 1)

    def store(g, lanes, edge):
        out_ref[g, :, lanes] = edge
        out_ref[sz.group + g, :, lanes] = edge

    first = position() * sz.rows
    pick = (r == e).astype(BF16)
    project_edges(sz, len_ref[0], first, w_ref[0], w_ref[1], pick, norm_ref, store)


def right_kernel(sz, len_ref, x_ref, ln_ref, w_ref, *refs):
    near, norm_ref = refs[: sz.group], refs[sz.group]
    cd, ch = sz.chans, sz.channels
    gain = ln_ref[...]
    for row in range(sz.rows):
        normalise(sz, row, x_ref[row].astype(F32), gain, norm_ref)
    me = position()
    mine = me & (sz.group - 1)
    r = lax.broadcasted_iota(jnp.int32, (ch, ch), 0)
    e = lax.broadcasted_iota(jnp.int32, (ch, ch), 1)
    partner = (sz.group - r // cd) & (sz.group - 1)
    pick = ((partner ^ mine) * cd + r % cd == e).astype(BF16)

    def store(g, lanes, edge):
        near[g][:, lanes] = edge

    project_edges(sz, len_ref[0], me * sz.rows, w_ref[2], w_ref[3], pick, norm_ref, store)


def relay_kernel(sz, x_ref, far_ref, *refs):
    near, (own_ref, far_rows_ref, pair_ref) = refs[: sz.group], refs[sz.group :]
    cd, me = sz.chans, position()
    mine = me & (sz.group - 1)
    upper = me >= sz.group
    for row in range(sz.rows):
        x = x_ref[row].astype(F32)
        rows = pl.ds(row * sz.columns, sz.columns)
        own_ref[rows, :] = jnp.where(upper, x[sz.columns :], x[: sz.columns])
        far_rows_ref[rows, :] = far_ref[row].astype(F32)
    for base, wide_ref in enumerate((own_ref, far_rows_ref)):
        for g in range(sz.group):
            for row in range(sz.rows):
                block = wide_ref[pl.ds(row * sz.columns + g * sz.rows, sz.rows), :]
                pair_ref[base, g, row * sz.rows : (row + 1) * sz.rows, :] = block
    for slot, partner in enumerate(sz.partners):
        for base in range(2):
            for t in range(sz.block_tiles):
                at = (base * sz.block_tiles + t) * LANES
                block = pair_ref[base, mine ^ partner, t * cd : (t + 1) * cd, :]
                near[slot][:, at : at + LANES] = block.astype(BF16)


def unpack(sz, ref, owner, main_ref, rest_ref):
    cd, w = sz.chans, sz.whole
    for tile in range(sz.tiles):
        block = ref[:, tile * LANES : (tile + 1) * LANES].astype(F32)
        if tile < sz.rows * w:
            row, m = divmod(tile, w)
            main_ref[m, pl.ds(pl.multiple_of((owner * sz.rows + row) * cd, 8), cd), :] = block
        else:
            row = owner * sz.rows + tile - sz.rows * w
            rest_ref[pl.ds(pl.multiple_of(row * cd, 8), cd), :] = block
            rest_ref[pl.ds(pl.multiple_of((row + sz.half) * cd, 8), cd), :] = pltpu.roll(
                block, sz.rest, 1
            )


def matrix(sz, c, size, main_ref, rest_ref):
    cd, w = sz.chans, sz.whole
    parts = [main_ref[m, pl.ds(c, size, stride=cd), :].astype(BF16) for m in range(w)]
    if sz.rest:
        parts.append(rest_ref[pl.ds(c, size, stride=cd), :].astype(BF16)[:, : sz.rest])
    return jnp.concatenate(parts, axis=1) if len(parts) > 1 else parts[0]


def arrange_kernel(sz, *refs):
    near, (out_ref, main_ref, rest_ref) = refs[: sz.group], refs[sz.group :]
    mine = position() & (sz.group - 1)
    for slot, partner in enumerate(sz.partners):
        unpack(sz, near[slot], mine ^ partner, main_ref, rest_ref)
    for c in range(sz.chans):
        out_ref[c] = matrix(sz, c, sz.columns, main_ref, rest_ref)


def outer_kernel(
    sz, left_ref, right_ref, away_ref, out_ref, lmain_ref, lrest_ref, omain_ref, orest_ref, sems
):
    cd, n, w, half = sz.chans, sz.crop, sz.whole, sz.half
    for d in range(sz.devices):
        unpack(sz, left_ref.at[d], jnp.int32(d), lmain_ref, lrest_ref)
    for c in range(cd):
        outer = dot(right_ref[c], matrix(sz, c, n, lmain_ref, lrest_ref), 1, 1)
        for m in range(w):
            omain_ref[m, pl.ds(c, sz.columns, stride=cd), :] = outer[:, m * LANES : (m + 1) * LANES]
        if sz.rest:
            part = outer[:, w * LANES :]
            orest_ref[pl.ds(c, sz.columns, stride=cd), :] = jnp.concatenate([part, part], axis=1)
    low = lax.broadcasted_iota(jnp.int32, (cd, LANES), 1) < sz.rest
    copies = [
        pltpu.make_async_copy(out_ref.at[g], away_ref.at[g], sems.at[g]) for g in range(sz.group)
    ]
    for g in range(sz.group):
        start = g * sz.rows
        for tile in range(sz.tiles):
            if tile < sz.rows * w:
                row, m = divmod(tile, w)
                block = omain_ref[m, pl.ds((start + row) * cd, cd), :]
            else:
                at = start + tile - sz.rows * w
                block = jnp.where(
                    low,
                    orest_ref[pl.ds(at * cd, cd), :],
                    orest_ref[pl.ds((at + half) * cd, cd), :],
                )
            out_ref[g, :, tile * LANES : (tile + 1) * LANES] = block.astype(BF16)
        copies[g].start()
    for copy in copies:
        copy.wait()


def take_columns(sz, near, cols_ref):
    cd, me = sz.chans, position()
    for slot, partner in enumerate(sz.partners):
        for base, owner in ((0, me ^ partner), (1, me ^ (sz.group + partner))):
            for t in range(sz.block_tiles):
                at = (base * sz.block_tiles + t) * LANES
                rows = pl.ds(pl.multiple_of(owner * sz.block + t * cd, 8), cd)
                cols_ref[rows, :] = near[slot][:, at : at + LANES].astype(F32)


def gating_kernel(sz, lnp_ref, gate_ref, *refs):
    near, (x_ref, gating_ref, cols_ref) = refs[: sz.group], refs[sz.group :]
    take_columns(sz, near, cols_ref)
    for j in range(sz.rows):
        x = cols_ref[pl.ds(j, sz.crop, stride=sz.rows), :]
        x_ref[j] = x.astype(BF16)
        normed = norm_last(x, lnp_ref[...]).astype(BF16)
        gating_ref[j] = sigmoid(dot(normed, gate_ref[...], 1, 0)).astype(BF16)


def update_kernel(
    sz, x_ref, gating_ref, lnh_ref, tri_ref, lna_ref, biasw_ref, sums_ref,
    first_ref, col_ref, bias_ref, brow_ref,
):
    n, w, half, ch = sz.crop, sz.whole, sz.half, sz.channels
    gain_h = jnp.transpose(jnp.broadcast_to(lnh_ref[...], (ch, ch)))
    tri = tri_ref[...]

    def update(tile):
        block = sums_ref[:, :, tile * LANES : (tile + 1) * LANES].astype(F32).reshape(ch, LANES)
        average = jnp.mean(block, axis=0, keepdims=True)
        centred = block - average
        variance = jnp.mean(centred * centred, axis=0, keepdims=True)
        hidden = (centred * lax.rsqrt(variance + EPS) * gain_h).astype(BF16)
        return dot(hidden, tri, 0, 0)

    rest = [update(sz.rows * w + q) for q in range(half)] if sz.rest else None
    for j in range(sz.rows):
        parts = [update(j * w + m) for m in range(w)]
        if sz.rest:
            h, q = divmod(j, half)
            parts.append(rest[q][h * sz.rest : (h + 1) * sz.rest])
        change = jnp.concatenate(parts, axis=0) if len(parts) > 1 else parts[0]
        first = (x_ref[j].astype(F32) + gating_ref[j].astype(F32) * change).astype(BF16)
        first_ref[j] = first
        col = norm_last(first.astype(F32), lna_ref[...]).astype(BF16)
        col_ref[j] = col
        heads = biasw_ref.shape[1]
        brow_ref[pl.ds(j * heads, heads), :] = dot(biasw_ref[...], col, 0, 1)
    rows = brow_ref[...]
    part = rows.shape[0] // 2
    one, two = rows[:part], rows[part:]
    message = [one[:, : w * LANES], two[:, : w * LANES]]
    if sz.rest:
        message += [one[:, w * LANES :], two[:, w * LANES :]]
    bias_ref[...] = jnp.concatenate(message, axis=1).astype(BF16)


def project_kernel(sz, col_ref, q_ref, k_ref, v_ref, g_ref, qo_ref, ko_ref, vo_ref, go_ref):
    joined = jnp.concatenate([ref[...] for ref in (q_ref, k_ref, v_ref, g_ref)], axis=1)
    width = q_ref.shape[1]
    for j in range(sz.rows):
        made = dot(col_ref[j], joined, 1, 0)
        qo_ref[j] = made[:, :width].astype(BF16)
        ko_ref[j] = made[:, width : 2 * width].astype(BF16)
        vo_ref[j] = made[:, 2 * width : 3 * width].astype(BF16)
        go_ref[j] = sigmoid(made[:, 3 * width :])


def attend_kernel(
    sz, heads, steps, len_ref, q_ref, k_ref, v_ref, g_ref, first_ref, aout_ref, *refs
):
    bias_refs, (away_ref, out_ref, rows_ref, bias_ref, sems) = refs[:-5], refs[-5:]
    n, w, ch = sz.crop, sz.whole, sz.channels
    length, me = len_ref[0], position()
    width = q_ref.shape[2]
    hd = width // heads
    per = sz.rows * heads // 2
    for ref, offsets in zip(bias_refs, steps):
        for place, offset in enumerate(offsets):
            block = ref[place].astype(F32) * LOG2E
            for p in range(2):
                at = pl.ds(pl.multiple_of(((me ^ offset) * 2 + p) * per, 8), per)
                for m in range(w):
                    rows_ref[m, at, :] = block[:, (p * w + m) * LANES : (p * w + m + 1) * LANES]
                if sz.rest:
                    tail = block[:, 2 * w * LANES :]
                    rows_ref[w, at, :] = pltpu.roll(tail, sz.rest, 1) if p else tail
    lane = lax.broadcasted_iota(jnp.int32, (1, LANES), 1)
    for m in range(w + (sz.rest > 0)):
        lanes = slice(m * LANES, min((m + 1) * LANES, n))
        dead = jnp.where(m * LANES + lane < length, 0.0, -1e9 * LOG2E).astype(F32)
        for head in range(heads):
            rows = rows_ref[m, pl.ds(head, n, stride=heads), :] + dead
            bias_ref[head, :, lanes] = rows[:, : lanes.stop - lanes.start]
    column = lax.broadcasted_iota(jnp.int32, (1, width), 1)
    head_masks = [(column >= h * hd) & (column < (h + 1) * hd) for h in range(heads)]
    scale = (hd ** (-0.5)) * LOG2E
    ones = jnp.ones((n, width), BF16)

    def score(j):
        query = [q_ref[j] * head_masks[h].astype(BF16) for h in range(heads)]
        return dot(jnp.concatenate(query, axis=0), k_ref[j], 1, 1)

    copies = [
        pltpu.make_async_copy(out_ref.at[j], away_ref.at[j], sems.at[j]) for j in range(sz.rows)
    ]
    scores = score(0)
    for j in range(sz.rows):
        now = scores
        if j + 1 < sz.rows:
            scores = score(j + 1)
        weights = []
        for h in range(heads):
            part = now[h * n : (h + 1) * n] * scale + bias_ref[h]
            weights.append(jnp.exp2(part - jnp.max(part, axis=1, keepdims=True)).astype(BF16))
        values = jnp.concatenate([v_ref[j], ones], axis=1)
        mixed = dot(jnp.concatenate(weights, axis=0), values, 1, 0)
        attended, total = mixed[:n, :width], mixed[:n, width:]
        for h in range(1, heads):
            rows = slice(h * n, (h + 1) * n)
            attended = jnp.where(head_masks[h], mixed[rows, :width], attended)
            total = jnp.where(head_masks[h], mixed[rows, width:], total)
        gated = (attended / total * g_ref[j]).astype(BF16)
        out_ref[j] = (first_ref[j].astype(F32) + dot(gated, aout_ref[...], 1, 0)).astype(BF16)
        copies[j].start()
    for copy in copies:
        copy.wait()


def spread(block, devices):
    pieces, offsets = [block[None]], [[0]]
    bit = devices // 2
    while bit:
        held = jnp.concatenate(pieces, axis=0) if len(pieces) > 1 else pieces[0]
        known = [o for part in offsets for o in part]
        pieces.append(lax.ppermute(held, AXES, [(d, d ^ bit) for d in range(devices)]))
        offsets.append([o ^ bit for o in known])
        bit //= 2
    return pieces, offsets


def shards(
    devices,
    pair_rep, length, ln_pair, tri_in, tri_gate, ln_hidden, tri_out, ln_att,
    att_q, att_k, att_v, att_bias, att_gate, att_out,
):
    rows, crop, ch = pair_rep.shape
    heads = att_bias.shape[1]
    sz = Sizes(rows, crop, devices, ch)
    n, cd = crop, sz.chans
    def bound(kernel, *extra):
        def run(*refs):
            return kernel(sz, *extra, *refs)

        return run

    shape = jax.ShapeDtypeStruct
    g, t, bt = sz.group, sz.tiles, sz.block_tiles

    def slab(tiles, *lead):
        return shape((*lead, cd, tiles * LANES), BF16)

    def send(blocks):
        return [
            lax.ppermute(block, AXES, [(d, d ^ partner) for d in range(devices)])
            if partner
            else block
            for partner, block in zip(sz.partners, blocks)
        ]

    upper = (lax.axis_index(AXES) >= g).astype(jnp.int32)
    far = lax.ppermute(
        lax.dynamic_slice_in_dim(pair_rep, (1 - upper) * sz.columns, sz.columns, 1),
        AXES,
        [(d, d ^ g) for d in range(devices)],
    )
    left = call(
        bound(left_kernel),
        slab(t, devices),
        (length, pair_rep, ln_pair[None], tri_in),
        scratch=[pltpu.VMEM((rows * crop, ch), BF16)],
        smem=(0,),
        name="left",
    )
    rights = call(
        bound(right_kernel),
        [slab(t)] * g,
        (length, pair_rep, ln_pair[None], tri_in),
        scratch=[pltpu.VMEM((rows * crop, ch), BF16)],
        smem=(0,),
        name="right",
    )
    pairs = call(
        bound(relay_kernel),
        [slab(2 * bt)] * g,
        (pair_rep, far),
        scratch=[
            pltpu.VMEM((rows * sz.columns, ch), F32),
            pltpu.VMEM((rows * sz.columns, ch), F32),
            pltpu.VMEM((2, g, bt * cd, ch), F32),
        ],
        name="relay",
        cost=pl.CostEstimate(flops=10**11, bytes_accessed=10**6, transcendentals=0),
    )
    left = lax.all_to_all(left, AXES, split_axis=0, concat_axis=0, tiled=True)
    near = send(rights)
    rest = sz.rest > 0
    left, pairs = lax.optimization_barrier((left, pairs))
    column_rows = sz.columns * cd
    right = call(
        bound(arrange_kernel),
        shape((cd, sz.columns, n), BF16),
        tuple(near),
        scratch=[
            pltpu.VMEM((sz.whole, column_rows, LANES), F32),
            pltpu.VMEM((column_rows if rest else 8, LANES), F32),
        ],
        name="arrange",
    )
    outer = call(
        bound(outer_kernel),
        slab(t, g),
        (left, right),
        scratch=[
            pltpu.VMEM((g, cd, t * LANES), BF16),
            pltpu.VMEM((sz.whole, n * cd, LANES), F32),
            pltpu.VMEM((n * cd if rest else 8, LANES), F32),
            pltpu.VMEM((sz.whole, column_rows, LANES), F32),
            pltpu.VMEM((column_rows if rest else 8, LANES), F32),
            pltpu.SemaphoreType.DMA((g,)),
        ],
        away=True,
        name="outer",
    )
    sums = lax.all_to_all(
        outer, AXES, split_axis=0, concat_axis=0, tiled=True,
        axis_index_groups=[list(range(g)), list(range(g, devices))],
    )
    pairs = send(pairs)
    columns, gating = call(
        bound(gating_kernel),
        [shape((rows, n, ch), BF16)] * 2,
        (ln_pair[None], tri_gate, *pairs),
        scratch=[pltpu.VMEM((devices * sz.block + cd, ch), F32)],
        name="gating",
    )
    first, col, bias = call(
        bound(update_kernel),
        [
            shape((rows, n, ch), BF16),
            shape((rows, n, ch), BF16),
            shape((rows * heads // 2, 2 * n), BF16),
        ],
        (
            columns, gating, ln_hidden[None], tri_out, ln_att[None], att_bias, sums,
        ),
        scratch=[pltpu.VMEM((rows * heads, n), F32)],
        name="update",
    )
    pieces, steps = spread(bias, devices)
    query, key, value, gate = call(
        bound(project_kernel),
        [
            shape((rows, n, att_q.shape[1]), BF16),
            shape((rows, n, att_q.shape[1]), BF16),
            shape((rows, n, att_q.shape[1]), BF16),
            shape((rows, n, att_q.shape[1]), F32),
        ],
        (col, att_q, att_k, att_v, att_gate),
        name="project",
    )
    out = call(
        bound(attend_kernel, heads, steps),
        shape((rows, n, ch), BF16),
        (length, query, key, value, gate, first, att_out, *pieces),
        scratch=[
            pltpu.VMEM((rows, n, ch), BF16),
            pltpu.VMEM((-(-n // LANES), n * heads, LANES), F32),
            pltpu.VMEM((heads, n, n), F32),
            pltpu.SemaphoreType.DMA((rows,)),
        ],
        smem=(0,),
        away=True,
        name="attend",
    )
    return jnp.swapaxes(out, 0, 1)


def solution(mesh):
    devices = mesh.shape["row"] * mesh.shape["node"]

    def body(*args):
        return shards(devices, *args)

    return jax.shard_map(
        body,
        mesh=mesh,
        in_specs=(P(("grp", "row", "node"), None, None), P("grp")) + (P(),) * 12,
        out_specs=P("grp", AXES, None),
        check_vma=False,
    )
```
